32 devices in a mesh: expert: 8 (over y, x, core), shard: 4 (over z).
Axes of the slice: x: 2, y: 2, z: 4, core: 2. Of those that a mesh axis runs over, the one named last changes fastest.
Arguments:
- hidden_in: bfloat16 [4096, 2048], P(('expert', 'shard')), may hold values from -6 to 6
- segments: int32 [4096], P(('expert', 'shard')), may hold values from 0 to 7, never falling along the last dimension, each value on 1 to 1024 neighbouring positions
- routes: int32 [4096, 8], P(('expert', 'shard')), may hold values from 0 to 15, all different within a row; in each aligned block of 128 rows (0 to 127, 128 to 255, ...) at most 96 rows name the same one
- norm_gains: bfloat16 [1, 2, 2048], P(None, None, 'shard'), may hold values from 0.099609375 to 1.8984375
- qk_gains: bfloat16 [1, 2, 128], P(None, None, 'shard'), may hold values from 0.099609375 to 1.8984375
- w_qkv: bfloat16 [1, 2048, 5120], P(None, 'shard'), may hold values from -0.125 to 0.125
- w_attn_out: bfloat16 [1, 4096, 2048], P(None, 'shard'), may hold values from -0.375 to 0.375
- w_router: bfloat16 [1, 2048, 16], P(None, 'shard'), may hold values from -0.0625 to 0.0625
- w_gate_up: bfloat16 [1, 16, 2048, 1536], P(None, 'expert', 'shard'), may hold values from -0.125 to 0.125
- w_down: bfloat16 [1, 16, 768, 2048], P(None, 'expert', None, 'shard'), may hold values from -0.875 to 0.875
- cotangent: bfloat16 [4096, 2048], P(('expert', 'shard')), may hold values from -6 to 6
Outputs:
- hidden_out: bfloat16 [4096, 2048], P(('expert', 'shard'))
- grad_hidden: float32 [4096, 2048], P(('expert', 'shard'))
- grad_norm_gains: float32 [1, 2, 2048], P(None, None, 'shard')
- grad_qk_gains: float32 [1, 2, 128], P(None, None, 'shard')
- grad_w_qkv: float32 [1, 2048, 5120], P(None, 'shard')
- grad_w_attn_out: float32 [1, 4096, 2048], P(None, 'shard')
- grad_w_router: float32 [1, 2048, 16], P(None, 'shard')
- grad_w_gate_up: float32 [1, 16, 2048, 1536], P(None, 'expert', 'shard')
- grad_w_down: float32 [1, 16, 768, 2048], P(None, 'expert', None, 'shard')
The draws below stay inside these ranges and needn't reach their ends.
Inputs may be any that keep to these rules, and one draw needn't show every extreme that they name: `segments`: segment numbers never fall along the tokens; a document has at most 1024 tokens, and one has exactly that many. `routes`: A row names 8 different experts. Tokens of one device are the aligned blocks of 128 rows; within such a block no expert is named more than 96 times, and in some blocks an expert is named exactly 96 times.
All inputs are finite; a program needn't handle non-finite values.
Results may differ from the reference program's by a relative error of at most 0.024.
Values may be sent and summed in bfloat16 or wider, within the bound.
A program may use at most 320 MiB of HBM per device.

```python
import math
import jax
import jax.numpy as jnp
import numpy as np
from jax import lax

D = 2048
HEADS = 32
KV_HEADS = 4
HEAD_DIM = 128
FF = 768
TOP = 8
LAYERS = 1
TOK_DEV = 128
EXPERTS = 16
CAP = 96
TOKENS = 4096
GROUP = 512
QKV = 5120
DOCS = 8
N_EXPERT = 8
N_SHARD = 4


def block_levels(rng, shape, split, low, largest):
    def one(dim, shards_of):
        heights = jax.random.uniform(jax.random.fold_in(jax.random.fold_in(rng, 6), dim), (shards_of,), jnp.float32, low / len(split), largest / len(split))
        return jnp.repeat(jnp.exp(heights), shape[dim] // shards_of).reshape((-1,) + (1,) * (len(shape) - dim - 1))

    gain = one(*split[0])
    for cut in split[1:]:
        gain = gain * one(*cut)
    return gain


def split_up(count, total, most, slope):
    weights = [(1 << 20) // math.isqrt(grade ** slope) + 1 for grade in range(2, count + 1)]
    rest, counts = total - most - (count - 1), [1] * (count - 1)
    while rest > 0:
        free = [i for i in range(count - 1) if counts[i] < most]
        pool, remaining = sum([weights[i] for i in free]), rest
        for i in free:
            more = min(most - counts[i], max(1, remaining * weights[i] // pool), rest)
            counts[i] = counts[i] + more
            rest = rest - more
    return np.array([most] + counts)


def ragged(own_key, count, total, most, lean):
    if count == 2:
        one = jax.random.randint(own_key, (), max(1, total - most), min(most, total - 1) + 1)
        return jnp.stack([one, total - one])
    tallies = jnp.asarray(split_up(count, total, most, lean), jnp.int32)
    couples = (count - 1) // 2
    giver, taker = tallies[1:1 + 2 * couples:2], tallies[2:2 + 2 * couples:2]
    slack = jnp.minimum(giver - 1, most - taker)
    passed = jax.random.randint(jax.random.fold_in(own_key, 1), (couples,), 0, 1 << 20) % (slack + 1)
    tallies = tallies.at[1:1 + 2 * couples:2].set(giver - passed).at[2:2 + 2 * couples:2].set(taker + passed)
    return tallies[jax.random.permutation(jax.random.fold_in(own_key, 2), count)]


def shared_out(stream_key, own, number, rows, count, top, most, skew):
    order = jax.random.permutation(stream_key, count)
    heavy_load, ordinary = portions_of(count, rows * top, most, skew, True), portions_of(count, rows * top, most, skew, False)
    places = jnp.arange(count)

    def named(sizes, rotation):
        used = int((sizes > 0).sum())
        fixed = max(1, used // 4)
        moved = fixed + (places - fixed + rotation * (used - fixed)) % max(1, count - fixed)
        return jnp.zeros((count,), jnp.int32).at[order[jnp.where(places < fixed, places, moved)]].set(jnp.asarray(sizes, jnp.int32))

    sizes = jnp.where(number % 4 == 0, named(heavy_load, number // 4), named(ordinary, number - number // 4 - 1))
    mixed = jax.random.permutation(jax.random.fold_in(own, 3), count)
    giver, sink = mixed[0:count // 2 * 2:2], mixed[1:count // 2 * 2:2]
    slack = jnp.minimum(sizes[giver] - 1, most - sizes[sink]) // 2
    slack = jnp.where((giver == order[0]) | (sink == order[0]) | (sizes[sink] == 0), 0, jnp.maximum(slack, 0))
    moved = jax.random.randint(jax.random.fold_in(own, 4), (count // 2,), 0, 1 << 20) % (slack + 1)
    sizes = sizes.at[giver].add(-moved).at[sink].add(moved)
    labels = jnp.searchsorted(jnp.cumsum(sizes), jnp.arange(rows * top), side="right").astype(jnp.int32)
    listing = labels.reshape(top, rows).T
    listing = listing[jax.random.permutation(jax.random.fold_in(own, 1), rows)]
    rotation = jax.random.randint(jax.random.fold_in(own, 2), (rows, 1), 0, top)
    return jnp.take_along_axis(listing, (jnp.arange(top)[None, :] + rotation) % top, axis=1)


def portions_of(number_of, total, limit, lean, full):
    portions = [(1 << 20) // math.isqrt(rank ** lean) + 1 for rank in range(1, number_of + 1)]
    largest = limit if full else min(limit, max(-(-total // number_of), total * portions[0] // sum(portions)))
    least = 1 if total - largest >= number_of - 1 else 0
    holding, spare = [largest] + [least] * (number_of - 1), total - largest - least * (number_of - 1)
    while spare > 0:
        movable = [i for i in range(1, number_of) if holding[i] < largest] or [i for i in range(1, number_of) if holding[i] < limit]
        pool, budget = sum([portions[i] for i in movable]), spare
        for i in movable:
            more = min(limit - holding[i], max(1, budget * portions[i] // pool), spare)
            holding[i] = holding[i] + more
            spare = spare - more
    return np.array(holding)


def bell_draw(rng, shape, width, reach, split=(), kind=jnp.bfloat16):
    drawn = width * jax.random.normal(rng, shape, jnp.float32)
    if split:
        drawn = drawn * block_levels(rng, shape, split, -0.22, 0.18)
    return jnp.clip(drawn, -reach, reach).astype(kind)


def setup_inputs(seed: int = 0) -> dict:
    splits = jax.random.split(jax.random.key(seed), 12)
    hidden_in = bell_draw(splits[0], (TOKENS, D), 1.0, 6.0, ((0, 32),))
    segments = jnp.searchsorted(jnp.cumsum(ragged(splits[1], DOCS, TOKENS, 8 * TOK_DEV, 1)), jnp.arange(TOKENS), side="right").astype(jnp.int32)
    routes_keys = jax.random.split(jax.random.fold_in(splits[2], 1), TOKENS // TOK_DEV)
    routes_turns = jax.random.permutation(jax.random.fold_in(splits[2], 3), TOKENS // TOK_DEV)
    routes = jax.vmap(lambda own, number: shared_out(jax.random.fold_in(splits[2], 2), own, number, TOK_DEV, EXPERTS, TOP, CAP, 2))(routes_keys, routes_turns).reshape((TOKENS, TOP))
    norm_gains = jnp.clip(1.0 + 0.18 * jax.random.normal(splits[3], (LAYERS, 2, D), jnp.float32), 0.099609375, 1.8984375).astype(jnp.bfloat16)
    qk_gains = jnp.clip(1.0 + 0.18 * jax.random.normal(splits[4], (LAYERS, 2, HEAD_DIM), jnp.float32), 0.099609375, 1.8984375).astype(jnp.bfloat16)
    w_qkv = bell_draw(splits[5], (LAYERS, D, QKV), D ** -0.5, 0.125, ((1, 4),))
    w_attn_out = bell_draw(splits[6], (LAYERS, HEADS * HEAD_DIM, D), (HEADS * HEAD_DIM // 16) ** -0.5, 0.375, ((1, 4),))
    w_router = bell_draw(splits[7], (LAYERS, D, EXPERTS), (4 * D) ** -0.5, 0.0625, ((1, 4),))
    w_gate_up = bell_draw(splits[8], (LAYERS, EXPERTS, D, 2 * FF), D ** -0.5, 0.125, ((1, 8), (2, 4)))
    w_down = bell_draw(splits[9], (LAYERS, EXPERTS, FF, D), (FF // 16) ** -0.5, 0.875, ((1, 8), (3, 4)))
    cotangent = bell_draw(splits[10], (TOKENS, D), 1.0, 6.0, ((0, 32),))
    return dict(hidden_in=hidden_in, segments=segments, routes=routes, norm_gains=norm_gains, qk_gains=qk_gains, w_qkv=w_qkv, w_attn_out=w_attn_out, w_router=w_router, w_gate_up=w_gate_up, w_down=w_down, cotangent=cotangent)


@jax.custom_vjp
def low(v):
    return lax.optimization_barrier(v.astype(jnp.bfloat16)).astype(jnp.float32)

@jax.custom_vjp
def low_back(v):
    return v

def low_keep(v):
    return (low(v), None)

def low_pass(kept, grad):
    return (grad,)

def back_keep(v):
    return (v, None)

def back_low(kept, grad):
    return (low(grad),)
low.defvjp(low_keep, low_pass)
low_back.defvjp(back_keep, back_low)
highest = lax.Precision.HIGHEST
eps_norm = 1e-06
rope_base = 1000000.0
neg_fill = -1e+30

def matmul_high(left, right):
    return jnp.dot(left, right, precision=highest, preferred_element_type=jnp.float32)

def rms_scale(value, gain_vec):
    return value * lax.rsqrt(lax.optimization_barrier(jnp.mean(value * value, axis=-1, keepdims=True)) + eps_norm) * gain_vec

def rotary_tables(position, head_width):
    half_width = head_width // 2
    frequency = rope_base ** (-(jnp.arange(half_width, dtype=jnp.float32) * 2.0) / head_width)
    angles = position[:, None] * frequency[None, :]
    return (jnp.cos(angles), jnp.sin(angles))

def apply_rotary(value, cos_table, sin_table):
    half_width = value.shape[-1] // 2
    lower_half = value[..., :half_width]
    upper_half = value[..., half_width:]
    cos_rows = cos_table[:, None, :]
    sin_rows = sin_table[:, None, :]
    return jnp.concatenate([lower_half * cos_rows - upper_half * sin_rows, upper_half * cos_rows + lower_half * sin_rows], axis=-1)

def post_qkv(qkv_out, qk_gain, cos_table, sin_table):
    length = qkv_out.shape[0]
    q_width = HEADS * HEAD_DIM
    kv_width = KV_HEADS * HEAD_DIM
    queries = qkv_out[:, :q_width].reshape(length, HEADS, HEAD_DIM)
    key_rows = qkv_out[:, q_width:q_width + kv_width].reshape(length, KV_HEADS, HEAD_DIM)
    values = qkv_out[:, q_width + kv_width:].reshape(length, KV_HEADS, HEAD_DIM)
    queries = apply_rotary(rms_scale(queries, qk_gain[0]), cos_table, sin_table)
    key_rows = apply_rotary(rms_scale(key_rows, qk_gain[1]), cos_table, sin_table)
    return (queries, key_rows, values)

def attend_group(queries, key_rows, values, seg_part):
    length = queries.shape[0]
    query_group = queries.reshape(length, KV_HEADS, HEADS // KV_HEADS, HEAD_DIM)
    scores = jnp.einsum('tkgd,skd->kgts', query_group, key_rows, precision=highest, preferred_element_type=jnp.float32) * HEAD_DIM ** (-0.5)
    scores = low_back(scores)
    positions = jnp.arange(length, dtype=jnp.int32)
    allowed = (positions[None, :] <= positions[:, None]) & (seg_part[None, :] == seg_part[:, None])
    masked = jnp.where(allowed[None, None], scores, neg_fill)
    row_max = lax.optimization_barrier(jnp.max(masked, axis=-1, keepdims=True))
    exp_scores = jnp.exp(masked - row_max)
    soft_low = low(exp_scores / lax.optimization_barrier(jnp.sum(exp_scores, axis=-1, keepdims=True)))
    mixed_heads = jnp.einsum('kgts,skd->tkgd', soft_low, values, precision=highest, preferred_element_type=jnp.float32)
    return mixed_heads.reshape(length, HEADS * HEAD_DIM)

def route_tables(routes):
    flat_routes = routes.reshape(-1).astype(jnp.int32)
    expert_ids = jnp.arange(EXPERTS, dtype=jnp.int32)
    one_hot = (flat_routes[:, None] == expert_ids[None, :]).astype(jnp.int32)
    slot_ranks = lax.optimization_barrier(jnp.sum((jnp.cumsum(one_hot, axis=0) - one_hot) * one_hot, axis=1)).astype(jnp.int32)
    slot_count = N_EXPERT * N_SHARD * CAP
    places = flat_routes * slot_count + slot_ranks
    assign_of = jnp.zeros((EXPERTS * slot_count,), jnp.int32).at[places].set(jnp.arange(flat_routes.shape[0], dtype=jnp.int32))
    live_slots = jnp.zeros((EXPERTS * slot_count,), jnp.float32).at[places].set(1.0)
    return (assign_of.reshape(EXPERTS, slot_count), live_slots.reshape(EXPERTS, slot_count))

def expert_mix(ffn_in, routes, assign_of, live_slots, router_weight, gate_up_weight, down_weight):
    router_logits = matmul_high(ffn_in, router_weight)
    chosen = jnp.take_along_axis(router_logits, routes, axis=1)
    chosen_exp = jnp.exp(chosen - lax.optimization_barrier(jnp.max(chosen, axis=1, keepdims=True)))
    route_weight = chosen_exp / lax.optimization_barrier(jnp.sum(chosen_exp, axis=1, keepdims=True))
    weight_flat = route_weight.reshape(-1)

    def one_expert(running, item_pack):
        gate_up_one, down_one, assign, live_flag = item_pack
        token_rows = assign // TOP
        rows_in = low_back(ffn_in[token_rows])
        pre_gu = low_back(matmul_high(rows_in, gate_up_one))
        pre_gate = pre_gu[:, :FF]
        pre_up = pre_gu[:, FF:]
        hidden = low(pre_gate * jax.nn.sigmoid(pre_gate) * pre_up)
        result = low_back(low(matmul_high(hidden, down_one)))
        coeff = weight_flat[assign] * live_flag
        return (running.at[token_rows].add(result * coeff[:, None]), None)
    mixed_rows, _ = lax.scan(jax.checkpoint(one_expert), jnp.zeros((TOKENS, D), jnp.float32), (gate_up_weight, down_weight, assign_of, live_slots))
    return mixed_rows

def layer_forward(residual, segments, routes, assign_of, live_slots, norm_gain, qk_gain, qkv_weight, out_weight, router_weight, gate_up_weight, down_weight):
    attn_in = low(rms_scale(residual, norm_gain[0]))
    qkv_out = low_back(matmul_high(attn_in, qkv_weight))
    cos_table, sin_table = rotary_tables(jnp.arange(GROUP, dtype=jnp.float32), HEAD_DIM)

    def one_group(item_pack):
        qkv_part, seg_part = item_pack
        queries, key_rows, values = post_qkv(qkv_part, qk_gain, cos_table, sin_table)
        return attend_group(low(queries), low(key_rows), low(values), seg_part)
    heads_out = lax.map(jax.checkpoint(one_group), (qkv_out.reshape(N_EXPERT, GROUP, QKV), segments.reshape(N_EXPERT, GROUP)))
    attn_mix = low_back(low(heads_out.reshape(TOKENS, HEADS * HEAD_DIM)))
    middle = residual + low_back(matmul_high(attn_mix, out_weight))
    ffn_in = low(rms_scale(middle, norm_gain[1]))
    return middle + expert_mix(ffn_in, routes, assign_of, live_slots, router_weight, gate_up_weight, down_weight)

def reference(hidden_in, segments, routes, norm_gains, qk_gains, w_qkv, w_attn_out, w_router, w_gate_up, w_down, cotangent):
    assign_of, live_slots = route_tables(routes)

    def forward(residual, gains_all, qk_all, qkv_all, out_all, router_all, gate_up_all, down_all):
        for layer_index in range(LAYERS):
            residual = layer_forward(residual, segments, routes, assign_of, live_slots, gains_all[layer_index], qk_all[layer_index], qkv_all[layer_index], out_all[layer_index], router_all[layer_index], gate_up_all[layer_index], down_all[layer_index])
        return residual
    result, pull_back = jax.vjp(forward, hidden_in.astype(jnp.float32), norm_gains.astype(jnp.float32), qk_gains.astype(jnp.float32), w_qkv.astype(jnp.float32), w_attn_out.astype(jnp.float32), w_router.astype(jnp.float32), w_gate_up.astype(jnp.float32), w_down.astype(jnp.float32))
    grads = pull_back(cotangent.astype(jnp.float32))
    return (result.astype(jnp.bfloat16), grads[0], grads[1], grads[2], grads[3], grads[4], grads[5], grads[6], grads[7])
```

```python
import functools

import jax
import jax.numpy as jnp
from jax import lax
from jax.experimental import pallas as pl
from jax.experimental.pallas import tpu as pltpu
from jax.sharding import PartitionSpec as P

HEADS = 32
KV_HEADS = 4
HEAD_DIM = 128
TOP = 8

bf16 = jnp.bfloat16
f32 = jnp.float32
highest = lax.Precision.HIGHEST
eps_norm = 1e-06
rope_base = 1000000.0
neg_fill = -1e30


def dot(left, right, dims, out=f32):
    return lax.dot_general(left, right, (dims, ((), ())), preferred_element_type=out)


def mm(left, right):
    return dot(left, right, ((1,), (0,)))


def mm_nt(left, right):
    return dot(left, right, ((1,), (1,)))


def mm_tn(left, right):
    return dot(left, right, ((0,), (0,)))


def inv_rms(value):
    return lax.rsqrt(jnp.mean(value * value, axis=-1, keepdims=True) + eps_norm)


def rms_back(value, gain, grad):
    r = inv_rms(value)
    c = grad * gain
    back = r * c - value * (r * r * r) * jnp.mean(c * value, axis=-1, keepdims=True)
    return back, grad * value * r


def rotary_tables(length):
    half = HEAD_DIM // 2
    frequency = rope_base ** (-(jnp.arange(half, dtype=f32) * 2.0) / HEAD_DIM)
    angles = jnp.arange(length, dtype=f32)[:, None] * frequency[None, :]
    cos, sin = jnp.cos(angles), jnp.sin(angles)
    return jnp.concatenate([cos, cos], axis=1), jnp.concatenate([-sin, sin], axis=1)


MESH = pl.DeviceIdType.MESH


class Place:
    def __init__(self, n_expert, n_shard, group):
        self.e = lax.axis_index("expert")
        self.z = lax.axis_index("shard")
        self.n_expert, self.n_shard, self.group = n_expert, n_shard, group
        self.chip, self.core = self.e // 2, self.e % 2
        self.chips = n_expert // 2

    def z_dev(self, t):
        return (self.e, self.z ^ t)

    def slot(self, t, other=0):
        return (self.chip ^ t) * 2 + (self.core ^ other)

    def chip_dev(self, t):
        return (self.slot(t), self.z)

    def mate(self):
        return (self.e ^ 1, self.z)


class Net:
    def __init__(self, send, recv, local):
        self.send, self.recv, self.local = send, recv, local
        self.n, self.m, self.open = 0, 0, []

    def push(self, src, dst, dev):
        i = self.n
        self.n += 1
        copy = pltpu.make_async_remote_copy(
            src_ref=src, dst_ref=dst, send_sem=self.send.at[i], recv_sem=self.recv.at[i],
            device_id=dev, device_id_type=MESH,
        )
        copy.start()
        self.open.append(copy)
        return copy

    def copy(self, src, dst):
        i = self.m
        self.m += 1
        copy = pltpu.make_async_copy(src, dst, self.local.at[i])
        copy.start()
        return copy

    def sent(self):
        for copy in self.open:
            copy.wait_send()
        self.open = []


def greet(devices):
    barrier = pltpu.get_barrier_semaphore()
    for dev in devices:
        pl.semaphore_signal(barrier, inc=1, device_id=dev, device_id_type=MESH)
    pl.semaphore_wait(barrier, len(devices))


def everyone(at):
    return (
        [at.z_dev(t) for t in range(1, at.n_shard)]
        + [at.chip_dev(t) for t in range(1, at.chips)]
        + [at.mate()]
    )


def arrive(copies):
    for copy in copies:
        copy.wait_recv()


def spread(net, at, pieces):
    own = [p(at.e) for p in pieces]
    mate = [net.push(o, o, at.mate()) for o in own]
    out = [(t, [net.push(o, o, at.chip_dev(t)) for o in own]) for t in range(1, at.chips)]
    return mate, out


def pass_on(net, at, pieces, state):
    mate, out = state
    for t, copies in out:
        for p, copy in zip(pieces, copies):
            copy.wait_recv()
            got = p(at.slot(t))
            mate.append(net.push(got, got, at.mate()))
    return mate


def comm_call(kernel, cid, n_remote, n_local, scratch, outs, vmem_mb, in_specs=None, out_specs=None, cost=None):
    any_spec = pl.BlockSpec(memory_space=pl.ANY)

    def call(*args):
        return pl.pallas_call(
            kernel,
            out_shape=outs,
            in_specs=in_specs or [any_spec] * len(args),
            out_specs=out_specs or [any_spec] * len(outs),
            scratch_shapes=list(scratch)
            + [
                pltpu.SemaphoreType.DMA((n_remote,)),
                pltpu.SemaphoreType.DMA((n_remote,)),
                pltpu.SemaphoreType.DMA((n_local,)),
            ],
            compiler_params=pltpu.CompilerParams(
                collective_id=cid, has_side_effects=True, vmem_limit_bytes=vmem_mb << 20
            ),
            cost_estimate=cost,
        )(*args)

    return call


def tiled(size, most):
    while size % most:
        most //= 2
    return most


def halves(at):
    return list(range(1, at.chips)) + [0]


def norm_kernel(
    dims, db, ex, ggu, gdn, x1, b, cot, rw, router_t, gains,
    gx1, do_all, gain_two, g_router, land_gu, land_dn,
    own, own_x, core_in, core_x, chip_in, chip_x, half_out, half_x, swap_in, swap_x, logit, d_out,
    send, recv, local,
):
    at = Place(*dims)
    net = Net(send, recv, local)
    z, e, group = at.z, at.e, at.group
    tok = x1.shape[0]
    loads = {}
    for t in halves(at):
        loads[t] = (net.copy(db.at[at.slot(t)], own.at[t]), net.copy(ex.at[at.slot(t)], own_x.at[t]))
    greet(everyone(at))
    mates = {}
    for t in halves(at):
        mates[t] = (
            net.push(db.at[at.slot(t, 1)], core_in.at[t], at.mate()),
            net.push(ex.at[at.slot(t, 1)], core_x.at[t], at.mate()),
        )
    d_slice = ggu.shape[1]
    landed = []
    for t in range(1, group):
        j = z ^ t ^ group
        landed.append(net.push(gdn.at[:, pl.ds(pl.multiple_of(j * d_slice, d_slice), d_slice)], land_dn.at[t - 1], at.z_dev(t)))
        landed.append(net.push(ggu.at[j], land_gu.at[t - 1], at.z_dev(t)))
    step = 16
    ins = []
    for t in halves(at):
        for c in loads[t]:
            c.wait()
        arrive(mates[t])

        def add(i, _, t=t):
            rows = pl.ds(pl.multiple_of(i * step, step), step)
            own[t, rows, :] = (own[t, rows, :].astype(f32) + core_in[t, rows, :].astype(f32)).astype(bf16)
            own_x[t, rows, :] = (own_x[t, rows, :].astype(f32) + core_x[t, rows, :].astype(f32)).astype(bf16)
            return 0

        lax.fori_loop(0, 2 * tok // step, add, 0)
        if t:
            ins.append(net.push(own.at[t], chip_in.at[t - 1], at.chip_dev(t)))
            ins.append(net.push(own_x.at[t], chip_x.at[t - 1], at.chip_dev(t)))
    arrive(ins)

    def partner(i, _):
        rows = pl.ds(pl.multiple_of(i * step, step), step)
        src = pl.ds(pl.multiple_of(tok + i * step, step), step)
        total, total_x = own[0, src, :].astype(f32), own_x[0, src, :].astype(f32)
        for t in range(1, at.chips):
            total += chip_in[t - 1, src, :].astype(f32)
            total_x += chip_x[t - 1, src, :].astype(f32)
        half_out[rows, :] = total.astype(bf16)
        half_x[rows, :] = total_x.astype(bf16)
        return 0

    lax.fori_loop(0, tok // step, partner, 0)
    swaps = [net.push(half_out, swap_in, at.z_dev(group)), net.push(half_x, swap_x, at.z_dev(group))]
    arrive(swaps)
    gain_two[...] = jnp.zeros_like(gain_two)

    def owner(i, _):
        rows = pl.ds(pl.multiple_of(i * step, step), step)
        grad = own[0, rows, :].astype(f32) + swap_in[rows, :].astype(f32)
        routed = own_x[0, rows, :].astype(f32) + swap_x[rows, :].astype(f32)
        for t in range(1, at.chips):
            grad += chip_in[t - 1, rows, :].astype(f32)
            routed += chip_x[t - 1, rows, :].astype(f32)
        routed = routed + pltpu.roll(routed, 64, 1)
        weight = rw[rows, :]
        d_logit = weight * (routed - jnp.sum(weight * routed, axis=1, keepdims=True))
        high = d_logit.astype(bf16)
        low = (d_logit - high.astype(f32)).astype(bf16)
        logit[0, rows, :] = high
        logit[1, rows, :] = low
        grad += mm(high, router_t[...]) + mm(low, router_t[...])
        value = x1[rows, :]
        r = inv_rms(value)
        c = grad * gains[1:2, :]
        back = cot[rows, :].astype(f32) + r * c - value * (r * r * r * jnp.mean(c * value, axis=-1, keepdims=True))
        gx1[rows, :] = back
        d_out[rows, :] = back.astype(bf16)
        per = grad * value * r
        gain_two[...] += per[:8] + per[8:]
        return 0

    lax.fori_loop(0, tok // step, owner, 0)
    mine = do_all.at[pl.ds(pl.multiple_of(z * tok, tok), tok)]
    keep = net.copy(d_out, mine)
    copies = [net.push(d_out, mine, at.z_dev(t)) for t in range(1, at.n_shard)]
    g_router[...] = mm_tn(logit[0], b[...]) + mm_tn(logit[1], b[...])
    keep.wait()
    arrive(copies + landed)
    net.sent()


def rope_rows(value, cos, sin):
    return value * cos + pltpu.roll(value, HEAD_DIM // 2, 1) * sin


def rope_rows_back(grad, cos, sin):
    return grad * cos + pltpu.roll(grad * sin, HEAD_DIM // 2, 1)


def eight(per):
    return jnp.sum(per.reshape(per.shape[0] // 8, 8, per.shape[1]), axis=0)


def span(i, size):
    if isinstance(i, int):
        return pl.ds(i * size, size)
    return pl.ds(pl.multiple_of(i * size, size), size)


def soft_block(q_ref, k_ref, seg_row, seg_col, h, i, block, scale):
    rows, keys = pl.ds(i * block, block), pl.ds(0, (i + 1) * block)
    scores = mm_nt(q_ref[rows, span(h, HEAD_DIM)], k_ref[keys, :]) * scale
    width = (i + 1) * block
    at_q = i * block + lax.broadcasted_iota(jnp.int32, (block, width), 0)
    at_k = lax.broadcasted_iota(jnp.int32, (block, width), 1)
    allowed = (at_k <= at_q) & (seg_row[0:1, keys] == seg_col[rows, 0:1])
    scores = jnp.where(allowed, scores, neg_fill)
    raised = jnp.exp(scores - jnp.max(scores, axis=-1, keepdims=True))
    return raised / jnp.sum(raised, axis=-1, keepdims=True)


def front_kernel(
    dims, x, small, seg_own, w_qkv, w_out, w_gu, w_dn, cot, mask, cos_h, sin_h,
    small_out, seg_out, heads_out, a_out, raw_out, q_out, k_out, v_out, o_out, x1_out, b_out,
    gate_up, down, cot_all, mask_all, b_all,
    x_all, small_all, seg_col, heads, a, raw, q, k, v, o, w_o, part, parts_in, cos, sin, gains, seg_row, x1, b_own,
    send, recv, local,
):
    at = Place(*dims)
    net = Net(send, recv, local)
    z, e, group = at.z, at.e, at.group
    tok = x.shape[0]
    length, width = x_all.shape
    mine = z // group
    rows_e, cols = heads.shape[2], heads.shape[3]
    hd = cols - 2 * HEAD_DIM
    n_heads = hd // HEAD_DIM
    q_width = HEADS * HEAD_DIM
    d_slice = w_gu.shape[1]
    scale = HEAD_DIM ** (-0.5)
    block = tok

    def heads_of(dest):
        kv = (dest * n_heads) // (HEADS // KV_HEADS)
        rows = span(e, rows_e)
        return [
            (w_qkv.at[rows, span(dest, hd)], heads.at[z, e, :, pl.ds(0, hd)]),
            (w_qkv.at[rows, span(HEADS + kv, HEAD_DIM)], heads.at[z, e, :, pl.ds(hd, HEAD_DIM)]),
            (w_qkv.at[rows, span(HEADS + KV_HEADS + kv, HEAD_DIM)], heads.at[z, e, :, pl.ds(hd + HEAD_DIM, HEAD_DIM)]),
        ]

    def d_cols(ref, who):
        return ref.at[:, span(who, d_slice)]

    half0, half1 = pl.ds(0, tok), pl.ds(tok, tok)
    first = [
        net.copy(x, x_all.at[span(z, tok)]),
        net.copy(small, small_all.at[z]),
        net.copy(seg_own, seg_col.at[span(z, tok)]),
        net.copy(cos_h, cos),
        net.copy(sin_h, sin),
    ]
    local_heads = [net.copy(s, d) for s, d in heads_of(z)]
    local_cot = [net.copy(cot, cot_all.at[e, half0]), net.copy(mask, mask_all.at[e, half0])]
    load_out = net.copy(w_out, w_o)
    here = [net.copy(w_gu.at[mine], gate_up.at[z]), net.copy(w_dn.at[mine], d_cols(down, z))]
    greet(everyone(at))
    got_heads = [net.push(s, d, at.z_dev(t)) for t in range(1, at.n_shard) for s, d in heads_of(z ^ t)]
    got_x = []
    for t in range(1, at.n_shard):
        got_x.append(net.push(small, small_all.at[z], at.z_dev(t)))
        got_x.append(net.push(seg_own, seg_col.at[span(z, tok)], at.z_dev(t)))
        got_x.append(net.push(x, x_all.at[span(z, tok)], at.z_dev(t)))
    for c in local_heads:
        c.wait()
    arrive(got_heads)
    pieces = [lambda who: heads.at[:, who]]
    heads_state = spread(net, at, pieces)
    for c in first:
        c.wait()
    arrive(got_x)
    other = (z ^ group) // group
    from_partner = [
        (net.push(w_gu.at[other], gate_up.at[z], at.z_dev(group)), gate_up.at[z ^ group]),
        (net.push(w_dn.at[other], d_cols(down, z), at.z_dev(group)), d_cols(down, z ^ group)),
    ]
    got_w = []
    for t in range(1, group):
        got_w.append(net.push(w_gu.at[mine], gate_up.at[z], at.z_dev(t)))
        got_w.append(net.push(w_dn.at[mine], d_cols(down, z), at.z_dev(t)))
    got_cot = [
        net.push(cot, cot_all.at[e, half1], at.z_dev(group)),
        net.push(mask, mask_all.at[e, half1], at.z_dev(group)),
    ]

    qk = []
    for s in range(at.n_shard):
        rows = small_all[s, 0:16, :].astype(f32)
        gains[0:2, span(s, d_slice)] = rows[0:2]
        seg_row[0:1, span(s, tok)] = rows[4:5, :tok]
        qk.append(rows[2:4, :HEAD_DIM])
    qk = sum(qk[1:], qk[0])
    step = 16

    def norm_rows(i, _):
        rows = span(i, step)
        value = x_all[rows, :].astype(f32)
        a[rows, :] = (value * inv_rms(value) * gains[0:1, :]).astype(bf16)
        return 0

    lax.fori_loop(0, length // step, norm_rows, 0)
    last = pass_on(net, at, pieces, heads_state)
    arrive(last)
    keep = [net.copy(heads, heads_out), net.copy(a, a_out), net.copy(small_all, small_out), net.copy(seg_col, seg_out)]

    wide = tiled(cols, 256)

    def project(i, _):
        tile = span(i, wide)
        raw[:, tile] = mm(a[...], heads[:, :, :, tile].reshape(width, wide))
        return 0

    lax.fori_loop(0, cols // wide, project, 0)
    keep.append(net.copy(raw, raw_out))

    def head_rows(i, _):
        rows = span(i, block)
        cos_b, sin_b = cos[rows, :], sin[rows, :]
        for h in range(n_heads + 1):
            value = raw[rows, pl.ds(h * HEAD_DIM, HEAD_DIM)]
            gain = qk[0:1] if h < n_heads else qk[1:2]
            value = rope_rows(value * inv_rms(value) * gain, cos_b, sin_b).astype(bf16)
            if h < n_heads:
                q[rows, pl.ds(h * HEAD_DIM, HEAD_DIM)] = value
            else:
                k[rows, :] = value
        v[rows, :] = raw[rows, pl.ds(hd + HEAD_DIM, HEAD_DIM)].astype(bf16)
        return 0

    lax.fori_loop(0, length // block, head_rows, 0)
    keep += [net.copy(q, q_out), net.copy(k, k_out), net.copy(v, v_out)]
    for c in local_cot:
        c.wait()
    arrive(got_cot)
    cots = [lambda who: cot_all.at[who], lambda who: mask_all.at[who]]
    cot_state = spread(net, at, cots)

    def one_head(h, _):
        for i in range(length // block):
            soft = soft_block(q, k, seg_row, seg_col, h, i, block, scale).astype(bf16)
            mixed = mm(soft, v[pl.ds(0, (i + 1) * block), :])
            o[pl.ds(i * block, block), span(h, HEAD_DIM)] = mixed.astype(bf16)
        return 0

    lax.fori_loop(0, n_heads, one_head, 0)
    keep.append(net.copy(o, o_out))
    load_out.wait()
    wide_o = tiled(width, 256)

    def out_tile(i, _):
        tile = span(i, wide_o)
        part[:, tile] = mm(o[...], w_o[:, tile]).astype(bf16)
        return 0

    lax.fori_loop(0, width // wide_o, out_tile, 0)
    sums = [net.push(part.at[span(z ^ t, tok)], parts_in.at[t - 1], at.z_dev(t)) for t in range(1, at.n_shard)]
    last = pass_on(net, at, cots, cot_state)
    for copy, ref in from_partner:
        copy.wait_recv()
        for t in range(1, group):
            got_w.append(net.push(ref, ref, at.z_dev(t)))
    arrive(sums)

    def middle_rows(i, _):
        rows = span(i, step)
        total = part[pl.ds(pl.multiple_of(z * tok + i * step, step), step), :].astype(f32)
        for t in range(1, at.n_shard):
            total += parts_in[t - 1, rows, :].astype(f32)
        value = x_all[pl.ds(pl.multiple_of(z * tok + i * step, step), step), :].astype(f32) + total
        x1[rows, :] = value
        b_own[rows, :] = (value * inv_rms(value) * gains[1:2, :]).astype(bf16)
        return 0

    lax.fori_loop(0, tok // step, middle_rows, 0)
    local_b = net.copy(b_own, b_all.at[e, half0])
    swap = net.push(b_own, b_all.at[e, half1], at.z_dev(group))
    keep += [net.copy(x1, x1_out), net.copy(b_own, b_out)]
    local_b.wait()
    swap.wait_recv()
    rows_b = [lambda who: b_all.at[who]]
    last += pass_on(net, at, rows_b, spread(net, at, rows_b))
    arrive(last + got_w)
    for c in keep + here:
        c.wait()
    net.sent()


def back_kernel(
    dims, do_h, w_out, o_h, q_h, k_h, v_h, raw_h, cos_h, sin_h, seg_h, small, ggu, gdn, land_gu, land_dn, out_part, x1,
    d_qkv_out, qk_gain, share_out, hidden, two_gu, two_dn, own_gu, own_dn, out_core,
    do_all, w_o, o, q, k, v, raw, cos, sin, seg_col, seg_row, mix, d_qkv, dk, dv,
    sum_gu, add_gu, sum_dn, add_dn, out_own, out_add, out_in, half_out, swap_in, g_out, g_core, g_in,
    send, recv, local,
):
    at = Place(*dims)
    net = Net(send, recv, local)
    z, e, group = at.z, at.e, at.group
    length, width = do_all.shape
    tok = x1.shape[0]
    cols = raw.shape[1]
    hd = cols - 2 * HEAD_DIM
    n_heads = hd // HEAD_DIM
    d_slice = ggu.shape[1]
    scale = HEAD_DIM ** (-0.5)
    block = tok
    step = 16
    far = z ^ group

    def d_cols(ref, who):
        return ref.at[:, span(who, d_slice)]

    load_dn = [net.copy(d_cols(gdn, far), sum_dn)] + [net.copy(land_dn.at[t - 1], add_dn.at[t - 1]) for t in range(1, group)]
    load_gu = [net.copy(ggu.at[far], sum_gu)] + [net.copy(land_gu.at[t - 1], add_gu.at[t - 1]) for t in range(1, group)]
    load_a = [net.copy(do_h, do_all), net.copy(o_h, o)]
    load_own = {t: net.copy(out_part.at[at.slot(t)], out_own.at[t]) for t in halves(at)}
    load_b = [
        net.copy(s, d)
        for s, d in ((w_out, w_o), (q_h, q), (k_h, k), (v_h, v), (raw_h, raw), (cos_h, cos), (sin_h, sin), (seg_h, seg_col))
    ]
    greet(everyone(at))
    mates = {t: net.push(out_part.at[at.slot(t, 1)], out_core.at[t], at.mate()) for t in halves(at)}

    def add_up(total, adds):
        def rows_of(i, _):
            rows = span(i, step)
            value = total[rows, :].astype(f32)
            for t in range(1, group):
                value += adds[t - 1, rows, :].astype(f32)
            total[rows, :] = value.astype(bf16)
            return 0

        lax.fori_loop(0, total.shape[0] // step, rows_of, 0)

    for c in load_gu:
        c.wait()
    add_up(sum_gu, add_gu)
    got = [net.push(sum_gu, two_gu, at.z_dev(group))]
    for c in load_dn:
        c.wait()
    add_up(sum_dn, add_dn)
    got.append(net.push(sum_dn, two_dn, at.z_dev(group)))
    for t in range(1, group):
        got.append(net.push(ggu.at[z ^ t], own_gu.at[t - 1], at.z_dev(t)))
        got.append(net.push(d_cols(gdn, z ^ t), own_dn.at[t - 1], at.z_dev(t)))

    for c in load_a:
        c.wait()
    share = share_out.shape[0]

    wide = tiled(hd, 256)
    each = wide // share

    def out_grad(i, _):
        tile = mm_tn(o[:, span(i, wide)], do_all[...]).astype(bf16)
        for j in range(each):
            g_out[each * i + j] = tile[j * share : (j + 1) * share]
        return 0

    lax.fori_loop(0, hd // wide, out_grad, 0)
    g_mates = {t: net.push(g_out.at[at.slot(t, 1)], g_core.at[t], at.mate()) for t in halves(at)}

    outs = []
    for t in halves(at):
        load_own[t].wait()
        mates[t].wait_recv()
        c = net.copy(out_core.at[t], out_add)
        c.wait()

        def add(i, _, t=t):
            rows = span(i, step)
            out_own[t, rows, :] = (out_own[t, rows, :].astype(f32) + out_add[rows, :].astype(f32)).astype(bf16)
            return 0

        lax.fori_loop(0, 2 * tok // step, add, 0)
        if t:
            outs.append(net.push(out_own.at[t], out_in.at[t - 1], at.chip_dev(t)))
    for c in load_b:
        c.wait()
    qk = []
    for s in range(at.n_shard):
        rows = small[s, 0:16, :].astype(f32)
        seg_row[0:1, span(s, tok)] = rows[4:5, :tok]
        qk.append(rows[2:4, :HEAD_DIM])
    qk = sum(qk[1:], qk[0])

    def mix_tile(i, _):
        tile = span(i, wide)
        mix[:, tile] = mm_nt(do_all[...], w_o[tile, :]).astype(bf16)
        return 0

    lax.fori_loop(0, hd // wide, mix_tile, 0)
    g_outs = []
    for t in halves(at):
        g_mates[t].wait_recv()

        def add(i, _, t=t):
            rows = span(i, step)
            s = at.slot(t)
            g_out[s, rows, :] = (g_out[s, rows, :].astype(f32) + g_core[t, rows, :].astype(f32)).astype(bf16)
            return 0

        lax.fori_loop(0, share // step, add, 0)
        if t:
            g_outs.append(net.push(g_out.at[at.slot(t)], g_in.at[t - 1], at.chip_dev(t)))

    dk[...] = jnp.zeros_like(dk)
    dv[...] = jnp.zeros_like(dv)
    qk_gain[...] = jnp.zeros_like(qk_gain)

    def one_head(h, _):
        lanes = span(h, HEAD_DIM)
        for i in range(length // block):
            rows, keys = pl.ds(i * block, block), pl.ds(0, (i + 1) * block)
            soft = soft_block(q, k, seg_row, seg_col, h, i, block, scale)
            d_mix = mix[rows, lanes]
            d_soft = mm_nt(d_mix, v[keys, :])
            d_scores = (soft * (d_soft - jnp.sum(soft * d_soft, axis=-1, keepdims=True))).astype(bf16)
            dv[keys, :] += mm_tn(soft.astype(bf16), d_mix)
            dk[keys, :] += mm_tn(d_scores, q[rows, lanes]) * scale
            dq = mm(d_scores, k[keys, :]) * scale
            value = raw[rows, lanes]
            back, per = rms_back(value, qk[0:1], rope_rows_back(dq, cos[rows, :], sin[rows, :]))
            d_qkv[rows, lanes] = back.astype(bf16)
            qk_gain[0:8, :] += eight(per)
        return 0

    lax.fori_loop(0, n_heads, one_head, 0)
    for i in range(length // block):
        rows = pl.ds(i * block, block)
        value = raw[rows, pl.ds(hd, HEAD_DIM)]
        back, per = rms_back(value, qk[1:2], rope_rows_back(dk[rows, :], cos[rows, :], sin[rows, :]))
        d_qkv[rows, pl.ds(hd, HEAD_DIM)] = back.astype(bf16)
        d_qkv[rows, pl.ds(hd + HEAD_DIM, HEAD_DIM)] = dv[rows, :].astype(bf16)
        qk_gain[8:16, :] += eight(per)
    keep = net.copy(d_qkv, d_qkv_out)

    arrive(outs)

    def sum_in(rows):
        total = out_own[0, rows, :].astype(f32)
        for t in range(1, at.chips):
            total += out_in[t - 1, rows, :].astype(f32)
        return total

    def partner(i, _):
        half_out[span(i, step), :] = sum_in(pl.ds(pl.multiple_of(tok + i * step, step), step)).astype(bf16)
        return 0

    lax.fori_loop(0, tok // step, partner, 0)
    swap = net.push(half_out, swap_in, at.z_dev(group))
    arrive(g_outs)

    def own_share(i, _):
        rows = span(i, step)
        total = g_out[e, rows, :].astype(f32)
        for t in range(1, at.chips):
            total += g_in[t - 1, rows, :].astype(f32)
        share_out[rows, :] = total.astype(bf16)
        return 0

    lax.fori_loop(0, share // step, own_share, 0)
    swap.wait_recv()

    def hidden_rows(i, _):
        rows = span(i, step)
        hidden[rows, :] = (x1[rows, :] + sum_in(rows) + swap_in[rows, :].astype(f32)).astype(bf16)
        return 0

    lax.fori_loop(0, tok // step, hidden_rows, 0)
    arrive(got)
    keep.wait()
    net.sent()


def tail_kernel(
    dims, d_qkv_h, heads_h, a_h, gx1, x, gains, gain_two, g_router, qk_gain, share_out,
    g_hidden, g_qkv, g_att, small_sum,
    d_qkv, heads, a, part, parts_in, g_heads, core_in, chip_in, mine, turn_in, share, sm, sm_z, sm_core, sm_chip,
    send, recv, local,
):
    at = Place(*dims)
    net = Net(send, recv, local)
    z, e, group = at.z, at.e, at.group
    length, cols = d_qkv.shape
    tok, width = x.shape
    hd = cols - 2 * HEAD_DIM
    n_heads = hd // HEAD_DIM
    rows_e = heads.shape[2]
    d_slice = width // at.n_shard
    step = 16
    load_a = [net.copy(d_qkv_h, d_qkv), net.copy(heads_h, heads)]
    load_b = net.copy(a_h, a)
    own_att = net.copy(share_out, g_att.at[e])
    greet(everyone(at))
    own_att.wait()
    atts = [lambda who: g_att.at[who]]
    att_state = spread(net, at, atts)
    for c in load_a:
        c.wait()

    wide = tiled(d_slice, 256)
    each = wide // rows_e

    def rows_tile(s, _):
        for j in range(d_slice // wide):
            some = heads[s, pl.ds(each * j, each)].reshape(wide, cols)
            here = pl.ds(pl.multiple_of(s * d_slice + j * wide, wide), wide)
            part[:, here] = mm_nt(d_qkv[...], some).astype(bf16)
        return 0

    lax.fori_loop(0, at.n_shard, rows_tile, 0)
    sums = [net.push(part.at[span(z ^ t, tok)], parts_in.at[t - 1], at.z_dev(t)) for t in range(1, at.n_shard)]
    load_b.wait()

    def grad_tile(s, _):
        for j in range(d_slice // wide):
            some = a[:, pl.ds(pl.multiple_of(s * d_slice + j * wide, wide), wide)]
            tile = mm_tn(some, d_qkv[...]).astype(bf16)
            for i in range(each):
                g_heads[each * j + i, s] = tile[i * rows_e : (i + 1) * rows_e]
        return 0

    lax.fori_loop(0, at.n_shard, grad_tile, 0)
    mates = {t: net.push(g_heads.at[at.slot(t, 1)], core_in.at[t], at.mate()) for t in halves(at)}
    chips = []
    for t in halves(at):
        mates[t].wait_recv()
        who = at.slot(t)

        def add(s, _, t=t, who=who):
            g_heads[who, s] = (g_heads[who, s].astype(f32) + core_in[t, s].astype(f32)).astype(bf16)
            return 0

        lax.fori_loop(0, at.n_shard, add, 0)
        if t:
            chips.append(net.push(g_heads.at[who], chip_in.at[t - 1], at.chip_dev(t)))
    atts_last = pass_on(net, at, atts, att_state)
    arrive(sums)
    sm[...] = jnp.zeros_like(sm)
    gain_one = jnp.zeros((8, width), f32)

    def owner(i, gain_one):
        rows = span(i, step)
        here = pl.ds(pl.multiple_of(z * tok + i * step, step), step)
        da = part[here, :].astype(f32)
        for t in range(1, at.n_shard):
            da += parts_in[t - 1, rows, :].astype(f32)
        back, per = rms_back(x[rows, :].astype(f32), gains[0:1, :], da)
        g_hidden[rows, :] = gx1[rows, :] + back
        return gain_one + eight(per)

    gain_one = lax.fori_loop(0, tok // step, owner, gain_one)
    row_one = jnp.sum(gain_one, axis=0, keepdims=True)
    row_two = jnp.sum(gain_two[...], axis=0, keepdims=True)
    row_q = jnp.sum(qk_gain[0:8, :], axis=0, keepdims=True)
    row_k = jnp.sum(qk_gain[8:16, :], axis=0, keepdims=True)
    for s in range(at.n_shard):
        piece = pl.ds(s * d_slice, d_slice)
        lanes = slice(s * d_slice, (s + 1) * d_slice)
        sm[s, 0:1, :] = row_one[:, lanes]
        sm[s, 1:2, :] = row_two[:, lanes]
        sm[s, 2:3, pl.ds(0, HEAD_DIM)] = row_q
        sm[s, 3:4, pl.ds(0, HEAD_DIM)] = row_k
        sm[s, 8:, :] = g_router[0 : sm.shape[1] - 8, piece]
    small_z = [net.push(sm.at[z ^ t], sm_z.at[t - 1], at.z_dev(t)) for t in range(1, at.n_shard)]
    arrive(chips)

    def total(s, _):
        value = g_heads[e, s].astype(f32)
        for t in range(1, at.chips):
            value += chip_in[t - 1, s].astype(f32)
        mine[s] = value.astype(bf16)
        return 0

    lax.fori_loop(0, at.n_shard, total, 0)
    turns = [net.push(mine.at[z ^ t], turn_in.at[z], at.z_dev(t)) for t in range(1, at.n_shard)]
    turn_own = net.copy(mine.at[z], turn_in.at[z])
    arrive(small_z)
    value = sm[z]
    for t in range(1, at.n_shard):
        value += sm_z[t - 1]
    sm[z] = value
    c = net.push(sm.at[z], sm_core, at.mate())
    turn_own.wait()
    arrive(turns)
    for s in range(at.n_shard):
        share[:, pl.ds(s * hd, hd)] = turn_in[s, :, pl.ds(0, hd)]
    for m in range(KV_HEADS):
        some = [s for s in range(at.n_shard) if (s * n_heads) // (HEADS // KV_HEADS) == m]
        for first, to in ((hd, HEADS + m), (hd + HEAD_DIM, HEADS + KV_HEADS + m)):
            value = turn_in[some[0], :, pl.ds(first, HEAD_DIM)].astype(f32)
            for s in some[1:]:
                value += turn_in[s, :, pl.ds(first, HEAD_DIM)].astype(f32)
            share[:, pl.ds(to * HEAD_DIM, HEAD_DIM)] = value.astype(bf16)
    keep = net.copy(share, g_qkv.at[e])
    c.wait_recv()
    sm_core[...] = sm[z] + sm_core[...]
    smalls = [net.push(sm_core, sm_chip.at[t - 1], at.chip_dev(t)) for t in range(1, at.chips)]
    keep.wait()
    qkvs = [lambda who: g_qkv.at[who]]
    last = pass_on(net, at, qkvs, spread(net, at, qkvs))
    arrive(smalls)
    value = sm_core[...]
    for t in range(1, at.chips):
        value += sm_chip[t - 1]
    small_sum[...] = value
    arrive(last + atts_last)
    net.sent()


def shards(
    hidden_in,
    segments,
    routes,
    norm_gains,
    qk_gains,
    w_qkv,
    w_attn_out,
    w_router,
    w_gate_up,
    w_down,
    cotangent,
):
    n_expert = lax.axis_size("expert")
    n_shard = lax.axis_size("shard")
    me_e = lax.axis_index("expert")
    me_z = lax.axis_index("shard")
    tok, width = hidden_in.shape
    exp_dev = w_gate_up.shape[1]
    experts_all = w_router.shape[2]
    d_slice, ff2 = w_gate_up.shape[2:]
    ff = ff2 // 2
    group = n_shard // exp_dev
    mine = me_z // group
    length = n_shard * tok
    h_dev = HEADS // n_shard
    hd = h_dev * HEAD_DIM
    cols = hd + 2 * HEAD_DIM
    qkv_cols = w_qkv.shape[2]
    rows_e = d_slice // n_expert
    share = hd // n_expert
    chips = n_expert // 2
    qk_part = HEAD_DIM // n_shard
    dims = (n_expert, n_shard, group)
    n_small = 16 + experts_all
    sds = jax.ShapeDtypeStruct
    vm = pltpu.VMEM
    any_spec = pl.BlockSpec(memory_space=pl.ANY)
    vmem_spec = pl.BlockSpec(memory_space=pltpu.VMEM)

    small = jnp.zeros((16, d_slice), bf16)
    small = small.at[0:2, :].set(norm_gains[0])
    small = lax.dynamic_update_slice(small, qk_gains[0], (2, me_z * qk_part))
    small = small.at[4, :tok].set(segments.astype(bf16))
    small = jnp.concatenate([small, w_router[0].T], axis=0)
    seg_own = jnp.broadcast_to(segments.astype(f32)[:, None], (tok, 128))
    ids = jnp.arange(128, dtype=jnp.int32)
    mask = jnp.sum((routes[:, :, None] == ids[None, None, :]).astype(f32), axis=1).astype(bf16)
    cos, sin = rotary_tables(length)

    outs = [
        sds((n_shard, n_small, d_slice), bf16),
        sds((length, 128), f32),
        sds((n_shard, n_expert, rows_e, cols), bf16),
        sds((length, width), bf16),
        sds((length, cols), f32),
        sds((length, hd), bf16),
        sds((length, HEAD_DIM), bf16),
        sds((length, HEAD_DIM), bf16),
        sds((length, hd), bf16),
        sds((tok, width), f32),
        sds((tok, width), bf16),
        sds((n_shard, d_slice, ff2), bf16),
        sds((ff, width), bf16),
        sds((n_expert, 2 * tok, width), bf16),
        sds((n_expert, 2 * tok, 128), bf16),
        sds((n_expert, 2 * tok, width), bf16),
    ]
    front = comm_call(
        functools.partial(front_kernel, dims),
        0,
        160,
        40,
        [
            vm((length, width), bf16),
            vm((n_shard, n_small, d_slice), bf16),
            vm((length, 128), f32),
            vm((n_shard, n_expert, rows_e, cols), bf16),
            vm((length, width), bf16),
            vm((length, cols), f32),
            vm((length, hd), bf16),
            vm((length, HEAD_DIM), bf16),
            vm((length, HEAD_DIM), bf16),
            vm((length, hd), bf16),
            vm((hd, width), bf16),
            vm((length, width), bf16),
            vm((n_shard - 1, tok, width), bf16),
            vm((length, HEAD_DIM), f32),
            vm((length, HEAD_DIM), f32),
            vm((8, width), f32),
            vm((8, length), f32),
            vm((tok, width), f32),
            vm((tok, width), bf16),
        ],
        outs,
        56,
    )
    (small_all, seg_col, heads, a, raw, q, k, v, o, x1, b, gate_up, down, cot_all, mask_all, b_all) = front(
        hidden_in, small, seg_own, w_qkv[0], w_attn_out[0], w_gate_up[0], w_down[0], cotangent, mask, cos, sin
    )
    gains = jnp.zeros((8, width), f32)
    gains = gains.at[0:2].set(small_all[:, 0:2].astype(f32).transpose(1, 0, 2).reshape(2, width))
    router_t = small_all[:, 16:].transpose(1, 0, 2).reshape(experts_all, width)

    def route_weights(rows, chosen):
        logits = mm_nt(rows, router_t)
        masked = jnp.where(chosen, logits, neg_fill)
        raised = jnp.where(chosen, jnp.exp(masked - jnp.max(masked, axis=1, keepdims=True)), 0.0)
        return raised / jnp.sum(raised, axis=1, keepdims=True)

    rows_all = n_expert * 2 * tok
    b_rows = b_all.reshape(rows_all, width)
    my_expert = me_e * exp_dev + mine
    rw_all = route_weights(b_rows, mask_all.reshape(rows_all, 128)[:, :experts_all] > 0)
    is_mine = ids[:experts_all] == my_expert
    rw_mine = jnp.sum(jnp.where(is_mine[None, :], rw_all, 0.0), axis=1, keepdims=True)
    rw = route_weights(b, mask[:, :experts_all] > 0)
    rw = jnp.concatenate([rw, jnp.zeros((tok, 128 - experts_all), f32)], axis=1)
    w_gu = gate_up.reshape(width, ff2)
    pre = mm(b_rows, w_gu)
    g, u = pre[:, :ff], pre[:, ff:]
    sig = jax.nn.sigmoid(g)
    act = g * sig
    hidden = (act * u).astype(bf16)
    y_f = mm(hidden, down).astype(bf16).astype(f32)
    cot_f = cot_all.reshape(rows_all, width).astype(f32)
    d_route = jnp.sum(cot_f * y_f, axis=1, keepdims=True)
    out_part = (rw_mine * y_f).astype(bf16)
    d_y = (rw_mine * cot_f).astype(bf16)
    d_hidden = mm_nt(d_y, down)
    d_pre = jnp.concatenate(
        [d_hidden * u * sig * (1.0 + g * (1.0 - sig)), d_hidden * act], axis=1
    ).astype(bf16)
    d_b = mm_nt(d_pre, w_gu).astype(bf16)
    grad_down = mm_tn(hidden, d_y).astype(bf16)
    grad_gate_up = mm_tn(b_rows, d_pre).astype(bf16).reshape(n_shard, d_slice, ff2)
    high = lax.reduce_precision(d_route, 8, 7)
    low = d_route - high
    extra = jnp.where(ids[None] == my_expert, high, jnp.where(ids[None] == my_expert + 64, low, 0.0)).astype(bf16)

    per_e = (n_expert, 2 * tok)
    piece = (chips, 2 * tok)
    router_pad = jnp.concatenate([router_t, jnp.zeros((128 - experts_all, width), bf16)], axis=0)
    gx1, d_o, gain_two, g_router, land_gu, land_dn = comm_call(
        functools.partial(norm_kernel, dims),
        1,
        60,
        40,
        [
            vm(piece + (width,), bf16),
            vm(piece + (128,), bf16),
            vm(piece + (width,), bf16),
            vm(piece + (128,), bf16),
            vm((chips - 1, 2 * tok, width), bf16),
            vm((chips - 1, 2 * tok, 128), bf16),
            vm((tok, width), bf16),
            vm((tok, 128), bf16),
            vm((tok, width), bf16),
            vm((tok, 128), bf16),
            vm((2, tok, 128), bf16),
            vm((tok, width), bf16),
        ],
        [
            sds((tok, width), f32),
            sds((length, width), bf16),
            sds((8, width), f32),
            sds((128, width), f32),
            sds((group - 1, d_slice, ff2), bf16),
            sds((group - 1, ff, d_slice), bf16),
        ],
        56,
        in_specs=[any_spec] * 4 + [vmem_spec] * 6,
        out_specs=[vmem_spec, any_spec, vmem_spec, vmem_spec, any_spec, any_spec],
    )(
        d_b.reshape(per_e + (width,)),
        extra.reshape(per_e + (128,)),
        grad_gate_up,
        grad_down,
        x1,
        b,
        cotangent,
        rw,
        router_pad,
        gains,
    )

    d_qkv, qk_gain, share_out, hidden_out, two_gu, two_dn, own_gu, own_dn, _ = comm_call(
        functools.partial(back_kernel, dims),
        2,
        80,
        60,
        [
            vm((length, width), bf16),
            vm((hd, width), bf16),
            vm((length, hd), bf16),
            vm((length, hd), bf16),
            vm((length, HEAD_DIM), bf16),
            vm((length, HEAD_DIM), bf16),
            vm((length, cols), f32),
            vm((length, HEAD_DIM), f32),
            vm((length, HEAD_DIM), f32),
            vm((length, 128), f32),
            vm((8, length), f32),
            vm((length, hd), bf16),
            vm((length, cols), bf16),
            vm((length, HEAD_DIM), f32),
            vm((length, HEAD_DIM), f32),
            vm((d_slice, ff2), bf16),
            vm((group - 1, d_slice, ff2), bf16),
            vm((ff, d_slice), bf16),
            vm((group - 1, ff, d_slice), bf16),
            vm(piece + (width,), bf16),
            vm((2 * tok, width), bf16),
            vm((chips - 1, 2 * tok, width), bf16),
            vm((tok, width), bf16),
            vm((tok, width), bf16),
            vm((n_expert, share, width), bf16),
            vm((chips, share, width), bf16),
            vm((chips - 1, share, width), bf16),
        ],
        [
            sds((length, cols), bf16),
            sds((16, HEAD_DIM), f32),
            sds((share, width), bf16),
            sds((tok, width), bf16),
            sds((d_slice, ff2), bf16),
            sds((ff, d_slice), bf16),
            sds((group - 1, d_slice, ff2), bf16),
            sds((group - 1, ff, d_slice), bf16),
            sds((chips, 2 * tok, width), bf16),
        ],
        60,
        in_specs=[any_spec] * 10 + [vmem_spec] + [any_spec] * 5 + [vmem_spec],
        out_specs=[any_spec] + [vmem_spec] * 3 + [any_spec] * 5,
    )(
        d_o,
        w_attn_out[0],
        o,
        q,
        k,
        v,
        raw,
        cos,
        sin,
        seg_col,
        small_all,
        grad_gate_up,
        grad_down,
        land_gu,
        land_dn,
        out_part.reshape(per_e + (width,)),
        x1,
    )

    small_rows = (8 + -(-experts_all // 8) * 8, d_slice)
    grad_hidden, grad_qkv, grad_out, sums = comm_call(
        functools.partial(tail_kernel, dims),
        3,
        100,
        16,
        [
            vm((length, cols), bf16),
            vm((n_shard, n_expert, rows_e, cols), bf16),
            vm((length, width), bf16),
            vm((length, width), bf16),
            vm((n_shard - 1, tok, width), bf16),
            vm((n_expert, n_shard, rows_e, cols), bf16),
            vm((chips, n_shard, rows_e, cols), bf16),
            vm((chips - 1, n_shard, rows_e, cols), bf16),
            vm((n_shard, rows_e, cols), bf16),
            vm((n_shard, rows_e, cols), bf16),
            vm((rows_e, qkv_cols), bf16),
            vm((n_shard,) + small_rows, f32),
            vm((n_shard - 1,) + small_rows, f32),
            vm(small_rows, f32),
            vm((chips - 1,) + small_rows, f32),
        ],
        [
            sds((tok, width), f32),
            sds((n_expert, rows_e, qkv_cols), bf16),
            sds((n_expert, share, width), bf16),
            sds(small_rows, f32),
        ],
        56,
        in_specs=[any_spec] * 3 + [vmem_spec] * 6 + [any_spec],
        out_specs=[vmem_spec, any_spec, any_spec, vmem_spec],
    )(d_qkv, heads, a, gx1, hidden_in, gains, gain_two, g_router, qk_gain, share_out)

    def settle(own, others, other):
        total = own.astype(f32) + jnp.sum(others.astype(f32), axis=0)
        other = other.astype(f32)
        return jnp.stack([jnp.where(mine == 0, total, other), jnp.where(mine == 0, other, total)])[None]

    own_gate_up = lax.dynamic_index_in_dim(grad_gate_up, me_z, 0, keepdims=False)
    own_down = lax.dynamic_slice_in_dim(grad_down, me_z * d_slice, d_slice, 1)
    qk_grad = lax.dynamic_slice_in_dim(sums[2:4, :HEAD_DIM], me_z * qk_part, qk_part, 1)
    return (
        hidden_out,
        grad_hidden,
        sums[0:2][None],
        qk_grad[None],
        grad_qkv.reshape(d_slice, qkv_cols).astype(f32)[None],
        grad_out.reshape(hd, width).astype(f32)[None],
        sums[8 : 8 + experts_all].T[None],
        settle(own_gate_up, own_gu, two_gu),
        settle(own_down, own_dn, two_dn),
    )


def solution(mesh):
    in_specs = (
        P(("expert", "shard"), None),
        P(("expert", "shard")),
        P(("expert", "shard"), None),
        P(None, None, "shard"),
        P(None, None, "shard"),
        P(None, "shard", None),
        P(None, "shard", None),
        P(None, "shard", None),
        P(None, "expert", "shard", None),
        P(None, "expert", None, "shard"),
        P(("expert", "shard"), None),
    )
    out_specs = (
        P(("expert", "shard"), None),
        P(("expert", "shard"), None),
        P(None, None, "shard"),
        P(None, None, "shard"),
        P(None, "shard", None),
        P(None, "shard", None),
        P(None, "shard", None),
        P(None, "expert", "shard", None),
        P(None, "expert", None, "shard"),
    )
    return jax.shard_map(shards, mesh=mesh, in_specs=in_specs, out_specs=out_specs, check_vma=False)
```

```python
import functools

import jax
import jax.numpy as jnp
from jax import lax
from jax.experimental import pallas as pl
from jax.experimental.pallas import tpu as pltpu
from jax.sharding import PartitionSpec as P

HEADS = 32
KV_HEADS = 4
HEAD_DIM = 128
TOP = 8

bf16 = jnp.bfloat16
f32 = jnp.float32
highest = lax.Precision.HIGHEST
eps_norm = 1e-06
rope_base = 1000000.0
neg_fill = -1e30


def dot(left, right, dims, out=f32):
    return lax.dot_general(left, right, (dims, ((), ())), preferred_element_type=out)


def mm(left, right):
    return dot(left, right, ((1,), (0,)))


def mm_nt(left, right):
    return dot(left, right, ((1,), (1,)))


def mm_tn(left, right):
    return dot(left, right, ((0,), (0,)))


def inv_rms(value):
    return lax.rsqrt(jnp.mean(value * value, axis=-1, keepdims=True) + eps_norm)


def rms_back(value, gain, grad):
    r = inv_rms(value)
    c = grad * gain
    back = r * c - value * (r * r * r) * jnp.mean(c * value, axis=-1, keepdims=True)
    return back, grad * value * r


def rotary_tables(length):
    half = HEAD_DIM // 2
    frequency = rope_base ** (-(jnp.arange(half, dtype=f32) * 2.0) / HEAD_DIM)
    angles = jnp.arange(length, dtype=f32)[:, None] * frequency[None, :]
    cos, sin = jnp.cos(angles), jnp.sin(angles)
    return jnp.concatenate([cos, cos], axis=1), jnp.concatenate([-sin, sin], axis=1)


MESH = pl.DeviceIdType.MESH


class Place:
    def __init__(self, n_expert, n_shard, group):
        self.e = lax.axis_index("expert")
        self.z = lax.axis_index("shard")
        self.n_expert, self.n_shard, self.group = n_expert, n_shard, group
        self.chip, self.core = self.e // 2, self.e % 2
        self.chips = n_expert // 2

    def z_dev(self, t):
        return (self.e, self.z ^ t)

    def slot(self, t, other=0):
        return (self.chip ^ t) * 2 + (self.core ^ other)

    def chip_dev(self, t):
        return (self.slot(t), self.z)

    def mate(self):
        return (self.e ^ 1, self.z)


class Net:
    def __init__(self, send, recv, local):
        self.send, self.recv, self.local = send, recv, local
        self.n, self.m, self.open = 0, 0, []

    def push(self, src, dst, dev):
        i = self.n
        self.n += 1
        copy = pltpu.make_async_remote_copy(
            src_ref=src, dst_ref=dst, send_sem=self.send.at[i], recv_sem=self.recv.at[i],
            device_id=dev, device_id_type=MESH,
        )
        copy.start()
        self.open.append(copy)
        return copy

    def copy(self, src, dst):
        i = self.m
        self.m += 1
        copy = pltpu.make_async_copy(src, dst, self.local.at[i])
        copy.start()
        return copy

    def done(self, copy):
        copy.wait_send()
        self.open = [c for c in self.open if c is not copy]

    def sent(self):
        for copy in self.open:
            copy.wait_send()
        self.open = []


def greet(devices):
    barrier = pltpu.get_barrier_semaphore()
    for dev in devices:
        pl.semaphore_signal(barrier, inc=1, device_id=dev, device_id_type=MESH)
    pl.semaphore_wait(barrier, len(devices))


def everyone(at):
    return (
        [at.z_dev(t) for t in range(1, at.n_shard)]
        + [at.chip_dev(t) for t in range(1, at.chips)]
        + [at.mate()]
    )


def arrive(copies):
    for copy in copies:
        copy.wait_recv()


def spread(net, at, pieces):
    own = [p(at.e) for p in pieces]
    mate = [net.push(o, o, at.mate()) for o in own]
    out = [(t, [net.push(o, o, at.chip_dev(t)) for o in own]) for t in range(1, at.chips)]
    return mate, out


def pass_on(net, at, pieces, state):
    mate, out = state
    for t, copies in out:
        for p, copy in zip(pieces, copies):
            copy.wait_recv()
            got = p(at.slot(t))
            mate.append(net.push(got, got, at.mate()))
    return mate


def comm_call(kernel, cid, n_remote, n_local, scratch, outs, vmem_mb, in_specs=None, out_specs=None, cost=None):
    any_spec = pl.BlockSpec(memory_space=pl.ANY)

    def call(*args):
        return pl.pallas_call(
            kernel,
            out_shape=outs,
            in_specs=in_specs or [any_spec] * len(args),
            out_specs=out_specs or [any_spec] * len(outs),
            scratch_shapes=list(scratch)
            + [
                pltpu.SemaphoreType.DMA((n_remote,)),
                pltpu.SemaphoreType.DMA((n_remote,)),
                pltpu.SemaphoreType.DMA((n_local,)),
            ],
            compiler_params=pltpu.CompilerParams(
                collective_id=cid, has_side_effects=True, vmem_limit_bytes=vmem_mb << 20
            ),
            cost_estimate=cost,
        )(*args)

    return call


def tiled(size, most):
    while size % most:
        most //= 2
    return most


def halves(at):
    return list(range(1, at.chips)) + [0]


def rope_rows(value, cos, sin):
    return value * cos + pltpu.roll(value, HEAD_DIM // 2, 1) * sin


def rope_rows_back(grad, cos, sin):
    return grad * cos + pltpu.roll(grad * sin, HEAD_DIM // 2, 1)


def eight(per):
    return jnp.sum(per.reshape(per.shape[0] // 8, 8, per.shape[1]), axis=0)


def span(i, size):
    if isinstance(i, int):
        return pl.ds(i * size, size)
    return pl.ds(pl.multiple_of(i * size, size), size)


def soft_block(q_ref, k_ref, seg_row, seg_col, h, i, block, scale):
    rows, keys = pl.ds(i * block, block), pl.ds(0, (i + 1) * block)
    scores = mm_nt(q_ref[rows, span(h, HEAD_DIM)], k_ref[keys, :]) * scale
    width = (i + 1) * block
    at_q = i * block + lax.broadcasted_iota(jnp.int32, (block, width), 0)
    at_k = lax.broadcasted_iota(jnp.int32, (block, width), 1)
    allowed = (at_k <= at_q) & (seg_row[0:1, keys] == seg_col[rows, 0:1])
    scores = jnp.where(allowed, scores, neg_fill)
    raised = jnp.exp(scores - jnp.max(scores, axis=-1, keepdims=True))
    return raised / jnp.sum(raised, axis=-1, keepdims=True)


def front_kernel(
    dims, x, small, seg_own, w_qkv, w_out, w_gu, w_dn, cot, mask, cos_h, sin_h,
    small_out, seg_out, heads_out, a_out, raw_out, q_out, k_out, v_out, o_out, x1_out, b_out,
    gate_up, down, cot_all, mask_all, b_pair,
    x_all, small_all, seg_col, heads, a, raw, q, k, v, o, w_o, part, parts_in, cos, sin, gains, seg_row, x1, b_own,
    send, recv, local,
):
    at = Place(*dims)
    net = Net(send, recv, local)
    z, e, group = at.z, at.e, at.group
    tok = x.shape[0]
    length, width = x_all.shape
    mine = z // group
    rows_e, cols = heads.shape[2], heads.shape[3]
    hd = cols - 2 * HEAD_DIM
    n_heads = hd // HEAD_DIM
    q_width = HEADS * HEAD_DIM
    d_slice = w_gu.shape[1]
    scale = HEAD_DIM ** (-0.5)
    block = tok

    def heads_of(dest):
        kv = (dest * n_heads) // (HEADS // KV_HEADS)
        rows = span(e, rows_e)
        return [
            (w_qkv.at[rows, span(dest, hd)], heads.at[z, e, :, pl.ds(0, hd)]),
            (w_qkv.at[rows, span(HEADS + kv, HEAD_DIM)], heads.at[z, e, :, pl.ds(hd, HEAD_DIM)]),
            (w_qkv.at[rows, span(HEADS + KV_HEADS + kv, HEAD_DIM)], heads.at[z, e, :, pl.ds(hd + HEAD_DIM, HEAD_DIM)]),
        ]

    def d_cols(ref, who):
        return ref.at[:, span(who, d_slice)]

    half0, half1 = pl.ds(0, tok), pl.ds(tok, tok)
    first = [
        net.copy(x, x_all.at[span(z, tok)]),
        net.copy(small, small_all.at[z]),
        net.copy(seg_own, seg_col.at[span(z, tok)]),
        net.copy(cos_h, cos),
        net.copy(sin_h, sin),
    ]
    local_heads = [net.copy(s, d) for s, d in heads_of(z)]
    local_cot = [net.copy(cot, cot_all.at[e, half0]), net.copy(mask, mask_all.at[e, half0])]
    load_out = net.copy(w_out, w_o)
    here = [net.copy(w_gu.at[mine], gate_up.at[z]), net.copy(w_dn.at[mine], d_cols(down, z))]
    greet(everyone(at))
    got_heads = [net.push(s, d, at.z_dev(t)) for t in range(1, at.n_shard) for s, d in heads_of(z ^ t)]
    got_x = []
    for t in range(1, at.n_shard):
        got_x.append(net.push(small, small_all.at[z], at.z_dev(t)))
        got_x.append(net.push(seg_own, seg_col.at[span(z, tok)], at.z_dev(t)))
        got_x.append(net.push(x, x_all.at[span(z, tok)], at.z_dev(t)))
    for c in local_heads:
        c.wait()
    arrive(got_heads)
    pieces = [lambda who: heads.at[:, who]]
    heads_state = spread(net, at, pieces)
    for c in first:
        c.wait()
    arrive(got_x)
    other = (z ^ group) // group
    cut = d_slice // 2
    low, high = pl.ds(0, cut), pl.ds(cut, cut)
    pieces_w = [
        (w_gu.at[other, low], gate_up.at[z, low], gate_up.at[z ^ group, low]),
        (w_gu.at[other, high], gate_up.at[z, high], gate_up.at[z ^ group, high]),
        (w_dn.at[other], d_cols(down, z), d_cols(down, z ^ group)),
    ]
    from_partner = {}

    def fetch_piece(i):
        src, dst, got = pieces_w[i]
        from_partner[i] = (net.push(src, dst, at.z_dev(group)), got)

    fetch_piece(0)

    def hand_on(i):
        copy, ref = from_partner[i]
        copy.wait_recv()
        for t in range(1, group):
            got_w.append(net.push(ref, ref, at.z_dev(t)))

    got_w = []
    for t in range(1, group):
        got_w.append(net.push(w_gu.at[mine], gate_up.at[z], at.z_dev(t)))
        got_w.append(net.push(w_dn.at[mine], d_cols(down, z), at.z_dev(t)))
    got_cot = [
        net.push(cot, cot_all.at[e, half1], at.z_dev(group)),
        net.push(mask, mask_all.at[e, half1], at.z_dev(group)),
    ]

    qk = []
    for s in range(at.n_shard):
        rows = small_all[s, 0:16, :].astype(f32)
        gains[0:2, span(s, d_slice)] = rows[0:2]
        seg_row[0:1, span(s, tok)] = rows[4:5, :tok]
        qk.append(rows[2:4, :HEAD_DIM])
    qk = sum(qk[1:], qk[0])
    step = 16

    def norm_rows(i, _):
        rows = span(i, step)
        value = x_all[rows, :].astype(f32)
        a[rows, :] = (value * inv_rms(value) * gains[0:1, :]).astype(bf16)
        return 0

    lax.fori_loop(0, length // step, norm_rows, 0)
    last = pass_on(net, at, pieces, heads_state)
    arrive(last)
    keep = [net.copy(heads, heads_out), net.copy(a, a_out), net.copy(small_all, small_out), net.copy(seg_col, seg_out)]

    wide = tiled(cols, 256)

    def project(i, _):
        tile = span(i, wide)
        raw[:, tile] = mm(a[...], heads[:, :, :, tile].reshape(width, wide))
        return 0

    lax.fori_loop(0, cols // wide, project, 0)
    keep.append(net.copy(raw, raw_out))

    def head_rows(i, _):
        rows = span(i, block)
        cos_b, sin_b = cos[rows, :], sin[rows, :]
        for h in range(n_heads + 1):
            value = raw[rows, pl.ds(h * HEAD_DIM, HEAD_DIM)]
            gain = qk[0:1] if h < n_heads else qk[1:2]
            value = rope_rows(value * inv_rms(value) * gain, cos_b, sin_b).astype(bf16)
            if h < n_heads:
                q[rows, pl.ds(h * HEAD_DIM, HEAD_DIM)] = value
            else:
                k[rows, :] = value
        v[rows, :] = raw[rows, pl.ds(hd + HEAD_DIM, HEAD_DIM)].astype(bf16)
        return 0

    lax.fori_loop(0, length // block, head_rows, 0)
    keep += [net.copy(q, q_out), net.copy(k, k_out), net.copy(v, v_out)]
    for c in local_cot:
        c.wait()
    arrive(got_cot)
    cots = [lambda who: cot_all.at[who], lambda who: mask_all.at[who]]
    cot_state = spread(net, at, cots)

    fetch_piece(1)

    def one_head(h, _):
        for i in range(length // block):
            soft = soft_block(q, k, seg_row, seg_col, h, i, block, scale).astype(bf16)
            mixed = mm(soft, v[pl.ds(0, (i + 1) * block), :])
            o[pl.ds(i * block, block), span(h, HEAD_DIM)] = mixed.astype(bf16)
        return 0

    lax.fori_loop(0, n_heads, one_head, 0)
    hand_on(0)
    fetch_piece(2)
    keep.append(net.copy(o, o_out))
    load_out.wait()
    wide_o = tiled(width, 256)

    def out_tile(i, _):
        tile = span(i, wide_o)
        part[:, tile] = mm(o[...], w_o[:, tile]).astype(bf16)
        return 0

    lax.fori_loop(0, width // wide_o, out_tile, 0)
    sums = [net.push(part.at[span(z ^ t, tok)], parts_in.at[t - 1], at.z_dev(t)) for t in range(1, at.n_shard)]
    last = pass_on(net, at, cots, cot_state)
    hand_on(1)
    arrive(sums)

    def middle_rows(i, _):
        rows = span(i, step)
        total = part[pl.ds(pl.multiple_of(z * tok + i * step, step), step), :].astype(f32)
        for t in range(1, at.n_shard):
            total += parts_in[t - 1, rows, :].astype(f32)
        value = x_all[pl.ds(pl.multiple_of(z * tok + i * step, step), step), :].astype(f32) + total
        x1[rows, :] = value
        b_own[rows, :] = (value * inv_rms(value) * gains[1:2, :]).astype(bf16)
        return 0

    lax.fori_loop(0, tok // step, middle_rows, 0)
    swap = net.push(b_own, b_pair.at[half1], at.z_dev(group))
    keep += [net.copy(b_own, b_pair.at[half0]), net.copy(x1, x1_out), net.copy(b_own, b_out)]
    hand_on(2)
    swap.wait_recv()
    arrive(last + got_w)
    for c in keep + here:
        c.wait()
    net.sent()


def expert_kernel(
    dims, b_pair, cot_all, mask_all, gate_up, down, router_t,
    out_part, ggu, gdn, db_in, ex_in, land_gu, land_dn, core_in, core_x,
    w_gu, w_dn, rows, cot_t, mask_t, gu, hid, d_pre, d_y, stage, stage_x, own, own_x, add, add_x, w_r, d_r, g_tile, d_tile,
    tile_sem, send, recv, local,
):
    at = Place(*dims)
    net = Net(send, recv, local)
    z, e, group = at.z, at.e, at.group
    n_slices, d_slice, ff2 = gate_up.shape
    ff, width = w_dn.shape
    two = b_pair.shape[0]
    four = 2 * two
    expert = e * (at.n_shard // group) + z // group
    step = 16
    fine = tiled(ff, 256)
    wide = tiled(width, 512)

    pair = net.copy(b_pair, rows.at[0, 1])
    loads = [net.copy(gate_up.at[s], w_gu.at[pl.ds(s * d_slice, d_slice)]) for s in range(n_slices)]
    loads.append(net.copy(down, w_dn))

    def fetch(t):
        return [
            net.copy(cot_all.at[at.slot(t, 1)], cot_t.at[0]),
            net.copy(cot_all.at[at.slot(t)], cot_t.at[1]),
            net.copy(mask_all.at[at.slot(t, 1)], mask_t.at[0]),
            net.copy(mask_all.at[at.slot(t)], mask_t.at[1]),
        ]

    fetched = fetch(0)
    greet([at.chip_dev(t) for t in range(1, at.chips)] + [at.mate()] + [at.z_dev(t) for t in range(1, group)])
    from_mate = {0: net.push(b_pair, rows.at[0, 0], at.mate())}
    near = [t for t in (1, 2) if t < at.chips]
    far = [t for t in range(1, at.chips) if t not in near]
    from_chip = {t: net.push(b_pair, rows.at[t, 1], at.chip_dev(t)) for t in near}

    def pass_rows(t):
        from_chip[t].wait_recv()
        from_mate[t] = net.push(rows.at[t, 1], rows.at[t, 0], at.mate())

    mates, outs = {}, []

    def finish(t):
        arrive(mates[t])
        c, cx = net.copy(core_in.at[t], add), net.copy(core_x.at[t], add_x)
        c.wait()
        cx.wait()

        def add_rows(i, _):
            r = span(i, step)
            own[t, r, :] = (own[t, r, :].astype(f32) + add[r, :].astype(f32)).astype(bf16)
            own_x[t, r, :] = (own_x[t, r, :].astype(f32) + add_x[r, :].astype(f32)).astype(bf16)
            return 0

        lax.fori_loop(0, two // step, add_rows, 0)
        if t:
            outs.append(net.push(own.at[t], db_in.at[t], at.chip_dev(t)))
            outs.append(net.push(own_x.at[t], ex_in.at[t], at.chip_dev(t)))

    lanes = lax.broadcasted_iota(jnp.int32, (four, 128), 1)
    used = {}

    def work(t, fetched, before, after):
        logits = mm_nt(rows[t].reshape(four, width), router_t[...])
        chosen = mask_t[...].reshape(four, 128).astype(f32) > 0
        masked = jnp.where(chosen, logits, neg_fill)
        raised = jnp.where(chosen, jnp.exp(masked - jnp.max(masked, axis=1, keepdims=True)), 0.0)
        weight = raised / jnp.sum(raised, axis=1, keepdims=True)
        weight = jnp.sum(jnp.where(lanes == expert, weight, 0.0), axis=1, keepdims=True)
        w_r[...] = jnp.broadcast_to(weight, (four, 128))
        d_r[...] = jnp.zeros_like(d_r)

        def up(j, _):
            tile, tile_u = span(j, fine), pl.ds(pl.multiple_of(ff + j * fine, fine), fine)
            x = rows[t].reshape(four, width)
            g = mm(x, w_gu[:, tile])
            u = mm(x, w_gu[:, tile_u])
            gu[:, tile] = g
            gu[:, tile_u] = u
            hid[t, :, tile] = (g * jax.nn.sigmoid(g) * u).astype(bf16)
            return 0

        lax.fori_loop(0, ff // fine, up, 0)
        before()
        for c in fetched:
            c.wait()

        def back_y(n, _):
            tile = span(n, wide)
            y = mm(hid[t], w_dn[:, tile]).astype(bf16).astype(f32)
            c = cot_t[:, :, tile].reshape(four, wide).astype(f32)
            w = w_r[:, 0:1]
            d_r[...] += jnp.broadcast_to(jnp.sum(c * y, axis=1, keepdims=True), (four, 128))
            d_y[t, :, tile] = (w * c).astype(bf16)
            cot_t[:, :, tile] = (w * y).astype(bf16).reshape(2, two, wide)
            return 0

        lax.fori_loop(0, width // wide, back_y, 0)
        kept = [
            net.copy(cot_t.at[0], out_part.at[at.slot(t, 1)]),
            net.copy(cot_t.at[1], out_part.at[at.slot(t)]),
        ]

        def back_h(j, _):
            tile, tile_u = span(j, fine), pl.ds(pl.multiple_of(ff + j * fine, fine), fine)
            d_h = mm_nt(d_y[t], w_dn[tile, :])
            g, u = gu[:, tile], gu[:, tile_u]
            sig = jax.nn.sigmoid(g)
            d_pre[t, :, tile] = (d_h * u * sig * (1.0 + g * (1.0 - sig))).astype(bf16)
            d_pre[t, :, tile_u] = (d_h * g * sig).astype(bf16)
            return 0

        lax.fori_loop(0, ff // fine, back_h, 0)
        for c in kept:
            c.wait()
        after()
        p = t % 2
        for c in used.pop(p, []):
            net.done(c)

        def back_b(n, _):
            tile = span(n, wide)
            value = mm_nt(d_pre[t], w_gu[tile, :]).astype(bf16)
            stage[p, :, tile] = value[:two]
            own[t, :, tile] = value[two:]
            return 0

        lax.fori_loop(0, width // wide, back_b, 0)
        routed = d_r[...]
        high = routed.astype(bf16)
        low = (routed - high.astype(f32)).astype(bf16)
        none = jnp.zeros_like(high)
        extra = jnp.where(lanes == expert, high, jnp.where(lanes == expert + 64, low, none))
        stage_x[p] = extra[:two]
        own_x[t] = extra[two:]
        mates[t] = [
            net.push(stage.at[p], core_in.at[t], at.mate()),
            net.push(stage_x.at[p], core_x.at[t], at.mate()),
        ]
        used[p] = mates[t]

    pair.wait()
    from_mate[0].wait_recv()
    for c in loads:
        c.wait()
    for c in fetched[2:]:
        c.wait()
    order = list(range(at.chips))
    state = {"next": fetched[:2]}
    for t in order:
        if t == 1:
            for i in near:
                pass_rows(i)
            for i in far:
                from_chip[i] = net.push(b_pair, rows.at[i, 1], at.chip_dev(i))
        if t:
            if t in far:
                pass_rows(t)
            from_mate[t].wait_recv()

        def before(t=t):
            if t:
                finish(t - 1)

        def after(t=t):
            if t + 1 < at.chips:
                more = fetch(t + 1)
                state["next"] = more[:2]
                state["mask"] = more[2:]

        work(t, state["next"], before, after)
        for c in state.pop("mask", []):
            c.wait()
    finish(at.chips - 1)
    keep = [net.copy(own.at[0], db_in.at[0]), net.copy(own_x.at[0], ex_in.at[0])]

    part = tiled(width, 256)
    per = d_slice // part

    def out_copy(slot, i):
        who = z ^ (n_slices - 1 - i // per)
        return pltpu.make_async_copy(g_tile.at[slot], ggu.at[who, span(i % per, part)], tile_sem.at[slot])

    def grad_up(i, _):
        slot = i % 2

        @pl.when(i >= 2)
        def _():
            out_copy(slot, i - 2).wait()

        who = z ^ (n_slices - 1 - i // per)
        x = rows[:, :, :, span(who * per + i % per, part)].reshape(at.chips * four, part)
        g_tile[slot] = mm_tn(x, d_pre[...].reshape(at.chips * four, ff2)).astype(bf16)
        out_copy(slot, i).start()
        return 0

    def down_copy(slot, i):
        return pltpu.make_async_copy(d_tile.at[slot], gdn.at[span(i, fine)], tile_sem.at[slot])

    def grad_down(i, _):
        slot = i % 2

        @pl.when(i >= 2)
        def _():
            down_copy(slot, i - 2).wait()

        h = hid[:, :, span(i, fine)].reshape(at.chips * four, fine)
        d_tile[slot] = mm_tn(h, d_y[...].reshape(at.chips * four, width)).astype(bf16)
        down_copy(slot, i).start()
        return 0

    n_down = ff // fine
    lax.fori_loop(0, n_down, grad_down, 0)
    for i in range(max(0, n_down - 2), n_down):
        down_copy(i % 2, i).wait()
    for t in range(1, group):
        outs.append(net.push(gdn.at[:, span(z ^ t ^ group, d_slice)], land_dn.at[t - 1], at.z_dev(t)))
    n_up, n_early = width // part, (group - 1) * per
    lax.fori_loop(0, n_early, grad_up, 0)
    for i in range(n_early - 2, n_early):
        out_copy(i % 2, i).wait()
    half = pl.ds(0, d_slice // 2)
    for t in range(1, group):
        outs.append(net.push(ggu.at[z ^ t ^ group, half], land_gu.at[t - 1], at.z_dev(t)))

    def grad_rest(i, _):
        slot = i % 2

        @pl.when(i >= n_early + 2)
        def _():
            out_copy(slot, i - 2).wait()

        who = z ^ (n_slices - 1 - i // per)
        x = rows[:, :, :, span(who * per + i % per, part)].reshape(at.chips * four, part)
        g_tile[slot] = mm_tn(x, d_pre[...].reshape(at.chips * four, ff2)).astype(bf16)
        out_copy(slot, i).start()
        return 0

    lax.fori_loop(n_early, n_up, grad_rest, 0)
    for i in range(n_up - 2, n_up):
        out_copy(i % 2, i).wait()
    for c in keep:
        c.wait()
    arrive(outs)
    net.sent()


def norm_kernel(
    dims, early, db, ex, ggu, gdn, out_part, x1, b, cot, rw, router_t, gains,
    gx1, do_all, gain_two, g_router, land_gu, late_gu, land_dn, out_in,
    own, own_x, half_out, half_x, swap_in, swap_x, logit, d_out, out_own, out_core,
    send, recv, local,
):
    at = Place(*dims)
    net = Net(send, recv, local)
    z, e, group = at.z, at.e, at.group
    tok = x1.shape[0]
    n_parts = db.shape[0]
    loads = [net.copy(db, own), net.copy(ex, own_x)]
    load_own = {t: net.copy(out_part.at[at.slot(t)], out_own.at[t]) for t in halves(at)}
    greet(everyone(at))
    step = 16
    for c in loads:
        c.wait()

    def sums(src):
        total, total_x = own[0, src, :].astype(f32), own_x[0, src, :].astype(f32)
        for t in range(1, n_parts):
            total += own[t, src, :].astype(f32)
            total_x += own_x[t, src, :].astype(f32)
        return total, total_x

    def partner(i, _):
        total, total_x = sums(pl.ds(pl.multiple_of(tok + i * step, step), step))
        half_out[span(i, step), :] = total.astype(bf16)
        half_x[span(i, step), :] = total_x.astype(bf16)
        return 0

    lax.fori_loop(0, tok // step, partner, 0)
    swaps = [net.push(half_out, swap_in, at.z_dev(group)), net.push(half_x, swap_x, at.z_dev(group))]
    d_slice = ggu.shape[1]
    landed = []
    for t in range(1, group):
        j = z ^ t ^ group
        if not early:
            landed.append(net.push(ggu.at[j, pl.ds(0, d_slice // 2)], land_gu.at[t - 1], at.z_dev(t)))
            landed.append(net.push(gdn.at[:, span(j, d_slice)], land_dn.at[t - 1], at.z_dev(t)))
        landed.append(net.push(ggu.at[j, pl.ds(d_slice // 2, d_slice // 2)], late_gu.at[t - 1], at.z_dev(t)))
    mates = {t: net.push(out_part.at[at.slot(t, 1)], out_core.at[t], at.mate()) for t in halves(at)}
    outs = []
    for t in halves(at):
        load_own[t].wait()
        mates[t].wait_recv()

        def add(i, _, t=t):
            rows = span(i, step)
            out_own[t, rows, :] = (out_own[t, rows, :].astype(f32) + out_core[t, rows, :].astype(f32)).astype(bf16)
            return 0

        lax.fori_loop(0, 2 * tok // step, add, 0)
        if t:
            outs.append(net.push(out_own.at[t], out_in.at[t], at.chip_dev(t)))
    keep_own = net.copy(out_own.at[0], out_in.at[0])
    arrive(swaps)
    gain_two[...] = jnp.zeros_like(gain_two)

    def owner(i, _):
        rows = span(i, step)
        grad, routed = sums(rows)
        grad += swap_in[rows, :].astype(f32)
        routed += swap_x[rows, :].astype(f32)
        routed = routed + pltpu.roll(routed, 64, 1)
        weight = rw[rows, :]
        d_logit = weight * (routed - jnp.sum(weight * routed, axis=1, keepdims=True))
        high = d_logit.astype(bf16)
        low = (d_logit - high.astype(f32)).astype(bf16)
        logit[0, rows, :] = high
        logit[1, rows, :] = low
        grad += mm(high, router_t[...]) + mm(low, router_t[...])
        value = x1[rows, :]
        r = inv_rms(value)
        c = grad * gains[1:2, :]
        back = cot[rows, :].astype(f32) + r * c - value * (r * r * r * jnp.mean(c * value, axis=-1, keepdims=True))
        gx1[rows, :] = back
        d_out[rows, :] = back.astype(bf16)
        gain_two[...] += eight(grad * value * r)
        return 0

    lax.fori_loop(0, tok // step, owner, 0)
    mine = do_all.at[span(z, tok)]
    keep = net.copy(d_out, mine)
    copies = [net.push(d_out, mine, at.z_dev(t)) for t in range(1, at.n_shard)]
    g_router[...] = mm_tn(logit[0], b[...]) + mm_tn(logit[1], b[...])
    keep.wait()
    keep_own.wait()
    arrive(copies + landed + outs)
    net.sent()


def back_kernel(
    dims, do_h, w_out, o_h, q_h, k_h, v_h, raw_h, cos_h, sin_h, seg_h, small, ggu, gdn, land_gu, late_gu, land_dn, out_parts, x1,
    d_qkv_out, qk_gain, g_att, hidden, two_gu, own_gu, far_dn,
    do_all, w_o, o, q, k, v, raw, cos, sin, seg_col, seg_row, mix, d_qkv, dk, dv,
    sum_gu, add_gu, sum_dn, add_dn, out_in, half_out, swap_in, g_out, g_core, g_in, share_own,
    send, recv, local,
):
    at = Place(*dims)
    net = Net(send, recv, local)
    z, e, group = at.z, at.e, at.group
    length, width = do_all.shape
    tok = x1.shape[0]
    cols = raw.shape[1]
    hd = cols - 2 * HEAD_DIM
    n_heads = hd // HEAD_DIM
    d_slice = ggu.shape[1]
    scale = HEAD_DIM ** (-0.5)
    block = tok
    step = 16
    far = z ^ group

    def d_cols(ref, who):
        return ref.at[:, span(who, d_slice)]

    load_dn = [net.copy(d_cols(gdn, far), sum_dn)] + [net.copy(land_dn.at[t - 1], add_dn.at[t - 1]) for t in range(1, group)]
    cut = d_slice // 2
    halves_gu = [pl.ds(0, cut), pl.ds(cut, cut)]
    load_gu = [
        [net.copy(ggu.at[far, r], sum_gu.at[i])] + [net.copy(land.at[t - 1], add_gu.at[i, t - 1]) for t in range(1, group)]
        for i, (r, land) in enumerate(zip(halves_gu, (land_gu, late_gu)))
    ]
    load_a = [net.copy(do_h, do_all), net.copy(o_h, o)]
    load_out = net.copy(out_parts, out_in)
    load_b = [
        net.copy(s, d)
        for s, d in ((w_out, w_o), (q_h, q), (k_h, k), (v_h, v), (raw_h, raw), (cos_h, cos), (sin_h, sin), (seg_h, seg_col))
    ]
    greet(everyone(at))

    def sum_in(rows):
        total = out_in[0, rows, :].astype(f32)
        for t in range(1, at.chips):
            total += out_in[t, rows, :].astype(f32)
        return total

    def partner(i, _):
        half_out[span(i, step), :] = sum_in(pl.ds(pl.multiple_of(tok + i * step, step), step)).astype(bf16)
        return 0

    def add_up(total, adds):
        def rows_of(i, _):
            rows = span(i, step)
            value = total[rows, :].astype(f32)
            for t in range(1, group):
                value += adds[t - 1, rows, :].astype(f32)
            total[rows, :] = value.astype(bf16)
            return 0

        lax.fori_loop(0, total.shape[0] // step, rows_of, 0)

    load_out.wait()
    lax.fori_loop(0, tok // step, partner, 0)
    swap = net.push(half_out, swap_in, at.z_dev(group))
    got = []
    for i in range(2):
        for c in load_gu[i]:
            c.wait()
        add_up(sum_gu.at[i], add_gu.at[i])
        got.append(net.push(sum_gu.at[i], two_gu.at[halves_gu[i]], at.z_dev(group)))
    for t in range(1, group):
        got.append(net.push(ggu.at[z ^ t], own_gu.at[t - 1], at.z_dev(t)))
    for c in load_dn:
        c.wait()
    add_up(sum_dn, add_dn)
    keep_dn = net.copy(sum_dn, far_dn)

    for c in load_a:
        c.wait()
    share = share_own.shape[0]

    wide = tiled(hd, 256)
    each = wide // share

    def out_grad(i, _):
        tile = mm_tn(o[:, span(i, wide)], do_all[...]).astype(bf16)
        for j in range(each):
            g_out[each * i + j] = tile[j * share : (j + 1) * share]
        return 0

    lax.fori_loop(0, hd // wide, out_grad, 0)
    g_mates = {t: net.push(g_out.at[at.slot(t, 1)], g_core.at[t], at.mate()) for t in halves(at)}

    for c in load_b:
        c.wait()
    qk = []
    for s in range(at.n_shard):
        rows = small[s, 0:16, :].astype(f32)
        seg_row[0:1, span(s, tok)] = rows[4:5, :tok]
        qk.append(rows[2:4, :HEAD_DIM])
    qk = sum(qk[1:], qk[0])

    def mix_tile(i, _):
        tile = span(i, wide)
        mix[:, tile] = mm_nt(do_all[...], w_o[tile, :]).astype(bf16)
        return 0

    lax.fori_loop(0, hd // wide, mix_tile, 0)
    g_outs = []
    for t in halves(at):
        g_mates[t].wait_recv()

        def add(i, _, t=t):
            rows = span(i, step)
            s = at.slot(t)
            g_out[s, rows, :] = (g_out[s, rows, :].astype(f32) + g_core[t, rows, :].astype(f32)).astype(bf16)
            return 0

        lax.fori_loop(0, share // step, add, 0)
        if t:
            g_outs.append(net.push(g_out.at[at.slot(t)], g_in.at[t - 1], at.chip_dev(t)))

    dk[...] = jnp.zeros_like(dk)
    dv[...] = jnp.zeros_like(dv)
    qk_gain[...] = jnp.zeros_like(qk_gain)

    def one_head(h, _):
        lanes = span(h, HEAD_DIM)
        for i in range(length // block):
            rows, keys = pl.ds(i * block, block), pl.ds(0, (i + 1) * block)
            soft = soft_block(q, k, seg_row, seg_col, h, i, block, scale)
            d_mix = mix[rows, lanes]
            d_soft = mm_nt(d_mix, v[keys, :])
            d_scores = (soft * (d_soft - jnp.sum(soft * d_soft, axis=-1, keepdims=True))).astype(bf16)
            dv[keys, :] += mm_tn(soft.astype(bf16), d_mix)
            dk[keys, :] += mm_tn(d_scores, q[rows, lanes]) * scale
            dq = mm(d_scores, k[keys, :]) * scale
            value = raw[rows, lanes]
            back, per = rms_back(value, qk[0:1], rope_rows_back(dq, cos[rows, :], sin[rows, :]))
            d_qkv[rows, lanes] = back.astype(bf16)
            qk_gain[0:8, :] += eight(per)
        return 0

    lax.fori_loop(0, n_heads, one_head, 0)
    for i in range(length // block):
        rows = pl.ds(i * block, block)
        value = raw[rows, pl.ds(hd, HEAD_DIM)]
        back, per = rms_back(value, qk[1:2], rope_rows_back(dk[rows, :], cos[rows, :], sin[rows, :]))
        d_qkv[rows, pl.ds(hd, HEAD_DIM)] = back.astype(bf16)
        d_qkv[rows, pl.ds(hd + HEAD_DIM, HEAD_DIM)] = dv[rows, :].astype(bf16)
        qk_gain[8:16, :] += eight(per)
    keep = net.copy(d_qkv, d_qkv_out)

    arrive(g_outs)

    def own_share(i, _):
        rows = span(i, step)
        total = g_out[e, rows, :].astype(f32)
        for t in range(1, at.chips):
            total += g_in[t - 1, rows, :].astype(f32)
        share_own[rows, :] = total.astype(bf16)
        return 0

    lax.fori_loop(0, share // step, own_share, 0)
    keep_att = net.copy(share_own, g_att.at[e])
    keep_att.wait()
    atts = [lambda who: g_att.at[who]]
    att_state = spread(net, at, atts)
    swap.wait_recv()

    def hidden_rows(i, _):
        rows = span(i, step)
        hidden[rows, :] = (x1[rows, :] + sum_in(rows) + swap_in[rows, :].astype(f32)).astype(bf16)
        return 0

    lax.fori_loop(0, tok // step, hidden_rows, 0)
    arrive(pass_on(net, at, atts, att_state) + got)
    keep.wait()
    keep_dn.wait()
    net.sent()


def tail_kernel(
    dims, d_qkv_h, heads_h, a_h, gdn, far_dn, gx1, x, gains, gain_two, g_router, qk_gain,
    g_hidden, g_qkv, small_sum, two_dn, own_dn,
    d_qkv, heads, a, part, parts_in, g_heads, core_in, chip_in, mine, turn_in, share, sm, sm_z, sm_core, sm_chip,
    send, recv, local,
):
    at = Place(*dims)
    net = Net(send, recv, local)
    z, e, group = at.z, at.e, at.group
    length, cols = d_qkv.shape
    tok, width = x.shape
    hd = cols - 2 * HEAD_DIM
    n_heads = hd // HEAD_DIM
    rows_e = heads.shape[2]
    d_slice = width // at.n_shard
    step = 16
    load_a = [net.copy(d_qkv_h, d_qkv), net.copy(heads_h, heads)]
    load_b = net.copy(a_h, a)
    greet(everyone(at))
    for c in load_a:
        c.wait()

    wide = tiled(d_slice, 256)
    each = wide // rows_e

    load_b.wait()

    def grad_tile(s, _):
        for j in range(d_slice // wide):
            some = a[:, pl.ds(pl.multiple_of(s * d_slice + j * wide, wide), wide)]
            tile = mm_tn(some, d_qkv[...]).astype(bf16)
            for i in range(each):
                g_heads[each * j + i, s] = tile[i * rows_e : (i + 1) * rows_e]
        return 0

    lax.fori_loop(0, at.n_shard, grad_tile, 0)
    mates = {t: net.push(g_heads.at[at.slot(t, 1)], core_in.at[t], at.mate()) for t in halves(at)}

    def rows_tile(s, _):
        for j in range(d_slice // wide):
            some = heads[s, pl.ds(each * j, each)].reshape(wide, cols)
            here = pl.ds(pl.multiple_of(s * d_slice + j * wide, wide), wide)
            part[:, here] = mm_nt(d_qkv[...], some).astype(bf16)
        return 0

    lax.fori_loop(0, at.n_shard, rows_tile, 0)
    sums = [net.push(part.at[span(z ^ t, tok)], parts_in.at[t - 1], at.z_dev(t)) for t in range(1, at.n_shard)]
    chips = []
    for t in halves(at):
        mates[t].wait_recv()
        who = at.slot(t)

        def add(s, _, t=t, who=who):
            g_heads[who, s] = (g_heads[who, s].astype(f32) + core_in[t, s].astype(f32)).astype(bf16)
            return 0

        lax.fori_loop(0, at.n_shard, add, 0)
        if t:
            chips.append(net.push(g_heads.at[who], chip_in.at[t - 1], at.chip_dev(t)))
    arrive(chips)

    def total(s, _):
        value = g_heads[e, s].astype(f32)
        for t in range(1, at.chips):
            value += chip_in[t - 1, s].astype(f32)
        mine[s] = value.astype(bf16)
        return 0

    lax.fori_loop(0, at.n_shard, total, 0)
    turns = [net.push(mine.at[z ^ t], turn_in.at[z], at.z_dev(t)) for t in range(1, at.n_shard)]
    turn_own = net.copy(mine.at[z], turn_in.at[z])
    got = [net.push(far_dn, two_dn, at.z_dev(group))]
    for t in range(1, group):
        got.append(net.push(gdn.at[:, span(z ^ t, d_slice)], own_dn.at[t - 1], at.z_dev(t)))
    arrive(sums)
    sm[...] = jnp.zeros_like(sm)
    gain_one = jnp.zeros((8, width), f32)

    def owner(i, gain_one):
        rows = span(i, step)
        here = pl.ds(pl.multiple_of(z * tok + i * step, step), step)
        da = part[here, :].astype(f32)
        for t in range(1, at.n_shard):
            da += parts_in[t - 1, rows, :].astype(f32)
        back, per = rms_back(x[rows, :].astype(f32), gains[0:1, :], da)
        g_hidden[rows, :] = gx1[rows, :] + back
        return gain_one + eight(per)

    gain_one = lax.fori_loop(0, tok // step, owner, gain_one)
    row_one = jnp.sum(gain_one, axis=0, keepdims=True)
    row_two = jnp.sum(gain_two[...], axis=0, keepdims=True)
    row_q = jnp.sum(qk_gain[0:8, :], axis=0, keepdims=True)
    row_k = jnp.sum(qk_gain[8:16, :], axis=0, keepdims=True)
    for s in range(at.n_shard):
        piece = pl.ds(s * d_slice, d_slice)
        lanes = slice(s * d_slice, (s + 1) * d_slice)
        sm[s, 0:1, :] = row_one[:, lanes]
        sm[s, 1:2, :] = row_two[:, lanes]
        sm[s, 2:3, pl.ds(0, HEAD_DIM)] = row_q
        sm[s, 3:4, pl.ds(0, HEAD_DIM)] = row_k
        sm[s, 8:, :] = g_router[0 : sm.shape[1] - 8, piece]
    small_z = [net.push(sm.at[z ^ t], sm_z.at[t - 1], at.z_dev(t)) for t in range(1, at.n_shard)]
    turn_own.wait()
    arrive(turns)
    for s in range(at.n_shard):
        share[:, pl.ds(s * hd, hd)] = turn_in[s, :, pl.ds(0, hd)]
    for m in range(KV_HEADS):
        some = [s for s in range(at.n_shard) if (s * n_heads) // (HEADS // KV_HEADS) == m]
        for first, to in ((hd, HEADS + m), (hd + HEAD_DIM, HEADS + KV_HEADS + m)):
            value = turn_in[some[0], :, pl.ds(first, HEAD_DIM)].astype(f32)
            for s in some[1:]:
                value += turn_in[s, :, pl.ds(first, HEAD_DIM)].astype(f32)
            share[:, pl.ds(to * HEAD_DIM, HEAD_DIM)] = value.astype(bf16)
    keep = net.copy(share, g_qkv.at[e])
    keep.wait()
    qkvs = [lambda who: g_qkv.at[who]]
    state = spread(net, at, qkvs)
    arrive(small_z)
    value = sm[z]
    for t in range(1, at.n_shard):
        value += sm_z[t - 1]
    sm[z] = value
    c = net.push(sm.at[z], sm_core, at.mate())
    c.wait_recv()
    sm_core[...] = sm[z] + sm_core[...]
    smalls = [net.push(sm_core, sm_chip.at[t - 1], at.chip_dev(t)) for t in range(1, at.chips)]
    last = pass_on(net, at, qkvs, state)
    arrive(smalls)
    value = sm_core[...]
    for t in range(1, at.chips):
        value += sm_chip[t - 1]
    small_sum[...] = value
    arrive(last + got)
    net.sent()


def shards(
    hidden_in,
    segments,
    routes,
    norm_gains,
    qk_gains,
    w_qkv,
    w_attn_out,
    w_router,
    w_gate_up,
    w_down,
    cotangent,
):
    n_expert = lax.axis_size("expert")
    n_shard = lax.axis_size("shard")
    me_e = lax.axis_index("expert")
    me_z = lax.axis_index("shard")
    tok, width = hidden_in.shape
    exp_dev = w_gate_up.shape[1]
    experts_all = w_router.shape[2]
    d_slice, ff2 = w_gate_up.shape[2:]
    ff = ff2 // 2
    group = n_shard // exp_dev
    mine = me_z // group
    length = n_shard * tok
    h_dev = HEADS // n_shard
    hd = h_dev * HEAD_DIM
    cols = hd + 2 * HEAD_DIM
    qkv_cols = w_qkv.shape[2]
    rows_e = d_slice // n_expert
    share = hd // n_expert
    chips = n_expert // 2
    qk_part = HEAD_DIM // n_shard
    dims = (n_expert, n_shard, group)
    n_small = 16 + experts_all
    sds = jax.ShapeDtypeStruct
    vm = pltpu.VMEM
    any_spec = pl.BlockSpec(memory_space=pl.ANY)
    vmem_spec = pl.BlockSpec(memory_space=pltpu.VMEM)

    small = jnp.zeros((16, d_slice), bf16)
    small = small.at[0:2, :].set(norm_gains[0])
    small = lax.dynamic_update_slice(small, qk_gains[0], (2, me_z * qk_part))
    small = small.at[4, :tok].set(segments.astype(bf16))
    small = jnp.concatenate([small, w_router[0].T], axis=0)
    seg_own = jnp.broadcast_to(segments.astype(f32)[:, None], (tok, 128))
    ids = jnp.arange(128, dtype=jnp.int32)
    mask = jnp.sum((routes[:, :, None] == ids[None, None, :]).astype(f32), axis=1).astype(bf16)
    cos, sin = rotary_tables(length)

    outs = [
        sds((n_shard, n_small, d_slice), bf16),
        sds((length, 128), f32),
        sds((n_shard, n_expert, rows_e, cols), bf16),
        sds((length, width), bf16),
        sds((length, cols), f32),
        sds((length, hd), bf16),
        sds((length, HEAD_DIM), bf16),
        sds((length, HEAD_DIM), bf16),
        sds((length, hd), bf16),
        sds((tok, width), f32),
        sds((tok, width), bf16),
        sds((n_shard, d_slice, ff2), bf16),
        sds((ff, width), bf16),
        sds((n_expert, 2 * tok, width), bf16),
        sds((n_expert, 2 * tok, 128), bf16),
        sds((2 * tok, width), bf16),
    ]
    front = comm_call(
        functools.partial(front_kernel, dims),
        0,
        160,
        40,
        [
            vm((length, width), bf16),
            vm((n_shard, n_small, d_slice), bf16),
            vm((length, 128), f32),
            vm((n_shard, n_expert, rows_e, cols), bf16),
            vm((length, width), bf16),
            vm((length, cols), f32),
            vm((length, hd), bf16),
            vm((length, HEAD_DIM), bf16),
            vm((length, HEAD_DIM), bf16),
            vm((length, hd), bf16),
            vm((hd, width), bf16),
            vm((length, width), bf16),
            vm((n_shard - 1, tok, width), bf16),
            vm((length, HEAD_DIM), f32),
            vm((length, HEAD_DIM), f32),
            vm((8, width), f32),
            vm((8, length), f32),
            vm((tok, width), f32),
            vm((tok, width), bf16),
        ],
        outs,
        56,
    )
    (small_all, seg_col, heads, a, raw, q, k, v, o, x1, b, gate_up, down, cot_all, mask_all, b_pair) = front(
        hidden_in, small, seg_own, w_qkv[0], w_attn_out[0], w_gate_up[0], w_down[0], cotangent, mask, cos, sin
    )
    gains = jnp.zeros((8, width), f32)
    gains = gains.at[0:2].set(small_all[:, 0:2].astype(f32).transpose(1, 0, 2).reshape(2, width))
    router_t = small_all[:, 16:].transpose(1, 0, 2).reshape(experts_all, width)

    def route_weights(rows, chosen):
        logits = mm_nt(rows, router_t)
        masked = jnp.where(chosen, logits, neg_fill)
        raised = jnp.where(chosen, jnp.exp(masked - jnp.max(masked, axis=1, keepdims=True)), 0.0)
        return raised / jnp.sum(raised, axis=1, keepdims=True)

    rw = route_weights(b, mask[:, :experts_all] > 0)
    rw = jnp.concatenate([rw, jnp.zeros((tok, 128 - experts_all), f32)], axis=1)
    router_pad = jnp.concatenate([router_t, jnp.zeros((128 - experts_all, width), bf16)], axis=0)
    per_e = (n_expert, 2 * tok)
    piece = (chips, 2 * tok)
    four = 4 * tok
    if chips <= 4:
        out_part, grad_gate_up, grad_down, db_in, ex_in, land_gu, land_dn, _, _ = comm_call(
            functools.partial(expert_kernel, dims),
            4,
            60,
            60,
            [
                vm((width, ff2), bf16),
                vm((ff, width), bf16),
                vm((chips, 2, 2 * tok, width), bf16),
                vm((2, 2 * tok, width), bf16),
                vm((2, 2 * tok, 128), bf16),
                vm((four, ff2), f32),
                vm((chips, four, ff), bf16),
                vm((chips, four, ff2), bf16),
                vm((chips, four, width), bf16),
                vm((2, 2 * tok, width), bf16),
                vm((2, 2 * tok, 128), bf16),
                vm(piece + (width,), bf16),
                vm(piece + (128,), bf16),
                vm((2 * tok, width), bf16),
                vm((2 * tok, 128), bf16),
                vm((four, 128), f32),
                vm((four, 128), f32),
                vm((2, tiled(width, 256), ff2), bf16),
                vm((2, tiled(ff, 256), width), bf16),
                pltpu.SemaphoreType.DMA((2,)),
            ],
            [
                sds(per_e + (width,), bf16),
                sds((n_shard, d_slice, ff2), bf16),
                sds((ff, width), bf16),
                sds(piece + (width,), bf16),
                sds(piece + (128,), bf16),
                sds((group - 1, d_slice // 2, ff2), bf16),
                sds((group - 1, ff, d_slice), bf16),
                sds(piece + (width,), bf16),
                sds(piece + (128,), bf16),
            ],
            60,
            in_specs=[any_spec] * 5 + [vmem_spec],
        )(b_pair, cot_all, mask_all, gate_up, down, router_pad)
    else:
        rows_all = n_expert * 2 * tok
        b_rows = lax.all_gather(b_pair, "expert", axis=0, tiled=True)
        my_expert = me_e * exp_dev + mine
        rw_all = route_weights(b_rows, mask_all.reshape(rows_all, 128)[:, :experts_all] > 0)
        is_mine = ids[:experts_all] == my_expert
        rw_mine = jnp.sum(jnp.where(is_mine[None, :], rw_all, 0.0), axis=1, keepdims=True)
        w_gu = gate_up.reshape(width, ff2)
        pre = mm(b_rows, w_gu)
        g, u = pre[:, :ff], pre[:, ff:]
        sig = jax.nn.sigmoid(g)
        act = g * sig
        hidden = (act * u).astype(bf16)
        y_f = mm(hidden, down).astype(bf16).astype(f32)
        cot_f = cot_all.reshape(rows_all, width).astype(f32)
        d_route = jnp.sum(cot_f * y_f, axis=1, keepdims=True)
        out_part = (rw_mine * y_f).astype(bf16)
        d_y = (rw_mine * cot_f).astype(bf16)
        d_hidden = mm_nt(d_y, down)
        d_pre = jnp.concatenate(
            [d_hidden * u * sig * (1.0 + g * (1.0 - sig)), d_hidden * act], axis=1
        ).astype(bf16)
        d_b = mm_nt(d_pre, w_gu).astype(bf16)
        grad_down = mm_tn(hidden, d_y).astype(bf16)
        grad_gate_up = mm_tn(b_rows, d_pre).astype(bf16).reshape(n_shard, d_slice, ff2)
        high = lax.reduce_precision(d_route, 8, 7)
        low = d_route - high
        extra = jnp.where(ids[None] == my_expert, high, jnp.where(ids[None] == my_expert + 64, low, 0.0)).astype(bf16)

        def home(value):
            return lax.psum_scatter(value, "expert", scatter_dimension=0, tiled=True)[None]

        db_in, ex_in = home(d_b), home(extra)

    n_parts = db_in.shape[0]
    early = chips <= 4
    gx1, d_o, gain_two, g_router, norm_gu, late_gu, norm_dn, out_in = comm_call(
        functools.partial(norm_kernel, dims, early),
        1,
        60,
        24,
        [
            vm((n_parts, 2 * tok, width), bf16),
            vm((n_parts, 2 * tok, 128), bf16),
            vm((tok, width), bf16),
            vm((tok, 128), bf16),
            vm((tok, width), bf16),
            vm((tok, 128), bf16),
            vm((2, tok, 128), bf16),
            vm((tok, width), bf16),
            vm(piece + (width,), bf16),
            vm(piece + (width,), bf16),
        ],
        [
            sds((tok, width), f32),
            sds((length, width), bf16),
            sds((8, width), f32),
            sds((128, width), f32),
            sds((group - 1, d_slice // 2, ff2), bf16) if not early else sds((16, 128), bf16),
            sds((group - 1, d_slice // 2, ff2), bf16),
            sds((group - 1, ff, d_slice), bf16) if not early else sds((16, 128), bf16),
            sds(piece + (width,), bf16),
        ],
        60,
        in_specs=[any_spec] * 5 + [vmem_spec] * 6,
        out_specs=[vmem_spec, any_spec, vmem_spec, vmem_spec] + [any_spec] * 4,
    )(db_in, ex_in, grad_gate_up, grad_down, out_part.reshape(per_e + (width,)), x1, b, cotangent, rw, router_pad, gains)
    if not early:
        land_gu, land_dn = norm_gu, norm_dn

    d_qkv, qk_gain, grad_out, hidden_out, two_gu, own_gu, far_dn = comm_call(
        functools.partial(back_kernel, dims),
        2,
        80,
        60,
        [
            vm((length, width), bf16),
            vm((hd, width), bf16),
            vm((length, hd), bf16),
            vm((length, hd), bf16),
            vm((length, HEAD_DIM), bf16),
            vm((length, HEAD_DIM), bf16),
            vm((length, cols), f32),
            vm((length, HEAD_DIM), f32),
            vm((length, HEAD_DIM), f32),
            vm((length, 128), f32),
            vm((8, length), f32),
            vm((length, hd), bf16),
            vm((length, cols), bf16),
            vm((length, HEAD_DIM), f32),
            vm((length, HEAD_DIM), f32),
            vm((2, d_slice // 2, ff2), bf16),
            vm((2, group - 1, d_slice // 2, ff2), bf16),
            vm((ff, d_slice), bf16),
            vm((group - 1, ff, d_slice), bf16),
            vm(piece + (width,), bf16),
            vm((tok, width), bf16),
            vm((tok, width), bf16),
            vm((n_expert, share, width), bf16),
            vm((chips, share, width), bf16),
            vm((chips - 1, share, width), bf16),
            vm((share, width), bf16),
        ],
        [
            sds((length, cols), bf16),
            sds((16, HEAD_DIM), f32),
            sds((n_expert, share, width), bf16),
            sds((tok, width), bf16),
            sds((d_slice, ff2), bf16),
            sds((group - 1, d_slice, ff2), bf16),
            sds((ff, d_slice), bf16),
        ],
        60,
        in_specs=[any_spec] * 10 + [vmem_spec] + [any_spec] * 6 + [vmem_spec],
        out_specs=[any_spec, vmem_spec, any_spec, vmem_spec] + [any_spec] * 3,
    )(
        d_o,
        w_attn_out[0],
        o,
        q,
        k,
        v,
        raw,
        cos,
        sin,
        seg_col,
        small_all,
        grad_gate_up,
        grad_down,
        land_gu,
        late_gu,
        land_dn,
        out_in,
        x1,
    )

    small_rows = (8 + -(-experts_all // 8) * 8, d_slice)
    grad_hidden, grad_qkv, sums, two_dn, own_dn = comm_call(
        functools.partial(tail_kernel, dims),
        3,
        100,
        16,
        [
            vm((length, cols), bf16),
            vm((n_shard, n_expert, rows_e, cols), bf16),
            vm((length, width), bf16),
            vm((length, width), bf16),
            vm((n_shard - 1, tok, width), bf16),
            vm((n_expert, n_shard, rows_e, cols), bf16),
            vm((chips, n_shard, rows_e, cols), bf16),
            vm((chips - 1, n_shard, rows_e, cols), bf16),
            vm((n_shard, rows_e, cols), bf16),
            vm((n_shard, rows_e, cols), bf16),
            vm((rows_e, qkv_cols), bf16),
            vm((n_shard,) + small_rows, f32),
            vm((n_shard - 1,) + small_rows, f32),
            vm(small_rows, f32),
            vm((chips - 1,) + small_rows, f32),
        ],
        [
            sds((tok, width), f32),
            sds((n_expert, rows_e, qkv_cols), bf16),
            sds(small_rows, f32),
            sds((ff, d_slice), bf16),
            sds((group - 1, ff, d_slice), bf16),
        ],
        56,
        in_specs=[any_spec] * 5 + [vmem_spec] * 6,
        out_specs=[vmem_spec, any_spec, vmem_spec, any_spec, any_spec],
    )(d_qkv, heads, a, grad_down, far_dn, gx1, hidden_in, gains, gain_two, g_router, qk_gain)

    def settle(own, others, other):
        total = own.astype(f32) + jnp.sum(others.astype(f32), axis=0)
        other = other.astype(f32)
        return jnp.stack([jnp.where(mine == 0, total, other), jnp.where(mine == 0, other, total)])[None]

    own_gate_up = lax.dynamic_index_in_dim(grad_gate_up, me_z, 0, keepdims=False)
    own_down = lax.dynamic_slice_in_dim(grad_down, me_z * d_slice, d_slice, 1)
    qk_grad = lax.dynamic_slice_in_dim(sums[2:4, :HEAD_DIM], me_z * qk_part, qk_part, 1)
    return (
        hidden_out,
        grad_hidden,
        sums[0:2][None],
        qk_grad[None],
        grad_qkv.reshape(d_slice, qkv_cols).astype(f32)[None],
        grad_out.reshape(hd, width).astype(f32)[None],
        sums[8 : 8 + experts_all].T[None],
        settle(own_gate_up, own_gu, two_gu),
        settle(own_down, own_dn, two_dn),
    )


def solution(mesh):
    in_specs = (
        P(("expert", "shard"), None),
        P(("expert", "shard")),
        P(("expert", "shard"), None),
        P(None, None, "shard"),
        P(None, None, "shard"),
        P(None, "shard", None),
        P(None, "shard", None),
        P(None, "shard", None),
        P(None, "expert", "shard", None),
        P(None, "expert", None, "shard"),
        P(("expert", "shard"), None),
    )
    out_specs = (
        P(("expert", "shard"), None),
        P(("expert", "shard"), None),
        P(None, None, "shard"),
        P(None, None, "shard"),
        P(None, "shard", None),
        P(None, "shard", None),
        P(None, "shard", None),
        P(None, "expert", "shard", None),
        P(None, "expert", None, "shard"),
    )
    return jax.shard_map(shards, mesh=mesh, in_specs=in_specs, out_specs=out_specs, check_vma=False)
```

```python
import functools

import jax
import jax.numpy as jnp
from jax import lax
from jax.experimental import pallas as pl
from jax.experimental.pallas import tpu as pltpu
from jax.sharding import PartitionSpec as P

HEADS = 32
KV_HEADS = 4
HEAD_DIM = 128
TOP = 8

bf16 = jnp.bfloat16
f32 = jnp.float32
highest = lax.Precision.HIGHEST
eps_norm = 1e-06
rope_base = 1000000.0
neg_fill = -1e30


def dot(left, right, dims, out=f32):
    return lax.dot_general(left, right, (dims, ((), ())), preferred_element_type=out)


def mm(left, right):
    return dot(left, right, ((1,), (0,)))


def mm_nt(left, right):
    return dot(left, right, ((1,), (1,)))


def mm_tn(left, right):
    return dot(left, right, ((0,), (0,)))


def inv_rms(value):
    return lax.rsqrt(jnp.mean(value * value, axis=-1, keepdims=True) + eps_norm)


def rms_back(value, gain, grad):
    r = inv_rms(value)
    c = grad * gain
    back = r * c - value * (r * r * r) * jnp.mean(c * value, axis=-1, keepdims=True)
    return back, grad * value * r


def rotary_tables(length):
    half = HEAD_DIM // 2
    frequency = rope_base ** (-(jnp.arange(half, dtype=f32) * 2.0) / HEAD_DIM)
    angles = jnp.arange(length, dtype=f32)[:, None] * frequency[None, :]
    cos, sin = jnp.cos(angles), jnp.sin(angles)
    return jnp.concatenate([cos, cos], axis=1), jnp.concatenate([-sin, sin], axis=1)


MESH = pl.DeviceIdType.MESH


class Place:
    def __init__(self, n_expert, n_shard, group):
        self.e = lax.axis_index("expert")
        self.z = lax.axis_index("shard")
        self.n_expert, self.n_shard, self.group = n_expert, n_shard, group
        self.chip, self.core = self.e // 2, self.e % 2
        self.chips = n_expert // 2

    def z_dev(self, t):
        return (self.e, self.z ^ t)

    def slot(self, t, other=0):
        return (self.chip ^ t) * 2 + (self.core ^ other)

    def chip_dev(self, t):
        return (self.slot(t), self.z)

    def mate(self):
        return (self.e ^ 1, self.z)


class Net:
    def __init__(self, send, recv, local):
        self.send, self.recv, self.local = send, recv, local
        self.n, self.m, self.open = 0, 0, []

    def push(self, src, dst, dev):
        i = self.n
        self.n += 1
        copy = pltpu.make_async_remote_copy(
            src_ref=src, dst_ref=dst, send_sem=self.send.at[i], recv_sem=self.recv.at[i],
            device_id=dev, device_id_type=MESH,
        )
        copy.start()
        self.open.append(copy)
        return copy

    def copy(self, src, dst):
        i = self.m
        self.m += 1
        copy = pltpu.make_async_copy(src, dst, self.local.at[i])
        copy.start()
        return copy

    def done(self, copy):
        copy.wait_send()
        self.open = [c for c in self.open if c is not copy]

    def sent(self):
        for copy in self.open:
            copy.wait_send()
        self.open = []


def greet(devices):
    barrier = pltpu.get_barrier_semaphore()
    for dev in devices:
        pl.semaphore_signal(barrier, inc=1, device_id=dev, device_id_type=MESH)
    pl.semaphore_wait(barrier, len(devices))


def everyone(at):
    return (
        [at.z_dev(t) for t in range(1, at.n_shard)]
        + [at.chip_dev(t) for t in range(1, at.chips)]
        + [at.mate()]
    )


def arrive(copies):
    for copy in copies:
        copy.wait_recv()


def spread(net, at, pieces):
    own = [p(at.e) for p in pieces]
    mate = [net.push(o, o, at.mate()) for o in own]
    out = [(t, [net.push(o, o, at.chip_dev(t)) for o in own]) for t in range(1, at.chips)]
    return mate, out


def pass_on(net, at, pieces, state):
    mate, out = state
    for t, copies in out:
        for p, copy in zip(pieces, copies):
            copy.wait_recv()
            got = p(at.slot(t))
            mate.append(net.push(got, got, at.mate()))
    return mate


def comm_call(kernel, cid, n_remote, n_local, scratch, outs, vmem_mb, in_specs=None, out_specs=None, cost=None):
    any_spec = pl.BlockSpec(memory_space=pl.ANY)

    def call(*args):
        return pl.pallas_call(
            kernel,
            out_shape=outs,
            in_specs=in_specs or [any_spec] * len(args),
            out_specs=out_specs or [any_spec] * len(outs),
            scratch_shapes=list(scratch)
            + [
                pltpu.SemaphoreType.DMA((n_remote,)),
                pltpu.SemaphoreType.DMA((n_remote,)),
                pltpu.SemaphoreType.DMA((n_local,)),
            ],
            compiler_params=pltpu.CompilerParams(
                collective_id=cid, has_side_effects=True, vmem_limit_bytes=vmem_mb << 20
            ),
            cost_estimate=cost,
        )(*args)

    return call


def tiled(size, most):
    while size % most:
        most //= 2
    return most


def halves(at):
    return list(range(1, at.chips)) + [0]


def rope_rows(value, cos, sin):
    return value * cos + pltpu.roll(value, HEAD_DIM // 2, 1) * sin


def rope_rows_back(grad, cos, sin):
    return grad * cos + pltpu.roll(grad * sin, HEAD_DIM // 2, 1)


def eight(per):
    return jnp.sum(per.reshape(per.shape[0] // 8, 8, per.shape[1]), axis=0)


def span(i, size):
    if isinstance(i, int):
        return pl.ds(i * size, size)
    return pl.ds(pl.multiple_of(i * size, size), size)


def soft_block(q_ref, k_ref, seg_row, seg_col, h, i, block, scale):
    rows, keys = pl.ds(i * block, block), pl.ds(0, (i + 1) * block)
    scores = mm_nt(q_ref[rows, span(h, HEAD_DIM)], k_ref[keys, :]) * scale
    width = (i + 1) * block
    at_q = i * block + lax.broadcasted_iota(jnp.int32, (block, width), 0)
    at_k = lax.broadcasted_iota(jnp.int32, (block, width), 1)
    allowed = (at_k <= at_q) & (seg_row[0:1, keys] == seg_col[rows, 0:1])
    scores = jnp.where(allowed, scores, neg_fill)
    raised = jnp.exp(scores - jnp.max(scores, axis=-1, keepdims=True))
    return raised / jnp.sum(raised, axis=-1, keepdims=True)


def front_kernel(
    dims, x, small, seg_own, w_qkv, w_out, w_gu, cot, mask, cos_h, sin_h,
    small_out, seg_out, heads_out, a_out, raw_out, q_out, k_out, v_out, o_out, x1_out, b_out,
    gate_up, cot_all, mask_all, b_pair,
    x_all, small_all, seg_col, heads, a, raw, q, k, v, o, w_o, part, parts_in, cos, sin, gains, seg_row, x1, b_own,
    send, recv, local,
):
    at = Place(*dims)
    net = Net(send, recv, local)
    z, e, group = at.z, at.e, at.group
    tok = x.shape[0]
    length, width = x_all.shape
    mine = z // group
    rows_e, cols = heads.shape[2], heads.shape[3]
    hd = cols - 2 * HEAD_DIM
    n_heads = hd // HEAD_DIM
    q_width = HEADS * HEAD_DIM
    d_slice = w_gu.shape[1]
    scale = HEAD_DIM ** (-0.5)
    block = tok

    def heads_of(dest):
        kv = (dest * n_heads) // (HEADS // KV_HEADS)
        rows = span(e, rows_e)
        return [
            (w_qkv.at[rows, span(dest, hd)], heads.at[z, e, :, pl.ds(0, hd)]),
            (w_qkv.at[rows, span(HEADS + kv, HEAD_DIM)], heads.at[z, e, :, pl.ds(hd, HEAD_DIM)]),
            (w_qkv.at[rows, span(HEADS + KV_HEADS + kv, HEAD_DIM)], heads.at[z, e, :, pl.ds(hd + HEAD_DIM, HEAD_DIM)]),
        ]

    half0, half1 = pl.ds(0, tok), pl.ds(tok, tok)
    first = [
        net.copy(x, x_all.at[span(z, tok)]),
        net.copy(small, small_all.at[z]),
        net.copy(seg_own, seg_col.at[span(z, tok)]),
        net.copy(cos_h, cos),
        net.copy(sin_h, sin),
    ]
    local_heads = [net.copy(s, d) for s, d in heads_of(z)]
    local_cot = [net.copy(cot, cot_all.at[e, half0]), net.copy(mask, mask_all.at[e, half0])]
    load_out = net.copy(w_out, w_o)
    greet(everyone(at))
    got_heads = [net.push(s, d, at.z_dev(t)) for t in range(1, at.n_shard) for s, d in heads_of(z ^ t)]
    got_x = []
    for t in range(1, at.n_shard):
        got_x.append(net.push(small, small_all.at[z], at.z_dev(t)))
        got_x.append(net.push(seg_own, seg_col.at[span(z, tok)], at.z_dev(t)))
        got_x.append(net.push(x, x_all.at[span(z, tok)], at.z_dev(t)))
    for c in local_heads:
        c.wait()
    arrive(got_heads)
    pieces = [lambda who: heads.at[:, who]]
    heads_state = spread(net, at, pieces)
    for c in first:
        c.wait()
    arrive(got_x)
    other = (z ^ group) // group
    cut = d_slice // 2
    low, high = pl.ds(0, cut), pl.ds(cut, cut)
    pieces_w = [
        (w_gu.at[other, low], gate_up.at[z, low], gate_up.at[z ^ group, low]),
        (w_gu.at[other, high], gate_up.at[z, high], gate_up.at[z ^ group, high]),
    ]
    from_partner = {}

    def fetch_piece(i):
        src, dst, got = pieces_w[i]
        from_partner[i] = (net.push(src, dst, at.z_dev(group)), got)

    fetch_piece(0)

    def hand_on(i):
        copy, ref = from_partner[i]
        copy.wait_recv()
        for t in range(1, group):
            got_w.append(net.push(ref, ref, at.z_dev(t)))

    got_w = []
    for t in range(1, group):
        got_w.append(net.push(w_gu.at[mine], gate_up.at[z], at.z_dev(t)))
    got_cot = [
        net.push(cot, cot_all.at[e, half1], at.z_dev(group)),
        net.push(mask, mask_all.at[e, half1], at.z_dev(group)),
    ]

    qk = []
    for s in range(at.n_shard):
        rows = small_all[s, 0:16, :].astype(f32)
        gains[0:2, span(s, d_slice)] = rows[0:2]
        seg_row[0:1, span(s, tok)] = rows[4:5, :tok]
        qk.append(rows[2:4, :HEAD_DIM])
    qk = sum(qk[1:], qk[0])
    step = 16

    def norm_rows(i, _):
        rows = span(i, step)
        value = x_all[rows, :].astype(f32)
        a[rows, :] = (value * inv_rms(value) * gains[0:1, :]).astype(bf16)
        return 0

    lax.fori_loop(0, length // step, norm_rows, 0)
    last = pass_on(net, at, pieces, heads_state)
    arrive(last)
    keep = [net.copy(heads, heads_out), net.copy(a, a_out), net.copy(small_all, small_out), net.copy(seg_col, seg_out)]

    wide = tiled(cols, 256)

    def project(i, _):
        tile = span(i, wide)
        raw[:, tile] = mm(a[...], heads[:, :, :, tile].reshape(width, wide))
        return 0

    lax.fori_loop(0, cols // wide, project, 0)
    keep.append(net.copy(raw, raw_out))

    def head_rows(i, _):
        rows = span(i, block)
        cos_b, sin_b = cos[rows, :], sin[rows, :]
        for h in range(n_heads + 1):
            value = raw[rows, pl.ds(h * HEAD_DIM, HEAD_DIM)]
            gain = qk[0:1] if h < n_heads else qk[1:2]
            value = rope_rows(value * inv_rms(value) * gain, cos_b, sin_b).astype(bf16)
            if h < n_heads:
                q[rows, pl.ds(h * HEAD_DIM, HEAD_DIM)] = value
            else:
                k[rows, :] = value
        v[rows, :] = raw[rows, pl.ds(hd + HEAD_DIM, HEAD_DIM)].astype(bf16)
        return 0

    lax.fori_loop(0, length // block, head_rows, 0)
    keep += [net.copy(q, q_out), net.copy(k, k_out), net.copy(v, v_out)]
    for c in local_cot:
        c.wait()
    arrive(got_cot)
    cots = [lambda who: cot_all.at[who], lambda who: mask_all.at[who]]
    cot_state = spread(net, at, cots)

    fetch_piece(1)

    def one_head(h, _):
        for i in range(length // block):
            soft = soft_block(q, k, seg_row, seg_col, h, i, block, scale).astype(bf16)
            mixed = mm(soft, v[pl.ds(0, (i + 1) * block), :])
            o[pl.ds(i * block, block), span(h, HEAD_DIM)] = mixed.astype(bf16)
        return 0

    lax.fori_loop(0, n_heads, one_head, 0)
    hand_on(0)
    keep.append(net.copy(o, o_out))
    load_out.wait()
    wide_o = tiled(width, 256)

    def out_tile(i, _):
        tile = span(i, wide_o)
        part[:, tile] = mm(o[...], w_o[:, tile]).astype(bf16)
        return 0

    lax.fori_loop(0, width // wide_o, out_tile, 0)
    sums = [net.push(part.at[span(z ^ t, tok)], parts_in.at[t - 1], at.z_dev(t)) for t in range(1, at.n_shard)]
    last = pass_on(net, at, cots, cot_state)
    arrive(sums)

    def middle_rows(i, _):
        rows = span(i, step)
        total = part[pl.ds(pl.multiple_of(z * tok + i * step, step), step), :].astype(f32)
        for t in range(1, at.n_shard):
            total += parts_in[t - 1, rows, :].astype(f32)
        value = x_all[pl.ds(pl.multiple_of(z * tok + i * step, step), step), :].astype(f32) + total
        x1[rows, :] = value
        b_own[rows, :] = (value * inv_rms(value) * gains[1:2, :]).astype(bf16)
        return 0

    lax.fori_loop(0, tok // step, middle_rows, 0)
    swap = net.push(b_own, b_pair.at[half1], at.z_dev(group))
    keep += [net.copy(b_own, b_pair.at[half0]), net.copy(x1, x1_out), net.copy(b_own, b_out)]
    hand_on(1)
    swap.wait_recv()
    arrive(last + got_w)
    for c in keep:
        c.wait()
    net.sent()


def expert_kernel(
    dims, b_pair, cot_all, mask_all, gate_up, w_gu_in, w_dn_in, router_t,
    out_part, ggu, gdn, db_in, ex_in, land_gu, land_dn,
    w_gu, w_dn, rows, cot_t, mask_t, hid, d_pre, d_y, stage, stage_x, own, own_x, core_in, core_x, w_r, d_r, g_tile, d_tile,
    tile_sem, send, recv, local,
):
    at = Place(*dims)
    net = Net(send, recv, local)
    z, e, group = at.z, at.e, at.group
    n_slices, d_slice, ff2 = gate_up.shape
    ff, width = w_dn.shape
    two = b_pair.shape[0]
    four = 2 * two
    mine, other = z // group, (z ^ group) // group
    expert = e * (at.n_shard // group) + mine
    step = 16
    fine = tiled(ff, 256)
    wide = tiled(width, 1024)
    far = z ^ group

    def d_cols(who):
        return w_dn.at[:, span(who, d_slice)]

    pair = net.copy(b_pair, rows.at[0, 1])
    masks = []
    for t in range(at.chips):
        masks.append(net.copy(mask_all.at[at.slot(t, 1)], mask_t.at[t, 0]))
        masks.append(net.copy(mask_all.at[at.slot(t)], mask_t.at[t, 1]))
    loads = [net.copy(w_gu_in.at[mine], w_gu.at[span(z, d_slice)])]
    for k in range(1, n_slices):
        loads.append(net.copy(gate_up.at[z ^ k], w_gu.at[span(z ^ k, d_slice)]))
    load_dn = net.copy(w_dn_in.at[mine], d_cols(z))

    def fetch(t):
        return [
            net.copy(cot_all.at[at.slot(t, 1)], cot_t.at[0]),
            net.copy(cot_all.at[at.slot(t)], cot_t.at[1]),
        ]

    order = list(range(1, at.chips)) + [0]
    fetched = {order[0]: fetch(order[0])}
    greet(
        [at.chip_dev(t) for t in range(1, at.chips)] + [at.mate()] + [at.z_dev(t) for t in range(1, group + 1)]
    )
    from_mate = {0: net.push(b_pair, rows.at[0, 0], at.mate())}
    near = [t for t in (1, 2) if t < at.chips]
    beyond = [t for t in range(1, at.chips) if t not in near]
    from_chip = {t: net.push(b_pair, rows.at[t, 1], at.chip_dev(t)) for t in near}
    from_partner = net.push(w_dn_in.at[other], d_cols(z), at.z_dev(group))
    got_dn = [net.push(w_dn_in.at[mine], d_cols(z), at.z_dev(t)) for t in range(1, group)]

    relayed = []

    def pass_rows(t):
        if t in from_chip:
            from_chip[t].wait_recv()
        else:
            arrive(relayed)
        from_mate[t] = net.push(rows.at[t, 1], rows.at[t, 0], at.mate())

    lanes = lax.broadcasted_iota(jnp.int32, (four, 128), 1)

    def up_rows(t):
        logits = mm_nt(rows[t].reshape(four, width), router_t[...])
        chosen = mask_t[t].reshape(four, 128).astype(f32) > 0
        masked = jnp.where(chosen, logits, neg_fill)
        raised = jnp.where(chosen, jnp.exp(masked - jnp.max(masked, axis=1, keepdims=True)), 0.0)
        weight = raised / jnp.sum(raised, axis=1, keepdims=True)
        weight = jnp.sum(jnp.where(lanes == expert, weight, 0.0), axis=1, keepdims=True)
        w_r[t] = jnp.broadcast_to(weight, (four, 128))

        def up(j, _):
            tile, tile_u = span(j, fine), pl.ds(pl.multiple_of(ff + j * fine, fine), fine)
            x = rows[t].reshape(four, width)
            g = mm(x, w_gu[:, tile])
            u = mm(x, w_gu[:, tile_u])
            d_pre[t, :, tile] = g.astype(bf16)
            d_pre[t, :, tile_u] = u.astype(bf16)
            hid[t, :, tile] = (g * jax.nn.sigmoid(g) * u).astype(bf16)
            return 0

        lax.fori_loop(0, ff // fine, up, 0)

    for c in masks:
        c.wait()
    pair.wait()
    from_mate[0].wait_recv()
    for c in loads:
        c.wait()
    up_rows(0)
    for i in near:
        pass_rows(i)
        if beyond:
            part = pl.ds((2 - i) * (two // 2), two // 2)
            relayed.append(net.push(rows.at[i, 1, part], rows.at[3, 1, part], at.chip_dev(3 - i)))
    from_partner.wait_recv()
    for t in range(1, group):
        got_dn.append(net.push(d_cols(far), d_cols(far), at.z_dev(t)))
    for t in near:
        from_mate[t].wait_recv()
        up_rows(t)
    for t in beyond:
        pass_rows(t)
        from_mate[t].wait_recv()
        up_rows(t)
    load_dn.wait()
    arrive(got_dn)

    mates, outs = {}, []

    def finish(t):
        arrive(mates[t])

        def add_rows(i, _):
            r = span(i, step)
            own[t, r, :] = (own[t, r, :].astype(f32) + core_in[t, r, :].astype(f32)).astype(bf16)
            own_x[t, r, :] = (own_x[t, r, :].astype(f32) + core_x[t, r, :].astype(f32)).astype(bf16)
            return 0

        lax.fori_loop(0, two // step, add_rows, 0)
        if t:
            outs.append(net.push(own.at[t], db_in.at[t], at.chip_dev(t)))
            outs.append(net.push(own_x.at[t], ex_in.at[t], at.chip_dev(t)))

    used = {}
    for i, t in enumerate(order):
        d_r[...] = jnp.zeros_like(d_r)
        for c in fetched[t]:
            c.wait()

        def back_y(n, _, t=t):
            tile = span(n, wide)
            y = mm(hid[t], w_dn[:, tile]).astype(bf16).astype(f32)
            c = cot_t[:, :, tile].reshape(four, wide).astype(f32)
            w = w_r[t, :, 0:1]
            d_r[...] += jnp.broadcast_to(jnp.sum(c * y, axis=1, keepdims=True), (four, 128))
            d_y[t, :, tile] = (w * c).astype(bf16)
            cot_t[:, :, tile] = (w * y).astype(bf16).reshape(2, two, wide)
            return 0

        lax.fori_loop(0, width // wide, back_y, 0)
        kept = [
            net.copy(cot_t.at[0], out_part.at[at.slot(t, 1)]),
            net.copy(cot_t.at[1], out_part.at[at.slot(t)]),
        ]
        if i:
            finish(order[i - 1])

        def back_h(j, _, t=t):
            tile, tile_u = span(j, fine), pl.ds(pl.multiple_of(ff + j * fine, fine), fine)
            d_h = mm_nt(d_y[t], w_dn[tile, :])
            g, u = d_pre[t, :, tile].astype(f32), d_pre[t, :, tile_u].astype(f32)
            sig = jax.nn.sigmoid(g)
            d_pre[t, :, tile] = (d_h * u * sig * (1.0 + g * (1.0 - sig))).astype(bf16)
            d_pre[t, :, tile_u] = (d_h * g * sig).astype(bf16)
            return 0

        lax.fori_loop(0, ff // fine, back_h, 0)
        for c in kept:
            c.wait()
        if i + 1 < at.chips:
            fetched[order[i + 1]] = fetch(order[i + 1])
        p = i % 2
        for c in used.pop(p, []):
            net.done(c)

        def back_b(n, _, t=t, p=p):
            tile = span(n, wide)
            value = mm_nt(d_pre[t], w_gu[tile, :]).astype(bf16)
            stage[p, :, tile] = value[:two]
            own[t, :, tile] = value[two:]
            return 0

        lax.fori_loop(0, width // wide, back_b, 0)
        routed = d_r[...]
        high = routed.astype(bf16)
        low = (routed - high.astype(f32)).astype(bf16)
        none = jnp.zeros_like(high)
        extra = jnp.where(lanes == expert, high, jnp.where(lanes == expert + 64, low, none))
        stage_x[p] = extra[:two]
        own_x[t] = extra[two:]
        mates[t] = [
            net.push(stage.at[p], core_in.at[t], at.mate()),
            net.push(stage_x.at[p], core_x.at[t], at.mate()),
        ]
        used[p] = mates[t]
    finish(order[-1])
    keep = [net.copy(own.at[0], db_in.at[0]), net.copy(own_x.at[0], ex_in.at[0])]

    part = tiled(width, 256)
    per = d_slice // part

    def out_copy(slot, i):
        who = z ^ (n_slices - 1 - i // per)
        return pltpu.make_async_copy(g_tile.at[slot], ggu.at[who, span(i % per, part)], tile_sem.at[slot])

    def grad_up(i, _):
        slot = i % 2

        @pl.when(i >= 2)
        def _():
            out_copy(slot, i - 2).wait()

        who = z ^ (n_slices - 1 - i // per)
        x = rows[:, :, :, span(who * per + i % per, part)].reshape(at.chips * four, part)
        g_tile[slot] = mm_tn(x, d_pre[...].reshape(at.chips * four, ff2)).astype(bf16)
        out_copy(slot, i).start()
        return 0

    def down_copy(slot, i):
        return pltpu.make_async_copy(d_tile.at[slot], gdn.at[span(i, fine)], tile_sem.at[slot])

    def grad_down(i, _):
        slot = i % 2

        @pl.when(i >= 2)
        def _():
            down_copy(slot, i - 2).wait()

        h = hid[:, :, span(i, fine)].reshape(at.chips * four, fine)
        d_tile[slot] = mm_tn(h, d_y[...].reshape(at.chips * four, width)).astype(bf16)
        down_copy(slot, i).start()
        return 0

    n_down = ff // fine
    lax.fori_loop(0, n_down, grad_down, 0)
    for i in range(max(0, n_down - 2), n_down):
        down_copy(i % 2, i).wait()
    for t in range(1, group):
        outs.append(net.push(gdn.at[:, span(z ^ t ^ group, d_slice)], land_dn.at[t - 1], at.z_dev(t)))
    n_up, n_early = width // part, (group - 1) * per
    lax.fori_loop(0, n_early, grad_up, 0)
    for i in range(n_early - 2, n_early):
        out_copy(i % 2, i).wait()
    half = pl.ds(0, d_slice // 2)
    for t in range(1, group):
        outs.append(net.push(ggu.at[z ^ t ^ group, half], land_gu.at[t - 1], at.z_dev(t)))

    def grad_rest(i, _):
        slot = i % 2

        @pl.when(i >= n_early + 2)
        def _():
            out_copy(slot, i - 2).wait()

        who = z ^ (n_slices - 1 - i // per)
        x = rows[:, :, :, span(who * per + i % per, part)].reshape(at.chips * four, part)
        g_tile[slot] = mm_tn(x, d_pre[...].reshape(at.chips * four, ff2)).astype(bf16)
        out_copy(slot, i).start()
        return 0

    lax.fori_loop(n_early, n_up, grad_rest, 0)
    for i in range(n_up - 2, n_up):
        out_copy(i % 2, i).wait()
    for c in keep:
        c.wait()
    arrive(outs)
    net.sent()


def norm_kernel(
    dims, early, db, ex, ggu, gdn, out_part, x1, b, cot, rw, router_t, gains,
    gx1, do_all, gain_two, g_router, land_gu, late_gu, land_dn, out_sum,
    own, own_x, half_out, half_x, swap_in, swap_x, logit, d_out, out_own, out_core, out_in,
    send, recv, local,
):
    at = Place(*dims)
    net = Net(send, recv, local)
    z, e, group = at.z, at.e, at.group
    tok = x1.shape[0]
    n_parts = db.shape[0]
    loads = [net.copy(db, own), net.copy(ex, own_x)]
    load_own = {t: net.copy(out_part.at[at.slot(t)], out_own.at[t]) for t in halves(at)}
    greet(everyone(at))
    step = 16
    for c in loads:
        c.wait()

    def sums(src):
        total, total_x = own[0, src, :].astype(f32), own_x[0, src, :].astype(f32)
        for t in range(1, n_parts):
            total += own[t, src, :].astype(f32)
            total_x += own_x[t, src, :].astype(f32)
        return total, total_x

    def partner(i, _):
        total, total_x = sums(pl.ds(pl.multiple_of(tok + i * step, step), step))
        half_out[span(i, step), :] = total.astype(bf16)
        half_x[span(i, step), :] = total_x.astype(bf16)
        return 0

    lax.fori_loop(0, tok // step, partner, 0)
    swaps = [net.push(half_out, swap_in, at.z_dev(group)), net.push(half_x, swap_x, at.z_dev(group))]
    d_slice = ggu.shape[1]
    landed = []
    for t in range(1, group):
        j = z ^ t ^ group
        if not early:
            landed.append(net.push(ggu.at[j, pl.ds(0, d_slice // 2)], land_gu.at[t - 1], at.z_dev(t)))
            landed.append(net.push(gdn.at[:, span(j, d_slice)], land_dn.at[t - 1], at.z_dev(t)))
        landed.append(net.push(ggu.at[j, pl.ds(d_slice // 2, d_slice // 2)], late_gu.at[t - 1], at.z_dev(t)))
    mates = {t: net.push(out_part.at[at.slot(t, 1)], out_core.at[t], at.mate()) for t in halves(at)}
    outs = []
    for t in halves(at):
        load_own[t].wait()
        mates[t].wait_recv()

        def add(i, _, t=t):
            rows = span(i, step)
            out_own[t, rows, :] = (out_own[t, rows, :].astype(f32) + out_core[t, rows, :].astype(f32)).astype(bf16)
            return 0

        lax.fori_loop(0, 2 * tok // step, add, 0)
        if t:
            outs.append(net.push(out_own.at[t], out_in.at[t - 1], at.chip_dev(t)))
    arrive(swaps)
    gain_two[...] = jnp.zeros_like(gain_two)

    def owner(i, _):
        rows = span(i, step)
        grad, routed = sums(rows)
        grad += swap_in[rows, :].astype(f32)
        routed += swap_x[rows, :].astype(f32)
        routed = routed + pltpu.roll(routed, 64, 1)
        weight = rw[rows, :]
        d_logit = weight * (routed - jnp.sum(weight * routed, axis=1, keepdims=True))
        high = d_logit.astype(bf16)
        low = (d_logit - high.astype(f32)).astype(bf16)
        logit[0, rows, :] = high
        logit[1, rows, :] = low
        grad += mm(high, router_t[...]) + mm(low, router_t[...])
        value = x1[rows, :]
        r = inv_rms(value)
        c = grad * gains[1:2, :]
        back = cot[rows, :].astype(f32) + r * c - value * (r * r * r * jnp.mean(c * value, axis=-1, keepdims=True))
        gx1[rows, :] = back
        d_out[rows, :] = back.astype(bf16)
        gain_two[...] += eight(grad * value * r)
        return 0

    lax.fori_loop(0, tok // step, owner, 0)
    mine = do_all.at[span(z, tok)]
    keep = net.copy(d_out, mine)
    copies = [net.push(d_out, mine, at.z_dev(t)) for t in range(1, at.n_shard)]
    g_router[...] = mm_tn(logit[0], b[...]) + mm_tn(logit[1], b[...])
    arrive(outs)

    def out_rows(i, _):
        rows = span(i, step)
        total = out_own[0, rows, :].astype(f32)
        for t in range(1, at.chips):
            total += out_in[t - 1, rows, :].astype(f32)
        out_sum[rows, :] = total.astype(bf16)
        return 0

    lax.fori_loop(0, 2 * tok // step, out_rows, 0)
    keep.wait()
    arrive(copies + landed)
    net.sent()


def back_kernel(
    dims, do_h, w_out, o_h, q_h, k_h, v_h, raw_h, cos_h, sin_h, seg_h, a_h, heads_h, ggu, gdn, land_gu, late_gu, land_dn, out_sum,
    out_sum_own, small, x1, gx1, x, gains, gain_two, g_router,
    hidden, g_hidden, small_sum, g_att, g_qkv, two_gu, own_gu, two_dn, own_dn,
    do_all, w_o, o, q, k, v, raw, cos, sin, seg_col, seg_row, mix, d_qkv, dk, dv, qk_gain, a, heads,
    sum_gu, add_gu, sum_dn, add_dn, swap_in, g_out, g_core, g_in, share_own,
    parts_in, g_heads, core_in, chip_in, mine, turn_in, share_qkv, sm, sm_z, sm_core, sm_chip,
    send, recv, local,
):
    at = Place(*dims)
    net = Net(send, recv, local)
    z, e, group = at.z, at.e, at.group
    length, width = do_all.shape
    tok = x1.shape[0]
    cols = raw.shape[1]
    hd = cols - 2 * HEAD_DIM
    n_heads = hd // HEAD_DIM
    rows_e = heads.shape[2]
    d_slice = ggu.shape[1]
    scale = HEAD_DIM ** (-0.5)
    block = tok
    step = 16
    far = z ^ group

    def d_cols(ref, who):
        return ref.at[:, span(who, d_slice)]

    cut = d_slice // 2
    halves_gu = [pl.ds(0, cut), pl.ds(cut, cut)]
    load_gu = [
        [net.copy(ggu.at[far, r], sum_gu.at[i])] + [net.copy(land.at[t - 1], add_gu.at[i, t - 1]) for t in range(1, group)]
        for i, (r, land) in enumerate(zip(halves_gu, (land_gu, late_gu)))
    ]
    load_a = [net.copy(do_h, do_all), net.copy(o_h, o)]
    load_b = [
        net.copy(s, d)
        for s, d in ((w_out, w_o), (q_h, q), (k_h, k), (v_h, v), (raw_h, raw), (cos_h, cos), (sin_h, sin), (seg_h, seg_col))
    ]
    load_c = [net.copy(a_h, a), net.copy(heads_h, heads)]
    load_dn = [net.copy(d_cols(gdn, far), sum_dn)] + [net.copy(land_dn.at[t - 1], add_dn.at[t - 1]) for t in range(1, group)]
    greet(everyone(at))
    swap = net.push(out_sum.at[pl.ds(tok, tok)], swap_in, at.z_dev(group))

    def add_up(total, adds):
        def rows_of(i, _):
            rows = span(i, step)
            value = total[rows, :].astype(f32)
            for t in range(1, group):
                value += adds[t - 1, rows, :].astype(f32)
            total[rows, :] = value.astype(bf16)
            return 0

        lax.fori_loop(0, total.shape[0] // step, rows_of, 0)

    got = []

    def send_half(i):
        for c in load_gu[i]:
            c.wait()
        add_up(sum_gu.at[i], add_gu.at[i])
        got.append(net.push(sum_gu.at[i], two_gu.at[halves_gu[i]], at.z_dev(group)))

    send_half(0)
    for t in range(1, group):
        got.append(net.push(ggu.at[z ^ t], own_gu.at[t - 1], at.z_dev(t)))

    for c in load_a:
        c.wait()
    share = share_own.shape[0]
    wide = tiled(hd, 256)
    each = wide // share

    def out_grad(i, _):
        tile = mm_tn(o[:, span(i, wide)], do_all[...]).astype(bf16)
        for j in range(each):
            g_out[each * i + j] = tile[j * share : (j + 1) * share]
        return 0

    lax.fori_loop(0, hd // wide, out_grad, 0)
    g_mates = {t: net.push(g_out.at[at.slot(t, 1)], g_core.at[t], at.mate()) for t in halves(at)}
    for c in load_b:
        c.wait()
    qk = []
    for s in range(at.n_shard):
        rows = small[s, 0:16, :].astype(f32)
        seg_row[0:1, span(s, tok)] = rows[4:5, :tok]
        qk.append(rows[2:4, :HEAD_DIM])
    qk = sum(qk[1:], qk[0])

    def mix_tile(i, _):
        tile = span(i, wide)
        mix[:, tile] = mm_nt(do_all[...], w_o[tile, :]).astype(bf16)
        return 0

    lax.fori_loop(0, hd // wide, mix_tile, 0)
    g_outs = []
    for t in halves(at):
        g_mates[t].wait_recv()

        def add(i, _, t=t):
            rows = span(i, step)
            s = at.slot(t)
            g_out[s, rows, :] = (g_out[s, rows, :].astype(f32) + g_core[t, rows, :].astype(f32)).astype(bf16)
            return 0

        lax.fori_loop(0, share // step, add, 0)
        if t:
            g_outs.append(net.push(g_out.at[at.slot(t)], g_in.at[t - 1], at.chip_dev(t)))
    send_half(1)

    dk[...] = jnp.zeros_like(dk)
    dv[...] = jnp.zeros_like(dv)
    qk_gain[...] = jnp.zeros_like(qk_gain)

    def one_head(h, _):
        lanes = span(h, HEAD_DIM)
        for i in range(length // block):
            rows, keys = pl.ds(i * block, block), pl.ds(0, (i + 1) * block)
            soft = soft_block(q, k, seg_row, seg_col, h, i, block, scale)
            d_mix = mix[rows, lanes]
            d_soft = mm_nt(d_mix, v[keys, :])
            d_scores = (soft * (d_soft - jnp.sum(soft * d_soft, axis=-1, keepdims=True))).astype(bf16)
            dv[keys, :] += mm_tn(soft.astype(bf16), d_mix)
            dk[keys, :] += mm_tn(d_scores, q[rows, lanes]) * scale
            dq = mm(d_scores, k[keys, :]) * scale
            value = raw[rows, lanes]
            back, per = rms_back(value, qk[0:1], rope_rows_back(dq, cos[rows, :], sin[rows, :]))
            d_qkv[rows, lanes] = back.astype(bf16)
            qk_gain[0:8, :] += eight(per)
        return 0

    lax.fori_loop(0, n_heads, one_head, 0)
    for i in range(length // block):
        rows = pl.ds(i * block, block)
        value = raw[rows, pl.ds(hd, HEAD_DIM)]
        back, per = rms_back(value, qk[1:2], rope_rows_back(dk[rows, :], cos[rows, :], sin[rows, :]))
        d_qkv[rows, pl.ds(hd, HEAD_DIM)] = back.astype(bf16)
        d_qkv[rows, pl.ds(hd + HEAD_DIM, HEAD_DIM)] = dv[rows, :].astype(bf16)
        qk_gain[8:16, :] += eight(per)

    for c in load_c:
        c.wait()
    wide_d = tiled(d_slice, 256)
    each_d = wide_d // rows_e

    def grad_tile(s, _):
        for j in range(d_slice // wide_d):
            some = a[:, pl.ds(pl.multiple_of(s * d_slice + j * wide_d, wide_d), wide_d)]
            tile = mm_tn(some, d_qkv[...]).astype(bf16)
            for i in range(each_d):
                g_heads[each_d * j + i, s] = tile[i * rows_e : (i + 1) * rows_e]
        return 0

    lax.fori_loop(0, at.n_shard, grad_tile, 0)
    mates = {t: net.push(g_heads.at[at.slot(t, 1)], core_in.at[t], at.mate()) for t in halves(at)}
    part = do_all

    def rows_tile(s, _):
        for j in range(d_slice // wide_d):
            some = heads[s, pl.ds(each_d * j, each_d)].reshape(wide_d, cols)
            here = pl.ds(pl.multiple_of(s * d_slice + j * wide_d, wide_d), wide_d)
            part[:, here] = mm_nt(d_qkv[...], some).astype(bf16)
        return 0

    lax.fori_loop(0, at.n_shard, rows_tile, 0)
    sums = [net.push(part.at[span(z ^ t, tok)], parts_in.at[t - 1], at.z_dev(t)) for t in range(1, at.n_shard)]
    chips = []
    for t in halves(at):
        mates[t].wait_recv()
        who = at.slot(t)

        def add(s, _, t=t, who=who):
            g_heads[who, s] = (g_heads[who, s].astype(f32) + core_in[t, s].astype(f32)).astype(bf16)
            return 0

        lax.fori_loop(0, at.n_shard, add, 0)
        if t:
            chips.append(net.push(g_heads.at[who], chip_in.at[t - 1], at.chip_dev(t)))
    arrive(g_outs)

    def own_share(i, _):
        rows = span(i, step)
        total = g_out[e, rows, :].astype(f32)
        for t in range(1, at.chips):
            total += g_in[t - 1, rows, :].astype(f32)
        share_own[rows, :] = total.astype(bf16)
        return 0

    lax.fori_loop(0, share // step, own_share, 0)
    keep_att = net.copy(share_own, g_att.at[e])
    for c in load_dn:
        c.wait()
    add_up(sum_dn, add_dn)
    swap.wait_recv()

    def hidden_rows(i, _):
        rows = span(i, step)
        hidden[rows, :] = (x1[rows, :] + out_sum_own[rows, :].astype(f32) + swap_in[rows, :].astype(f32)).astype(bf16)
        return 0

    lax.fori_loop(0, tok // step, hidden_rows, 0)
    arrive(chips)

    def total(s, _):
        value = g_heads[e, s].astype(f32)
        for t in range(1, at.chips):
            value += chip_in[t - 1, s].astype(f32)
        mine[s] = value.astype(bf16)
        return 0

    lax.fori_loop(0, at.n_shard, total, 0)
    turns = [net.push(mine.at[z ^ t], turn_in.at[z], at.z_dev(t)) for t in range(1, at.n_shard)]
    turn_own = net.copy(mine.at[z], turn_in.at[z])
    keep_att.wait()
    atts = [lambda who: g_att.at[who]]
    att_state = spread(net, at, atts)
    got.append(net.push(sum_dn, two_dn, at.z_dev(group)))
    for t in range(1, group):
        got.append(net.push(d_cols(gdn, z ^ t), own_dn.at[t - 1], at.z_dev(t)))
    arrive(sums)
    sm[...] = jnp.zeros_like(sm)
    gain_one = jnp.zeros((8, width), f32)

    def owner(i, gain_one):
        rows = span(i, step)
        here = pl.ds(pl.multiple_of(z * tok + i * step, step), step)
        da = part[here, :].astype(f32)
        for t in range(1, at.n_shard):
            da += parts_in[t - 1, rows, :].astype(f32)
        back, per = rms_back(x[rows, :].astype(f32), gains[0:1, :], da)
        g_hidden[rows, :] = gx1[rows, :] + back
        return gain_one + eight(per)

    gain_one = lax.fori_loop(0, tok // step, owner, gain_one)
    row_one = jnp.sum(gain_one, axis=0, keepdims=True)
    row_two = jnp.sum(gain_two[...], axis=0, keepdims=True)
    row_q = jnp.sum(qk_gain[0:8, :], axis=0, keepdims=True)
    row_k = jnp.sum(qk_gain[8:16, :], axis=0, keepdims=True)
    for s in range(at.n_shard):
        piece = pl.ds(s * d_slice, d_slice)
        lanes = slice(s * d_slice, (s + 1) * d_slice)
        sm[s, 0:1, :] = row_one[:, lanes]
        sm[s, 1:2, :] = row_two[:, lanes]
        sm[s, 2:3, pl.ds(0, HEAD_DIM)] = row_q
        sm[s, 3:4, pl.ds(0, HEAD_DIM)] = row_k
        sm[s, 8:, :] = g_router[0 : sm.shape[1] - 8, piece]
    small_z = [net.push(sm.at[z ^ t], sm_z.at[t - 1], at.z_dev(t)) for t in range(1, at.n_shard)]
    turn_own.wait()
    arrive(turns)
    for s in range(at.n_shard):
        share_qkv[:, pl.ds(s * hd, hd)] = turn_in[s, :, pl.ds(0, hd)]
    for m in range(KV_HEADS):
        some = [s for s in range(at.n_shard) if (s * n_heads) // (HEADS // KV_HEADS) == m]
        for first, to in ((hd, HEADS + m), (hd + HEAD_DIM, HEADS + KV_HEADS + m)):
            value = turn_in[some[0], :, pl.ds(first, HEAD_DIM)].astype(f32)
            for s in some[1:]:
                value += turn_in[s, :, pl.ds(first, HEAD_DIM)].astype(f32)
            share_qkv[:, pl.ds(to * HEAD_DIM, HEAD_DIM)] = value.astype(bf16)
    keep = net.copy(share_qkv, g_qkv.at[e])
    keep.wait()
    qkvs = [lambda who: g_qkv.at[who]]
    state = spread(net, at, qkvs)
    last = pass_on(net, at, atts, att_state)
    arrive(small_z)
    value = sm[z]
    for t in range(1, at.n_shard):
        value += sm_z[t - 1]
    sm[z] = value
    c = net.push(sm.at[z], sm_core, at.mate())
    c.wait_recv()
    sm_core[...] = sm[z] + sm_core[...]
    smalls = [net.push(sm_core, sm_chip.at[t - 1], at.chip_dev(t)) for t in range(1, at.chips)]
    last += pass_on(net, at, qkvs, state)
    arrive(smalls)
    value = sm_core[...]
    for t in range(1, at.chips):
        value += sm_chip[t - 1]
    small_sum[...] = value
    arrive(last + got)
    net.sent()


def shards(
    hidden_in,
    segments,
    routes,
    norm_gains,
    qk_gains,
    w_qkv,
    w_attn_out,
    w_router,
    w_gate_up,
    w_down,
    cotangent,
):
    n_expert = lax.axis_size("expert")
    n_shard = lax.axis_size("shard")
    me_e = lax.axis_index("expert")
    me_z = lax.axis_index("shard")
    tok, width = hidden_in.shape
    exp_dev = w_gate_up.shape[1]
    experts_all = w_router.shape[2]
    d_slice, ff2 = w_gate_up.shape[2:]
    ff = ff2 // 2
    group = n_shard // exp_dev
    mine = me_z // group
    length = n_shard * tok
    h_dev = HEADS // n_shard
    hd = h_dev * HEAD_DIM
    cols = hd + 2 * HEAD_DIM
    qkv_cols = w_qkv.shape[2]
    rows_e = d_slice // n_expert
    share = hd // n_expert
    chips = n_expert // 2
    qk_part = HEAD_DIM // n_shard
    dims = (n_expert, n_shard, group)
    n_small = 16 + experts_all
    sds = jax.ShapeDtypeStruct
    vm = pltpu.VMEM
    any_spec = pl.BlockSpec(memory_space=pl.ANY)
    vmem_spec = pl.BlockSpec(memory_space=pltpu.VMEM)

    small = jnp.zeros((16, d_slice), bf16)
    small = small.at[0:2, :].set(norm_gains[0])
    small = lax.dynamic_update_slice(small, qk_gains[0], (2, me_z * qk_part))
    small = small.at[4, :tok].set(segments.astype(bf16))
    small = jnp.concatenate([small, w_router[0].T], axis=0)
    seg_own = jnp.broadcast_to(segments.astype(f32)[:, None], (tok, 128))
    ids = jnp.arange(128, dtype=jnp.int32)
    mask = jnp.sum((routes[:, :, None] == ids[None, None, :]).astype(f32), axis=1).astype(bf16)
    cos, sin = rotary_tables(length)

    outs = [
        sds((n_shard, n_small, d_slice), bf16),
        sds((length, 128), f32),
        sds((n_shard, n_expert, rows_e, cols), bf16),
        sds((length, width), bf16),
        sds((length, cols), f32),
        sds((length, hd), bf16),
        sds((length, HEAD_DIM), bf16),
        sds((length, HEAD_DIM), bf16),
        sds((length, hd), bf16),
        sds((tok, width), f32),
        sds((tok, width), bf16),
        sds((n_shard, d_slice, ff2), bf16),
        sds((n_expert, 2 * tok, width), bf16),
        sds((n_expert, 2 * tok, 128), bf16),
        sds((2 * tok, width), bf16),
    ]
    front = comm_call(
        functools.partial(front_kernel, dims),
        0,
        160,
        40,
        [
            vm((length, width), bf16),
            vm((n_shard, n_small, d_slice), bf16),
            vm((length, 128), f32),
            vm((n_shard, n_expert, rows_e, cols), bf16),
            vm((length, width), bf16),
            vm((length, cols), f32),
            vm((length, hd), bf16),
            vm((length, HEAD_DIM), bf16),
            vm((length, HEAD_DIM), bf16),
            vm((length, hd), bf16),
            vm((hd, width), bf16),
            vm((length, width), bf16),
            vm((n_shard - 1, tok, width), bf16),
            vm((length, HEAD_DIM), f32),
            vm((length, HEAD_DIM), f32),
            vm((8, width), f32),
            vm((8, length), f32),
            vm((tok, width), f32),
            vm((tok, width), bf16),
        ],
        outs,
        56,
    )
    (small_all, seg_col, heads, a, raw, q, k, v, o, x1, b, gate_up, cot_all, mask_all, b_pair) = front(
        hidden_in, small, seg_own, w_qkv[0], w_attn_out[0], w_gate_up[0], cotangent, mask, cos, sin
    )
    gains = jnp.zeros((8, width), f32)
    gains = gains.at[0:2].set(small_all[:, 0:2].astype(f32).transpose(1, 0, 2).reshape(2, width))
    router_t = small_all[:, 16:].transpose(1, 0, 2).reshape(experts_all, width)

    def route_weights(rows, chosen):
        logits = mm_nt(rows, router_t)
        masked = jnp.where(chosen, logits, neg_fill)
        raised = jnp.where(chosen, jnp.exp(masked - jnp.max(masked, axis=1, keepdims=True)), 0.0)
        return raised / jnp.sum(raised, axis=1, keepdims=True)

    rw = route_weights(b, mask[:, :experts_all] > 0)
    rw = jnp.concatenate([rw, jnp.zeros((tok, 128 - experts_all), f32)], axis=1)
    router_pad = jnp.concatenate([router_t, jnp.zeros((128 - experts_all, width), bf16)], axis=0)
    per_e = (n_expert, 2 * tok)
    piece = (chips, 2 * tok)
    four = 4 * tok
    if chips <= 4:
        out_part, grad_gate_up, grad_down, db_in, ex_in, land_gu, land_dn = comm_call(
            functools.partial(expert_kernel, dims),
            4,
            60,
            60,
            [
                vm((width, ff2), bf16),
                vm((ff, width), bf16),
                vm((chips, 2, 2 * tok, width), bf16),
                vm((2, 2 * tok, width), bf16),
                vm((chips, 2, 2 * tok, 128), bf16),
                vm((chips, four, ff), bf16),
                vm((chips, four, ff2), bf16),
                vm((chips, four, width), bf16),
                vm((2, 2 * tok, width), bf16),
                vm((2, 2 * tok, 128), bf16),
                vm(piece + (width,), bf16),
                vm(piece + (128,), bf16),
                vm(piece + (width,), bf16),
                vm(piece + (128,), bf16),
                vm((chips, four, 128), f32),
                vm((four, 128), f32),
                vm((2, tiled(width, 256), ff2), bf16),
                vm((2, tiled(ff, 256), width), bf16),
                pltpu.SemaphoreType.DMA((2,)),
            ],
            [
                sds(per_e + (width,), bf16),
                sds((n_shard, d_slice, ff2), bf16),
                sds((ff, width), bf16),
                sds(piece + (width,), bf16),
                sds(piece + (128,), bf16),
                sds((group - 1, d_slice // 2, ff2), bf16),
                sds((group - 1, ff, d_slice), bf16),
            ],
            60,
            in_specs=[any_spec] * 6 + [vmem_spec],
        )(b_pair, cot_all, mask_all, gate_up, w_gate_up[0], w_down[0], router_pad)
    else:
        rows_all = n_expert * 2 * tok
        w_mine = lax.dynamic_index_in_dim(w_gate_up[0], mine, 0, keepdims=False)
        gate_up = lax.dynamic_update_index_in_dim(gate_up, w_mine, me_z, 0)
        down = lax.all_gather(w_down[0], "shard", axis=2, tiled=True)
        down = lax.dynamic_index_in_dim(down, mine, 0, keepdims=False)
        b_rows = lax.all_gather(b_pair, "expert", axis=0, tiled=True)
        my_expert = me_e * exp_dev + mine
        rw_all = route_weights(b_rows, mask_all.reshape(rows_all, 128)[:, :experts_all] > 0)
        is_mine = ids[:experts_all] == my_expert
        rw_mine = jnp.sum(jnp.where(is_mine[None, :], rw_all, 0.0), axis=1, keepdims=True)
        w_gu = gate_up.reshape(width, ff2)
        pre = mm(b_rows, w_gu)
        g, u = pre[:, :ff], pre[:, ff:]
        sig = jax.nn.sigmoid(g)
        act = g * sig
        hidden = (act * u).astype(bf16)
        y_f = mm(hidden, down).astype(bf16).astype(f32)
        cot_f = cot_all.reshape(rows_all, width).astype(f32)
        d_route = jnp.sum(cot_f * y_f, axis=1, keepdims=True)
        out_part = (rw_mine * y_f).astype(bf16)
        d_y = (rw_mine * cot_f).astype(bf16)
        d_hidden = mm_nt(d_y, down)
        d_pre = jnp.concatenate(
            [d_hidden * u * sig * (1.0 + g * (1.0 - sig)), d_hidden * act], axis=1
        ).astype(bf16)
        d_b = mm_nt(d_pre, w_gu).astype(bf16)
        grad_down = mm_tn(hidden, d_y).astype(bf16)
        grad_gate_up = mm_tn(b_rows, d_pre).astype(bf16).reshape(n_shard, d_slice, ff2)
        high = lax.reduce_precision(d_route, 8, 7)
        low = d_route - high
        extra = jnp.where(ids[None] == my_expert, high, jnp.where(ids[None] == my_expert + 64, low, 0.0)).astype(bf16)

        def home(value):
            return lax.psum_scatter(value, "expert", scatter_dimension=0, tiled=True)[None]

        db_in, ex_in = home(d_b), home(extra)

    n_parts = db_in.shape[0]
    early = chips <= 4
    gx1, d_o, gain_two, g_router, norm_gu, late_gu, norm_dn, out_sum = comm_call(
        functools.partial(norm_kernel, dims, early),
        1,
        60,
        24,
        [
            vm((n_parts, 2 * tok, width), bf16),
            vm((n_parts, 2 * tok, 128), bf16),
            vm((tok, width), bf16),
            vm((tok, 128), bf16),
            vm((tok, width), bf16),
            vm((tok, 128), bf16),
            vm((2, tok, 128), bf16),
            vm((tok, width), bf16),
            vm(piece + (width,), bf16),
            vm(piece + (width,), bf16),
            vm((chips - 1, 2 * tok, width), bf16),
        ],
        [
            sds((tok, width), f32),
            sds((length, width), bf16),
            sds((8, width), f32),
            sds((128, width), f32),
            sds((group - 1, d_slice // 2, ff2), bf16) if not early else sds((16, 128), bf16),
            sds((group - 1, d_slice // 2, ff2), bf16),
            sds((group - 1, ff, d_slice), bf16) if not early else sds((16, 128), bf16),
            sds((2 * tok, width), bf16),
        ],
        60,
        in_specs=[any_spec] * 5 + [vmem_spec] * 6,
        out_specs=[vmem_spec, any_spec, vmem_spec, vmem_spec] + [any_spec] * 3 + [vmem_spec],
    )(db_in, ex_in, grad_gate_up, grad_down, out_part.reshape(per_e + (width,)), x1, b, cotangent, rw, router_pad, gains)
    if not early:
        land_gu, land_dn = norm_gu, norm_dn

    small_rows = (8 + -(-experts_all // 8) * 8, d_slice)
    hidden_out, grad_hidden, sums, grad_out, grad_qkv, two_gu, own_gu, two_dn, own_dn = comm_call(
        functools.partial(back_kernel, dims),
        2,
        140,
        60,
        [
            vm((length, width), bf16),
            vm((hd, width), bf16),
            vm((length, hd), bf16),
            vm((length, hd), bf16),
            vm((length, HEAD_DIM), bf16),
            vm((length, HEAD_DIM), bf16),
            vm((length, cols), f32),
            vm((length, HEAD_DIM), f32),
            vm((length, HEAD_DIM), f32),
            vm((length, 128), f32),
            vm((8, length), f32),
            vm((length, hd), bf16),
            vm((length, cols), bf16),
            vm((length, HEAD_DIM), f32),
            vm((length, HEAD_DIM), f32),
            vm((16, HEAD_DIM), f32),
            vm((length, width), bf16),
            vm((n_shard, n_expert, rows_e, cols), bf16),
            vm((2, d_slice // 2, ff2), bf16),
            vm((2, group - 1, d_slice // 2, ff2), bf16),
            vm((ff, d_slice), bf16),
            vm((group - 1, ff, d_slice), bf16),
            vm((tok, width), bf16),
            vm((n_expert, share, width), bf16),
            vm((chips, share, width), bf16),
            vm((chips - 1, share, width), bf16),
            vm((share, width), bf16),
            vm((n_shard - 1, tok, width), bf16),
            vm((n_expert, n_shard, rows_e, cols), bf16),
            vm((chips, n_shard, rows_e, cols), bf16),
            vm((chips - 1, n_shard, rows_e, cols), bf16),
            vm((n_shard, rows_e, cols), bf16),
            vm((n_shard, rows_e, cols), bf16),
            vm((rows_e, qkv_cols), bf16),
            vm((n_shard,) + small_rows, f32),
            vm((n_shard - 1,) + small_rows, f32),
            vm(small_rows, f32),
            vm((chips - 1,) + small_rows, f32),
        ],
        [
            sds((tok, width), bf16),
            sds((tok, width), f32),
            sds(small_rows, f32),
            sds((n_expert, share, width), bf16),
            sds((n_expert, rows_e, qkv_cols), bf16),
            sds((d_slice, ff2), bf16),
            sds((group - 1, d_slice, ff2), bf16),
            sds((ff, d_slice), bf16),
            sds((group - 1, ff, d_slice), bf16),
        ],
        60,
        in_specs=[any_spec] * 18 + [vmem_spec] * 8,
        out_specs=[vmem_spec] * 3 + [any_spec] * 6,
    )(
        d_o,
        w_attn_out[0],
        o,
        q,
        k,
        v,
        raw,
        cos,
        sin,
        seg_col,
        a,
        heads,
        grad_gate_up,
        grad_down,
        land_gu,
        late_gu,
        land_dn,
        out_sum,
        out_sum[:tok],
        small_all,
        x1,
        gx1,
        hidden_in,
        gains,
        gain_two,
        g_router,
    )

    def settle(own, others, other):
        total = own.astype(f32) + jnp.sum(others.astype(f32), axis=0)
        other = other.astype(f32)
        return jnp.stack([jnp.where(mine == 0, total, other), jnp.where(mine == 0, other, total)])[None]

    own_gate_up = lax.dynamic_index_in_dim(grad_gate_up, me_z, 0, keepdims=False)
    own_down = lax.dynamic_slice_in_dim(grad_down, me_z * d_slice, d_slice, 1)
    qk_grad = lax.dynamic_slice_in_dim(sums[2:4, :HEAD_DIM], me_z * qk_part, qk_part, 1)
    return (
        hidden_out,
        grad_hidden,
        sums[0:2][None],
        qk_grad[None],
        grad_qkv.reshape(d_slice, qkv_cols).astype(f32)[None],
        grad_out.reshape(hd, width).astype(f32)[None],
        sums[8 : 8 + experts_all].T[None],
        settle(own_gate_up, own_gu, two_gu),
        settle(own_down, own_dn, two_dn),
    )


def solution(mesh):
    in_specs = (
        P(("expert", "shard"), None),
        P(("expert", "shard")),
        P(("expert", "shard"), None),
        P(None, None, "shard"),
        P(None, None, "shard"),
        P(None, "shard", None),
        P(None, "shard", None),
        P(None, "shard", None),
        P(None, "expert", "shard", None),
        P(None, "expert", None, "shard"),
        P(("expert", "shard"), None),
    )
    out_specs = (
        P(("expert", "shard"), None),
        P(("expert", "shard"), None),
        P(None, None, "shard"),
        P(None, None, "shard"),
        P(None, "shard", None),
        P(None, "shard", None),
        P(None, "shard", None),
        P(None, "expert", "shard", None),
        P(None, "expert", None, "shard"),
    )
    return jax.shard_map(shards, mesh=mesh, in_specs=in_specs, out_specs=out_specs, check_vma=False)
```

```python
import functools

import jax
import jax.numpy as jnp
from jax import lax
from jax.experimental import pallas as pl
from jax.experimental.pallas import tpu as pltpu
from jax.sharding import PartitionSpec as P

HEADS = 32
KV_HEADS = 4
HEAD_DIM = 128
TOP = 8

bf16 = jnp.bfloat16
f32 = jnp.float32
highest = lax.Precision.HIGHEST
eps_norm = 1e-06
rope_base = 1000000.0
neg_fill = -1e30


def dot(left, right, dims, out=f32):
    return lax.dot_general(left, right, (dims, ((), ())), preferred_element_type=out)


def mm(left, right):
    return dot(left, right, ((1,), (0,)))


def mm_nt(left, right):
    return dot(left, right, ((1,), (1,)))


def mm_tn(left, right):
    return dot(left, right, ((0,), (0,)))


def inv_rms(value):
    return lax.rsqrt(jnp.mean(value * value, axis=-1, keepdims=True) + eps_norm)


def rms_back(value, gain, grad):
    r = inv_rms(value)
    c = grad * gain
    back = r * c - value * (r * r * r) * jnp.mean(c * value, axis=-1, keepdims=True)
    return back, grad * value * r


def rotary_tables(length):
    half = HEAD_DIM // 2
    frequency = rope_base ** (-(jnp.arange(half, dtype=f32) * 2.0) / HEAD_DIM)
    angles = jnp.arange(length, dtype=f32)[:, None] * frequency[None, :]
    cos, sin = jnp.cos(angles), jnp.sin(angles)
    return jnp.concatenate([cos, cos], axis=1), jnp.concatenate([-sin, sin], axis=1)


MESH = pl.DeviceIdType.MESH


class Place:
    def __init__(self, n_expert, n_shard, group):
        self.e = lax.axis_index("expert")
        self.z = lax.axis_index("shard")
        self.n_expert, self.n_shard, self.group = n_expert, n_shard, group
        self.chip, self.core = self.e // 2, self.e % 2
        self.chips = n_expert // 2

    def z_dev(self, t):
        return (self.e, self.z ^ t)

    def slot(self, t, other=0):
        return (self.chip ^ t) * 2 + (self.core ^ other)

    def chip_dev(self, t):
        return (self.slot(t), self.z)

    def mate(self):
        return (self.e ^ 1, self.z)


class Net:
    def __init__(self, send, recv, local):
        self.send, self.recv, self.local = send, recv, local
        self.n, self.m, self.open = 0, 0, []

    def push(self, src, dst, dev):
        i = self.n
        self.n += 1
        copy = pltpu.make_async_remote_copy(
            src_ref=src, dst_ref=dst, send_sem=self.send.at[i], recv_sem=self.recv.at[i],
            device_id=dev, device_id_type=MESH,
        )
        copy.start()
        self.open.append(copy)
        return copy

    def copy(self, src, dst):
        i = self.m
        self.m += 1
        copy = pltpu.make_async_copy(src, dst, self.local.at[i])
        copy.start()
        return copy

    def done(self, copy):
        copy.wait_send()
        self.open = [c for c in self.open if c is not copy]

    def sent(self):
        for copy in self.open:
            copy.wait_send()
        self.open = []


def greet(devices):
    barrier = pltpu.get_barrier_semaphore()
    for dev in devices:
        pl.semaphore_signal(barrier, inc=1, device_id=dev, device_id_type=MESH)
    pl.semaphore_wait(barrier, len(devices))


def everyone(at):
    return (
        [at.z_dev(t) for t in range(1, at.n_shard)]
        + [at.chip_dev(t) for t in range(1, at.chips)]
        + [at.mate()]
    )


def arrive(copies):
    for copy in copies:
        copy.wait_recv()


def spread(net, at, pieces):
    own = [p(at.e) for p in pieces]
    mate = [net.push(o, o, at.mate()) for o in own]
    out = [(t, [net.push(o, o, at.chip_dev(t)) for o in own]) for t in range(1, at.chips)]
    return mate, out


def pass_on(net, at, pieces, state):
    mate, out = state
    for t, copies in out:
        for p, copy in zip(pieces, copies):
            copy.wait_recv()
            got = p(at.slot(t))
            mate.append(net.push(got, got, at.mate()))
    return mate


def low_bit(k):
    return k & -k


class Gather:
    def __init__(self, net, at, own, ref, rows):
        self.net, self.at, self.ref, self.rows = net, at, ref, rows
        bits = [b for b in (1 << i for i in range(10)) if b < at.n_shard]
        self.bits = bits[::-1]
        here = self.place(0)
        self.copies = {b: net.push(own, here, at.z_dev(b)) for b in self.bits}

    def place(self, k):
        return self.ref.at[span(self.at.z ^ k, self.rows)]

    def finish(self, then=None):
        waiting = list(self.bits)
        while waiting:
            k = waiting.pop(0)
            self.copies[k].wait_recv()
            for b in self.bits:
                if b < low_bit(k):
                    got = self.place(k)
                    self.copies[k | b] = self.net.push(got, got, self.at.z_dev(b))
                    waiting.append(k | b)
            if then:
                then()
                then = None


class Scatter:
    def __init__(self, net, at, part, landing, rows, step):
        self.net, self.at, self.part, self.landing, self.rows, self.step = net, at, part, landing, rows, step
        self.slot, self.bit, self.last = 0, 1, []
        self.start()

    def block(self, k):
        return self.part.at[span(self.at.z ^ k, self.rows)]

    def start(self):
        bit, self.copies = self.bit, []
        for k in [k for k in range(self.at.n_shard - 1, 0, -1) if k % (2 * bit) == bit]:
            copy = self.net.push(self.block(k), self.landing.at[self.slot], self.at.z_dev(bit))
            self.copies.append((k ^ bit, self.slot, copy))
            self.slot += 1

    def advance(self):
        self.bit *= 2
        for to, i, copy in self.copies:
            copy.wait_recv()
            if not to:
                self.last.append(i)
                continue

            def add(j, _, to=to, i=i):
                r = span(j, self.step)
                here = pl.ds(pl.multiple_of((self.at.z ^ to) * self.rows + j * self.step, self.step), self.step)
                value = self.part[here, :].astype(f32) + self.landing[i, r, :].astype(f32)
                self.part[here, :] = value.astype(bf16)
                return 0

            lax.fori_loop(0, self.rows // self.step, add, 0)
        if self.bit < self.at.n_shard:
            self.start()
            return True
        return False

    def finish(self):
        while self.advance():
            pass
        return self.last


def spread_near(net, at, ref):
    own = ref.at[at.e]
    mate = [net.push(own, own, at.mate())]
    out = {t: net.push(own, own, at.chip_dev(t)) for t in (1, 2)}
    half = ref.shape[1] // 2

    def go_on():
        relayed = []
        for t in (1, 2):
            out[t].wait_recv()
            got = ref.at[at.slot(t)]
            mate.append(net.push(got, got, at.mate()))
            part = ref.at[at.slot(t), pl.ds((2 - t) * half, half)]
            relayed.append(net.push(part, part, at.chip_dev(3 - t)))
        arrive(relayed)
        got = ref.at[at.slot(3)]
        mate.append(net.push(got, got, at.mate()))
        return mate

    return go_on


def comm_call(kernel, cid, n_remote, n_local, scratch, outs, vmem_mb, in_specs=None, out_specs=None, cost=None):
    any_spec = pl.BlockSpec(memory_space=pl.ANY)

    def call(*args):
        return pl.pallas_call(
            kernel,
            out_shape=outs,
            in_specs=in_specs or [any_spec] * len(args),
            out_specs=out_specs or [any_spec] * len(outs),
            scratch_shapes=list(scratch)
            + [
                pltpu.SemaphoreType.DMA((n_remote,)),
                pltpu.SemaphoreType.DMA((n_remote,)),
                pltpu.SemaphoreType.DMA((n_local,)),
            ],
            compiler_params=pltpu.CompilerParams(
                collective_id=cid, has_side_effects=True, vmem_limit_bytes=vmem_mb << 20
            ),
            cost_estimate=cost,
        )(*args)

    return call


def tiled(size, most):
    while size % most:
        most //= 2
    return most


def halves(at):
    return list(range(1, at.chips)) + [0]


def rope_rows(value, cos, sin):
    return value * cos + pltpu.roll(value, HEAD_DIM // 2, 1) * sin


def rope_rows_back(grad, cos, sin):
    return grad * cos + pltpu.roll(grad * sin, HEAD_DIM // 2, 1)


def eight(per):
    return jnp.sum(per.reshape(per.shape[0] // 8, 8, per.shape[1]), axis=0)


def span(i, size):
    if isinstance(i, int):
        return pl.ds(i * size, size)
    return pl.ds(pl.multiple_of(i * size, size), size)


def soft_block(q_ref, k_ref, seg_row, seg_col, h, i, block, scale):
    rows, keys = pl.ds(i * block, block), pl.ds(0, (i + 1) * block)
    scores = mm_nt(q_ref[rows, span(h, HEAD_DIM)], k_ref[keys, :]) * scale
    width = (i + 1) * block
    at_q = i * block + lax.broadcasted_iota(jnp.int32, (block, width), 0)
    at_k = lax.broadcasted_iota(jnp.int32, (block, width), 1)
    allowed = (at_k <= at_q) & (seg_row[0:1, keys] == seg_col[rows, 0:1])
    scores = jnp.where(allowed, scores, neg_fill)
    raised = jnp.exp(scores - jnp.max(scores, axis=-1, keepdims=True))
    return raised / jnp.sum(raised, axis=-1, keepdims=True)


def front_kernel(
    dims, x, small, seg_own, w_qkv, w_out, w_gu, cot, mask, cos_h, sin_h,
    small_out, seg_out, heads_out, a_out, raw_out, q_out, k_out, v_out, o_out, x1_out, b_out,
    gate_up, cot_all, mask_all, b_pair,
    x_all, small_all, seg_col, heads, a, raw, q, k, v, o, w_o, part, parts_in, cos, sin, gains, seg_row, x1, b_own,
    send, recv, local,
):
    at = Place(*dims)
    net = Net(send, recv, local)
    z, e, group = at.z, at.e, at.group
    tok = x.shape[0]
    length, width = x_all.shape
    mine = z // group
    rows_e, cols = heads.shape[2], heads.shape[3]
    hd = cols - 2 * HEAD_DIM
    n_heads = hd // HEAD_DIM
    q_width = HEADS * HEAD_DIM
    d_slice = w_gu.shape[1]
    scale = HEAD_DIM ** (-0.5)
    block = tok

    def heads_of(dest):
        kv = (dest * n_heads) // (HEADS // KV_HEADS)
        rows = span(e, rows_e)
        return [
            (w_qkv.at[rows, span(dest, hd)], heads.at[z, e, :, pl.ds(0, hd)]),
            (w_qkv.at[rows, span(HEADS + kv, HEAD_DIM)], heads.at[z, e, :, pl.ds(hd, HEAD_DIM)]),
            (w_qkv.at[rows, span(HEADS + KV_HEADS + kv, HEAD_DIM)], heads.at[z, e, :, pl.ds(hd + HEAD_DIM, HEAD_DIM)]),
        ]

    half0, half1 = pl.ds(0, tok), pl.ds(tok, tok)
    first = [
        net.copy(x, x_all.at[span(z, tok)]),
        net.copy(small, small_all.at[z]),
        net.copy(seg_own, seg_col.at[span(z, tok)]),
        net.copy(cos_h, cos),
        net.copy(sin_h, sin),
    ]
    local_heads = [net.copy(s, d) for s, d in heads_of(z)]
    local_cot = [net.copy(cot, cot_all.at[e, half0]), net.copy(mask, mask_all.at[e, half0])]
    load_out = net.copy(w_out, w_o)
    greet(everyone(at))
    got_heads = [net.push(s, d, at.z_dev(t)) for t in range(1, at.n_shard) for s, d in heads_of(z ^ t)]
    got_x = []
    for t in range(1, at.n_shard):
        got_x.append(net.push(small, small_all.at[z], at.z_dev(t)))
        got_x.append(net.push(seg_own, seg_col.at[span(z, tok)], at.z_dev(t)))
    gather_x = Gather(net, at, x, x_all, tok)
    for c in local_heads:
        c.wait()
    arrive(got_heads)
    pieces = [lambda who: heads.at[:, who]]
    heads_state = spread(net, at, pieces)
    other = (z ^ group) // group
    cut = d_slice // 2
    low, high = pl.ds(0, cut), pl.ds(cut, cut)
    pieces_w = [
        (w_gu.at[other, low], gate_up.at[z, low], gate_up.at[z ^ group, low]),
        (w_gu.at[other, high], gate_up.at[z, high], gate_up.at[z ^ group, high]),
    ]
    from_partner = {}

    def fetch_piece(i):
        src, dst, got = pieces_w[i]
        from_partner[i] = (net.push(src, dst, at.z_dev(group)), got)

    for c in first:
        c.wait()
    gather_x.finish(lambda: fetch_piece(0))
    arrive(got_x)

    def hand_on(i):
        copy, ref = from_partner[i]
        copy.wait_recv()
        for t in range(1, group):
            got_w.append(net.push(ref, ref, at.z_dev(t)))

    got_w = []
    for t in range(1, group):
        got_w.append(net.push(w_gu.at[mine], gate_up.at[z], at.z_dev(t)))
    got_cot = [
        net.push(cot, cot_all.at[e, half1], at.z_dev(group)),
        net.push(mask, mask_all.at[e, half1], at.z_dev(group)),
    ]

    qk = []
    for s in range(at.n_shard):
        rows = small_all[s, 0:16, :].astype(f32)
        gains[0:2, span(s, d_slice)] = rows[0:2]
        seg_row[0:1, span(s, tok)] = rows[4:5, :tok]
        qk.append(rows[2:4, :HEAD_DIM])
    qk = sum(qk[1:], qk[0])
    step = 16

    def norm_rows(i, _):
        rows = span(i, step)
        value = x_all[rows, :].astype(f32)
        a[rows, :] = (value * inv_rms(value) * gains[0:1, :]).astype(bf16)
        return 0

    lax.fori_loop(0, length // step, norm_rows, 0)
    fetch_piece(1)
    last = pass_on(net, at, pieces, heads_state)
    arrive(last)
    keep = [net.copy(heads, heads_out), net.copy(a, a_out), net.copy(small_all, small_out), net.copy(seg_col, seg_out)]

    wide = tiled(cols, 256)

    def project(i, _):
        tile = span(i, wide)
        raw[:, tile] = mm(a[...], heads[:, :, :, tile].reshape(width, wide))
        return 0

    lax.fori_loop(0, cols // wide, project, 0)
    keep.append(net.copy(raw, raw_out))

    def head_rows(i, _):
        rows = span(i, block)
        cos_b, sin_b = cos[rows, :], sin[rows, :]
        for h in range(n_heads + 1):
            value = raw[rows, pl.ds(h * HEAD_DIM, HEAD_DIM)]
            gain = qk[0:1] if h < n_heads else qk[1:2]
            value = rope_rows(value * inv_rms(value) * gain, cos_b, sin_b).astype(bf16)
            if h < n_heads:
                q[rows, pl.ds(h * HEAD_DIM, HEAD_DIM)] = value
            else:
                k[rows, :] = value
        v[rows, :] = raw[rows, pl.ds(hd + HEAD_DIM, HEAD_DIM)].astype(bf16)
        return 0

    lax.fori_loop(0, length // block, head_rows, 0)
    keep += [net.copy(q, q_out), net.copy(k, k_out), net.copy(v, v_out)]
    for c in local_cot:
        c.wait()
    arrive(got_cot)
    cots = [lambda who: cot_all.at[who], lambda who: mask_all.at[who]]
    cot_state = spread(net, at, cots)


    def one_head(h, _):
        for i in range(length // block):
            soft = soft_block(q, k, seg_row, seg_col, h, i, block, scale).astype(bf16)
            mixed = mm(soft, v[pl.ds(0, (i + 1) * block), :])
            o[pl.ds(i * block, block), span(h, HEAD_DIM)] = mixed.astype(bf16)
        return 0

    lax.fori_loop(0, n_heads, one_head, 0)
    hand_on(0)
    keep.append(net.copy(o, o_out))
    load_out.wait()
    wide_o = tiled(width, 256)

    def out_tile(i, _):
        tile = span(i, wide_o)
        part[:, tile] = mm(o[...], w_o[:, tile]).astype(bf16)
        return 0

    lax.fori_loop(0, width // wide_o, out_tile, 0)
    summing = Scatter(net, at, part, parts_in, tok, step)
    more = summing.advance()
    hand_on(1)
    slots = summing.finish() if more else summing.last

    def middle_rows(i, _):
        rows = span(i, step)
        total = part[pl.ds(pl.multiple_of(z * tok + i * step, step), step), :].astype(f32)
        for t in slots:
            total += parts_in[t, rows, :].astype(f32)
        value = x_all[pl.ds(pl.multiple_of(z * tok + i * step, step), step), :].astype(f32) + total
        x1[rows, :] = value
        b_own[rows, :] = (value * inv_rms(value) * gains[1:2, :]).astype(bf16)
        return 0

    lax.fori_loop(0, tok // step, middle_rows, 0)
    swap = net.push(b_own, b_pair.at[half1], at.z_dev(group))
    keep += [net.copy(b_own, b_pair.at[half0]), net.copy(x1, x1_out), net.copy(b_own, b_out)]
    last = pass_on(net, at, cots, cot_state)
    swap.wait_recv()
    arrive(last + got_w)
    for c in keep:
        c.wait()
    net.sent()


def expert_kernel(
    dims, b_pair, cot_all, mask_all, gate_up, w_gu_in, w_dn_in, router_t,
    out_part, ggu, gdn, db_in, ex_in, land_gu, land_dn,
    w_gu, w_dn, rows, cot_t, mask_t, hid, d_pre, d_y, stage, stage_x, own, own_x, core_in, core_x, w_r, d_r, g_tile, d_tile,
    tile_sem, send, recv, local,
):
    at = Place(*dims)
    net = Net(send, recv, local)
    z, e, group = at.z, at.e, at.group
    n_slices, d_slice, ff2 = gate_up.shape
    ff, width = w_dn.shape
    two = b_pair.shape[0]
    four = 2 * two
    mine, other = z // group, (z ^ group) // group
    expert = e * (at.n_shard // group) + mine
    step = 16
    fine = tiled(ff, 256)
    wide = tiled(width, 1024)
    far = z ^ group

    def d_cols(who):
        return w_dn.at[:, span(who, d_slice)]

    pair = net.copy(b_pair, rows.at[0, 1])
    masks = []
    for t in range(at.chips):
        masks.append(net.copy(mask_all.at[at.slot(t, 1)], mask_t.at[t, 0]))
        masks.append(net.copy(mask_all.at[at.slot(t)], mask_t.at[t, 1]))
    loads = [net.copy(w_gu_in.at[mine], w_gu.at[span(z, d_slice)])]
    for k in range(1, n_slices):
        loads.append(net.copy(gate_up.at[z ^ k], w_gu.at[span(z ^ k, d_slice)]))
    load_dn = net.copy(w_dn_in.at[mine], d_cols(z))

    def fetch(t):
        return [
            net.copy(cot_all.at[at.slot(t, 1)], cot_t.at[0]),
            net.copy(cot_all.at[at.slot(t)], cot_t.at[1]),
        ]

    order = list(range(1, at.chips)) + [0]
    fetched = {order[0]: fetch(order[0])}
    greet(
        [at.chip_dev(t) for t in range(1, at.chips)] + [at.mate()] + [at.z_dev(t) for t in range(1, group + 1)]
    )
    from_mate = {0: net.push(b_pair, rows.at[0, 0], at.mate())}
    near = [t for t in (1, 2) if t < at.chips]
    beyond = [t for t in range(1, at.chips) if t not in near]
    from_chip = {t: net.push(b_pair, rows.at[t, 1], at.chip_dev(t)) for t in near}
    from_partner = net.push(w_dn_in.at[other], d_cols(z), at.z_dev(group))
    got_dn = [net.push(w_dn_in.at[mine], d_cols(z), at.z_dev(t)) for t in range(1, group)]

    relayed = []

    def pass_rows(t):
        if t in from_chip:
            from_chip[t].wait_recv()
        else:
            arrive(relayed)
        from_mate[t] = net.push(rows.at[t, 1], rows.at[t, 0], at.mate())

    lanes = lax.broadcasted_iota(jnp.int32, (four, 128), 1)

    def up_rows(t):
        logits = mm_nt(rows[t].reshape(four, width), router_t[...])
        chosen = mask_t[t].reshape(four, 128).astype(f32) > 0
        masked = jnp.where(chosen, logits, neg_fill)
        raised = jnp.where(chosen, jnp.exp(masked - jnp.max(masked, axis=1, keepdims=True)), 0.0)
        weight = raised / jnp.sum(raised, axis=1, keepdims=True)
        weight = jnp.sum(jnp.where(lanes == expert, weight, 0.0), axis=1, keepdims=True)
        w_r[t] = jnp.broadcast_to(weight, (four, 128))

        def up(j, _):
            tile, tile_u = span(j, fine), pl.ds(pl.multiple_of(ff + j * fine, fine), fine)
            x = rows[t].reshape(four, width)
            g = mm(x, w_gu[:, tile])
            u = mm(x, w_gu[:, tile_u])
            d_pre[t, :, tile] = g.astype(bf16)
            d_pre[t, :, tile_u] = u.astype(bf16)
            hid[t, :, tile] = (g * jax.nn.sigmoid(g) * u).astype(bf16)
            return 0

        lax.fori_loop(0, ff // fine, up, 0)

    for c in masks:
        c.wait()
    pair.wait()
    from_mate[0].wait_recv()
    for c in loads:
        c.wait()
    up_rows(0)
    for i in near:
        pass_rows(i)
        if beyond:
            part = pl.ds((2 - i) * (two // 2), two // 2)
            relayed.append(net.push(rows.at[i, 1, part], rows.at[3, 1, part], at.chip_dev(3 - i)))
    from_partner.wait_recv()
    for t in range(1, group):
        got_dn.append(net.push(d_cols(far), d_cols(far), at.z_dev(t)))
    for t in near:
        from_mate[t].wait_recv()
        up_rows(t)
    for t in beyond:
        pass_rows(t)
        from_mate[t].wait_recv()
        up_rows(t)
    load_dn.wait()
    arrive(got_dn)

    mates, outs = {}, []

    def finish(t):
        arrive(mates[t])

        def add_rows(i, _):
            r = span(i, step)
            own[t, r, :] = (own[t, r, :].astype(f32) + core_in[t, r, :].astype(f32)).astype(bf16)
            own_x[t, r, :] = (own_x[t, r, :].astype(f32) + core_x[t, r, :].astype(f32)).astype(bf16)
            return 0

        lax.fori_loop(0, two // step, add_rows, 0)
        if t:
            outs.append(net.push(own.at[t], db_in.at[t], at.chip_dev(t)))
            outs.append(net.push(own_x.at[t], ex_in.at[t], at.chip_dev(t)))

    used = {}
    for i, t in enumerate(order):
        d_r[...] = jnp.zeros_like(d_r)
        for c in fetched[t]:
            c.wait()

        def back_y(n, _, t=t):
            tile = span(n, wide)
            y = mm(hid[t], w_dn[:, tile]).astype(bf16).astype(f32)
            c = cot_t[:, :, tile].reshape(four, wide).astype(f32)
            w = w_r[t, :, 0:1]
            d_r[...] += jnp.broadcast_to(jnp.sum(c * y, axis=1, keepdims=True), (four, 128))
            d_y[t, :, tile] = (w * c).astype(bf16)
            cot_t[:, :, tile] = (w * y).astype(bf16).reshape(2, two, wide)
            return 0

        lax.fori_loop(0, width // wide, back_y, 0)
        kept = [
            net.copy(cot_t.at[0], out_part.at[at.slot(t, 1)]),
            net.copy(cot_t.at[1], out_part.at[at.slot(t)]),
        ]
        if i:
            finish(order[i - 1])

        def back_h(j, _, t=t):
            tile, tile_u = span(j, fine), pl.ds(pl.multiple_of(ff + j * fine, fine), fine)
            d_h = mm_nt(d_y[t], w_dn[tile, :])
            g, u = d_pre[t, :, tile].astype(f32), d_pre[t, :, tile_u].astype(f32)
            sig = jax.nn.sigmoid(g)
            d_pre[t, :, tile] = (d_h * u * sig * (1.0 + g * (1.0 - sig))).astype(bf16)
            d_pre[t, :, tile_u] = (d_h * g * sig).astype(bf16)
            return 0

        lax.fori_loop(0, ff // fine, back_h, 0)
        for c in kept:
            c.wait()
        if i + 1 < at.chips:
            fetched[order[i + 1]] = fetch(order[i + 1])
        p = i % 2
        for c in used.pop(p, []):
            net.done(c)

        def back_b(n, _, t=t, p=p):
            tile = span(n, wide)
            value = mm_nt(d_pre[t], w_gu[tile, :]).astype(bf16)
            stage[p, :, tile] = value[:two]
            own[t, :, tile] = value[two:]
            return 0

        lax.fori_loop(0, width // wide, back_b, 0)
        routed = d_r[...]
        high = routed.astype(bf16)
        low = (routed - high.astype(f32)).astype(bf16)
        none = jnp.zeros_like(high)
        extra = jnp.where(lanes == expert, high, jnp.where(lanes == expert + 64, low, none))
        stage_x[p] = extra[:two]
        own_x[t] = extra[two:]
        mates[t] = [
            net.push(stage.at[p], core_in.at[t], at.mate()),
            net.push(stage_x.at[p], core_x.at[t], at.mate()),
        ]
        used[p] = mates[t]
    finish(order[-1])
    keep = [net.copy(own.at[0], db_in.at[0]), net.copy(own_x.at[0], ex_in.at[0])]

    part = tiled(width, 256)
    per = d_slice // part

    def out_copy(slot, i):
        who = z ^ (n_slices - 1 - i // per)
        return pltpu.make_async_copy(g_tile.at[slot], ggu.at[who, span(i % per, part)], tile_sem.at[slot])

    def grad_up(i, _):
        slot = i % 2

        @pl.when(i >= 2)
        def _():
            out_copy(slot, i - 2).wait()

        who = z ^ (n_slices - 1 - i // per)
        x = rows[:, :, :, span(who * per + i % per, part)].reshape(at.chips * four, part)
        g_tile[slot] = mm_tn(x, d_pre[...].reshape(at.chips * four, ff2)).astype(bf16)
        out_copy(slot, i).start()
        return 0

    def down_copy(slot, i):
        return pltpu.make_async_copy(d_tile.at[slot], gdn.at[span(i, fine)], tile_sem.at[slot])

    def grad_down(i, _):
        slot = i % 2

        @pl.when(i >= 2)
        def _():
            down_copy(slot, i - 2).wait()

        h = hid[:, :, span(i, fine)].reshape(at.chips * four, fine)
        d_tile[slot] = mm_tn(h, d_y[...].reshape(at.chips * four, width)).astype(bf16)
        down_copy(slot, i).start()
        return 0

    n_down = ff // fine
    lax.fori_loop(0, n_down, grad_down, 0)
    for i in range(max(0, n_down - 2), n_down):
        down_copy(i % 2, i).wait()
    for t in range(1, group):
        outs.append(net.push(gdn.at[:, span(z ^ t ^ group, d_slice)], land_dn.at[t - 1], at.z_dev(t)))
    n_up, n_early = width // part, (group - 1) * per
    lax.fori_loop(0, n_early, grad_up, 0)
    for i in range(n_early - 2, n_early):
        out_copy(i % 2, i).wait()
    half = pl.ds(0, d_slice // 2)
    for t in range(1, group):
        outs.append(net.push(ggu.at[z ^ t ^ group, half], land_gu.at[t - 1], at.z_dev(t)))

    def grad_rest(i, _):
        slot = i % 2

        @pl.when(i >= n_early + 2)
        def _():
            out_copy(slot, i - 2).wait()

        who = z ^ (n_slices - 1 - i // per)
        x = rows[:, :, :, span(who * per + i % per, part)].reshape(at.chips * four, part)
        g_tile[slot] = mm_tn(x, d_pre[...].reshape(at.chips * four, ff2)).astype(bf16)
        out_copy(slot, i).start()
        return 0

    lax.fori_loop(n_early, n_up, grad_rest, 0)
    for i in range(n_up - 2, n_up):
        out_copy(i % 2, i).wait()
    for c in keep:
        c.wait()
    arrive(outs)
    net.sent()


def norm_kernel(
    dims, early, db, ex, ggu, gdn, out_part, x1, b, cot, rw, router_t, gains,
    gx1, do_all, gain_two, g_router, land_gu, late_gu, land_dn, out_sum,
    own, own_x, half_out, half_x, swap_in, swap_x, logit, d_out, out_own, out_core, out_in,
    send, recv, local,
):
    at = Place(*dims)
    net = Net(send, recv, local)
    z, e, group = at.z, at.e, at.group
    tok = x1.shape[0]
    n_parts = db.shape[0]
    loads = [net.copy(db, own), net.copy(ex, own_x)]
    load_own = {t: net.copy(out_part.at[at.slot(t)], out_own.at[t]) for t in halves(at)}
    greet(everyone(at))
    step = 16
    for c in loads:
        c.wait()

    def sums(src):
        total, total_x = own[0, src, :].astype(f32), own_x[0, src, :].astype(f32)
        for t in range(1, n_parts):
            total += own[t, src, :].astype(f32)
            total_x += own_x[t, src, :].astype(f32)
        return total, total_x

    def partner(i, _):
        total, total_x = sums(pl.ds(pl.multiple_of(tok + i * step, step), step))
        half_out[span(i, step), :] = total.astype(bf16)
        half_x[span(i, step), :] = total_x.astype(bf16)
        return 0

    lax.fori_loop(0, tok // step, partner, 0)
    swaps = [net.push(half_out, swap_in, at.z_dev(group)), net.push(half_x, swap_x, at.z_dev(group))]
    d_slice = ggu.shape[1]
    landed = []
    for t in range(1, group):
        j = z ^ t ^ group
        if not early:
            landed.append(net.push(ggu.at[j, pl.ds(0, d_slice // 2)], land_gu.at[t - 1], at.z_dev(t)))
            landed.append(net.push(gdn.at[:, span(j, d_slice)], land_dn.at[t - 1], at.z_dev(t)))
        landed.append(net.push(ggu.at[j, pl.ds(d_slice // 2, d_slice // 2)], late_gu.at[t - 1], at.z_dev(t)))
    mates = {t: net.push(out_part.at[at.slot(t, 1)], out_core.at[t], at.mate()) for t in halves(at)}
    outs = []
    for t in halves(at):
        load_own[t].wait()
        mates[t].wait_recv()

        def add(i, _, t=t):
            rows = span(i, step)
            out_own[t, rows, :] = (out_own[t, rows, :].astype(f32) + out_core[t, rows, :].astype(f32)).astype(bf16)
            return 0

        lax.fori_loop(0, 2 * tok // step, add, 0)
        if t:
            outs.append(net.push(out_own.at[t], out_in.at[t - 1], at.chip_dev(t)))
    arrive(swaps)
    gain_two[...] = jnp.zeros_like(gain_two)

    def owner(i, _):
        rows = span(i, step)
        grad, routed = sums(rows)
        grad += swap_in[rows, :].astype(f32)
        routed += swap_x[rows, :].astype(f32)
        routed = routed + pltpu.roll(routed, 64, 1)
        weight = rw[rows, :]
        d_logit = weight * (routed - jnp.sum(weight * routed, axis=1, keepdims=True))
        high = d_logit.astype(bf16)
        low = (d_logit - high.astype(f32)).astype(bf16)
        logit[0, rows, :] = high
        logit[1, rows, :] = low
        grad += mm(high, router_t[...]) + mm(low, router_t[...])
        value = x1[rows, :]
        r = inv_rms(value)
        c = grad * gains[1:2, :]
        back = cot[rows, :].astype(f32) + r * c - value * (r * r * r * jnp.mean(c * value, axis=-1, keepdims=True))
        gx1[rows, :] = back
        d_out[rows, :] = back.astype(bf16)
        gain_two[...] += eight(grad * value * r)
        return 0

    lax.fori_loop(0, tok // step, owner, 0)
    mine = do_all.at[span(z, tok)]
    keep = net.copy(d_out, mine)
    copies = [net.push(d_out, mine, at.z_dev(t)) for t in range(1, at.n_shard)]
    g_router[...] = mm_tn(logit[0], b[...]) + mm_tn(logit[1], b[...])
    arrive(outs)

    def out_rows(i, _):
        rows = span(i, step)
        total = out_own[0, rows, :].astype(f32)
        for t in range(1, at.chips):
            total += out_in[t - 1, rows, :].astype(f32)
        out_sum[rows, :] = total.astype(bf16)
        return 0

    lax.fori_loop(0, 2 * tok // step, out_rows, 0)
    keep.wait()
    arrive(copies + landed)
    net.sent()


def back_kernel(
    dims, do_h, w_out, o_h, q_h, k_h, v_h, raw_h, cos_h, sin_h, seg_h, a_h, heads_h, ggu, gdn, land_gu, late_gu, land_dn, out_sum,
    out_sum_own, small, x1, gx1, x, gains, gain_two, g_router,
    hidden, g_hidden, small_sum, g_att, g_qkv, two_gu, own_gu, two_dn, own_dn,
    do_all, w_o, o, q, k, v, raw, cos, sin, seg_col, seg_row, mix, d_qkv, dk, dv, qk_gain, a, heads,
    sum_gu, add_gu, sum_dn, add_dn, swap_in, g_out, g_core, g_in, share_own,
    parts_in, g_heads, core_in, chip_in, mine, turn_in, share_qkv, sm, sm_z, sm_core, sm_chip,
    send, recv, local,
):
    at = Place(*dims)
    net = Net(send, recv, local)
    z, e, group = at.z, at.e, at.group
    length, width = do_all.shape
    tok = x1.shape[0]
    cols = raw.shape[1]
    hd = cols - 2 * HEAD_DIM
    n_heads = hd // HEAD_DIM
    rows_e = heads.shape[2]
    d_slice = ggu.shape[1]
    scale = HEAD_DIM ** (-0.5)
    block = tok
    step = 16
    far = z ^ group

    def d_cols(ref, who):
        return ref.at[:, span(who, d_slice)]

    cut = d_slice // 2
    halves_gu = [pl.ds(0, cut), pl.ds(cut, cut)]
    load_gu = [
        [net.copy(ggu.at[far, r], sum_gu.at[i])] + [net.copy(land.at[t - 1], add_gu.at[i, t - 1]) for t in range(1, group)]
        for i, (r, land) in enumerate(zip(halves_gu, (land_gu, late_gu)))
    ]
    load_a = [net.copy(do_h, do_all), net.copy(o_h, o)]
    load_b = [
        net.copy(s, d)
        for s, d in ((w_out, w_o), (q_h, q), (k_h, k), (v_h, v), (raw_h, raw), (cos_h, cos), (sin_h, sin), (seg_h, seg_col))
    ]
    load_c = [net.copy(a_h, a), net.copy(heads_h, heads)]
    load_dn = [net.copy(d_cols(gdn, far), sum_dn)] + [net.copy(land_dn.at[t - 1], add_dn.at[t - 1]) for t in range(1, group)]
    greet(everyone(at))
    swap = net.push(out_sum.at[pl.ds(tok, tok)], swap_in, at.z_dev(group))

    def add_up(total, adds):
        def rows_of(i, _):
            rows = span(i, step)
            value = total[rows, :].astype(f32)
            for t in range(1, group):
                value += adds[t - 1, rows, :].astype(f32)
            total[rows, :] = value.astype(bf16)
            return 0

        lax.fori_loop(0, total.shape[0] // step, rows_of, 0)

    got = []

    def send_half(i):
        for c in load_gu[i]:
            c.wait()
        add_up(sum_gu.at[i], add_gu.at[i])
        got.append(net.push(sum_gu.at[i], two_gu.at[halves_gu[i]], at.z_dev(group)))

    send_half(0)
    for t in range(1, group):
        got.append(net.push(ggu.at[z ^ t], own_gu.at[t - 1], at.z_dev(t)))

    for c in load_a:
        c.wait()
    share = share_own.shape[0]
    wide = tiled(hd, 256)
    each = wide // share

    def out_grad(i, _):
        tile = mm_tn(o[:, span(i, wide)], do_all[...]).astype(bf16)
        for j in range(each):
            g_out[each * i + j] = tile[j * share : (j + 1) * share]
        return 0

    lax.fori_loop(0, hd // wide, out_grad, 0)
    g_mates = {t: net.push(g_out.at[at.slot(t, 1)], g_core.at[t], at.mate()) for t in halves(at)}
    for c in load_b:
        c.wait()
    qk = []
    for s in range(at.n_shard):
        rows = small[s, 0:16, :].astype(f32)
        seg_row[0:1, span(s, tok)] = rows[4:5, :tok]
        qk.append(rows[2:4, :HEAD_DIM])
    qk = sum(qk[1:], qk[0])

    def mix_tile(i, _):
        tile = span(i, wide)
        mix[:, tile] = mm_nt(do_all[...], w_o[tile, :]).astype(bf16)
        return 0

    lax.fori_loop(0, hd // wide, mix_tile, 0)
    g_outs = []
    for t in halves(at):
        g_mates[t].wait_recv()

        def add(i, _, t=t):
            rows = span(i, step)
            s = at.slot(t)
            g_out[s, rows, :] = (g_out[s, rows, :].astype(f32) + g_core[t, rows, :].astype(f32)).astype(bf16)
            return 0

        lax.fori_loop(0, share // step, add, 0)
        if t:
            g_outs.append(net.push(g_out.at[at.slot(t)], g_in.at[t - 1], at.chip_dev(t)))
    send_half(1)

    dk[...] = jnp.zeros_like(dk)
    dv[...] = jnp.zeros_like(dv)
    qk_gain[...] = jnp.zeros_like(qk_gain)

    def one_head(h, _):
        lanes = span(h, HEAD_DIM)
        for i in range(length // block):
            rows, keys = pl.ds(i * block, block), pl.ds(0, (i + 1) * block)
            soft = soft_block(q, k, seg_row, seg_col, h, i, block, scale)
            d_mix = mix[rows, lanes]
            d_soft = mm_nt(d_mix, v[keys, :])
            d_scores = (soft * (d_soft - jnp.sum(soft * d_soft, axis=-1, keepdims=True))).astype(bf16)
            dv[keys, :] += mm_tn(soft.astype(bf16), d_mix)
            dk[keys, :] += mm_tn(d_scores, q[rows, lanes]) * scale
            dq = mm(d_scores, k[keys, :]) * scale
            value = raw[rows, lanes]
            back, per = rms_back(value, qk[0:1], rope_rows_back(dq, cos[rows, :], sin[rows, :]))
            d_qkv[rows, lanes] = back.astype(bf16)
            qk_gain[0:8, :] += eight(per)
        return 0

    lax.fori_loop(0, n_heads, one_head, 0)
    for i in range(length // block):
        rows = pl.ds(i * block, block)
        value = raw[rows, pl.ds(hd, HEAD_DIM)]
        back, per = rms_back(value, qk[1:2], rope_rows_back(dk[rows, :], cos[rows, :], sin[rows, :]))
        d_qkv[rows, pl.ds(hd, HEAD_DIM)] = back.astype(bf16)
        d_qkv[rows, pl.ds(hd + HEAD_DIM, HEAD_DIM)] = dv[rows, :].astype(bf16)
        qk_gain[8:16, :] += eight(per)

    arrive(g_outs)

    def own_share(i, _):
        rows = span(i, step)
        total = g_out[e, rows, :].astype(f32)
        for t in range(1, at.chips):
            total += g_in[t - 1, rows, :].astype(f32)
        share_own[rows, :] = total.astype(bf16)
        return 0

    lax.fori_loop(0, share // step, own_share, 0)
    keep_att = net.copy(share_own, g_att.at[e])
    keep_att.wait()
    atts = [lambda who: g_att.at[who]]
    att_state = spread(net, at, atts)
    for c in load_c:
        c.wait()
    wide_d = tiled(d_slice, 256)
    each_d = wide_d // rows_e

    def grad_tile(s, _):
        for j in range(d_slice // wide_d):
            some = a[:, pl.ds(pl.multiple_of(s * d_slice + j * wide_d, wide_d), wide_d)]
            tile = mm_tn(some, d_qkv[...]).astype(bf16)
            for i in range(each_d):
                g_heads[each_d * j + i, s] = tile[i * rows_e : (i + 1) * rows_e]
        return 0

    lax.fori_loop(0, at.n_shard, grad_tile, 0)
    mates = {t: net.push(g_heads.at[at.slot(t, 1)], core_in.at[t], at.mate()) for t in halves(at)}
    part = do_all

    def rows_tile(s, _):
        for j in range(d_slice // wide_d):
            some = heads[s, pl.ds(each_d * j, each_d)].reshape(wide_d, cols)
            here = pl.ds(pl.multiple_of(s * d_slice + j * wide_d, wide_d), wide_d)
            part[:, here] = mm_nt(d_qkv[...], some).astype(bf16)
        return 0

    lax.fori_loop(0, at.n_shard, rows_tile, 0)
    sums = Scatter(net, at, part, parts_in, tok, step)
    chips = []
    for t in halves(at):
        mates[t].wait_recv()
        who = at.slot(t)

        def add(s, _, t=t, who=who):
            g_heads[who, s] = (g_heads[who, s].astype(f32) + core_in[t, s].astype(f32)).astype(bf16)
            return 0

        lax.fori_loop(0, at.n_shard, add, 0)
        if t:
            chips.append(net.push(g_heads.at[who], chip_in.at[t - 1], at.chip_dev(t)))
    more = sums.advance()
    for c in load_dn:
        c.wait()
    add_up(sum_dn, add_dn)
    swap.wait_recv()

    def hidden_rows(i, _):
        rows = span(i, step)
        hidden[rows, :] = (x1[rows, :] + out_sum_own[rows, :].astype(f32) + swap_in[rows, :].astype(f32)).astype(bf16)
        return 0

    lax.fori_loop(0, tok // step, hidden_rows, 0)
    arrive(chips)

    def total(s, _):
        value = g_heads[e, s].astype(f32)
        for t in range(1, at.chips):
            value += chip_in[t - 1, s].astype(f32)
        mine[s] = value.astype(bf16)
        return 0

    lax.fori_loop(0, at.n_shard, total, 0)
    turns = [net.push(mine.at[z ^ t], turn_in.at[z], at.z_dev(t)) for t in range(1, at.n_shard)]
    turn_own = net.copy(mine.at[z], turn_in.at[z])
    got.append(net.push(sum_dn, two_dn, at.z_dev(group)))
    for t in range(1, group):
        got.append(net.push(d_cols(gdn, z ^ t), own_dn.at[t - 1], at.z_dev(t)))
    slots = sums.finish() if more else sums.last
    sm[...] = jnp.zeros_like(sm)
    gain_one = jnp.zeros((8, width), f32)

    def owner(i, gain_one):
        rows = span(i, step)
        here = pl.ds(pl.multiple_of(z * tok + i * step, step), step)
        da = part[here, :].astype(f32)
        for t in slots:
            da += parts_in[t, rows, :].astype(f32)
        back, per = rms_back(x[rows, :].astype(f32), gains[0:1, :], da)
        g_hidden[rows, :] = gx1[rows, :] + back
        return gain_one + eight(per)

    gain_one = lax.fori_loop(0, tok // step, owner, gain_one)
    row_one = jnp.sum(gain_one, axis=0, keepdims=True)
    row_two = jnp.sum(gain_two[...], axis=0, keepdims=True)
    row_q = jnp.sum(qk_gain[0:8, :], axis=0, keepdims=True)
    row_k = jnp.sum(qk_gain[8:16, :], axis=0, keepdims=True)
    for s in range(at.n_shard):
        piece = pl.ds(s * d_slice, d_slice)
        lanes = slice(s * d_slice, (s + 1) * d_slice)
        sm[s, 0:1, :] = row_one[:, lanes]
        sm[s, 1:2, :] = row_two[:, lanes]
        sm[s, 2:3, pl.ds(0, HEAD_DIM)] = row_q
        sm[s, 3:4, pl.ds(0, HEAD_DIM)] = row_k
        sm[s, 8:, :] = g_router[0 : sm.shape[1] - 8, piece]
    small_z = [net.push(sm.at[z ^ t], sm_z.at[t - 1], at.z_dev(t)) for t in range(1, at.n_shard)]
    turn_own.wait()
    arrive(turns)
    for s in range(at.n_shard):
        share_qkv[:, pl.ds(s * hd, hd)] = turn_in[s, :, pl.ds(0, hd)]
    for m in range(KV_HEADS):
        some = [s for s in range(at.n_shard) if (s * n_heads) // (HEADS // KV_HEADS) == m]
        for first, to in ((hd, HEADS + m), (hd + HEAD_DIM, HEADS + KV_HEADS + m)):
            value = turn_in[some[0], :, pl.ds(first, HEAD_DIM)].astype(f32)
            for s in some[1:]:
                value += turn_in[s, :, pl.ds(first, HEAD_DIM)].astype(f32)
            share_qkv[:, pl.ds(to * HEAD_DIM, HEAD_DIM)] = value.astype(bf16)
    keep = net.copy(share_qkv, g_qkv.at[e])
    keep.wait()
    if at.chips == 4:
        go_on = spread_near(net, at, g_qkv)
    else:
        qkvs = [lambda who: g_qkv.at[who]]
        state = spread(net, at, qkvs)
        go_on = functools.partial(pass_on, net, at, qkvs, state)
    last = pass_on(net, at, atts, att_state)
    arrive(small_z)
    value = sm[z]
    for t in range(1, at.n_shard):
        value += sm_z[t - 1]
    sm[z] = value
    c = net.push(sm.at[z], sm_core, at.mate())
    c.wait_recv()
    sm_core[...] = sm[z] + sm_core[...]
    smalls = [net.push(sm_core, sm_chip.at[t - 1], at.chip_dev(t)) for t in range(1, at.chips)]
    last += go_on()
    arrive(smalls)
    value = sm_core[...]
    for t in range(1, at.chips):
        value += sm_chip[t - 1]
    small_sum[...] = value
    arrive(last + got)
    net.sent()


def shards(
    hidden_in,
    segments,
    routes,
    norm_gains,
    qk_gains,
    w_qkv,
    w_attn_out,
    w_router,
    w_gate_up,
    w_down,
    cotangent,
):
    n_expert = lax.axis_size("expert")
    n_shard = lax.axis_size("shard")
    me_e = lax.axis_index("expert")
    me_z = lax.axis_index("shard")
    tok, width = hidden_in.shape
    exp_dev = w_gate_up.shape[1]
    experts_all = w_router.shape[2]
    d_slice, ff2 = w_gate_up.shape[2:]
    ff = ff2 // 2
    group = n_shard // exp_dev
    mine = me_z // group
    length = n_shard * tok
    h_dev = HEADS // n_shard
    hd = h_dev * HEAD_DIM
    cols = hd + 2 * HEAD_DIM
    qkv_cols = w_qkv.shape[2]
    rows_e = d_slice // n_expert
    share = hd // n_expert
    chips = n_expert // 2
    qk_part = HEAD_DIM // n_shard
    dims = (n_expert, n_shard, group)
    n_small = 16 + experts_all
    sds = jax.ShapeDtypeStruct
    vm = pltpu.VMEM
    any_spec = pl.BlockSpec(memory_space=pl.ANY)
    vmem_spec = pl.BlockSpec(memory_space=pltpu.VMEM)

    small = jnp.zeros((16, d_slice), bf16)
    small = small.at[0:2, :].set(norm_gains[0])
    small = lax.dynamic_update_slice(small, qk_gains[0], (2, me_z * qk_part))
    small = small.at[4, :tok].set(segments.astype(bf16))
    small = jnp.concatenate([small, w_router[0].T], axis=0)
    seg_own = jnp.broadcast_to(segments.astype(f32)[:, None], (tok, 128))
    ids = jnp.arange(128, dtype=jnp.int32)
    mask = jnp.sum((routes[:, :, None] == ids[None, None, :]).astype(f32), axis=1).astype(bf16)
    cos, sin = rotary_tables(length)

    outs = [
        sds((n_shard, n_small, d_slice), bf16),
        sds((length, 128), f32),
        sds((n_shard, n_expert, rows_e, cols), bf16),
        sds((length, width), bf16),
        sds((length, cols), f32),
        sds((length, hd), bf16),
        sds((length, HEAD_DIM), bf16),
        sds((length, HEAD_DIM), bf16),
        sds((length, hd), bf16),
        sds((tok, width), f32),
        sds((tok, width), bf16),
        sds((n_shard, d_slice, ff2), bf16),
        sds((n_expert, 2 * tok, width), bf16),
        sds((n_expert, 2 * tok, 128), bf16),
        sds((2 * tok, width), bf16),
    ]
    front = comm_call(
        functools.partial(front_kernel, dims),
        0,
        160,
        40,
        [
            vm((length, width), bf16),
            vm((n_shard, n_small, d_slice), bf16),
            vm((length, 128), f32),
            vm((n_shard, n_expert, rows_e, cols), bf16),
            vm((length, width), bf16),
            vm((length, cols), f32),
            vm((length, hd), bf16),
            vm((length, HEAD_DIM), bf16),
            vm((length, HEAD_DIM), bf16),
            vm((length, hd), bf16),
            vm((hd, width), bf16),
            vm((length, width), bf16),
            vm((n_shard - 1, tok, width), bf16),
            vm((length, HEAD_DIM), f32),
            vm((length, HEAD_DIM), f32),
            vm((8, width), f32),
            vm((8, length), f32),
            vm((tok, width), f32),
            vm((tok, width), bf16),
        ],
        outs,
        56,
    )
    (small_all, seg_col, heads, a, raw, q, k, v, o, x1, b, gate_up, cot_all, mask_all, b_pair) = front(
        hidden_in, small, seg_own, w_qkv[0], w_attn_out[0], w_gate_up[0], cotangent, mask, cos, sin
    )
    gains = jnp.zeros((8, width), f32)
    gains = gains.at[0:2].set(small_all[:, 0:2].astype(f32).transpose(1, 0, 2).reshape(2, width))
    router_t = small_all[:, 16:].transpose(1, 0, 2).reshape(experts_all, width)

    def route_weights(rows, chosen):
        logits = mm_nt(rows, router_t)
        masked = jnp.where(chosen, logits, neg_fill)
        raised = jnp.where(chosen, jnp.exp(masked - jnp.max(masked, axis=1, keepdims=True)), 0.0)
        return raised / jnp.sum(raised, axis=1, keepdims=True)

    rw = route_weights(b, mask[:, :experts_all] > 0)
    rw = jnp.concatenate([rw, jnp.zeros((tok, 128 - experts_all), f32)], axis=1)
    router_pad = jnp.concatenate([router_t, jnp.zeros((128 - experts_all, width), bf16)], axis=0)
    per_e = (n_expert, 2 * tok)
    piece = (chips, 2 * tok)
    four = 4 * tok
    if chips <= 4:
        out_part, grad_gate_up, grad_down, db_in, ex_in, land_gu, land_dn = comm_call(
            functools.partial(expert_kernel, dims),
            4,
            60,
            60,
            [
                vm((width, ff2), bf16),
                vm((ff, width), bf16),
                vm((chips, 2, 2 * tok, width), bf16),
                vm((2, 2 * tok, width), bf16),
                vm((chips, 2, 2 * tok, 128), bf16),
                vm((chips, four, ff), bf16),
                vm((chips, four, ff2), bf16),
                vm((chips, four, width), bf16),
                vm((2, 2 * tok, width), bf16),
                vm((2, 2 * tok, 128), bf16),
                vm(piece + (width,), bf16),
                vm(piece + (128,), bf16),
                vm(piece + (width,), bf16),
                vm(piece + (128,), bf16),
                vm((chips, four, 128), f32),
                vm((four, 128), f32),
                vm((2, tiled(width, 256), ff2), bf16),
                vm((2, tiled(ff, 256), width), bf16),
                pltpu.SemaphoreType.DMA((2,)),
            ],
            [
                sds(per_e + (width,), bf16),
                sds((n_shard, d_slice, ff2), bf16),
                sds((ff, width), bf16),
                sds(piece + (width,), bf16),
                sds(piece + (128,), bf16),
                sds((group - 1, d_slice // 2, ff2), bf16),
                sds((group - 1, ff, d_slice), bf16),
            ],
            60,
            in_specs=[any_spec] * 6 + [vmem_spec],
        )(b_pair, cot_all, mask_all, gate_up, w_gate_up[0], w_down[0], router_pad)
    else:
        rows_all = n_expert * 2 * tok
        w_mine = lax.dynamic_index_in_dim(w_gate_up[0], mine, 0, keepdims=False)
        gate_up = lax.dynamic_update_index_in_dim(gate_up, w_mine, me_z, 0)
        down = lax.all_gather(w_down[0], "shard", axis=2, tiled=True)
        down = lax.dynamic_index_in_dim(down, mine, 0, keepdims=False)
        b_rows = lax.all_gather(b_pair, "expert", axis=0, tiled=True)
        my_expert = me_e * exp_dev + mine
        rw_all = route_weights(b_rows, mask_all.reshape(rows_all, 128)[:, :experts_all] > 0)
        is_mine = ids[:experts_all] == my_expert
        rw_mine = jnp.sum(jnp.where(is_mine[None, :], rw_all, 0.0), axis=1, keepdims=True)
        w_gu = gate_up.reshape(width, ff2)
        pre = mm(b_rows, w_gu)
        g, u = pre[:, :ff], pre[:, ff:]
        sig = jax.nn.sigmoid(g)
        act = g * sig
        hidden = (act * u).astype(bf16)
        y_f = mm(hidden, down).astype(bf16).astype(f32)
        cot_f = cot_all.reshape(rows_all, width).astype(f32)
        d_route = jnp.sum(cot_f * y_f, axis=1, keepdims=True)
        out_part = (rw_mine * y_f).astype(bf16)
        d_y = (rw_mine * cot_f).astype(bf16)
        d_hidden = mm_nt(d_y, down)
        d_pre = jnp.concatenate(
            [d_hidden * u * sig * (1.0 + g * (1.0 - sig)), d_hidden * act], axis=1
        ).astype(bf16)
        d_b = mm_nt(d_pre, w_gu).astype(bf16)
        grad_down = mm_tn(hidden, d_y).astype(bf16)
        grad_gate_up = mm_tn(b_rows, d_pre).astype(bf16).reshape(n_shard, d_slice, ff2)
        high = lax.reduce_precision(d_route, 8, 7)
        low = d_route - high
        extra = jnp.where(ids[None] == my_expert, high, jnp.where(ids[None] == my_expert + 64, low, 0.0)).astype(bf16)

        def home(value):
            return lax.psum_scatter(value, "expert", scatter_dimension=0, tiled=True)[None]

        db_in, ex_in = home(d_b), home(extra)

    n_parts = db_in.shape[0]
    early = chips <= 4
    gx1, d_o, gain_two, g_router, norm_gu, late_gu, norm_dn, out_sum = comm_call(
        functools.partial(norm_kernel, dims, early),
        1,
        60,
        24,
        [
            vm((n_parts, 2 * tok, width), bf16),
            vm((n_parts, 2 * tok, 128), bf16),
            vm((tok, width), bf16),
            vm((tok, 128), bf16),
            vm((tok, width), bf16),
            vm((tok, 128), bf16),
            vm((2, tok, 128), bf16),
            vm((tok, width), bf16),
            vm(piece + (width,), bf16),
            vm(piece + (width,), bf16),
            vm((chips - 1, 2 * tok, width), bf16),
        ],
        [
            sds((tok, width), f32),
            sds((length, width), bf16),
            sds((8, width), f32),
            sds((128, width), f32),
            sds((group - 1, d_slice // 2, ff2), bf16) if not early else sds((16, 128), bf16),
            sds((group - 1, d_slice // 2, ff2), bf16),
            sds((group - 1, ff, d_slice), bf16) if not early else sds((16, 128), bf16),
            sds((2 * tok, width), bf16),
        ],
        60,
        in_specs=[any_spec] * 5 + [vmem_spec] * 6,
        out_specs=[vmem_spec, any_spec, vmem_spec, vmem_spec] + [any_spec] * 3 + [vmem_spec],
    )(db_in, ex_in, grad_gate_up, grad_down, out_part.reshape(per_e + (width,)), x1, b, cotangent, rw, router_pad, gains)
    if not early:
        land_gu, land_dn = norm_gu, norm_dn

    small_rows = (8 + -(-experts_all // 8) * 8, d_slice)
    hidden_out, grad_hidden, sums, grad_out, grad_qkv, two_gu, own_gu, two_dn, own_dn = comm_call(
        functools.partial(back_kernel, dims),
        2,
        140,
        60,
        [
            vm((length, width), bf16),
            vm((hd, width), bf16),
            vm((length, hd), bf16),
            vm((length, hd), bf16),
            vm((length, HEAD_DIM), bf16),
            vm((length, HEAD_DIM), bf16),
            vm((length, cols), f32),
            vm((length, HEAD_DIM), f32),
            vm((length, HEAD_DIM), f32),
            vm((length, 128), f32),
            vm((8, length), f32),
            vm((length, hd), bf16),
            vm((length, cols), bf16),
            vm((length, HEAD_DIM), f32),
            vm((length, HEAD_DIM), f32),
            vm((16, HEAD_DIM), f32),
            vm((length, width), bf16),
            vm((n_shard, n_expert, rows_e, cols), bf16),
            vm((2, d_slice // 2, ff2), bf16),
            vm((2, group - 1, d_slice // 2, ff2), bf16),
            vm((ff, d_slice), bf16),
            vm((group - 1, ff, d_slice), bf16),
            vm((tok, width), bf16),
            vm((n_expert, share, width), bf16),
            vm((chips, share, width), bf16),
            vm((chips - 1, share, width), bf16),
            vm((share, width), bf16),
            vm((n_shard - 1, tok, width), bf16),
            vm((n_expert, n_shard, rows_e, cols), bf16),
            vm((chips, n_shard, rows_e, cols), bf16),
            vm((chips - 1, n_shard, rows_e, cols), bf16),
            vm((n_shard, rows_e, cols), bf16),
            vm((n_shard, rows_e, cols), bf16),
            vm((rows_e, qkv_cols), bf16),
            vm((n_shard,) + small_rows, f32),
            vm((n_shard - 1,) + small_rows, f32),
            vm(small_rows, f32),
            vm((chips - 1,) + small_rows, f32),
        ],
        [
            sds((tok, width), bf16),
            sds((tok, width), f32),
            sds(small_rows, f32),
            sds((n_expert, share, width), bf16),
            sds((n_expert, rows_e, qkv_cols), bf16),
            sds((d_slice, ff2), bf16),
            sds((group - 1, d_slice, ff2), bf16),
            sds((ff, d_slice), bf16),
            sds((group - 1, ff, d_slice), bf16),
        ],
        60,
        in_specs=[any_spec] * 18 + [vmem_spec] * 8,
        out_specs=[vmem_spec] * 3 + [any_spec] * 6,
    )(
        d_o,
        w_attn_out[0],
        o,
        q,
        k,
        v,
        raw,
        cos,
        sin,
        seg_col,
        a,
        heads,
        grad_gate_up,
        grad_down,
        land_gu,
        late_gu,
        land_dn,
        out_sum,
        out_sum[:tok],
        small_all,
        x1,
        gx1,
        hidden_in,
        gains,
        gain_two,
        g_router,
    )

    def settle(own, others, other):
        total = own.astype(f32) + jnp.sum(others.astype(f32), axis=0)
        other = other.astype(f32)
        return jnp.stack([jnp.where(mine == 0, total, other), jnp.where(mine == 0, other, total)])[None]

    own_gate_up = lax.dynamic_index_in_dim(grad_gate_up, me_z, 0, keepdims=False)
    own_down = lax.dynamic_slice_in_dim(grad_down, me_z * d_slice, d_slice, 1)
    qk_grad = lax.dynamic_slice_in_dim(sums[2:4, :HEAD_DIM], me_z * qk_part, qk_part, 1)
    return (
        hidden_out,
        grad_hidden,
        sums[0:2][None],
        qk_grad[None],
        grad_qkv.reshape(d_slice, qkv_cols).astype(f32)[None],
        grad_out.reshape(hd, width).astype(f32)[None],
        sums[8 : 8 + experts_all].T[None],
        settle(own_gate_up, own_gu, two_gu),
        settle(own_down, own_dn, two_dn),
    )


def solution(mesh):
    in_specs = (
        P(("expert", "shard"), None),
        P(("expert", "shard")),
        P(("expert", "shard"), None),
        P(None, None, "shard"),
        P(None, None, "shard"),
        P(None, "shard", None),
        P(None, "shard", None),
        P(None, "shard", None),
        P(None, "expert", "shard", None),
        P(None, "expert", None, "shard"),
        P(("expert", "shard"), None),
    )
    out_specs = (
        P(("expert", "shard"), None),
        P(("expert", "shard"), None),
        P(None, None, "shard"),
        P(None, None, "shard"),
        P(None, "shard", None),
        P(None, "shard", None),
        P(None, "shard", None),
        P(None, "expert", "shard", None),
        P(None, "expert", None, "shard"),
    )
    return jax.shard_map(shards, mesh=mesh, in_specs=in_specs, out_specs=out_specs, check_vma=False)
```

```python
import functools

import jax
import jax.numpy as jnp
import numpy as np
from jax import lax
from jax.experimental import pallas as pl
from jax.experimental.pallas import tpu as pltpu
from jax.sharding import PartitionSpec as P

HEADS = 32
KV_HEADS = 4
HEAD_DIM = 128
TOP = 8

bf16 = jnp.bfloat16
f32 = jnp.float32
highest = lax.Precision.HIGHEST
eps_norm = 1e-06
rope_base = 1000000.0
neg_fill = -1e30


def dot(left, right, dims, out=f32):
    return lax.dot_general(left, right, (dims, ((), ())), preferred_element_type=out)


def mm(left, right):
    return dot(left, right, ((1,), (0,)))


def mm_nt(left, right):
    return dot(left, right, ((1,), (1,)))


def mm_tn(left, right):
    return dot(left, right, ((0,), (0,)))


def inv_rms(value):
    return lax.rsqrt(jnp.mean(value * value, axis=-1, keepdims=True) + eps_norm)


def rms_back(value, gain, grad):
    r = inv_rms(value)
    c = grad * gain
    back = r * c - value * (r * r * r) * jnp.mean(c * value, axis=-1, keepdims=True)
    return back, grad * value * r


def rotary_tables(length):
    half = HEAD_DIM // 2
    frequency = np.float32(rope_base) ** (-(np.arange(half, dtype=np.float32) * np.float32(2.0)) / np.float32(HEAD_DIM))
    angles = np.arange(length, dtype=np.float32)[:, None] * frequency[None, :].astype(np.float32)
    cos, sin = np.cos(angles), np.sin(angles)
    return jnp.asarray(np.concatenate([cos, cos], axis=1)), jnp.asarray(np.concatenate([-sin, sin], axis=1))


MESH = pl.DeviceIdType.MESH


class Place:
    def __init__(self, n_expert, n_shard, group):
        self.e = lax.axis_index("expert")
        self.z = lax.axis_index("shard")
        self.n_expert, self.n_shard, self.group = n_expert, n_shard, group
        self.chip, self.core = self.e // 2, self.e % 2
        self.chips = n_expert // 2

    def z_dev(self, t):
        return (self.e, self.z ^ t)

    def slot(self, t, other=0):
        return (self.chip ^ t) * 2 + (self.core ^ other)

    def chip_dev(self, t):
        return (self.slot(t), self.z)

    def mate(self):
        return (self.e ^ 1, self.z)


class Net:
    def __init__(self, send, recv, local):
        self.send, self.recv, self.local = send, recv, local
        self.n, self.m, self.open = 0, 0, []

    def push(self, src, dst, dev):
        i = self.n
        self.n += 1
        copy = pltpu.make_async_remote_copy(
            src_ref=src, dst_ref=dst, send_sem=self.send.at[i], recv_sem=self.recv.at[i],
            device_id=dev, device_id_type=MESH,
        )
        copy.start()
        self.open.append(copy)
        return copy

    def copy(self, src, dst):
        i = self.m
        self.m += 1
        copy = pltpu.make_async_copy(src, dst, self.local.at[i])
        copy.start()
        return copy

    def done(self, copy):
        copy.wait_send()
        self.open = [c for c in self.open if c is not copy]

    def sent(self):
        for copy in self.open:
            copy.wait_send()
        self.open = []


def greet(devices):
    barrier = pltpu.get_barrier_semaphore()
    for dev in devices:
        pl.semaphore_signal(barrier, inc=1, device_id=dev, device_id_type=MESH)
    pl.semaphore_wait(barrier, len(devices))


def everyone(at):
    return (
        [at.z_dev(t) for t in range(1, at.n_shard)]
        + [at.chip_dev(t) for t in range(1, at.chips)]
        + [at.mate()]
    )


def arrive(copies):
    for copy in copies:
        copy.wait_recv()


def spread(net, at, pieces):
    own = [p(at.e) for p in pieces]
    mate = [net.push(o, o, at.mate()) for o in own]
    out = [(t, [net.push(o, o, at.chip_dev(t)) for o in own]) for t in range(1, at.chips)]
    return mate, out


def pass_on(net, at, pieces, state):
    mate, out = state
    for t, copies in out:
        for p, copy in zip(pieces, copies):
            copy.wait_recv()
            got = p(at.slot(t))
            mate.append(net.push(got, got, at.mate()))
    return mate


def low_bit(k):
    return k & -k


class Gather:
    def __init__(self, net, at, own, ref, rows):
        self.net, self.at, self.ref, self.rows = net, at, ref, rows
        bits = [b for b in (1 << i for i in range(10)) if b < at.n_shard]
        self.bits = bits[::-1]
        here = self.place(0)
        self.copies = {b: net.push(own, here, at.z_dev(b)) for b in self.bits}

    def place(self, k):
        return self.ref.at[span(self.at.z ^ k, self.rows)]

    def finish(self, then=None):
        waiting = list(self.bits)
        while waiting:
            k = waiting.pop(0)
            self.copies[k].wait_recv()
            for b in self.bits:
                if b < low_bit(k):
                    got = self.place(k)
                    self.copies[k | b] = self.net.push(got, got, self.at.z_dev(b))
                    waiting.append(k | b)
            if then:
                then()
                then = None


class Scatter:
    def __init__(self, net, at, part, landing, rows, step):
        self.net, self.at, self.part, self.landing, self.rows, self.step = net, at, part, landing, rows, step
        self.slot, self.bit, self.last = 0, 1, []
        self.start()

    def block(self, k):
        return self.part.at[span(self.at.z ^ k, self.rows)]

    def start(self):
        bit, self.copies = self.bit, []
        for k in [k for k in range(self.at.n_shard - 1, 0, -1) if k % (2 * bit) == bit]:
            copy = self.net.push(self.block(k), self.landing.at[self.slot], self.at.z_dev(bit))
            self.copies.append((k ^ bit, self.slot, copy))
            self.slot += 1

    def advance(self):
        self.bit *= 2
        for to, i, copy in self.copies:
            copy.wait_recv()
            if not to:
                self.last.append(i)
                continue

            def add(j, _, to=to, i=i):
                r = span(j, self.step)
                here = pl.ds(pl.multiple_of((self.at.z ^ to) * self.rows + j * self.step, self.step), self.step)
                value = self.part[here, :].astype(f32) + self.landing[i, r, :].astype(f32)
                self.part[here, :] = value.astype(bf16)
                return 0

            lax.fori_loop(0, self.rows // self.step, add, 0)
        if self.bit < self.at.n_shard:
            self.start()
            return True
        return False

    def finish(self):
        while self.advance():
            pass
        return self.last


def spread_near(net, at, ref):
    own = ref.at[at.e]
    mate = [net.push(own, own, at.mate())]
    out = {t: net.push(own, own, at.chip_dev(t)) for t in (1, 2)}
    half = ref.shape[1] // 2

    def go_on():
        relayed = []
        for t in (1, 2):
            out[t].wait_recv()
            got = ref.at[at.slot(t)]
            mate.append(net.push(got, got, at.mate()))
            part = ref.at[at.slot(t), pl.ds((2 - t) * half, half)]
            relayed.append(net.push(part, part, at.chip_dev(3 - t)))
        arrive(relayed)
        got = ref.at[at.slot(3)]
        mate.append(net.push(got, got, at.mate()))
        return mate

    return go_on


def comm_call(kernel, cid, n_remote, n_local, scratch, outs, vmem_mb, in_specs=None, out_specs=None, cost=None):
    any_spec = pl.BlockSpec(memory_space=pl.ANY)

    def call(*args):
        return pl.pallas_call(
            kernel,
            out_shape=outs,
            in_specs=in_specs or [any_spec] * len(args),
            out_specs=out_specs or [any_spec] * len(outs),
            scratch_shapes=list(scratch)
            + [
                pltpu.SemaphoreType.DMA((n_remote,)),
                pltpu.SemaphoreType.DMA((n_remote,)),
                pltpu.SemaphoreType.DMA((n_local,)),
            ],
            compiler_params=pltpu.CompilerParams(
                collective_id=cid, has_side_effects=True, vmem_limit_bytes=vmem_mb << 20
            ),
            cost_estimate=cost,
        )(*args)

    return call


def tiled(size, most):
    while size % most:
        most //= 2
    return most


def halves(at):
    return list(range(1, at.chips)) + [0]


def rope_rows(value, cos, sin):
    return value * cos + pltpu.roll(value, HEAD_DIM // 2, 1) * sin


def rope_rows_back(grad, cos, sin):
    return grad * cos + pltpu.roll(grad * sin, HEAD_DIM // 2, 1)


def eight(per):
    return jnp.sum(per.reshape(per.shape[0] // 8, 8, per.shape[1]), axis=0)


def span(i, size):
    if isinstance(i, int):
        return pl.ds(i * size, size)
    return pl.ds(pl.multiple_of(i * size, size), size)


def soft_block(q_ref, k_ref, seg_row, seg_col, h, i, block, scale):
    rows, keys = pl.ds(i * block, block), pl.ds(0, (i + 1) * block)
    scores = mm_nt(q_ref[rows, span(h, HEAD_DIM)], k_ref[keys, :]) * scale
    width = (i + 1) * block
    at_q = i * block + lax.broadcasted_iota(jnp.int32, (block, width), 0)
    at_k = lax.broadcasted_iota(jnp.int32, (block, width), 1)
    allowed = (at_k <= at_q) & (seg_row[0:1, keys] == seg_col[rows, 0:1])
    scores = jnp.where(allowed, scores, neg_fill)
    raised = jnp.exp(scores - jnp.max(scores, axis=-1, keepdims=True))
    return raised / jnp.sum(raised, axis=-1, keepdims=True)


def front_kernel(
    dims, x, small, seg_own, w_qkv, w_out, w_gu, cot, mask, cos_h, sin_h,
    small_out, seg_out, heads_out, a_out, raw_out, q_out, k_out, v_out, o_out, x1_out, b_out,
    gate_up, cot_all, mask_all, b_pair, gains, router_pad,
    x_all, small_all, seg_col, heads, a, raw, q, k, v, o, w_o, part, parts_in, cos, sin, seg_row, x1, b_own,
    send, recv, local,
):
    at = Place(*dims)
    net = Net(send, recv, local)
    z, e, group = at.z, at.e, at.group
    tok = x.shape[0]
    length, width = x_all.shape
    mine = z // group
    rows_e, cols = heads.shape[2], heads.shape[3]
    hd = cols - 2 * HEAD_DIM
    n_heads = hd // HEAD_DIM
    q_width = HEADS * HEAD_DIM
    d_slice = w_gu.shape[1]
    scale = HEAD_DIM ** (-0.5)
    block = tok

    def heads_of(dest):
        kv = (dest * n_heads) // (HEADS // KV_HEADS)
        rows = span(e, rows_e)
        return [
            (w_qkv.at[rows, span(dest, hd)], heads.at[z, e, :, pl.ds(0, hd)]),
            (w_qkv.at[rows, span(HEADS + kv, HEAD_DIM)], heads.at[z, e, :, pl.ds(hd, HEAD_DIM)]),
            (w_qkv.at[rows, span(HEADS + KV_HEADS + kv, HEAD_DIM)], heads.at[z, e, :, pl.ds(hd + HEAD_DIM, HEAD_DIM)]),
        ]

    half0, half1 = pl.ds(0, tok), pl.ds(tok, tok)
    first = [
        net.copy(x, x_all.at[span(z, tok)]),
        net.copy(small, small_all.at[z]),
        net.copy(seg_own, seg_col.at[span(z, tok)]),
        net.copy(cos_h, cos),
        net.copy(sin_h, sin),
    ]
    local_heads = [net.copy(s, d) for s, d in heads_of(z)]
    local_cot = [net.copy(cot, cot_all.at[e, half0]), net.copy(mask, mask_all.at[e, half0])]
    load_out = net.copy(w_out, w_o)
    greet(everyone(at))
    got_heads = [net.push(s, d, at.z_dev(t)) for t in range(1, at.n_shard) for s, d in heads_of(z ^ t)]
    got_x = []
    for t in range(1, at.n_shard):
        got_x.append(net.push(small, small_all.at[z], at.z_dev(t)))
        got_x.append(net.push(seg_own, seg_col.at[span(z, tok)], at.z_dev(t)))
    gather_x = Gather(net, at, x, x_all, tok)
    for c in local_heads:
        c.wait()
    arrive(got_heads)
    pieces = [lambda who: heads.at[:, who]]
    heads_state = spread(net, at, pieces)
    other = (z ^ group) // group
    cut = d_slice // 2
    low, high = pl.ds(0, cut), pl.ds(cut, cut)
    pieces_w = [
        (w_gu.at[other, low], gate_up.at[z, low], gate_up.at[z ^ group, low]),
        (w_gu.at[other, high], gate_up.at[z, high], gate_up.at[z ^ group, high]),
    ]
    from_partner = {}

    def fetch_piece(i):
        src, dst, got = pieces_w[i]
        from_partner[i] = (net.push(src, dst, at.z_dev(group)), got)

    for c in first:
        c.wait()
    gather_x.finish(lambda: fetch_piece(0))
    arrive(got_x)

    def hand_on(i):
        copy, ref = from_partner[i]
        copy.wait_recv()
        for t in range(1, group):
            got_w.append(net.push(ref, ref, at.z_dev(t)))

    got_w = []
    for t in range(1, group):
        got_w.append(net.push(w_gu.at[mine], gate_up.at[z], at.z_dev(t)))
    got_cot = [
        net.push(cot, cot_all.at[e, half1], at.z_dev(group)),
        net.push(mask, mask_all.at[e, half1], at.z_dev(group)),
    ]

    gains[...] = jnp.zeros_like(gains)
    router_pad[...] = jnp.zeros_like(router_pad)
    qk = []
    for s in range(at.n_shard):
        rows = small_all[s, 0:16, :].astype(f32)
        gains[0:2, span(s, d_slice)] = rows[0:2]
        router_pad[0 : small.shape[0] - 16, span(s, d_slice)] = small_all[s, 16:, :]
        seg_row[0:1, span(s, tok)] = rows[4:5, :tok]
        qk.append(rows[2:4, :HEAD_DIM])
    qk = sum(qk[1:], qk[0])
    step = 16

    def norm_rows(i, _):
        rows = span(i, step)
        value = x_all[rows, :].astype(f32)
        a[rows, :] = (value * inv_rms(value) * gains[0:1, :]).astype(bf16)
        return 0

    lax.fori_loop(0, length // step, norm_rows, 0)
    fetch_piece(1)
    last = pass_on(net, at, pieces, heads_state)
    arrive(last)
    keep = [net.copy(heads, heads_out), net.copy(a, a_out), net.copy(small_all, small_out), net.copy(seg_col, seg_out)]

    wide = tiled(cols, 256)

    def project(i, _):
        tile = span(i, wide)
        raw[:, tile] = mm(a[...], heads[:, :, :, tile].reshape(width, wide))
        return 0

    lax.fori_loop(0, cols // wide, project, 0)
    keep.append(net.copy(raw, raw_out))

    def head_rows(i, _):
        rows = span(i, block)
        cos_b, sin_b = cos[rows, :], sin[rows, :]
        for h in range(n_heads + 1):
            value = raw[rows, pl.ds(h * HEAD_DIM, HEAD_DIM)]
            gain = qk[0:1] if h < n_heads else qk[1:2]
            value = rope_rows(value * inv_rms(value) * gain, cos_b, sin_b).astype(bf16)
            if h < n_heads:
                q[rows, pl.ds(h * HEAD_DIM, HEAD_DIM)] = value
            else:
                k[rows, :] = value
        v[rows, :] = raw[rows, pl.ds(hd + HEAD_DIM, HEAD_DIM)].astype(bf16)
        return 0

    lax.fori_loop(0, length // block, head_rows, 0)
    keep += [net.copy(q, q_out), net.copy(k, k_out), net.copy(v, v_out)]
    for c in local_cot:
        c.wait()
    arrive(got_cot)
    cots = [lambda who: cot_all.at[who], lambda who: mask_all.at[who]]
    cot_state = spread(net, at, cots)


    def one_head(h, _):
        for i in range(length // block):
            soft = soft_block(q, k, seg_row, seg_col, h, i, block, scale).astype(bf16)
            mixed = mm(soft, v[pl.ds(0, (i + 1) * block), :])
            o[pl.ds(i * block, block), span(h, HEAD_DIM)] = mixed.astype(bf16)
        return 0

    lax.fori_loop(0, n_heads, one_head, 0)
    hand_on(0)
    keep.append(net.copy(o, o_out))
    load_out.wait()
    wide_o = tiled(width, 256)

    def out_tile(i, _):
        tile = span(i, wide_o)
        part[:, tile] = mm(o[...], w_o[:, tile]).astype(bf16)
        return 0

    lax.fori_loop(0, width // wide_o, out_tile, 0)
    summing = Scatter(net, at, part, parts_in, tok, step)
    more = summing.advance()
    hand_on(1)
    slots = summing.finish() if more else summing.last

    def middle_rows(i, _):
        rows = span(i, step)
        total = part[pl.ds(pl.multiple_of(z * tok + i * step, step), step), :].astype(f32)
        for t in slots:
            total += parts_in[t, rows, :].astype(f32)
        value = x_all[pl.ds(pl.multiple_of(z * tok + i * step, step), step), :].astype(f32) + total
        x1[rows, :] = value
        b_own[rows, :] = (value * inv_rms(value) * gains[1:2, :]).astype(bf16)
        return 0

    lax.fori_loop(0, tok // step, middle_rows, 0)
    swap = net.push(b_own, b_pair.at[half1], at.z_dev(group))
    keep += [net.copy(b_own, b_pair.at[half0]), net.copy(x1, x1_out), net.copy(b_own, b_out)]
    last = pass_on(net, at, cots, cot_state)
    swap.wait_recv()
    arrive(last + got_w)
    for c in keep:
        c.wait()
    net.sent()


def expert_kernel(
    dims, b_pair, cot_all, mask_all, gate_up, w_gu_in, w_dn_in, router_t,
    out_part, ggu, gdn, db_in, ex_in, land_dn,
    w_gu, w_dn, rows, cot_t, mask_t, hid, d_pre, d_y, stage, stage_x, own, own_x, core_in, core_x, w_r, d_r, g_tile, d_tile,
    tile_sem, send, recv, local,
):
    at = Place(*dims)
    net = Net(send, recv, local)
    z, e, group = at.z, at.e, at.group
    n_slices, d_slice, ff2 = gate_up.shape
    ff, width = w_dn.shape
    two = b_pair.shape[0]
    four = 2 * two
    mine, other = z // group, (z ^ group) // group
    expert = e * (at.n_shard // group) + mine
    step = 16
    fine = tiled(ff, 256)
    wide = tiled(width, 1024)
    far = z ^ group

    def d_cols(who):
        return w_dn.at[:, span(who, d_slice)]

    pair = net.copy(b_pair, rows.at[0, 1])
    masks = []
    for t in range(at.chips):
        masks.append(net.copy(mask_all.at[at.slot(t, 1)], mask_t.at[t, 0]))
        masks.append(net.copy(mask_all.at[at.slot(t)], mask_t.at[t, 1]))
    loads = [net.copy(w_gu_in.at[mine], w_gu.at[span(z, d_slice)])]
    for k in range(1, n_slices):
        loads.append(net.copy(gate_up.at[z ^ k], w_gu.at[span(z ^ k, d_slice)]))
    load_dn = net.copy(w_dn_in.at[mine], d_cols(z))

    def fetch(t):
        return [
            net.copy(cot_all.at[at.slot(t, 1)], cot_t.at[0]),
            net.copy(cot_all.at[at.slot(t)], cot_t.at[1]),
        ]

    order = list(range(1, at.chips)) + [0]
    fetched = {order[0]: fetch(order[0])}
    greet(
        [at.chip_dev(t) for t in range(1, at.chips)] + [at.mate()] + [at.z_dev(t) for t in range(1, group + 1)]
    )
    from_mate = {0: net.push(b_pair, rows.at[0, 0], at.mate())}
    near = [t for t in (1, 2) if t < at.chips]
    beyond = [t for t in range(1, at.chips) if t not in near]
    from_chip = {t: net.push(b_pair, rows.at[t, 1], at.chip_dev(t)) for t in near}
    half_ff = [pl.ds(0, ff // 2), pl.ds(ff // 2, ff // 2)]

    def dn_part(who, i):
        return w_dn.at[half_ff[i], span(who, d_slice)]

    def fetch_dn(i):
        return net.push(w_dn_in.at[other, half_ff[i]], dn_part(z, i), at.z_dev(group))

    from_partner = [fetch_dn(0)]

    def hand_on(i):
        from_partner[i].wait_recv()
        for t in range(1, group):
            got_dn.append(net.push(dn_part(far, i), dn_part(far, i), at.z_dev(t)))

    got_dn = [net.push(w_dn_in.at[mine], d_cols(z), at.z_dev(t)) for t in range(1, group)]

    relayed = []

    def pass_rows(t):
        if t in from_chip:
            from_chip[t].wait_recv()
        else:
            arrive(relayed)
        from_mate[t] = net.push(rows.at[t, 1], rows.at[t, 0], at.mate())

    lanes = lax.broadcasted_iota(jnp.int32, (four, 128), 1)

    def up_rows(t):
        logits = mm_nt(rows[t].reshape(four, width), router_t[...])
        chosen = mask_t[t].reshape(four, 128).astype(f32) > 0
        masked = jnp.where(chosen, logits, neg_fill)
        raised = jnp.where(chosen, jnp.exp(masked - jnp.max(masked, axis=1, keepdims=True)), 0.0)
        weight = raised / jnp.sum(raised, axis=1, keepdims=True)
        weight = jnp.sum(jnp.where(lanes == expert, weight, 0.0), axis=1, keepdims=True)
        w_r[t] = jnp.broadcast_to(weight, (four, 128))

        def up(j, _):
            tile, tile_u = span(j, fine), pl.ds(pl.multiple_of(ff + j * fine, fine), fine)
            x = rows[t].reshape(four, width)
            g = mm(x, w_gu[:, tile])
            u = mm(x, w_gu[:, tile_u])
            d_pre[t, :, tile] = g.astype(bf16)
            d_pre[t, :, tile_u] = u.astype(bf16)
            hid[t, :, tile] = (g * jax.nn.sigmoid(g) * u).astype(bf16)
            return 0

        lax.fori_loop(0, ff // fine, up, 0)

    for c in masks:
        c.wait()
    pair.wait()
    from_mate[0].wait_recv()
    for c in loads:
        c.wait()
    up_rows(0)
    from_partner.append(fetch_dn(1))
    for i in near:
        pass_rows(i)
        if beyond:
            part = pl.ds((2 - i) * (two // 2), two // 2)
            relayed.append(net.push(rows.at[i, 1, part], rows.at[3, 1, part], at.chip_dev(3 - i)))
    hand_on(0)
    for t in near:
        from_mate[t].wait_recv()
        up_rows(t)
    hand_on(1)
    for t in beyond:
        pass_rows(t)
        from_mate[t].wait_recv()
        up_rows(t)
    load_dn.wait()
    arrive(got_dn)

    mates, outs = {}, []

    def finish(t):
        arrive(mates[t])

        def add_rows(i, _):
            r = span(i, step)
            own[t, r, :] = (own[t, r, :].astype(f32) + core_in[t, r, :].astype(f32)).astype(bf16)
            own_x[t, r, :] = (own_x[t, r, :].astype(f32) + core_x[t, r, :].astype(f32)).astype(bf16)
            return 0

        lax.fori_loop(0, two // step, add_rows, 0)
        if t:
            outs.append(net.push(own.at[t], db_in.at[t], at.chip_dev(t)))
            outs.append(net.push(own_x.at[t], ex_in.at[t], at.chip_dev(t)))

    used = {}
    for i, t in enumerate(order):
        d_r[...] = jnp.zeros_like(d_r)
        for c in fetched[t]:
            c.wait()

        def back_y(n, _, t=t):
            tile = span(n, wide)
            y = mm(hid[t], w_dn[:, tile]).astype(bf16).astype(f32)
            c = cot_t[:, :, tile].reshape(four, wide).astype(f32)
            w = w_r[t, :, 0:1]
            d_r[...] += jnp.broadcast_to(jnp.sum(c * y, axis=1, keepdims=True), (four, 128))
            d_y[t, :, tile] = (w * c).astype(bf16)
            cot_t[:, :, tile] = (w * y).astype(bf16).reshape(2, two, wide)
            return 0

        lax.fori_loop(0, width // wide, back_y, 0)
        kept = [
            net.copy(cot_t.at[0], out_part.at[at.slot(t, 1)]),
            net.copy(cot_t.at[1], out_part.at[at.slot(t)]),
        ]
        if i:
            finish(order[i - 1])

        def back_h(j, _, t=t):
            tile, tile_u = span(j, fine), pl.ds(pl.multiple_of(ff + j * fine, fine), fine)
            d_h = mm_nt(d_y[t], w_dn[tile, :])
            g, u = d_pre[t, :, tile].astype(f32), d_pre[t, :, tile_u].astype(f32)
            sig = jax.nn.sigmoid(g)
            d_pre[t, :, tile] = (d_h * u * sig * (1.0 + g * (1.0 - sig))).astype(bf16)
            d_pre[t, :, tile_u] = (d_h * g * sig).astype(bf16)
            return 0

        lax.fori_loop(0, ff // fine, back_h, 0)
        for c in kept:
            c.wait()
        if i + 1 < at.chips:
            fetched[order[i + 1]] = fetch(order[i + 1])
        p = i % 2
        for c in used.pop(p, []):
            net.done(c)

        def back_b(n, _, t=t, p=p):
            tile = span(n, wide)
            value = mm_nt(d_pre[t], w_gu[tile, :]).astype(bf16)
            stage[p, :, tile] = value[:two]
            own[t, :, tile] = value[two:]
            return 0

        lax.fori_loop(0, width // wide, back_b, 0)
        routed = d_r[...]
        high = routed.astype(bf16)
        low = (routed - high.astype(f32)).astype(bf16)
        none = jnp.zeros_like(high)
        extra = jnp.where(lanes == expert, high, jnp.where(lanes == expert + 64, low, none))
        stage_x[p] = extra[:two]
        own_x[t] = extra[two:]
        mates[t] = [
            net.push(stage.at[p], core_in.at[t], at.mate()),
            net.push(stage_x.at[p], core_x.at[t], at.mate()),
        ]
        used[p] = mates[t]
    finish(order[-1])
    keep = [net.copy(own.at[0], db_in.at[0]), net.copy(own_x.at[0], ex_in.at[0])]

    part = tiled(width, 256)
    per = d_slice // part

    def out_copy(slot, i):
        who = z ^ (n_slices - 1 - i // per)
        return pltpu.make_async_copy(g_tile.at[slot], ggu.at[who, span(i % per, part)], tile_sem.at[slot])

    def grad_up(i, _):
        slot = i % 2

        @pl.when(i >= 2)
        def _():
            out_copy(slot, i - 2).wait()

        who = z ^ (n_slices - 1 - i // per)
        x = rows[:, :, :, span(who * per + i % per, part)].reshape(at.chips * four, part)
        g_tile[slot] = mm_tn(x, d_pre[...].reshape(at.chips * four, ff2)).astype(bf16)
        out_copy(slot, i).start()
        return 0

    def down_copy(slot, i):
        return pltpu.make_async_copy(d_tile.at[slot], gdn.at[span(i, fine)], tile_sem.at[slot])

    def grad_down(i, _):
        slot = i % 2

        @pl.when(i >= 2)
        def _():
            down_copy(slot, i - 2).wait()

        h = hid[:, :, span(i, fine)].reshape(at.chips * four, fine)
        d_tile[slot] = mm_tn(h, d_y[...].reshape(at.chips * four, width)).astype(bf16)
        down_copy(slot, i).start()
        return 0

    n_down = ff // fine
    lax.fori_loop(0, n_down, grad_down, 0)
    for i in range(max(0, n_down - 2), n_down):
        down_copy(i % 2, i).wait()
    for t in range(1, group):
        outs.append(net.push(gdn.at[:, span(z ^ t ^ group, d_slice)], land_dn.at[t - 1], at.z_dev(t)))
    n_up, n_early = width // part, (group - 1) * per
    lax.fori_loop(0, n_early, grad_up, 0)
    for i in range(n_early - 2, n_early):
        out_copy(i % 2, i).wait()

    def grad_rest(i, _):
        slot = i % 2

        @pl.when(i >= n_early + 2)
        def _():
            out_copy(slot, i - 2).wait()

        who = z ^ (n_slices - 1 - i // per)
        x = rows[:, :, :, span(who * per + i % per, part)].reshape(at.chips * four, part)
        g_tile[slot] = mm_tn(x, d_pre[...].reshape(at.chips * four, ff2)).astype(bf16)
        out_copy(slot, i).start()
        return 0

    lax.fori_loop(n_early, n_up, grad_rest, 0)
    for i in range(n_up - 2, n_up):
        out_copy(i % 2, i).wait()
    for c in keep:
        c.wait()
    arrive(outs)
    net.sent()


def norm_kernel(
    dims, early, db, ex, ggu, gdn, out_part, x1, b, cot, mask, router_t, gains,
    gx1, do_all, gain_two, g_router, land_gu, late_gu, land_dn, out_own_sum, out_sum,
    own, own_x, half_out, half_x, swap_in, swap_x, logit, d_out, out_own, out_core, out_in, rw,
    send, recv, local,
):
    at = Place(*dims)
    net = Net(send, recv, local)
    z, e, group = at.z, at.e, at.group
    tok = x1.shape[0]
    n_parts = db.shape[0]
    loads = [net.copy(db, own), net.copy(ex, own_x)]
    load_own = {t: net.copy(out_part.at[at.slot(t)], out_own.at[t]) for t in halves(at)}
    greet(everyone(at))
    step = 16
    for c in loads:
        c.wait()

    def sums(src):
        total, total_x = own[0, src, :].astype(f32), own_x[0, src, :].astype(f32)
        for t in range(1, n_parts):
            total += own[t, src, :].astype(f32)
            total_x += own_x[t, src, :].astype(f32)
        return total, total_x

    def partner(i, _):
        total, total_x = sums(pl.ds(pl.multiple_of(tok + i * step, step), step))
        half_out[span(i, step), :] = total.astype(bf16)
        half_x[span(i, step), :] = total_x.astype(bf16)
        return 0

    lax.fori_loop(0, tok // step, partner, 0)
    swaps = [net.push(half_out, swap_in, at.z_dev(group)), net.push(half_x, swap_x, at.z_dev(group))]
    d_slice = ggu.shape[1]
    landed = []
    for t in range(1, group):
        j = z ^ t ^ group
        landed.append(net.push(ggu.at[j, pl.ds(0, d_slice // 2)], land_gu.at[t - 1], at.z_dev(t)))
        if not early:
            landed.append(net.push(gdn.at[:, span(j, d_slice)], land_dn.at[t - 1], at.z_dev(t)))
        landed.append(net.push(ggu.at[j, pl.ds(d_slice // 2, d_slice // 2)], late_gu.at[t - 1], at.z_dev(t)))
    mates = {t: net.push(out_part.at[at.slot(t, 1)], out_core.at[t], at.mate()) for t in halves(at)}
    logits = mm_nt(b[...], router_t[...])
    chosen = mask[...].astype(f32) > 0
    masked = jnp.where(chosen, logits, neg_fill)
    raised = jnp.where(chosen, jnp.exp(masked - jnp.max(masked, axis=1, keepdims=True)), 0.0)
    rw[...] = raised / jnp.sum(raised, axis=1, keepdims=True)
    outs = []
    for t in halves(at):
        load_own[t].wait()
        mates[t].wait_recv()

        def add(i, _, t=t):
            rows = span(i, step)
            out_own[t, rows, :] = (out_own[t, rows, :].astype(f32) + out_core[t, rows, :].astype(f32)).astype(bf16)
            return 0

        lax.fori_loop(0, 2 * tok // step, add, 0)
        if t:
            outs.append(net.push(out_own.at[t], out_in.at[t - 1], at.chip_dev(t)))
    arrive(swaps)
    gain_two[...] = jnp.zeros_like(gain_two)

    def owner(i, _):
        rows = span(i, step)
        grad, routed = sums(rows)
        grad += swap_in[rows, :].astype(f32)
        routed += swap_x[rows, :].astype(f32)
        routed = routed + pltpu.roll(routed, 64, 1)
        weight = rw[rows, :]
        d_logit = weight * (routed - jnp.sum(weight * routed, axis=1, keepdims=True))
        high = d_logit.astype(bf16)
        low = (d_logit - high.astype(f32)).astype(bf16)
        logit[0, rows, :] = high
        logit[1, rows, :] = low
        grad += mm(high, router_t[...]) + mm(low, router_t[...])
        value = x1[rows, :]
        r = inv_rms(value)
        c = grad * gains[1:2, :]
        back = cot[rows, :].astype(f32) + r * c - value * (r * r * r * jnp.mean(c * value, axis=-1, keepdims=True))
        gx1[rows, :] = back
        d_out[rows, :] = back.astype(bf16)
        gain_two[...] += eight(grad * value * r)
        return 0

    lax.fori_loop(0, tok // step, owner, 0)
    mine = do_all.at[span(z, tok)]
    keep = net.copy(d_out, mine)
    copies = [net.push(d_out, mine, at.z_dev(t)) for t in range(1, at.n_shard)]
    g_router[...] = mm_tn(logit[0], b[...]) + mm_tn(logit[1], b[...])
    arrive(outs)

    def out_rows(i):
        rows = span(i, step)
        total = out_own[0, rows, :].astype(f32)
        for t in range(1, at.chips):
            total += out_in[t - 1, rows, :].astype(f32)
        return total.astype(bf16)

    def own_rows(i, _):
        out_own_sum[span(i, step), :] = out_rows(i)
        return 0

    def partner_rows(i, _):
        out_sum[span(i, step), :] = out_rows(tok // step + i)
        return 0

    lax.fori_loop(0, tok // step, own_rows, 0)
    lax.fori_loop(0, tok // step, partner_rows, 0)
    keep.wait()
    arrive(copies + landed)
    net.sent()


def back_kernel(
    dims, do_h, w_out, o_h, q_h, k_h, v_h, raw_h, cos_h, sin_h, seg_h, a_h, heads_h, ggu, gdn, land_gu, late_gu, land_dn, out_sum,
    out_sum_own, small, x1, gx1, x, gains, gain_two, g_router,
    hidden, g_hidden, small_sum, g_att, g_qkv, two_gu, own_gu, two_dn, own_dn,
    do_all, w_o, o, q, k, v, raw, cos, sin, seg_col, seg_row, mix, d_qkv, dk, dv, qk_gain, a, heads,
    sum_gu, add_gu, sum_dn, add_dn, swap_in, g_out, g_core, g_in, share_own,
    parts_in, g_heads, core_in, chip_in, mine, turn_in, share_qkv, sm, sm_z, sm_core, sm_chip,
    send, recv, local,
):
    at = Place(*dims)
    net = Net(send, recv, local)
    z, e, group = at.z, at.e, at.group
    length, width = do_all.shape
    tok = x1.shape[0]
    cols = raw.shape[1]
    hd = cols - 2 * HEAD_DIM
    n_heads = hd // HEAD_DIM
    rows_e = heads.shape[2]
    d_slice = ggu.shape[1]
    scale = HEAD_DIM ** (-0.5)
    block = tok
    step = 16
    far = z ^ group

    def d_cols(ref, who):
        return ref.at[:, span(who, d_slice)]

    cut = d_slice // 2
    halves_gu = [pl.ds(0, cut), pl.ds(cut, cut)]
    load_gu = [
        [net.copy(ggu.at[far, r], sum_gu.at[i])] + [net.copy(land.at[t - 1], add_gu.at[i, t - 1]) for t in range(1, group)]
        for i, (r, land) in enumerate(zip(halves_gu, (land_gu, late_gu)))
    ]
    load_a = [net.copy(do_h, do_all), net.copy(o_h, o)]
    load_b = [
        net.copy(s, d)
        for s, d in ((w_out, w_o), (q_h, q), (k_h, k), (v_h, v), (raw_h, raw), (cos_h, cos), (sin_h, sin), (seg_h, seg_col))
    ]
    load_c = [net.copy(a_h, a), net.copy(heads_h, heads)]
    load_dn = [net.copy(d_cols(gdn, far), sum_dn)] + [net.copy(land_dn.at[t - 1], add_dn.at[t - 1]) for t in range(1, group)]
    greet(everyone(at))
    swap = net.push(out_sum, swap_in, at.z_dev(group))

    def add_up(total, adds):
        def rows_of(i, _):
            rows = span(i, step)
            value = total[rows, :].astype(f32)
            for t in range(1, group):
                value += adds[t - 1, rows, :].astype(f32)
            total[rows, :] = value.astype(bf16)
            return 0

        lax.fori_loop(0, total.shape[0] // step, rows_of, 0)

    got = []

    def send_half(i):
        for c in load_gu[i]:
            c.wait()
        add_up(sum_gu.at[i], add_gu.at[i])
        got.append(net.push(sum_gu.at[i], two_gu.at[halves_gu[i]], at.z_dev(group)))

    send_half(0)
    for t in range(1, group):
        got.append(net.push(ggu.at[z ^ t], own_gu.at[t - 1], at.z_dev(t)))

    for c in load_a:
        c.wait()
    share = share_own.shape[0]
    wide = tiled(hd, 256)
    each = wide // share

    def out_grad(i, _):
        tile = mm_tn(o[:, span(i, wide)], do_all[...]).astype(bf16)
        for j in range(each):
            g_out[each * i + j] = tile[j * share : (j + 1) * share]
        return 0

    lax.fori_loop(0, hd // wide, out_grad, 0)
    g_mates = {t: net.push(g_out.at[at.slot(t, 1)], g_core.at[t], at.mate()) for t in halves(at)}
    for c in load_b:
        c.wait()
    qk = []
    for s in range(at.n_shard):
        rows = small[s, 0:16, :].astype(f32)
        seg_row[0:1, span(s, tok)] = rows[4:5, :tok]
        qk.append(rows[2:4, :HEAD_DIM])
    qk = sum(qk[1:], qk[0])

    def mix_tile(i, _):
        tile = span(i, wide)
        mix[:, tile] = mm_nt(do_all[...], w_o[tile, :]).astype(bf16)
        return 0

    lax.fori_loop(0, hd // wide, mix_tile, 0)
    g_outs = []
    for t in halves(at):
        g_mates[t].wait_recv()

        def add(i, _, t=t):
            rows = span(i, step)
            s = at.slot(t)
            g_out[s, rows, :] = (g_out[s, rows, :].astype(f32) + g_core[t, rows, :].astype(f32)).astype(bf16)
            return 0

        lax.fori_loop(0, share // step, add, 0)
        if t:
            g_outs.append(net.push(g_out.at[at.slot(t)], g_in.at[t - 1], at.chip_dev(t)))
    send_half(1)

    dk[...] = jnp.zeros_like(dk)
    dv[...] = jnp.zeros_like(dv)
    qk_gain[...] = jnp.zeros_like(qk_gain)

    def one_head(h, _):
        lanes = span(h, HEAD_DIM)
        for i in range(length // block):
            rows, keys = pl.ds(i * block, block), pl.ds(0, (i + 1) * block)
            soft = soft_block(q, k, seg_row, seg_col, h, i, block, scale)
            d_mix = mix[rows, lanes]
            d_soft = mm_nt(d_mix, v[keys, :])
            d_scores = (soft * (d_soft - jnp.sum(soft * d_soft, axis=-1, keepdims=True))).astype(bf16)
            dv[keys, :] += mm_tn(soft.astype(bf16), d_mix)
            dk[keys, :] += mm_tn(d_scores, q[rows, lanes]) * scale
            dq = mm(d_scores, k[keys, :]) * scale
            value = raw[rows, lanes]
            back, per = rms_back(value, qk[0:1], rope_rows_back(dq, cos[rows, :], sin[rows, :]))
            d_qkv[rows, lanes] = back.astype(bf16)
            qk_gain[0:8, :] += eight(per)
        return 0

    lax.fori_loop(0, n_heads, one_head, 0)
    for i in range(length // block):
        rows = pl.ds(i * block, block)
        value = raw[rows, pl.ds(hd, HEAD_DIM)]
        back, per = rms_back(value, qk[1:2], rope_rows_back(dk[rows, :], cos[rows, :], sin[rows, :]))
        d_qkv[rows, pl.ds(hd, HEAD_DIM)] = back.astype(bf16)
        d_qkv[rows, pl.ds(hd + HEAD_DIM, HEAD_DIM)] = dv[rows, :].astype(bf16)
        qk_gain[8:16, :] += eight(per)

    arrive(g_outs)

    def own_share(i, _):
        rows = span(i, step)
        total = g_out[e, rows, :].astype(f32)
        for t in range(1, at.chips):
            total += g_in[t - 1, rows, :].astype(f32)
        share_own[rows, :] = total.astype(bf16)
        return 0

    lax.fori_loop(0, share // step, own_share, 0)
    keep_att = net.copy(share_own, g_att.at[e])
    keep_att.wait()
    atts = [lambda who: g_att.at[who]]
    att_state = spread(net, at, atts)
    for c in load_c:
        c.wait()
    wide_d = tiled(d_slice, 256)
    each_d = wide_d // rows_e

    def grad_tile(s, _):
        for j in range(d_slice // wide_d):
            some = a[:, pl.ds(pl.multiple_of(s * d_slice + j * wide_d, wide_d), wide_d)]
            tile = mm_tn(some, d_qkv[...]).astype(bf16)
            for i in range(each_d):
                g_heads[each_d * j + i, s] = tile[i * rows_e : (i + 1) * rows_e]
        return 0

    lax.fori_loop(0, at.n_shard, grad_tile, 0)
    mates = {t: net.push(g_heads.at[at.slot(t, 1)], core_in.at[t], at.mate()) for t in halves(at)}
    part = do_all

    def rows_tile(s, _):
        for j in range(d_slice // wide_d):
            some = heads[s, pl.ds(each_d * j, each_d)].reshape(wide_d, cols)
            here = pl.ds(pl.multiple_of(s * d_slice + j * wide_d, wide_d), wide_d)
            part[:, here] = mm_nt(d_qkv[...], some).astype(bf16)
        return 0

    lax.fori_loop(0, at.n_shard, rows_tile, 0)
    sums = Scatter(net, at, part, parts_in, tok, step)
    chips = []
    for t in halves(at):
        mates[t].wait_recv()
        who = at.slot(t)

        def add(s, _, t=t, who=who):
            g_heads[who, s] = (g_heads[who, s].astype(f32) + core_in[t, s].astype(f32)).astype(bf16)
            return 0

        lax.fori_loop(0, at.n_shard, add, 0)
        if t:
            chips.append(net.push(g_heads.at[who], chip_in.at[t - 1], at.chip_dev(t)))
    more = sums.advance()
    for c in load_dn:
        c.wait()
    add_up(sum_dn, add_dn)
    swap.wait_recv()

    def hidden_rows(i, _):
        rows = span(i, step)
        hidden[rows, :] = (x1[rows, :] + out_sum_own[rows, :].astype(f32) + swap_in[rows, :].astype(f32)).astype(bf16)
        return 0

    lax.fori_loop(0, tok // step, hidden_rows, 0)
    arrive(chips)

    def total(s, _):
        value = g_heads[e, s].astype(f32)
        for t in range(1, at.chips):
            value += chip_in[t - 1, s].astype(f32)
        mine[s] = value.astype(bf16)
        return 0

    lax.fori_loop(0, at.n_shard, total, 0)
    turns = [net.push(mine.at[z ^ t], turn_in.at[z], at.z_dev(t)) for t in range(1, at.n_shard)]
    turn_own = net.copy(mine.at[z], turn_in.at[z])
    got.append(net.push(sum_dn, two_dn, at.z_dev(group)))
    for t in range(1, group):
        got.append(net.push(d_cols(gdn, z ^ t), own_dn.at[t - 1], at.z_dev(t)))
    slots = sums.finish() if more else sums.last
    sm[...] = jnp.zeros_like(sm)
    gain_one = jnp.zeros((8, width), f32)

    def owner(i, gain_one):
        rows = span(i, step)
        here = pl.ds(pl.multiple_of(z * tok + i * step, step), step)
        da = part[here, :].astype(f32)
        for t in slots:
            da += parts_in[t, rows, :].astype(f32)
        back, per = rms_back(x[rows, :].astype(f32), gains[0:1, :], da)
        g_hidden[rows, :] = gx1[rows, :] + back
        return gain_one + eight(per)

    gain_one = lax.fori_loop(0, tok // step, owner, gain_one)
    row_one = jnp.sum(gain_one, axis=0, keepdims=True)
    row_two = jnp.sum(gain_two[...], axis=0, keepdims=True)
    row_q = jnp.sum(qk_gain[0:8, :], axis=0, keepdims=True)
    row_k = jnp.sum(qk_gain[8:16, :], axis=0, keepdims=True)
    for s in range(at.n_shard):
        piece = pl.ds(s * d_slice, d_slice)
        lanes = slice(s * d_slice, (s + 1) * d_slice)
        sm[s, 0:1, :] = row_one[:, lanes]
        sm[s, 1:2, :] = row_two[:, lanes]
        sm[s, 2:3, pl.ds(0, HEAD_DIM)] = row_q
        sm[s, 3:4, pl.ds(0, HEAD_DIM)] = row_k
        sm[s, 8:, :] = g_router[0 : sm.shape[1] - 8, piece]
    small_z = [net.push(sm.at[z ^ t], sm_z.at[t - 1], at.z_dev(t)) for t in range(1, at.n_shard)]
    turn_own.wait()
    arrive(turns)
    for s in range(at.n_shard):
        share_qkv[:, pl.ds(s * hd, hd)] = turn_in[s, :, pl.ds(0, hd)]
    for m in range(KV_HEADS):
        some = [s for s in range(at.n_shard) if (s * n_heads) // (HEADS // KV_HEADS) == m]
        for first, to in ((hd, HEADS + m), (hd + HEAD_DIM, HEADS + KV_HEADS + m)):
            value = turn_in[some[0], :, pl.ds(first, HEAD_DIM)].astype(f32)
            for s in some[1:]:
                value += turn_in[s, :, pl.ds(first, HEAD_DIM)].astype(f32)
            share_qkv[:, pl.ds(to * HEAD_DIM, HEAD_DIM)] = value.astype(bf16)
    keep = net.copy(share_qkv, g_qkv.at[e])
    keep.wait()
    if at.chips == 4:
        go_on = spread_near(net, at, g_qkv)
    else:
        qkvs = [lambda who: g_qkv.at[who]]
        state = spread(net, at, qkvs)
        go_on = functools.partial(pass_on, net, at, qkvs, state)
    last = pass_on(net, at, atts, att_state)
    arrive(small_z)
    value = sm[z]
    for t in range(1, at.n_shard):
        value += sm_z[t - 1]
    sm[z] = value
    c = net.push(sm.at[z], sm_core, at.mate())
    c.wait_recv()
    sm_core[...] = sm[z] + sm_core[...]
    smalls = [net.push(sm_core, sm_chip.at[t - 1], at.chip_dev(t)) for t in range(1, at.chips)]
    last += go_on()
    arrive(smalls)
    value = sm_core[...]
    for t in range(1, at.chips):
        value += sm_chip[t - 1]
    small_sum[...] = value
    arrive(last + got)
    net.sent()


def shards(
    hidden_in,
    segments,
    routes,
    norm_gains,
    qk_gains,
    w_qkv,
    w_attn_out,
    w_router,
    w_gate_up,
    w_down,
    cotangent,
):
    n_expert = lax.axis_size("expert")
    n_shard = lax.axis_size("shard")
    me_e = lax.axis_index("expert")
    me_z = lax.axis_index("shard")
    tok, width = hidden_in.shape
    exp_dev = w_gate_up.shape[1]
    experts_all = w_router.shape[2]
    d_slice, ff2 = w_gate_up.shape[2:]
    ff = ff2 // 2
    group = n_shard // exp_dev
    mine = me_z // group
    length = n_shard * tok
    h_dev = HEADS // n_shard
    hd = h_dev * HEAD_DIM
    cols = hd + 2 * HEAD_DIM
    qkv_cols = w_qkv.shape[2]
    rows_e = d_slice // n_expert
    share = hd // n_expert
    chips = n_expert // 2
    qk_part = HEAD_DIM // n_shard
    dims = (n_expert, n_shard, group)
    n_small = 16 + experts_all
    sds = jax.ShapeDtypeStruct
    vm = pltpu.VMEM
    any_spec = pl.BlockSpec(memory_space=pl.ANY)
    vmem_spec = pl.BlockSpec(memory_space=pltpu.VMEM)

    lane = jnp.arange(HEAD_DIM, dtype=jnp.int32)
    qk_placed = jnp.where((lane // qk_part == me_z)[None], jnp.tile(qk_gains[0], (1, n_shard)), jnp.zeros((), bf16))
    small = jnp.concatenate(
        [
            norm_gains[0],
            jnp.pad(qk_placed, ((0, 0), (0, d_slice - HEAD_DIM))),
            jnp.pad(segments.astype(bf16)[None], ((0, 11), (0, d_slice - tok))),
            w_router[0].T,
        ],
        axis=0,
    )
    seg_own = jnp.broadcast_to(segments.astype(f32)[:, None], (tok, 128))
    ids = jnp.arange(128, dtype=jnp.int32)
    mask = jnp.sum((routes[:, :, None] == ids[None, None, :]).astype(f32), axis=1).astype(bf16)
    cos, sin = rotary_tables(length)

    outs = [
        sds((n_shard, n_small, d_slice), bf16),
        sds((length, 128), f32),
        sds((n_shard, n_expert, rows_e, cols), bf16),
        sds((length, width), bf16),
        sds((length, cols), f32),
        sds((length, hd), bf16),
        sds((length, HEAD_DIM), bf16),
        sds((length, HEAD_DIM), bf16),
        sds((length, hd), bf16),
        sds((tok, width), f32),
        sds((tok, width), bf16),
        sds((n_shard, d_slice, ff2), bf16),
        sds((n_expert, 2 * tok, width), bf16),
        sds((n_expert, 2 * tok, 128), bf16),
        sds((2 * tok, width), bf16),
        sds((8, width), f32),
        sds((128, width), bf16),
    ]
    front = comm_call(
        functools.partial(front_kernel, dims),
        0,
        160,
        40,
        [
            vm((length, width), bf16),
            vm((n_shard, n_small, d_slice), bf16),
            vm((length, 128), f32),
            vm((n_shard, n_expert, rows_e, cols), bf16),
            vm((length, width), bf16),
            vm((length, cols), f32),
            vm((length, hd), bf16),
            vm((length, HEAD_DIM), bf16),
            vm((length, HEAD_DIM), bf16),
            vm((length, hd), bf16),
            vm((hd, width), bf16),
            vm((length, width), bf16),
            vm((n_shard - 1, tok, width), bf16),
            vm((length, HEAD_DIM), f32),
            vm((length, HEAD_DIM), f32),
            vm((8, length), f32),
            vm((tok, width), f32),
            vm((tok, width), bf16),
        ],
        outs,
        56,
        out_specs=[any_spec] * (len(outs) - 2) + [vmem_spec] * 2,
    )
    (small_all, seg_col, heads, a, raw, q, k, v, o, x1, b, gate_up, cot_all, mask_all, b_pair, gains, router_pad) = front(
        hidden_in, small, seg_own, w_qkv[0], w_attn_out[0], w_gate_up[0], cotangent, mask, cos, sin
    )
    router_t = router_pad[:experts_all]

    def route_weights(rows, chosen):
        logits = mm_nt(rows, router_t)
        masked = jnp.where(chosen, logits, neg_fill)
        raised = jnp.where(chosen, jnp.exp(masked - jnp.max(masked, axis=1, keepdims=True)), 0.0)
        return raised / jnp.sum(raised, axis=1, keepdims=True)

    per_e = (n_expert, 2 * tok)
    piece = (chips, 2 * tok)
    four = 4 * tok
    if chips <= 4:
        out_part, grad_gate_up, grad_down, db_in, ex_in, land_dn = comm_call(
            functools.partial(expert_kernel, dims),
            4,
            60,
            60,
            [
                vm((width, ff2), bf16),
                vm((ff, width), bf16),
                vm((chips, 2, 2 * tok, width), bf16),
                vm((2, 2 * tok, width), bf16),
                vm((chips, 2, 2 * tok, 128), bf16),
                vm((chips, four, ff), bf16),
                vm((chips, four, ff2), bf16),
                vm((chips, four, width), bf16),
                vm((2, 2 * tok, width), bf16),
                vm((2, 2 * tok, 128), bf16),
                vm(piece + (width,), bf16),
                vm(piece + (128,), bf16),
                vm(piece + (width,), bf16),
                vm(piece + (128,), bf16),
                vm((chips, four, 128), f32),
                vm((four, 128), f32),
                vm((2, tiled(width, 256), ff2), bf16),
                vm((2, tiled(ff, 256), width), bf16),
                pltpu.SemaphoreType.DMA((2,)),
            ],
            [
                sds(per_e + (width,), bf16),
                sds((n_shard, d_slice, ff2), bf16),
                sds((ff, width), bf16),
                sds(piece + (width,), bf16),
                sds(piece + (128,), bf16),
                sds((group - 1, ff, d_slice), bf16),
            ],
            60,
            in_specs=[any_spec] * 6 + [vmem_spec],
        )(b_pair, cot_all, mask_all, gate_up, w_gate_up[0], w_down[0], router_pad)
    else:
        rows_all = n_expert * 2 * tok
        w_mine = lax.dynamic_index_in_dim(w_gate_up[0], mine, 0, keepdims=False)
        gate_up = lax.dynamic_update_index_in_dim(gate_up, w_mine, me_z, 0)
        down = lax.all_gather(w_down[0], "shard", axis=2, tiled=True)
        down = lax.dynamic_index_in_dim(down, mine, 0, keepdims=False)
        b_rows = lax.all_gather(b_pair, "expert", axis=0, tiled=True)
        my_expert = me_e * exp_dev + mine
        rw_all = route_weights(b_rows, mask_all.reshape(rows_all, 128)[:, :experts_all] > 0)
        is_mine = ids[:experts_all] == my_expert
        rw_mine = jnp.sum(jnp.where(is_mine[None, :], rw_all, 0.0), axis=1, keepdims=True)
        w_gu = gate_up.reshape(width, ff2)
        pre = mm(b_rows, w_gu)
        g, u = pre[:, :ff], pre[:, ff:]
        sig = jax.nn.sigmoid(g)
        act = g * sig
        hidden = (act * u).astype(bf16)
        y_f = mm(hidden, down).astype(bf16).astype(f32)
        cot_f = cot_all.reshape(rows_all, width).astype(f32)
        d_route = jnp.sum(cot_f * y_f, axis=1, keepdims=True)
        out_part = (rw_mine * y_f).astype(bf16)
        d_y = (rw_mine * cot_f).astype(bf16)
        d_hidden = mm_nt(d_y, down)
        d_pre = jnp.concatenate(
            [d_hidden * u * sig * (1.0 + g * (1.0 - sig)), d_hidden * act], axis=1
        ).astype(bf16)
        d_b = mm_nt(d_pre, w_gu).astype(bf16)
        grad_down = mm_tn(hidden, d_y).astype(bf16)
        grad_gate_up = mm_tn(b_rows, d_pre).astype(bf16).reshape(n_shard, d_slice, ff2)
        high = lax.reduce_precision(d_route, 8, 7)
        low = d_route - high
        extra = jnp.where(ids[None] == my_expert, high, jnp.where(ids[None] == my_expert + 64, low, 0.0)).astype(bf16)

        def home(value):
            return lax.psum_scatter(value, "expert", scatter_dimension=0, tiled=True)[None]

        db_in, ex_in = home(d_b), home(extra)

    n_parts = db_in.shape[0]
    early = chips <= 4
    gx1, d_o, gain_two, g_router, land_gu, late_gu, norm_dn, out_own_sum, out_sum = comm_call(
        functools.partial(norm_kernel, dims, early),
        1,
        60,
        24,
        [
            vm((n_parts, 2 * tok, width), bf16),
            vm((n_parts, 2 * tok, 128), bf16),
            vm((tok, width), bf16),
            vm((tok, 128), bf16),
            vm((tok, width), bf16),
            vm((tok, 128), bf16),
            vm((2, tok, 128), bf16),
            vm((tok, width), bf16),
            vm(piece + (width,), bf16),
            vm(piece + (width,), bf16),
            vm((chips - 1, 2 * tok, width), bf16),
            vm((tok, 128), f32),
        ],
        [
            sds((tok, width), f32),
            sds((length, width), bf16),
            sds((8, width), f32),
            sds((128, width), f32),
            sds((group - 1, d_slice // 2, ff2), bf16),
            sds((group - 1, d_slice // 2, ff2), bf16),
            sds((group - 1, ff, d_slice), bf16) if not early else sds((16, 128), bf16),
            sds((tok, width), bf16),
            sds((tok, width), bf16),
        ],
        60,
        in_specs=[any_spec] * 5 + [vmem_spec] * 6,
        out_specs=[vmem_spec, any_spec, vmem_spec, vmem_spec] + [any_spec] * 3 + [vmem_spec] * 2,
    )(db_in, ex_in, grad_gate_up, grad_down, out_part.reshape(per_e + (width,)), x1, b, cotangent, mask, router_pad, gains)
    if not early:
        land_dn = norm_dn

    small_rows = (8 + -(-experts_all // 8) * 8, d_slice)
    hidden_out, grad_hidden, sums, grad_out, grad_qkv, two_gu, own_gu, two_dn, own_dn = comm_call(
        functools.partial(back_kernel, dims),
        2,
        140,
        60,
        [
            vm((length, width), bf16),
            vm((hd, width), bf16),
            vm((length, hd), bf16),
            vm((length, hd), bf16),
            vm((length, HEAD_DIM), bf16),
            vm((length, HEAD_DIM), bf16),
            vm((length, cols), f32),
            vm((length, HEAD_DIM), f32),
            vm((length, HEAD_DIM), f32),
            vm((length, 128), f32),
            vm((8, length), f32),
            vm((length, hd), bf16),
            vm((length, cols), bf16),
            vm((length, HEAD_DIM), f32),
            vm((length, HEAD_DIM), f32),
            vm((16, HEAD_DIM), f32),
            vm((length, width), bf16),
            vm((n_shard, n_expert, rows_e, cols), bf16),
            vm((2, d_slice // 2, ff2), bf16),
            vm((2, group - 1, d_slice // 2, ff2), bf16),
            vm((ff, d_slice), bf16),
            vm((group - 1, ff, d_slice), bf16),
            vm((tok, width), bf16),
            vm((n_expert, share, width), bf16),
            vm((chips, share, width), bf16),
            vm((chips - 1, share, width), bf16),
            vm((share, width), bf16),
            vm((n_shard - 1, tok, width), bf16),
            vm((n_expert, n_shard, rows_e, cols), bf16),
            vm((chips, n_shard, rows_e, cols), bf16),
            vm((chips - 1, n_shard, rows_e, cols), bf16),
            vm((n_shard, rows_e, cols), bf16),
            vm((n_shard, rows_e, cols), bf16),
            vm((rows_e, qkv_cols), bf16),
            vm((n_shard,) + small_rows, f32),
            vm((n_shard - 1,) + small_rows, f32),
            vm(small_rows, f32),
            vm((chips - 1,) + small_rows, f32),
        ],
        [
            sds((tok, width), bf16),
            sds((tok, width), f32),
            sds(small_rows, f32),
            sds((n_expert, share, width), bf16),
            sds((n_expert, rows_e, qkv_cols), bf16),
            sds((d_slice, ff2), bf16),
            sds((group - 1, d_slice, ff2), bf16),
            sds((ff, d_slice), bf16),
            sds((group - 1, ff, d_slice), bf16),
        ],
        60,
        in_specs=[any_spec] * 18 + [vmem_spec] * 8,
        out_specs=[vmem_spec] * 3 + [any_spec] * 6,
    )(
        d_o,
        w_attn_out[0],
        o,
        q,
        k,
        v,
        raw,
        cos,
        sin,
        seg_col,
        a,
        heads,
        grad_gate_up,
        grad_down,
        land_gu,
        late_gu,
        land_dn,
        out_sum,
        out_own_sum,
        small_all,
        x1,
        gx1,
        hidden_in,
        gains,
        gain_two,
        g_router,
    )

    def settle(own, others, other):
        total = own.astype(f32) + jnp.sum(others.astype(f32), axis=0)
        other = other.astype(f32)
        return jnp.stack([jnp.where(mine == 0, total, other), jnp.where(mine == 0, other, total)])[None]

    own_gate_up = lax.dynamic_index_in_dim(grad_gate_up, me_z, 0, keepdims=False)
    own_down = lax.dynamic_slice_in_dim(grad_down, me_z * d_slice, d_slice, 1)
    qk_grad = lax.dynamic_slice_in_dim(sums[2:4, :HEAD_DIM], me_z * qk_part, qk_part, 1)
    return (
        hidden_out,
        grad_hidden,
        sums[0:2][None],
        qk_grad[None],
        grad_qkv.reshape(d_slice, qkv_cols).astype(f32)[None],
        grad_out.reshape(hd, width).astype(f32)[None],
        sums[8 : 8 + experts_all].T[None],
        settle(own_gate_up, own_gu, two_gu),
        settle(own_down, own_dn, two_dn),
    )


def solution(mesh):
    in_specs = (
        P(("expert", "shard"), None),
        P(("expert", "shard")),
        P(("expert", "shard"), None),
        P(None, None, "shard"),
        P(None, None, "shard"),
        P(None, "shard", None),
        P(None, "shard", None),
        P(None, "shard", None),
        P(None, "expert", "shard", None),
        P(None, "expert", None, "shard"),
        P(("expert", "shard"), None),
    )
    out_specs = (
        P(("expert", "shard"), None),
        P(("expert", "shard"), None),
        P(None, None, "shard"),
        P(None, None, "shard"),
        P(None, "shard", None),
        P(None, "shard", None),
        P(None, "shard", None),
        P(None, "expert", "shard", None),
        P(None, "expert", None, "shard"),
    )
    return jax.shard_map(shards, mesh=mesh, in_specs=in_specs, out_specs=out_specs, check_vma=False)
```

```python
import functools

import jax
import jax.numpy as jnp
import numpy as np
from jax import lax
from jax.experimental import pallas as pl
from jax.experimental.pallas import tpu as pltpu
from jax.sharding import PartitionSpec as P

HEADS = 32
KV_HEADS = 4
HEAD_DIM = 128
TOP = 8

bf16 = jnp.bfloat16
f32 = jnp.float32
highest = lax.Precision.HIGHEST
eps_norm = 1e-06
rope_base = 1000000.0
neg_fill = -1e30


def dot(left, right, dims, out=f32):
    return lax.dot_general(left, right, (dims, ((), ())), preferred_element_type=out)


def mm(left, right):
    return dot(left, right, ((1,), (0,)))


def mm_nt(left, right):
    return dot(left, right, ((1,), (1,)))


def mm_tn(left, right):
    return dot(left, right, ((0,), (0,)))


def inv_rms(value):
    return lax.rsqrt(jnp.mean(value * value, axis=-1, keepdims=True) + eps_norm)


def rms_back(value, gain, grad):
    r = inv_rms(value)
    c = grad * gain
    back = r * c - value * (r * r * r) * jnp.mean(c * value, axis=-1, keepdims=True)
    return back, grad * value * r


def rotary_tables(length):
    half = HEAD_DIM // 2
    frequency = np.float32(rope_base) ** (-(np.arange(half, dtype=np.float32) * np.float32(2.0)) / np.float32(HEAD_DIM))
    angles = np.arange(length, dtype=np.float32)[:, None] * frequency[None, :].astype(np.float32)
    cos, sin = np.cos(angles), np.sin(angles)
    return jnp.asarray(np.concatenate([cos, cos], axis=1)), jnp.asarray(np.concatenate([-sin, sin], axis=1))


MESH = pl.DeviceIdType.MESH


class Place:
    def __init__(self, n_expert, n_shard, group):
        self.e = lax.axis_index("expert")
        self.z = lax.axis_index("shard")
        self.n_expert, self.n_shard, self.group = n_expert, n_shard, group
        self.chip, self.core = self.e // 2, self.e % 2
        self.chips = n_expert // 2

    def z_dev(self, t):
        return (self.e, self.z ^ t)

    def slot(self, t, other=0):
        return (self.chip ^ t) * 2 + (self.core ^ other)

    def chip_dev(self, t):
        return (self.slot(t), self.z)

    def mate(self):
        return (self.e ^ 1, self.z)


class Net:
    def __init__(self, send, recv, local):
        self.send, self.recv, self.local = send, recv, local
        self.n, self.m, self.open = 0, 0, []

    def push(self, src, dst, dev):
        i = self.n
        self.n += 1
        copy = pltpu.make_async_remote_copy(
            src_ref=src, dst_ref=dst, send_sem=self.send.at[i], recv_sem=self.recv.at[i],
            device_id=dev, device_id_type=MESH,
        )
        copy.start()
        self.open.append(copy)
        return copy

    def copy(self, src, dst):
        i = self.m
        self.m += 1
        copy = pltpu.make_async_copy(src, dst, self.local.at[i])
        copy.start()
        return copy

    def done(self, copy):
        copy.wait_send()
        self.open = [c for c in self.open if c is not copy]

    def sent(self):
        for copy in self.open:
            copy.wait_send()
        self.open = []


def greet(devices):
    barrier = pltpu.get_barrier_semaphore()
    for dev in devices:
        pl.semaphore_signal(barrier, inc=1, device_id=dev, device_id_type=MESH)
    pl.semaphore_wait(barrier, len(devices))


def everyone(at):
    return (
        [at.z_dev(t) for t in range(1, at.n_shard)]
        + [at.chip_dev(t) for t in range(1, at.chips)]
        + [at.mate()]
    )


def arrive(copies):
    for copy in copies:
        copy.wait_recv()


def spread(net, at, pieces):
    own = [p(at.e) for p in pieces]
    mate = [net.push(o, o, at.mate()) for o in own]
    out = [(t, [net.push(o, o, at.chip_dev(t)) for o in own]) for t in range(1, at.chips)]
    return mate, out


def pass_on(net, at, pieces, state):
    mate, out = state
    for t, copies in out:
        for p, copy in zip(pieces, copies):
            copy.wait_recv()
            got = p(at.slot(t))
            mate.append(net.push(got, got, at.mate()))
    return mate


def low_bit(k):
    return k & -k


class Gather:
    def __init__(self, net, at, own, ref, rows):
        self.net, self.at, self.ref, self.rows = net, at, ref, rows
        bits = [b for b in (1 << i for i in range(10)) if b < at.n_shard]
        self.bits = bits[::-1]
        here = self.place(0)
        self.copies = {b: net.push(own, here, at.z_dev(b)) for b in self.bits}

    def place(self, k):
        return self.ref.at[span(self.at.z ^ k, self.rows)]

    def finish(self, then=None):
        waiting = list(self.bits)
        while waiting:
            k = waiting.pop(0)
            self.copies[k].wait_recv()
            for b in self.bits:
                if b < low_bit(k):
                    got = self.place(k)
                    self.copies[k | b] = self.net.push(got, got, self.at.z_dev(b))
                    waiting.append(k | b)
            if then:
                then()
                then = None


class Scatter:
    def __init__(self, net, at, part, landing, rows, step):
        self.net, self.at, self.part, self.landing, self.rows, self.step = net, at, part, landing, rows, step
        self.slot, self.bit, self.last = 0, 1, []
        self.start()

    def block(self, k):
        return self.part.at[span(self.at.z ^ k, self.rows)]

    def start(self):
        bit, self.copies = self.bit, []
        for k in [k for k in range(self.at.n_shard - 1, 0, -1) if k % (2 * bit) == bit]:
            copy = self.net.push(self.block(k), self.landing.at[self.slot], self.at.z_dev(bit))
            self.copies.append((k ^ bit, self.slot, copy))
            self.slot += 1

    def advance(self):
        self.bit *= 2
        for to, i, copy in self.copies:
            copy.wait_recv()
            if not to:
                self.last.append(i)
                continue

            def add(j, _, to=to, i=i):
                r = span(j, self.step)
                here = pl.ds(pl.multiple_of((self.at.z ^ to) * self.rows + j * self.step, self.step), self.step)
                value = self.part[here, :].astype(f32) + self.landing[i, r, :].astype(f32)
                self.part[here, :] = value.astype(bf16)
                return 0

            lax.fori_loop(0, self.rows // self.step, add, 0)
        if self.bit < self.at.n_shard:
            self.start()
            return True
        return False

    def finish(self):
        while self.advance():
            pass
        return self.last


def spread_near(net, at, ref):
    own = ref.at[at.e]
    mate = [net.push(own, own, at.mate())]
    out = {t: net.push(own, own, at.chip_dev(t)) for t in (1, 2)}
    half = ref.shape[1] // 2

    def go_on():
        relayed = []
        for t in (1, 2):
            out[t].wait_recv()
            got = ref.at[at.slot(t)]
            mate.append(net.push(got, got, at.mate()))
            part = ref.at[at.slot(t), pl.ds((2 - t) * half, half)]
            relayed.append(net.push(part, part, at.chip_dev(3 - t)))
        arrive(relayed)
        got = ref.at[at.slot(3)]
        mate.append(net.push(got, got, at.mate()))
        return mate

    return go_on


def comm_call(kernel, cid, n_remote, n_local, scratch, outs, vmem_mb, in_specs=None, out_specs=None, cost=None):
    any_spec = pl.BlockSpec(memory_space=pl.ANY)

    def call(*args):
        return pl.pallas_call(
            kernel,
            out_shape=outs,
            in_specs=in_specs or [any_spec] * len(args),
            out_specs=out_specs or [any_spec] * len(outs),
            scratch_shapes=list(scratch)
            + [
                pltpu.SemaphoreType.DMA((n_remote,)),
                pltpu.SemaphoreType.DMA((n_remote,)),
                pltpu.SemaphoreType.DMA((n_local,)),
            ],
            compiler_params=pltpu.CompilerParams(
                collective_id=cid, has_side_effects=True, vmem_limit_bytes=vmem_mb << 20
            ),
            cost_estimate=cost,
        )(*args)

    return call


def tiled(size, most):
    while size % most:
        most //= 2
    return most


def halves(at):
    return list(range(1, at.chips)) + [0]


def rope_rows(value, cos, sin):
    return value * cos + pltpu.roll(value, HEAD_DIM // 2, 1) * sin


def rope_rows_back(grad, cos, sin):
    return grad * cos + pltpu.roll(grad * sin, HEAD_DIM // 2, 1)


def eight(per):
    return jnp.sum(per.reshape(per.shape[0] // 8, 8, per.shape[1]), axis=0)


def span(i, size):
    if isinstance(i, int):
        return pl.ds(i * size, size)
    return pl.ds(pl.multiple_of(i * size, size), size)


def soft_block(q_ref, k_ref, seg_row, seg_col, h, i, block, scale):
    rows, keys = pl.ds(i * block, block), pl.ds(0, (i + 1) * block)
    scores = mm_nt(q_ref[rows, span(h, HEAD_DIM)], k_ref[keys, :]) * scale
    width = (i + 1) * block
    at_q = i * block + lax.broadcasted_iota(jnp.int32, (block, width), 0)
    at_k = lax.broadcasted_iota(jnp.int32, (block, width), 1)
    allowed = (at_k <= at_q) & (seg_row[0:1, keys] == seg_col[rows, 0:1])
    scores = jnp.where(allowed, scores, neg_fill)
    raised = jnp.exp(scores - jnp.max(scores, axis=-1, keepdims=True))
    return raised / jnp.sum(raised, axis=-1, keepdims=True)


def front_kernel(
    dims, x, small, seg_own, w_qkv, w_out, w_gu, cot, mask, cos_h, sin_h,
    small_out, seg_out, heads_out, a_out, raw_out, q_out, k_out, v_out, o_out, x1_out, b_out,
    gate_up, cot_all, mask_all, b_pair, gains, router_pad,
    x_all, small_all, seg_col, heads, a, raw, q, k, v, o, w_o, part, parts_in, cos, sin, seg_row, x1, b_own,
    send, recv, local,
):
    at = Place(*dims)
    net = Net(send, recv, local)
    z, e, group = at.z, at.e, at.group
    tok = x.shape[0]
    length, width = x_all.shape
    mine = z // group
    rows_e, cols = heads.shape[2], heads.shape[3]
    hd = cols - 2 * HEAD_DIM
    n_heads = hd // HEAD_DIM
    q_width = HEADS * HEAD_DIM
    d_slice = w_gu.shape[1]
    scale = HEAD_DIM ** (-0.5)
    block = tok

    def heads_of(dest):
        kv = (dest * n_heads) // (HEADS // KV_HEADS)
        rows = span(e, rows_e)
        return [
            (w_qkv.at[rows, span(dest, hd)], heads.at[z, e, :, pl.ds(0, hd)]),
            (w_qkv.at[rows, span(HEADS + kv, HEAD_DIM)], heads.at[z, e, :, pl.ds(hd, HEAD_DIM)]),
            (w_qkv.at[rows, span(HEADS + KV_HEADS + kv, HEAD_DIM)], heads.at[z, e, :, pl.ds(hd + HEAD_DIM, HEAD_DIM)]),
        ]

    half0, half1 = pl.ds(0, tok), pl.ds(tok, tok)
    first = [
        net.copy(x, x_all.at[span(z, tok)]),
        net.copy(small, small_all.at[z]),
        net.copy(seg_own, seg_col.at[span(z, tok)]),
        net.copy(cos_h, cos),
        net.copy(sin_h, sin),
    ]
    local_heads = [net.copy(s, d) for s, d in heads_of(z)]
    local_cot = [net.copy(cot, cot_all.at[e, half0]), net.copy(mask, mask_all.at[e, half0])]
    load_out = net.copy(w_out, w_o)
    greet(everyone(at))
    got_heads = [net.push(s, d, at.z_dev(t)) for t in range(1, at.n_shard) for s, d in heads_of(z ^ t)]
    got_x = []
    for t in range(1, at.n_shard):
        got_x.append(net.push(small, small_all.at[z], at.z_dev(t)))
        got_x.append(net.push(seg_own, seg_col.at[span(z, tok)], at.z_dev(t)))
    gather_x = Gather(net, at, x, x_all, tok)
    for c in local_heads:
        c.wait()
    arrive(got_heads)
    pieces = [lambda who: heads.at[:, who]]
    heads_state = spread(net, at, pieces)
    other = (z ^ group) // group
    cut = d_slice // 2
    low, high = pl.ds(0, cut), pl.ds(cut, cut)
    pieces_w = [
        (w_gu.at[other, low], gate_up.at[z, low], gate_up.at[z ^ group, low]),
        (w_gu.at[other, high], gate_up.at[z, high], gate_up.at[z ^ group, high]),
    ]
    from_partner = {}

    def fetch_piece(i):
        src, dst, got = pieces_w[i]
        from_partner[i] = (net.push(src, dst, at.z_dev(group)), got)

    for c in first:
        c.wait()
    gather_x.finish(lambda: fetch_piece(0))
    arrive(got_x)

    def hand_on(i):
        copy, ref = from_partner[i]
        copy.wait_recv()
        for t in range(1, group):
            got_w.append(net.push(ref, ref, at.z_dev(t)))

    got_w = []
    for t in range(1, group):
        got_w.append(net.push(w_gu.at[mine], gate_up.at[z], at.z_dev(t)))
    got_cot = [
        net.push(cot, cot_all.at[e, half1], at.z_dev(group)),
        net.push(mask, mask_all.at[e, half1], at.z_dev(group)),
    ]

    gains[...] = jnp.zeros_like(gains)
    router_pad[...] = jnp.zeros_like(router_pad)
    qk = []
    for s in range(at.n_shard):
        rows = small_all[s, 0:16, :].astype(f32)
        gains[0:2, span(s, d_slice)] = rows[0:2]
        router_pad[0 : small.shape[0] - 16, span(s, d_slice)] = small_all[s, 16:, :]
        seg_row[0:1, span(s, tok)] = rows[4:5, :tok]
        qk.append(rows[2:4, :HEAD_DIM])
    qk = sum(qk[1:], qk[0])
    step = 16

    def norm_rows(i, _):
        rows = span(i, step)
        value = x_all[rows, :].astype(f32)
        a[rows, :] = (value * inv_rms(value) * gains[0:1, :]).astype(bf16)
        return 0

    lax.fori_loop(0, length // step, norm_rows, 0)
    fetch_piece(1)
    last = pass_on(net, at, pieces, heads_state)
    arrive(last)
    keep = [net.copy(heads, heads_out), net.copy(a, a_out), net.copy(small_all, small_out), net.copy(seg_col, seg_out)]

    wide = tiled(cols, 256)

    def project(i, _):
        tile = span(i, wide)
        raw[:, tile] = mm(a[...], heads[:, :, :, tile].reshape(width, wide))
        return 0

    lax.fori_loop(0, cols // wide, project, 0)
    keep.append(net.copy(raw, raw_out))

    def head_rows(i, _):
        rows = span(i, block)
        cos_b, sin_b = cos[rows, :], sin[rows, :]
        for h in range(n_heads + 1):
            value = raw[rows, pl.ds(h * HEAD_DIM, HEAD_DIM)]
            gain = qk[0:1] if h < n_heads else qk[1:2]
            value = rope_rows(value * inv_rms(value) * gain, cos_b, sin_b).astype(bf16)
            if h < n_heads:
                q[rows, pl.ds(h * HEAD_DIM, HEAD_DIM)] = value
            else:
                k[rows, :] = value
        v[rows, :] = raw[rows, pl.ds(hd + HEAD_DIM, HEAD_DIM)].astype(bf16)
        return 0

    lax.fori_loop(0, length // block, head_rows, 0)
    keep += [net.copy(q, q_out), net.copy(k, k_out), net.copy(v, v_out)]
    for c in local_cot:
        c.wait()
    arrive(got_cot)
    cots = [lambda who: cot_all.at[who], lambda who: mask_all.at[who]]
    cot_state = spread(net, at, cots)


    def one_head(h, _):
        for i in range(length // block):
            soft = soft_block(q, k, seg_row, seg_col, h, i, block, scale).astype(bf16)
            mixed = mm(soft, v[pl.ds(0, (i + 1) * block), :])
            o[pl.ds(i * block, block), span(h, HEAD_DIM)] = mixed.astype(bf16)
        return 0

    lax.fori_loop(0, n_heads, one_head, 0)
    hand_on(0)
    keep.append(net.copy(o, o_out))
    load_out.wait()
    wide_o = tiled(width, 256)

    def out_tile(i, _):
        tile = span(i, wide_o)
        part[:, tile] = mm(o[...], w_o[:, tile]).astype(bf16)
        return 0

    lax.fori_loop(0, width // wide_o, out_tile, 0)
    summing = Scatter(net, at, part, parts_in, tok, step)
    more = summing.advance()
    hand_on(1)
    slots = summing.finish() if more else summing.last

    def middle_rows(i, _):
        rows = span(i, step)
        total = part[pl.ds(pl.multiple_of(z * tok + i * step, step), step), :].astype(f32)
        for t in slots:
            total += parts_in[t, rows, :].astype(f32)
        value = x_all[pl.ds(pl.multiple_of(z * tok + i * step, step), step), :].astype(f32) + total
        x1[rows, :] = value
        b_own[rows, :] = (value * inv_rms(value) * gains[1:2, :]).astype(bf16)
        return 0

    lax.fori_loop(0, tok // step, middle_rows, 0)
    swap = net.push(b_own, b_pair.at[half1], at.z_dev(group))
    keep += [net.copy(b_own, b_pair.at[half0]), net.copy(x1, x1_out), net.copy(b_own, b_out)]
    last = pass_on(net, at, cots, cot_state)
    swap.wait_recv()
    arrive(last + got_w)
    for c in keep:
        c.wait()
    net.sent()


def expert_kernel(
    dims, b_pair, cot_all, mask_all, gate_up, w_gu_in, w_dn_in, router_t,
    out_part, ggu, gdn, db_in, ex_in, land_dn,
    w_gu, w_dn, rows, cot_t, mask_t, hid, d_pre, d_y, stage, stage_x, own, own_x, core_in, core_x, w_r, d_r, g_tile, d_tile,
    tile_sem, send, recv, local,
):
    at = Place(*dims)
    net = Net(send, recv, local)
    z, e, group = at.z, at.e, at.group
    n_slices, d_slice, ff2 = gate_up.shape
    ff, width = w_dn.shape
    two = b_pair.shape[0]
    four = 2 * two
    mine, other = z // group, (z ^ group) // group
    expert = e * (at.n_shard // group) + mine
    step = 16
    fine = tiled(ff, 256)
    wide = tiled(width, 1024)
    far = z ^ group

    def d_cols(who):
        return w_dn.at[:, span(who, d_slice)]

    pair = net.copy(b_pair, rows.at[0, 1])
    masks = []
    for t in range(at.chips):
        masks.append(net.copy(mask_all.at[at.slot(t, 1)], mask_t.at[t, 0]))
        masks.append(net.copy(mask_all.at[at.slot(t)], mask_t.at[t, 1]))
    loads = [net.copy(w_gu_in.at[mine], w_gu.at[span(z, d_slice)])]
    for k in range(1, n_slices):
        loads.append(net.copy(gate_up.at[z ^ k], w_gu.at[span(z ^ k, d_slice)]))
    load_dn = net.copy(w_dn_in.at[mine], d_cols(z))

    def fetch(t):
        return [
            net.copy(cot_all.at[at.slot(t, 1)], cot_t.at[0]),
            net.copy(cot_all.at[at.slot(t)], cot_t.at[1]),
        ]

    order = list(range(1, at.chips)) + [0]
    fetched = {order[0]: fetch(order[0])}
    greet(
        [at.chip_dev(t) for t in range(1, at.chips)] + [at.mate()] + [at.z_dev(t) for t in range(1, group + 1)]
    )
    from_mate = {0: net.push(b_pair, rows.at[0, 0], at.mate())}
    near = [t for t in (1, 2) if t < at.chips]
    beyond = [t for t in range(1, at.chips) if t not in near]
    from_chip = {t: net.push(b_pair, rows.at[t, 1], at.chip_dev(t)) for t in near}
    half_ff = [pl.ds(0, ff // 2), pl.ds(ff // 2, ff // 2)]

    def dn_part(who, i):
        return w_dn.at[half_ff[i], span(who, d_slice)]

    def fetch_dn(i):
        return net.push(w_dn_in.at[other, half_ff[i]], dn_part(z, i), at.z_dev(group))

    from_partner = [fetch_dn(0)]

    def hand_on(i):
        from_partner[i].wait_recv()
        for t in range(1, group):
            got_dn.append(net.push(dn_part(far, i), dn_part(far, i), at.z_dev(t)))

    got_dn = [net.push(w_dn_in.at[mine], d_cols(z), at.z_dev(t)) for t in range(1, group)]

    relayed = []

    def pass_rows(t):
        if t in from_chip:
            from_chip[t].wait_recv()
        else:
            arrive(relayed)
        from_mate[t] = net.push(rows.at[t, 1], rows.at[t, 0], at.mate())

    lanes = lax.broadcasted_iota(jnp.int32, (four, 128), 1)

    def up_rows(t):
        logits = mm_nt(rows[t].reshape(four, width), router_t[...])
        chosen = mask_t[t].reshape(four, 128).astype(f32) > 0
        masked = jnp.where(chosen, logits, neg_fill)
        raised = jnp.where(chosen, jnp.exp(masked - jnp.max(masked, axis=1, keepdims=True)), 0.0)
        weight = raised / jnp.sum(raised, axis=1, keepdims=True)
        weight = jnp.sum(jnp.where(lanes == expert, weight, 0.0), axis=1, keepdims=True)
        w_r[t] = jnp.broadcast_to(weight, (four, 128))

        def up(j, _):
            tile, tile_u = span(j, fine), pl.ds(pl.multiple_of(ff + j * fine, fine), fine)
            x = rows[t].reshape(four, width)
            g = mm(x, w_gu[:, tile])
            u = mm(x, w_gu[:, tile_u])
            d_pre[t, :, tile] = g.astype(bf16)
            d_pre[t, :, tile_u] = u.astype(bf16)
            hid[t, :, tile] = (g * jax.nn.sigmoid(g) * u).astype(bf16)
            return 0

        lax.fori_loop(0, ff // fine, up, 0)

    for c in masks:
        c.wait()
    pair.wait()
    from_mate[0].wait_recv()
    for c in loads:
        c.wait()
    up_rows(0)
    from_partner.append(fetch_dn(1))
    for i in near:
        pass_rows(i)
        if beyond:
            part = pl.ds((2 - i) * (two // 2), two // 2)
            relayed.append(net.push(rows.at[i, 1, part], rows.at[3, 1, part], at.chip_dev(3 - i)))
    hand_on(0)
    for t in near:
        from_mate[t].wait_recv()
        up_rows(t)
    hand_on(1)
    for t in beyond:
        pass_rows(t)
        from_mate[t].wait_recv()
        up_rows(t)
    load_dn.wait()
    arrive(got_dn)

    mates, outs = {}, []

    def finish(t):
        arrive(mates[t])

        def add_rows(i, _):
            r = span(i, step)
            own[t, r, :] = (own[t, r, :].astype(f32) + core_in[t, r, :].astype(f32)).astype(bf16)
            own_x[t, r, :] = (own_x[t, r, :].astype(f32) + core_x[t, r, :].astype(f32)).astype(bf16)
            return 0

        lax.fori_loop(0, two // step, add_rows, 0)
        if t:
            outs.append(net.push(own.at[t], db_in.at[t], at.chip_dev(t)))
            outs.append(net.push(own_x.at[t], ex_in.at[t], at.chip_dev(t)))

    used = {}
    for i, t in enumerate(order):
        d_r[...] = jnp.zeros_like(d_r)
        for c in fetched[t]:
            c.wait()

        def back_y(n, _, t=t):
            tile = span(n, wide)
            y = mm(hid[t], w_dn[:, tile]).astype(bf16).astype(f32)
            c = cot_t[:, :, tile].reshape(four, wide).astype(f32)
            w = w_r[t, :, 0:1]
            d_r[...] += jnp.broadcast_to(jnp.sum(c * y, axis=1, keepdims=True), (four, 128))
            d_y[t, :, tile] = (w * c).astype(bf16)
            cot_t[:, :, tile] = (w * y).astype(bf16).reshape(2, two, wide)
            return 0

        lax.fori_loop(0, width // wide, back_y, 0)
        kept = [
            net.copy(cot_t.at[0], out_part.at[at.slot(t, 1)]),
            net.copy(cot_t.at[1], out_part.at[at.slot(t)]),
        ]
        if i:
            finish(order[i - 1])

        def back_h(j, _, t=t):
            tile, tile_u = span(j, fine), pl.ds(pl.multiple_of(ff + j * fine, fine), fine)
            d_h = mm_nt(d_y[t], w_dn[tile, :])
            g, u = d_pre[t, :, tile].astype(f32), d_pre[t, :, tile_u].astype(f32)
            sig = jax.nn.sigmoid(g)
            d_pre[t, :, tile] = (d_h * u * sig * (1.0 + g * (1.0 - sig))).astype(bf16)
            d_pre[t, :, tile_u] = (d_h * g * sig).astype(bf16)
            return 0

        lax.fori_loop(0, ff // fine, back_h, 0)
        for c in kept:
            c.wait()
        if i + 1 < at.chips:
            fetched[order[i + 1]] = fetch(order[i + 1])
        p = i % 2
        for c in used.pop(p, []):
            net.done(c)

        def back_b(n, _, t=t, p=p):
            tile = span(n, wide)
            value = mm_nt(d_pre[t], w_gu[tile, :]).astype(bf16)
            stage[p, :, tile] = value[:two]
            own[t, :, tile] = value[two:]
            return 0

        lax.fori_loop(0, width // wide, back_b, 0)
        routed = d_r[...]
        high = routed.astype(bf16)
        low = (routed - high.astype(f32)).astype(bf16)
        none = jnp.zeros_like(high)
        extra = jnp.where(lanes == expert, high, jnp.where(lanes == expert + 64, low, none))
        stage_x[p] = extra[:two]
        own_x[t] = extra[two:]
        mates[t] = [
            net.push(stage.at[p], core_in.at[t], at.mate()),
            net.push(stage_x.at[p], core_x.at[t], at.mate()),
        ]
        used[p] = mates[t]
    finish(order[-1])
    keep = [net.copy(own.at[0], db_in.at[0]), net.copy(own_x.at[0], ex_in.at[0])]

    part = tiled(width, 256)
    per = d_slice // part

    def out_copy(slot, i):
        who = z ^ (n_slices - 1 - i // per)
        return pltpu.make_async_copy(g_tile.at[slot], ggu.at[who, span(i % per, part)], tile_sem.at[slot])

    def grad_up(i, _):
        slot = i % 2

        @pl.when(i >= 2)
        def _():
            out_copy(slot, i - 2).wait()

        who = z ^ (n_slices - 1 - i // per)
        x = rows[:, :, :, span(who * per + i % per, part)].reshape(at.chips * four, part)
        g_tile[slot] = mm_tn(x, d_pre[...].reshape(at.chips * four, ff2)).astype(bf16)
        out_copy(slot, i).start()
        return 0

    def down_copy(slot, i):
        return pltpu.make_async_copy(d_tile.at[slot], gdn.at[span(i, fine)], tile_sem.at[slot])

    def grad_down(i, _):
        slot = i % 2

        @pl.when(i >= 2)
        def _():
            down_copy(slot, i - 2).wait()

        h = hid[:, :, span(i, fine)].reshape(at.chips * four, fine)
        d_tile[slot] = mm_tn(h, d_y[...].reshape(at.chips * four, width)).astype(bf16)
        down_copy(slot, i).start()
        return 0

    n_down = ff // fine
    lax.fori_loop(0, n_down, grad_down, 0)
    for i in range(max(0, n_down - 2), n_down):
        down_copy(i % 2, i).wait()
    for t in range(1, group):
        outs.append(net.push(gdn.at[:, span(z ^ t ^ group, d_slice)], land_dn.at[t - 1], at.z_dev(t)))
    n_up, n_early = width // part, (group - 1) * per
    lax.fori_loop(0, n_early, grad_up, 0)
    for i in range(n_early - 2, n_early):
        out_copy(i % 2, i).wait()

    def grad_rest(i, _):
        slot = i % 2

        @pl.when(i >= n_early + 2)
        def _():
            out_copy(slot, i - 2).wait()

        who = z ^ (n_slices - 1 - i // per)
        x = rows[:, :, :, span(who * per + i % per, part)].reshape(at.chips * four, part)
        g_tile[slot] = mm_tn(x, d_pre[...].reshape(at.chips * four, ff2)).astype(bf16)
        out_copy(slot, i).start()
        return 0

    lax.fori_loop(n_early, n_up, grad_rest, 0)
    for i in range(n_up - 2, n_up):
        out_copy(i % 2, i).wait()
    for c in keep:
        c.wait()
    arrive(outs)
    net.sent()


def norm_kernel(
    dims, early, db, ex, ggu, gdn, out_part, x1, b, cot, mask, router_t, gains,
    gx1, do_all, gain_two, g_router, land_gu, late_gu, land_dn, out_own_sum, out_sum,
    own, own_x, half_out, half_x, swap_in, swap_x, logit, d_out, out_own, out_core, out_in, rw,
    send, recv, local,
):
    at = Place(*dims)
    net = Net(send, recv, local)
    z, e, group = at.z, at.e, at.group
    tok = x1.shape[0]
    n_parts = db.shape[0]
    loads = [net.copy(db, own), net.copy(ex, own_x)]
    load_own = {t: net.copy(out_part.at[at.slot(t)], out_own.at[t]) for t in halves(at)}
    greet(everyone(at))
    step = 16
    for c in loads:
        c.wait()

    def sums(src):
        total, total_x = own[0, src, :].astype(f32), own_x[0, src, :].astype(f32)
        for t in range(1, n_parts):
            total += own[t, src, :].astype(f32)
            total_x += own_x[t, src, :].astype(f32)
        return total, total_x

    def partner(i, _):
        total, total_x = sums(pl.ds(pl.multiple_of(tok + i * step, step), step))
        half_out[span(i, step), :] = total.astype(bf16)
        half_x[span(i, step), :] = total_x.astype(bf16)
        return 0

    lax.fori_loop(0, tok // step, partner, 0)
    swaps = [net.push(half_out, swap_in, at.z_dev(group)), net.push(half_x, swap_x, at.z_dev(group))]
    d_slice = ggu.shape[1]
    landed = []
    for t in range(1, group):
        j = z ^ t ^ group
        landed.append(net.push(ggu.at[j, pl.ds(0, d_slice // 2)], land_gu.at[t - 1], at.z_dev(t)))
        if not early:
            landed.append(net.push(gdn.at[:, span(j, d_slice)], land_dn.at[t - 1], at.z_dev(t)))
        landed.append(net.push(ggu.at[j, pl.ds(d_slice // 2, d_slice // 2)], late_gu.at[t - 1], at.z_dev(t)))
    mates = {t: net.push(out_part.at[at.slot(t, 1)], out_core.at[t], at.mate()) for t in halves(at)}
    logits = mm_nt(b[...], router_t[...])
    chosen = mask[...].astype(f32) > 0
    masked = jnp.where(chosen, logits, neg_fill)
    raised = jnp.where(chosen, jnp.exp(masked - jnp.max(masked, axis=1, keepdims=True)), 0.0)
    rw[...] = raised / jnp.sum(raised, axis=1, keepdims=True)
    outs = []
    for t in halves(at):
        load_own[t].wait()
        mates[t].wait_recv()

        def add(i, _, t=t):
            rows = span(i, step)
            out_own[t, rows, :] = (out_own[t, rows, :].astype(f32) + out_core[t, rows, :].astype(f32)).astype(bf16)
            return 0

        lax.fori_loop(0, 2 * tok // step, add, 0)
        if t:
            outs.append(net.push(out_own.at[t], out_in.at[t - 1], at.chip_dev(t)))
    arrive(swaps)
    gain_two[...] = jnp.zeros_like(gain_two)

    def owner(i, _):
        rows = span(i, step)
        grad, routed = sums(rows)
        grad += swap_in[rows, :].astype(f32)
        routed += swap_x[rows, :].astype(f32)
        routed = routed + pltpu.roll(routed, 64, 1)
        weight = rw[rows, :]
        d_logit = weight * (routed - jnp.sum(weight * routed, axis=1, keepdims=True))
        high = d_logit.astype(bf16)
        low = (d_logit - high.astype(f32)).astype(bf16)
        logit[0, rows, :] = high
        logit[1, rows, :] = low
        grad += mm(high, router_t[...]) + mm(low, router_t[...])
        value = x1[rows, :]
        r = inv_rms(value)
        c = grad * gains[1:2, :]
        back = cot[rows, :].astype(f32) + r * c - value * (r * r * r * jnp.mean(c * value, axis=-1, keepdims=True))
        gx1[rows, :] = back
        d_out[rows, :] = back.astype(bf16)
        gain_two[...] += eight(grad * value * r)
        return 0

    lax.fori_loop(0, tok // step, owner, 0)
    mine = do_all.at[span(z, tok)]
    keep = net.copy(d_out, mine)
    copies = [net.push(d_out, mine, at.z_dev(t)) for t in range(1, at.n_shard)]
    g_router[...] = mm_tn(logit[0], b[...]) + mm_tn(logit[1], b[...])
    arrive(outs)

    def out_rows(i):
        rows = span(i, step)
        total = out_own[0, rows, :].astype(f32)
        for t in range(1, at.chips):
            total += out_in[t - 1, rows, :].astype(f32)
        return total.astype(bf16)

    def own_rows(i, _):
        out_own_sum[span(i, step), :] = out_rows(i)
        return 0

    def partner_rows(i, _):
        out_sum[span(i, step), :] = out_rows(tok // step + i)
        return 0

    lax.fori_loop(0, tok // step, own_rows, 0)
    lax.fori_loop(0, tok // step, partner_rows, 0)
    keep.wait()
    arrive(copies + landed)
    net.sent()


def back_kernel(
    dims, do_h, w_out, o_h, q_h, k_h, v_h, raw_h, cos_h, sin_h, seg_h, a_h, heads_h, ggu, gdn, land_gu, late_gu, land_dn, out_sum,
    out_sum_own, small, x1, gx1, x, gains, gain_two, g_router,
    hidden, g_hidden, small_sum, g_att, g_qkv, two_gu, own_gu, two_dn, own_dn,
    do_all, w_o, o, q, k, v, raw, cos, sin, seg_col, seg_row, mix, d_qkv, dk, dv, qk_gain, a, heads,
    sum_gu, add_gu, sum_dn, add_dn, swap_in, g_out, g_core, g_in, share_own,
    parts_in, g_heads, core_in, chip_in, mine, turn_in, share_qkv, sm, sm_z, sm_core, sm_chip,
    send, recv, local,
):
    at = Place(*dims)
    net = Net(send, recv, local)
    z, e, group = at.z, at.e, at.group
    length, width = do_all.shape
    tok = x1.shape[0]
    cols = raw.shape[1]
    hd = cols - 2 * HEAD_DIM
    n_heads = hd // HEAD_DIM
    rows_e = heads.shape[2]
    d_slice = ggu.shape[1]
    scale = HEAD_DIM ** (-0.5)
    block = tok
    step = 16
    far = z ^ group

    def d_cols(ref, who):
        return ref.at[:, span(who, d_slice)]

    cut = d_slice // 2
    halves_gu = [pl.ds(0, cut), pl.ds(cut, cut)]
    load_gu = [
        [net.copy(ggu.at[far, r], sum_gu.at[i])] + [net.copy(land.at[t - 1], add_gu.at[i, t - 1]) for t in range(1, group)]
        for i, (r, land) in enumerate(zip(halves_gu, (land_gu, late_gu)))
    ]
    load_a = [net.copy(do_h, do_all), net.copy(o_h, o)]
    load_b = [
        net.copy(s, d)
        for s, d in ((w_out, w_o), (q_h, q), (k_h, k), (v_h, v), (raw_h, raw), (cos_h, cos), (sin_h, sin), (seg_h, seg_col))
    ]
    load_c = [net.copy(a_h, a), net.copy(heads_h, heads)]
    load_dn = [net.copy(d_cols(gdn, far), sum_dn)] + [net.copy(land_dn.at[t - 1], add_dn.at[t - 1]) for t in range(1, group)]
    greet(everyone(at))
    swap = net.push(out_sum, swap_in, at.z_dev(group))

    def add_up(total, adds):
        def rows_of(i, _):
            rows = span(i, step)
            value = total[rows, :].astype(f32)
            for t in range(1, group):
                value += adds[t - 1, rows, :].astype(f32)
            total[rows, :] = value.astype(bf16)
            return 0

        lax.fori_loop(0, total.shape[0] // step, rows_of, 0)

    got = []

    def send_half(i):
        for c in load_gu[i]:
            c.wait()
        add_up(sum_gu.at[i], add_gu.at[i])
        got.append(net.push(sum_gu.at[i], two_gu.at[halves_gu[i]], at.z_dev(group)))

    send_half(0)
    for t in range(1, group):
        got.append(net.push(ggu.at[z ^ t], own_gu.at[t - 1], at.z_dev(t)))

    for c in load_a:
        c.wait()
    share = share_own.shape[0]
    wide = tiled(hd, 256)
    each = wide // share

    def out_grad(i, _):
        tile = mm_tn(o[:, span(i, wide)], do_all[...]).astype(bf16)
        for j in range(each):
            g_out[each * i + j] = tile[j * share : (j + 1) * share]
        return 0

    lax.fori_loop(0, hd // wide, out_grad, 0)
    g_mates = {t: net.push(g_out.at[at.slot(t, 1)], g_core.at[t], at.mate()) for t in halves(at)}
    for c in load_b:
        c.wait()
    qk = []
    for s in range(at.n_shard):
        rows = small[s, 0:16, :].astype(f32)
        seg_row[0:1, span(s, tok)] = rows[4:5, :tok]
        qk.append(rows[2:4, :HEAD_DIM])
    qk = sum(qk[1:], qk[0])

    def mix_tile(i, _):
        tile = span(i, wide)
        mix[:, tile] = mm_nt(do_all[...], w_o[tile, :]).astype(bf16)
        return 0

    lax.fori_loop(0, hd // wide, mix_tile, 0)
    g_outs = []
    for t in halves(at):
        g_mates[t].wait_recv()

        def add(i, _, t=t):
            rows = span(i, step)
            s = at.slot(t)
            g_out[s, rows, :] = (g_out[s, rows, :].astype(f32) + g_core[t, rows, :].astype(f32)).astype(bf16)
            return 0

        lax.fori_loop(0, share // step, add, 0)
        if t:
            g_outs.append(net.push(g_out.at[at.slot(t)], g_in.at[t - 1], at.chip_dev(t)))
    send_half(1)

    dk[...] = jnp.zeros_like(dk)
    dv[...] = jnp.zeros_like(dv)
    qk_gain[...] = jnp.zeros_like(qk_gain)

    def one_head(h, _):
        lanes = span(h, HEAD_DIM)
        for i in range(length // block):
            rows, keys = pl.ds(i * block, block), pl.ds(0, (i + 1) * block)
            soft = soft_block(q, k, seg_row, seg_col, h, i, block, scale)
            d_mix = mix[rows, lanes]
            d_soft = mm_nt(d_mix, v[keys, :])
            d_scores = (soft * (d_soft - jnp.sum(soft * d_soft, axis=-1, keepdims=True))).astype(bf16)
            dv[keys, :] += mm_tn(soft.astype(bf16), d_mix)
            dk[keys, :] += mm_tn(d_scores, q[rows, lanes]) * scale
            dq = mm(d_scores, k[keys, :]) * scale
            value = raw[rows, lanes]
            back, per = rms_back(value, qk[0:1], rope_rows_back(dq, cos[rows, :], sin[rows, :]))
            d_qkv[rows, lanes] = back.astype(bf16)
            qk_gain[0:8, :] += eight(per)
        return 0

    lax.fori_loop(0, n_heads, one_head, 0)
    for i in range(length // block):
        rows = pl.ds(i * block, block)
        value = raw[rows, pl.ds(hd, HEAD_DIM)]
        back, per = rms_back(value, qk[1:2], rope_rows_back(dk[rows, :], cos[rows, :], sin[rows, :]))
        d_qkv[rows, pl.ds(hd, HEAD_DIM)] = back.astype(bf16)
        d_qkv[rows, pl.ds(hd + HEAD_DIM, HEAD_DIM)] = dv[rows, :].astype(bf16)
        qk_gain[8:16, :] += eight(per)

    arrive(g_outs)

    def own_share(i, _):
        rows = span(i, step)
        total = g_out[e, rows, :].astype(f32)
        for t in range(1, at.chips):
            total += g_in[t - 1, rows, :].astype(f32)
        share_own[rows, :] = total.astype(bf16)
        return 0

    lax.fori_loop(0, share // step, own_share, 0)
    keep_att = net.copy(share_own, g_att.at[e])
    keep_att.wait()
    atts = [lambda who: g_att.at[who]]
    att_state = spread(net, at, atts)
    for c in load_c:
        c.wait()
    wide_d = tiled(d_slice, 256)
    each_d = wide_d // rows_e

    def grad_tile(s, _):
        for j in range(d_slice // wide_d):
            some = a[:, pl.ds(pl.multiple_of(s * d_slice + j * wide_d, wide_d), wide_d)]
            tile = mm_tn(some, d_qkv[...]).astype(bf16)
            for i in range(each_d):
                g_heads[each_d * j + i, s] = tile[i * rows_e : (i + 1) * rows_e]
        return 0

    lax.fori_loop(0, at.n_shard, grad_tile, 0)
    mates = {t: net.push(g_heads.at[at.slot(t, 1)], core_in.at[t], at.mate()) for t in halves(at)}
    part = do_all

    def rows_tile(s, _):
        for j in range(d_slice // wide_d):
            some = heads[s, pl.ds(each_d * j, each_d)].reshape(wide_d, cols)
            here = pl.ds(pl.multiple_of(s * d_slice + j * wide_d, wide_d), wide_d)
            part[:, here] = mm_nt(d_qkv[...], some).astype(bf16)
        return 0

    lax.fori_loop(0, at.n_shard, rows_tile, 0)
    sums = Scatter(net, at, part, parts_in, tok, step)
    chips = []
    for t in halves(at):
        mates[t].wait_recv()
        who = at.slot(t)

        def add(s, _, t=t, who=who):
            g_heads[who, s] = (g_heads[who, s].astype(f32) + core_in[t, s].astype(f32)).astype(bf16)
            return 0

        lax.fori_loop(0, at.n_shard, add, 0)
        if t:
            chips.append(net.push(g_heads.at[who], chip_in.at[t - 1], at.chip_dev(t)))
    more = sums.advance()
    for c in load_dn:
        c.wait()
    add_up(sum_dn, add_dn)
    swap.wait_recv()

    def hidden_rows(i, _):
        rows = span(i, step)
        hidden[rows, :] = (x1[rows, :] + out_sum_own[rows, :].astype(f32) + swap_in[rows, :].astype(f32)).astype(bf16)
        return 0

    lax.fori_loop(0, tok // step, hidden_rows, 0)
    arrive(chips)

    def total(s, _):
        value = g_heads[e, s].astype(f32)
        for t in range(1, at.chips):
            value += chip_in[t - 1, s].astype(f32)
        mine[s] = value.astype(bf16)
        return 0

    lax.fori_loop(0, at.n_shard, total, 0)
    turns = [net.push(mine.at[z ^ t], turn_in.at[z], at.z_dev(t)) for t in range(1, at.n_shard)]
    turn_own = net.copy(mine.at[z], turn_in.at[z])
    got.append(net.push(sum_dn, two_dn, at.z_dev(group)))
    for t in range(1, group):
        got.append(net.push(d_cols(gdn, z ^ t), own_dn.at[t - 1], at.z_dev(t)))
    slots = sums.finish() if more else sums.last
    sm[...] = jnp.zeros_like(sm)
    gain_one = jnp.zeros((8, width), f32)

    def owner(i, gain_one):
        rows = span(i, step)
        here = pl.ds(pl.multiple_of(z * tok + i * step, step), step)
        da = part[here, :].astype(f32)
        for t in slots:
            da += parts_in[t, rows, :].astype(f32)
        back, per = rms_back(x[rows, :].astype(f32), gains[0:1, :], da)
        g_hidden[rows, :] = gx1[rows, :] + back
        return gain_one + eight(per)

    gain_one = lax.fori_loop(0, tok // step, owner, gain_one)
    row_one = jnp.sum(gain_one, axis=0, keepdims=True)
    row_two = jnp.sum(gain_two[...], axis=0, keepdims=True)
    row_q = jnp.sum(qk_gain[0:8, :], axis=0, keepdims=True)
    row_k = jnp.sum(qk_gain[8:16, :], axis=0, keepdims=True)
    for s in range(at.n_shard):
        piece = pl.ds(s * d_slice, d_slice)
        lanes = slice(s * d_slice, (s + 1) * d_slice)
        sm[s, 0:1, :] = row_one[:, lanes]
        sm[s, 1:2, :] = row_two[:, lanes]
        sm[s, 2:3, pl.ds(0, HEAD_DIM)] = row_q
        sm[s, 3:4, pl.ds(0, HEAD_DIM)] = row_k
        sm[s, 8:, :] = g_router[0 : sm.shape[1] - 8, piece]
    small_z = [net.push(sm.at[z ^ t], sm_z.at[t - 1], at.z_dev(t)) for t in range(1, at.n_shard)]
    turn_own.wait()
    arrive(turns)
    for s in range(at.n_shard):
        share_qkv[:, pl.ds(s * hd, hd)] = turn_in[s, :, pl.ds(0, hd)]
    for m in range(KV_HEADS):
        some = [s for s in range(at.n_shard) if (s * n_heads) // (HEADS // KV_HEADS) == m]
        for first, to in ((hd, HEADS + m), (hd + HEAD_DIM, HEADS + KV_HEADS + m)):
            value = turn_in[some[0], :, pl.ds(first, HEAD_DIM)].astype(f32)
            for s in some[1:]:
                value += turn_in[s, :, pl.ds(first, HEAD_DIM)].astype(f32)
            share_qkv[:, pl.ds(to * HEAD_DIM, HEAD_DIM)] = value.astype(bf16)
    keep = net.copy(share_qkv, g_qkv.at[e])
    keep.wait()
    if at.chips == 4:
        go_on = spread_near(net, at, g_qkv)
    else:
        qkvs = [lambda who: g_qkv.at[who]]
        state = spread(net, at, qkvs)
        go_on = functools.partial(pass_on, net, at, qkvs, state)
    last = pass_on(net, at, atts, att_state)
    arrive(small_z)
    value = sm[z]
    for t in range(1, at.n_shard):
        value += sm_z[t - 1]
    sm[z] = value
    c = net.push(sm.at[z], sm_core, at.mate())
    c.wait_recv()
    sm_core[...] = sm[z] + sm_core[...]
    smalls = [net.push(sm_core, sm_chip.at[t - 1], at.chip_dev(t)) for t in range(1, at.chips)]
    last += go_on()
    arrive(smalls)
    value = sm_core[...]
    for t in range(1, at.chips):
        value += sm_chip[t - 1]
    small_sum[...] = value
    arrive(last + got)
    net.sent()


def shards(
    hidden_in,
    segments,
    routes,
    norm_gains,
    qk_gains,
    w_qkv,
    w_attn_out,
    w_router,
    w_gate_up,
    w_down,
    cotangent,
):
    n_expert = lax.axis_size("expert")
    n_shard = lax.axis_size("shard")
    me_e = lax.axis_index("expert")
    me_z = lax.axis_index("shard")
    tok, width = hidden_in.shape
    exp_dev = w_gate_up.shape[1]
    experts_all = w_router.shape[2]
    d_slice, ff2 = w_gate_up.shape[2:]
    ff = ff2 // 2
    group = n_shard // exp_dev
    mine = me_z // group
    length = n_shard * tok
    h_dev = HEADS // n_shard
    hd = h_dev * HEAD_DIM
    cols = hd + 2 * HEAD_DIM
    qkv_cols = w_qkv.shape[2]
    rows_e = d_slice // n_expert
    share = hd // n_expert
    chips = n_expert // 2
    qk_part = HEAD_DIM // n_shard
    dims = (n_expert, n_shard, group)
    n_small = 16 + experts_all
    sds = jax.ShapeDtypeStruct
    vm = pltpu.VMEM
    any_spec = pl.BlockSpec(memory_space=pl.ANY)
    vmem_spec = pl.BlockSpec(memory_space=pltpu.VMEM)

    lane = jnp.arange(HEAD_DIM, dtype=jnp.int32)
    qk_placed = jnp.where((lane // qk_part == me_z)[None], jnp.tile(qk_gains[0], (1, n_shard)), jnp.zeros((), bf16))
    small = jnp.concatenate(
        [
            norm_gains[0],
            jnp.pad(qk_placed, ((0, 0), (0, d_slice - HEAD_DIM))),
            jnp.pad(segments.astype(bf16)[None], ((0, 11), (0, d_slice - tok))),
            w_router[0].T,
        ],
        axis=0,
    )
    seg_own = jnp.broadcast_to(segments.astype(f32)[:, None], (tok, 128))
    ids = jnp.arange(128, dtype=jnp.int32)
    mask = jnp.sum((routes[:, :, None] == ids[None, None, :]).astype(f32), axis=1).astype(bf16)
    cos, sin = rotary_tables(length)

    outs = [
        sds((n_shard, n_small, d_slice), bf16),
        sds((length, 128), f32),
        sds((n_shard, n_expert, rows_e, cols), bf16),
        sds((length, width), bf16),
        sds((length, cols), f32),
        sds((length, hd), bf16),
        sds((length, HEAD_DIM), bf16),
        sds((length, HEAD_DIM), bf16),
        sds((length, hd), bf16),
        sds((tok, width), f32),
        sds((tok, width), bf16),
        sds((n_shard, d_slice, ff2), bf16),
        sds((n_expert, 2 * tok, width), bf16),
        sds((n_expert, 2 * tok, 128), bf16),
        sds((2 * tok, width), bf16),
        sds((8, width), f32),
        sds((128, width), bf16),
    ]
    front = comm_call(
        functools.partial(front_kernel, dims),
        0,
        160,
        40,
        [
            vm((length, width), bf16),
            vm((n_shard, n_small, d_slice), bf16),
            vm((length, 128), f32),
            vm((n_shard, n_expert, rows_e, cols), bf16),
            vm((length, width), bf16),
            vm((length, cols), f32),
            vm((length, hd), bf16),
            vm((length, HEAD_DIM), bf16),
            vm((length, HEAD_DIM), bf16),
            vm((length, hd), bf16),
            vm((hd, width), bf16),
            vm((length, width), bf16),
            vm((n_shard - 1, tok, width), bf16),
            vm((length, HEAD_DIM), f32),
            vm((length, HEAD_DIM), f32),
            vm((8, length), f32),
            vm((tok, width), f32),
            vm((tok, width), bf16),
        ],
        outs,
        56,
        out_specs=[any_spec] * (len(outs) - 2) + [vmem_spec] * 2,
    )
    (small_all, seg_col, heads, a, raw, q, k, v, o, x1, b, gate_up, cot_all, mask_all, b_pair, gains, router_pad) = front(
        hidden_in, small, seg_own, w_qkv[0], w_attn_out[0], w_gate_up[0], cotangent, mask, cos, sin
    )
    router_t = router_pad[:experts_all]

    def route_weights(rows, chosen):
        logits = mm_nt(rows, router_t)
        masked = jnp.where(chosen, logits, neg_fill)
        raised = jnp.where(chosen, jnp.exp(masked - jnp.max(masked, axis=1, keepdims=True)), 0.0)
        return raised / jnp.sum(raised, axis=1, keepdims=True)

    per_e = (n_expert, 2 * tok)
    piece = (chips, 2 * tok)
    four = 4 * tok
    if chips <= 4:
        out_part, grad_gate_up, grad_down, db_in, ex_in, land_dn = comm_call(
            functools.partial(expert_kernel, dims),
            4,
            60,
            60,
            [
                vm((width, ff2), bf16),
                vm((ff, width), bf16),
                vm((chips, 2, 2 * tok, width), bf16),
                vm((2, 2 * tok, width), bf16),
                vm((chips, 2, 2 * tok, 128), bf16),
                vm((chips, four, ff), bf16),
                vm((chips, four, ff2), bf16),
                vm((chips, four, width), bf16),
                vm((2, 2 * tok, width), bf16),
                vm((2, 2 * tok, 128), bf16),
                vm(piece + (width,), bf16),
                vm(piece + (128,), bf16),
                vm(piece + (width,), bf16),
                vm(piece + (128,), bf16),
                vm((chips, four, 128), f32),
                vm((four, 128), f32),
                vm((2, tiled(width, 256), ff2), bf16),
                vm((2, tiled(ff, 256), width), bf16),
                pltpu.SemaphoreType.DMA((2,)),
            ],
            [
                sds(per_e + (width,), bf16),
                sds((n_shard, d_slice, ff2), bf16),
                sds((ff, width), bf16),
                sds(piece + (width,), bf16),
                sds(piece + (128,), bf16),
                sds((group - 1, ff, d_slice), bf16),
            ],
            60,
            in_specs=[any_spec] * 6 + [vmem_spec],
        )(b_pair, cot_all, mask_all, gate_up, w_gate_up[0], w_down[0], router_pad)
    else:
        rows_all = n_expert * 2 * tok
        w_mine = lax.dynamic_index_in_dim(w_gate_up[0], mine, 0, keepdims=False)
        gate_up = lax.dynamic_update_index_in_dim(gate_up, w_mine, me_z, 0)
        down = lax.all_gather(w_down[0], "shard", axis=2, tiled=True)
        down = lax.dynamic_index_in_dim(down, mine, 0, keepdims=False)
        b_rows = lax.all_gather(b_pair, "expert", axis=0, tiled=True)
        my_expert = me_e * exp_dev + mine
        rw_all = route_weights(b_rows, mask_all.reshape(rows_all, 128)[:, :experts_all] > 0)
        is_mine = ids[:experts_all] == my_expert
        rw_mine = jnp.sum(jnp.where(is_mine[None, :], rw_all, 0.0), axis=1, keepdims=True)
        w_gu = gate_up.reshape(width, ff2)
        pre = mm(b_rows, w_gu)
        g, u = pre[:, :ff], pre[:, ff:]
        sig = jax.nn.sigmoid(g)
        act = g * sig
        hidden = (act * u).astype(bf16)
        y_f = mm(hidden, down).astype(bf16).astype(f32)
        cot_f = cot_all.reshape(rows_all, width).astype(f32)
        d_route = jnp.sum(cot_f * y_f, axis=1, keepdims=True)
        out_part = (rw_mine * y_f).astype(bf16)
        d_y = (rw_mine * cot_f).astype(bf16)
        d_hidden = mm_nt(d_y, down)
        d_pre = jnp.concatenate(
            [d_hidden * u * sig * (1.0 + g * (1.0 - sig)), d_hidden * act], axis=1
        ).astype(bf16)
        d_b = mm_nt(d_pre, w_gu).astype(bf16)
        grad_down = mm_tn(hidden, d_y).astype(bf16)
        grad_gate_up = mm_tn(b_rows, d_pre).astype(bf16).reshape(n_shard, d_slice, ff2)
        high = lax.reduce_precision(d_route, 8, 7)
        low = d_route - high
        extra = jnp.where(ids[None] == my_expert, high, jnp.where(ids[None] == my_expert + 64, low, 0.0)).astype(bf16)

        def home(value):
            return lax.psum_scatter(value, "expert", scatter_dimension=0, tiled=True)[None]

        db_in, ex_in = home(d_b), home(extra)

    n_parts = db_in.shape[0]
    early = chips <= 4
    gx1, d_o, gain_two, g_router, land_gu, late_gu, norm_dn, out_own_sum, out_sum = comm_call(
        functools.partial(norm_kernel, dims, early),
        1,
        60,
        24,
        [
            vm((n_parts, 2 * tok, width), bf16),
            vm((n_parts, 2 * tok, 128), bf16),
            vm((tok, width), bf16),
            vm((tok, 128), bf16),
            vm((tok, width), bf16),
            vm((tok, 128), bf16),
            vm((2, tok, 128), bf16),
            vm((tok, width), bf16),
            vm(piece + (width,), bf16),
            vm(piece + (width,), bf16),
            vm((chips - 1, 2 * tok, width), bf16),
            vm((tok, 128), f32),
        ],
        [
            sds((tok, width), f32),
            sds((length, width), bf16),
            sds((8, width), f32),
            sds((128, width), f32),
            sds((group - 1, d_slice // 2, ff2), bf16),
            sds((group - 1, d_slice // 2, ff2), bf16),
            sds((group - 1, ff, d_slice), bf16) if not early else sds((16, 128), bf16),
            sds((tok, width), bf16),
            sds((tok, width), bf16),
        ],
        60,
        in_specs=[any_spec] * 5 + [vmem_spec] * 6,
        out_specs=[vmem_spec, any_spec, vmem_spec, vmem_spec] + [any_spec] * 3 + [vmem_spec] * 2,
    )(db_in, ex_in, grad_gate_up, grad_down, out_part.reshape(per_e + (width,)), x1, b, cotangent, mask, router_pad, gains)
    if not early:
        land_dn = norm_dn

    small_rows = (8 + -(-experts_all // 8) * 8, d_slice)
    hidden_out, grad_hidden, sums, grad_out, grad_qkv, two_gu, own_gu, two_dn, own_dn = comm_call(
        functools.partial(back_kernel, dims),
        2,
        140,
        60,
        [
            vm((length, width), bf16),
            vm((hd, width), bf16),
            vm((length, hd), bf16),
            vm((length, hd), bf16),
            vm((length, HEAD_DIM), bf16),
            vm((length, HEAD_DIM), bf16),
            vm((length, cols), f32),
            vm((length, HEAD_DIM), f32),
            vm((length, HEAD_DIM), f32),
            vm((length, 128), f32),
            vm((8, length), f32),
            vm((length, hd), bf16),
            vm((length, cols), bf16),
            vm((length, HEAD_DIM), f32),
            vm((length, HEAD_DIM), f32),
            vm((16, HEAD_DIM), f32),
            vm((length, width), bf16),
            vm((n_shard, n_expert, rows_e, cols), bf16),
            vm((2, d_slice // 2, ff2), bf16),
            vm((2, group - 1, d_slice // 2, ff2), bf16),
            vm((ff, d_slice), bf16),
            vm((group - 1, ff, d_slice), bf16),
            vm((tok, width), bf16),
            vm((n_expert, share, width), bf16),
            vm((chips, share, width), bf16),
            vm((chips - 1, share, width), bf16),
            vm((share, width), bf16),
            vm((n_shard - 1, tok, width), bf16),
            vm((n_expert, n_shard, rows_e, cols), bf16),
            vm((chips, n_shard, rows_e, cols), bf16),
            vm((chips - 1, n_shard, rows_e, cols), bf16),
            vm((n_shard, rows_e, cols), bf16),
            vm((n_shard, rows_e, cols), bf16),
            vm((rows_e, qkv_cols), bf16),
            vm((n_shard,) + small_rows, f32),
            vm((n_shard - 1,) + small_rows, f32),
            vm(small_rows, f32),
            vm((chips - 1,) + small_rows, f32),
        ],
        [
            sds((tok, width), bf16),
            sds((tok, width), f32),
            sds(small_rows, f32),
            sds((n_expert, share, width), bf16),
            sds((n_expert, rows_e, qkv_cols), bf16),
            sds((d_slice, ff2), bf16),
            sds((group - 1, d_slice, ff2), bf16),
            sds((ff, d_slice), bf16),
            sds((group - 1, ff, d_slice), bf16),
        ],
        60,
        in_specs=[any_spec] * 18 + [vmem_spec] * 8,
        out_specs=[vmem_spec] * 3 + [any_spec] * 6,
    )(
        d_o,
        w_attn_out[0],
        o,
        q,
        k,
        v,
        raw,
        cos,
        sin,
        seg_col,
        a,
        heads,
        grad_gate_up,
        grad_down,
        land_gu,
        late_gu,
        land_dn,
        out_sum,
        out_own_sum,
        small_all,
        x1,
        gx1,
        hidden_in,
        gains,
        gain_two,
        g_router,
    )

    def settle(own, others, other):
        total = own.astype(f32) + jnp.sum(others.astype(f32), axis=0)
        other = other.astype(f32)
        is_own = jnp.arange(exp_dev, dtype=jnp.int32)[:, None, None] == mine
        return jnp.where(is_own, total[None], other[None])[None]

    own_gate_up = lax.dynamic_index_in_dim(grad_gate_up, me_z, 0, keepdims=False)
    own_down = lax.dynamic_slice_in_dim(grad_down, me_z * d_slice, d_slice, 1)
    qk_grad = lax.dynamic_slice_in_dim(sums[2:4, :HEAD_DIM], me_z * qk_part, qk_part, 1)
    return (
        hidden_out,
        grad_hidden,
        sums[0:2][None],
        qk_grad[None],
        grad_qkv.reshape(d_slice, qkv_cols).astype(f32)[None],
        grad_out.reshape(hd, width).astype(f32)[None],
        sums[8 : 8 + experts_all].T[None],
        settle(own_gate_up, own_gu, two_gu),
        settle(own_down, own_dn, two_dn),
    )


def solution(mesh):
    in_specs = (
        P(("expert", "shard"), None),
        P(("expert", "shard")),
        P(("expert", "shard"), None),
        P(None, None, "shard"),
        P(None, None, "shard"),
        P(None, "shard", None),
        P(None, "shard", None),
        P(None, "shard", None),
        P(None, "expert", "shard", None),
        P(None, "expert", None, "shard"),
        P(("expert", "shard"), None),
    )
    out_specs = (
        P(("expert", "shard"), None),
        P(("expert", "shard"), None),
        P(None, None, "shard"),
        P(None, None, "shard"),
        P(None, "shard", None),
        P(None, "shard", None),
        P(None, "shard", None),
        P(None, "expert", "shard", None),
        P(None, "expert", None, "shard"),
    )
    return jax.shard_map(shards, mesh=mesh, in_specs=in_specs, out_specs=out_specs, check_vma=False)
```

```python
import functools

import jax
import jax.numpy as jnp
import numpy as np
from jax import lax
from jax.experimental import pallas as pl
from jax.experimental.pallas import tpu as pltpu
from jax.sharding import PartitionSpec as P

HEADS = 32
KV_HEADS = 4
HEAD_DIM = 128
TOP = 8

bf16 = jnp.bfloat16
f32 = jnp.float32
highest = lax.Precision.HIGHEST
eps_norm = 1e-06
rope_base = 1000000.0
neg_fill = -1e30


def dot(left, right, dims, out=f32):
    return lax.dot_general(left, right, (dims, ((), ())), preferred_element_type=out)


def mm(left, right):
    return dot(left, right, ((1,), (0,)))


def mm_nt(left, right):
    return dot(left, right, ((1,), (1,)))


def mm_tn(left, right):
    return dot(left, right, ((0,), (0,)))


def inv_rms(value):
    return lax.rsqrt(jnp.mean(value * value, axis=-1, keepdims=True) + eps_norm)


def rms_back(value, gain, grad):
    r = inv_rms(value)
    c = grad * gain
    back = r * c - value * (r * r * r) * jnp.mean(c * value, axis=-1, keepdims=True)
    return back, grad * value * r


def rotary_tables(length):
    half = HEAD_DIM // 2
    frequency = np.float32(rope_base) ** (-(np.arange(half, dtype=np.float32) * np.float32(2.0)) / np.float32(HEAD_DIM))
    angles = np.arange(length, dtype=np.float32)[:, None] * frequency[None, :].astype(np.float32)
    cos, sin = np.cos(angles), np.sin(angles)
    return jnp.asarray(np.concatenate([cos, cos], axis=1)), jnp.asarray(np.concatenate([-sin, sin], axis=1))


MESH = pl.DeviceIdType.MESH


class Place:
    def __init__(self, n_expert, n_shard, group):
        self.e = lax.axis_index("expert")
        self.z = lax.axis_index("shard")
        self.n_expert, self.n_shard, self.group = n_expert, n_shard, group
        self.chip, self.core = self.e // 2, self.e % 2
        self.chips = n_expert // 2

    def z_dev(self, t):
        return (self.e, self.z ^ t)

    def slot(self, t, other=0):
        return (self.chip ^ t) * 2 + (self.core ^ other)

    def chip_dev(self, t):
        return (self.slot(t), self.z)

    def mate(self):
        return (self.e ^ 1, self.z)


class Net:
    def __init__(self, send, recv, local):
        self.send, self.recv, self.local = send, recv, local
        self.n, self.m, self.open = 0, 0, []

    def push(self, src, dst, dev):
        i = self.n
        self.n += 1
        copy = pltpu.make_async_remote_copy(
            src_ref=src, dst_ref=dst, send_sem=self.send.at[i], recv_sem=self.recv.at[i],
            device_id=dev, device_id_type=MESH,
        )
        copy.start()
        self.open.append(copy)
        return copy

    def copy(self, src, dst):
        i = self.m
        self.m += 1
        copy = pltpu.make_async_copy(src, dst, self.local.at[i])
        copy.start()
        return copy

    def done(self, copy):
        copy.wait_send()
        self.open = [c for c in self.open if c is not copy]

    def sent(self):
        for copy in self.open:
            copy.wait_send()
        self.open = []


def greet(devices):
    barrier = pltpu.get_barrier_semaphore()
    for dev in devices:
        pl.semaphore_signal(barrier, inc=1, device_id=dev, device_id_type=MESH)
    pl.semaphore_wait(barrier, len(devices))


def everyone(at):
    return (
        [at.z_dev(t) for t in range(1, at.n_shard)]
        + [at.chip_dev(t) for t in range(1, at.chips)]
        + [at.mate()]
    )


def arrive(copies):
    for copy in copies:
        copy.wait_recv()


def spread(net, at, pieces):
    own = [p(at.e) for p in pieces]
    mate = [net.push(o, o, at.mate()) for o in own]
    out = [(t, [net.push(o, o, at.chip_dev(t)) for o in own]) for t in range(1, at.chips)]
    return mate, out


def pass_on(net, at, pieces, state):
    mate, out = state
    for t, copies in out:
        for p, copy in zip(pieces, copies):
            copy.wait_recv()
            got = p(at.slot(t))
            mate.append(net.push(got, got, at.mate()))
    return mate


def low_bit(k):
    return k & -k


class Gather:
    def __init__(self, net, at, own, ref, rows):
        self.net, self.at, self.ref, self.rows = net, at, ref, rows
        bits = [b for b in (1 << i for i in range(10)) if b < at.n_shard]
        self.bits = bits[::-1]
        here = self.place(0)
        self.copies = {b: net.push(own, here, at.z_dev(b)) for b in self.bits}

    def place(self, k):
        return self.ref.at[span(self.at.z ^ k, self.rows)]

    def finish(self, then=None):
        waiting = list(self.bits)
        while waiting:
            k = waiting.pop(0)
            self.copies[k].wait_recv()
            for b in self.bits:
                if b < low_bit(k):
                    got = self.place(k)
                    self.copies[k | b] = self.net.push(got, got, self.at.z_dev(b))
                    waiting.append(k | b)
            if then:
                then()
                then = None


class Scatter:
    def __init__(self, net, at, part, landing, rows, step):
        self.net, self.at, self.part, self.landing, self.rows, self.step = net, at, part, landing, rows, step
        self.slot, self.bit, self.last = 0, 1, []
        self.start()

    def block(self, k):
        return self.part.at[span(self.at.z ^ k, self.rows)]

    def start(self):
        bit, self.copies = self.bit, []
        for k in [k for k in range(self.at.n_shard - 1, 0, -1) if k % (2 * bit) == bit]:
            copy = self.net.push(self.block(k), self.landing.at[self.slot], self.at.z_dev(bit))
            self.copies.append((k ^ bit, self.slot, copy))
            self.slot += 1

    def advance(self):
        self.bit *= 2
        for to, i, copy in self.copies:
            copy.wait_recv()
            if not to:
                self.last.append(i)
                continue

            def add(j, _, to=to, i=i):
                r = span(j, self.step)
                here = pl.ds(pl.multiple_of((self.at.z ^ to) * self.rows + j * self.step, self.step), self.step)
                value = self.part[here, :].astype(f32) + self.landing[i, r, :].astype(f32)
                self.part[here, :] = value.astype(bf16)
                return 0

            lax.fori_loop(0, self.rows // self.step, add, 0)
        if self.bit < self.at.n_shard:
            self.start()
            return True
        return False

    def finish(self):
        while self.advance():
            pass
        return self.last


def spread_near(net, at, ref):
    own = ref.at[at.e]
    mate = [net.push(own, own, at.mate())]
    out = {t: net.push(own, own, at.chip_dev(t)) for t in (1, 2)}
    half = ref.shape[1] // 2

    def go_on():
        relayed = []
        for t in (1, 2):
            out[t].wait_recv()
            got = ref.at[at.slot(t)]
            mate.append(net.push(got, got, at.mate()))
            part = ref.at[at.slot(t), pl.ds((2 - t) * half, half)]
            relayed.append(net.push(part, part, at.chip_dev(3 - t)))
        arrive(relayed)
        got = ref.at[at.slot(3)]
        mate.append(net.push(got, got, at.mate()))
        return mate

    return go_on


def comm_call(kernel, cid, n_remote, n_local, scratch, outs, vmem_mb, in_specs=None, out_specs=None, cost=None):
    any_spec = pl.BlockSpec(memory_space=pl.ANY)

    def call(*args):
        return pl.pallas_call(
            kernel,
            out_shape=outs,
            in_specs=in_specs or [any_spec] * len(args),
            out_specs=out_specs or [any_spec] * len(outs),
            scratch_shapes=list(scratch)
            + [
                pltpu.SemaphoreType.DMA((n_remote,)),
                pltpu.SemaphoreType.DMA((n_remote,)),
                pltpu.SemaphoreType.DMA((n_local,)),
            ],
            compiler_params=pltpu.CompilerParams(
                collective_id=cid, has_side_effects=True, vmem_limit_bytes=vmem_mb << 20
            ),
            cost_estimate=cost,
        )(*args)

    return call


def tiled(size, most):
    while size % most:
        most //= 2
    return most


def halves(at):
    return list(range(1, at.chips)) + [0]


def rope_rows(value, cos, sin):
    return value * cos + pltpu.roll(value, HEAD_DIM // 2, 1) * sin


def rope_rows_back(grad, cos, sin):
    return grad * cos + pltpu.roll(grad * sin, HEAD_DIM // 2, 1)


def eight(per):
    return jnp.sum(per.reshape(per.shape[0] // 8, 8, per.shape[1]), axis=0)


def span(i, size):
    if isinstance(i, int):
        return pl.ds(i * size, size)
    return pl.ds(pl.multiple_of(i * size, size), size)


def soft_block(q_ref, k_ref, seg_row, seg_col, h, i, block, scale):
    rows, keys = pl.ds(i * block, block), pl.ds(0, (i + 1) * block)
    scores = mm_nt(q_ref[rows, span(h, HEAD_DIM)], k_ref[keys, :]) * scale
    width = (i + 1) * block
    at_q = i * block + lax.broadcasted_iota(jnp.int32, (block, width), 0)
    at_k = lax.broadcasted_iota(jnp.int32, (block, width), 1)
    allowed = (at_k <= at_q) & (seg_row[0:1, keys] == seg_col[rows, 0:1])
    scores = jnp.where(allowed, scores, neg_fill)
    raised = jnp.exp(scores - jnp.max(scores, axis=-1, keepdims=True))
    return raised / jnp.sum(raised, axis=-1, keepdims=True)


def front_kernel(
    dims, x, small, seg_own, w_qkv, w_out, w_gu, cot, mask, cos_h, sin_h,
    small_out, seg_out, heads_out, a_out, raw_out, q_out, k_out, v_out, o_out, x1_out, b_out,
    gate_up, cot_all, mask_all, b_pair, gains, router_pad,
    x_all, small_all, seg_col, heads, a, raw, q, k, v, o, w_o, part, parts_in, cos, sin, seg_row, x1, b_own,
    send, recv, local,
):
    at = Place(*dims)
    net = Net(send, recv, local)
    z, e, group = at.z, at.e, at.group
    tok = x.shape[0]
    length, width = x_all.shape
    mine = z // group
    rows_e, cols = heads.shape[2], heads.shape[3]
    hd = cols - 2 * HEAD_DIM
    n_heads = hd // HEAD_DIM
    q_width = HEADS * HEAD_DIM
    d_slice = w_gu.shape[1]
    scale = HEAD_DIM ** (-0.5)
    block = tok

    def heads_of(dest):
        kv = (dest * n_heads) // (HEADS // KV_HEADS)
        rows = span(e, rows_e)
        return [
            (w_qkv.at[rows, span(dest, hd)], heads.at[z, e, :, pl.ds(0, hd)]),
            (w_qkv.at[rows, span(HEADS + kv, HEAD_DIM)], heads.at[z, e, :, pl.ds(hd, HEAD_DIM)]),
            (w_qkv.at[rows, span(HEADS + KV_HEADS + kv, HEAD_DIM)], heads.at[z, e, :, pl.ds(hd + HEAD_DIM, HEAD_DIM)]),
        ]

    half0, half1 = pl.ds(0, tok), pl.ds(tok, tok)
    first = [
        net.copy(x, x_all.at[span(z, tok)]),
        net.copy(small, small_all.at[z]),
        net.copy(seg_own, seg_col.at[span(z, tok)]),
        net.copy(cos_h, cos),
        net.copy(sin_h, sin),
    ]
    local_heads = [net.copy(s, d) for s, d in heads_of(z)]
    local_cot = [net.copy(cot, cot_all.at[e, half0]), net.copy(mask, mask_all.at[e, half0])]
    load_out = net.copy(w_out, w_o)
    greet(everyone(at))
    got_heads = [net.push(s, d, at.z_dev(t)) for t in range(1, at.n_shard) for s, d in heads_of(z ^ t)]
    got_x = []
    for t in range(1, at.n_shard):
        got_x.append(net.push(small, small_all.at[z], at.z_dev(t)))
        got_x.append(net.push(seg_own, seg_col.at[span(z, tok)], at.z_dev(t)))
    gather_x = Gather(net, at, x, x_all, tok)
    for c in local_heads:
        c.wait()
    arrive(got_heads)
    pieces = [lambda who: heads.at[:, who]]
    heads_state = spread(net, at, pieces)
    other = (z ^ group) // group
    cut = d_slice // 2
    low, high = pl.ds(0, cut), pl.ds(cut, cut)
    pieces_w = [
        (w_gu.at[other, low], gate_up.at[z, low], gate_up.at[z ^ group, low]),
        (w_gu.at[other, high], gate_up.at[z, high], gate_up.at[z ^ group, high]),
    ]
    from_partner = {}

    def fetch_piece(i):
        src, dst, got = pieces_w[i]
        from_partner[i] = (net.push(src, dst, at.z_dev(group)), got)

    for c in first:
        c.wait()
    gather_x.finish(lambda: fetch_piece(0))
    arrive(got_x)

    def hand_on(i):
        copy, ref = from_partner[i]
        copy.wait_recv()
        for t in range(1, group):
            got_w.append(net.push(ref, ref, at.z_dev(t)))

    got_w = []
    for t in range(1, group):
        got_w.append(net.push(w_gu.at[mine], gate_up.at[z], at.z_dev(t)))
    got_cot = [
        net.push(cot, cot_all.at[e, half1], at.z_dev(group)),
        net.push(mask, mask_all.at[e, half1], at.z_dev(group)),
    ]

    gains[...] = jnp.zeros_like(gains)
    router_pad[...] = jnp.zeros_like(router_pad)
    qk = []
    for s in range(at.n_shard):
        rows = small_all[s, 0:16, :].astype(f32)
        gains[0:2, span(s, d_slice)] = rows[0:2]
        router_pad[0 : small.shape[0] - 16, span(s, d_slice)] = small_all[s, 16:, :]
        seg_row[0:1, span(s, tok)] = rows[4:5, :tok]
        qk.append(rows[2:4, :HEAD_DIM])
    qk = sum(qk[1:], qk[0])
    step = 16

    def norm_rows(i, _):
        rows = span(i, step)
        value = x_all[rows, :].astype(f32)
        a[rows, :] = (value * inv_rms(value) * gains[0:1, :]).astype(bf16)
        return 0

    lax.fori_loop(0, length // step, norm_rows, 0)
    fetch_piece(1)
    last = pass_on(net, at, pieces, heads_state)
    arrive(last)
    keep = [net.copy(heads, heads_out), net.copy(a, a_out), net.copy(small_all, small_out), net.copy(seg_col, seg_out)]

    wide = tiled(cols, 256)

    def project(i, _):
        tile = span(i, wide)
        raw[:, tile] = mm(a[...], heads[:, :, :, tile].reshape(width, wide))
        return 0

    lax.fori_loop(0, cols // wide, project, 0)
    keep.append(net.copy(raw, raw_out))

    def head_rows(i, _):
        rows = span(i, block)
        cos_b, sin_b = cos[rows, :], sin[rows, :]
        for h in range(n_heads + 1):
            value = raw[rows, pl.ds(h * HEAD_DIM, HEAD_DIM)]
            gain = qk[0:1] if h < n_heads else qk[1:2]
            value = rope_rows(value * inv_rms(value) * gain, cos_b, sin_b).astype(bf16)
            if h < n_heads:
                q[rows, pl.ds(h * HEAD_DIM, HEAD_DIM)] = value
            else:
                k[rows, :] = value
        v[rows, :] = raw[rows, pl.ds(hd + HEAD_DIM, HEAD_DIM)].astype(bf16)
        return 0

    lax.fori_loop(0, length // block, head_rows, 0)
    keep += [net.copy(q, q_out), net.copy(k, k_out), net.copy(v, v_out)]
    for c in local_cot:
        c.wait()
    arrive(got_cot)
    cots = [lambda who: cot_all.at[who], lambda who: mask_all.at[who]]
    cot_state = spread(net, at, cots)


    def one_head(h, _):
        for i in range(length // block):
            soft = soft_block(q, k, seg_row, seg_col, h, i, block, scale).astype(bf16)
            mixed = mm(soft, v[pl.ds(0, (i + 1) * block), :])
            o[pl.ds(i * block, block), span(h, HEAD_DIM)] = mixed.astype(bf16)
        return 0

    lax.fori_loop(0, n_heads, one_head, 0)
    hand_on(0)
    keep.append(net.copy(o, o_out))
    load_out.wait()
    wide_o = tiled(width, 256)

    def out_tile(i, _):
        tile = span(i, wide_o)
        part[:, tile] = mm(o[...], w_o[:, tile]).astype(bf16)
        return 0

    lax.fori_loop(0, width // wide_o, out_tile, 0)
    summing = Scatter(net, at, part, parts_in, tok, step)
    more = summing.advance()
    hand_on(1)
    slots = summing.finish() if more else summing.last

    def middle_rows(i, _):
        rows = span(i, step)
        total = part[pl.ds(pl.multiple_of(z * tok + i * step, step), step), :].astype(f32)
        for t in slots:
            total += parts_in[t, rows, :].astype(f32)
        value = x_all[pl.ds(pl.multiple_of(z * tok + i * step, step), step), :].astype(f32) + total
        x1[rows, :] = value
        b_own[rows, :] = (value * inv_rms(value) * gains[1:2, :]).astype(bf16)
        return 0

    lax.fori_loop(0, tok // step, middle_rows, 0)
    swap = net.push(b_own, b_pair.at[half1], at.z_dev(group))
    keep += [net.copy(b_own, b_pair.at[half0]), net.copy(x1, x1_out), net.copy(b_own, b_out)]
    last = pass_on(net, at, cots, cot_state)
    swap.wait_recv()
    arrive(last + got_w)
    for c in keep:
        c.wait()
    net.sent()


def expert_kernel(
    dims, b_pair, cot_all, mask_all, gate_up, w_gu_in, w_dn_in, router_t,
    out_part, ggu, gdn, db_in, ex_in, land_dn,
    w_gu, w_dn, rows, cot_t, mask_t, hid, d_pre, d_y, stage, stage_x, own, own_x, core_in, core_x, w_r, d_r, g_tile, d_tile,
    tile_sem, send, recv, local,
):
    at = Place(*dims)
    net = Net(send, recv, local)
    z, e, group = at.z, at.e, at.group
    n_slices, d_slice, ff2 = gate_up.shape
    ff, width = w_dn.shape
    two = b_pair.shape[0]
    four = 2 * two
    mine, other = z // group, (z ^ group) // group
    expert = e * (at.n_shard // group) + mine
    step = 16
    fine = tiled(ff, 256)
    wide = tiled(width, 1024)
    far = z ^ group

    def d_cols(who):
        return w_dn.at[:, span(who, d_slice)]

    pair = net.copy(b_pair, rows.at[0, 1])
    masks = []
    for t in range(at.chips):
        masks.append(net.copy(mask_all.at[at.slot(t, 1)], mask_t.at[t, 0]))
        masks.append(net.copy(mask_all.at[at.slot(t)], mask_t.at[t, 1]))
    loads = [net.copy(w_gu_in.at[mine], w_gu.at[span(z, d_slice)])]
    for k in range(1, n_slices):
        loads.append(net.copy(gate_up.at[z ^ k], w_gu.at[span(z ^ k, d_slice)]))
    load_dn = net.copy(w_dn_in.at[mine], d_cols(z))

    def fetch(t):
        return [
            net.copy(cot_all.at[at.slot(t, 1)], cot_t.at[0]),
            net.copy(cot_all.at[at.slot(t)], cot_t.at[1]),
        ]

    order = list(range(1, at.chips)) + [0]
    fetched = {order[0]: fetch(order[0])}
    greet(
        [at.chip_dev(t) for t in range(1, at.chips)] + [at.mate()] + [at.z_dev(t) for t in range(1, group + 1)]
    )
    from_mate = {0: net.push(b_pair, rows.at[0, 0], at.mate())}
    near = [t for t in (1, 2) if t < at.chips]
    beyond = [t for t in range(1, at.chips) if t not in near]
    from_chip = {t: net.push(b_pair, rows.at[t, 1], at.chip_dev(t)) for t in near}
    half_ff = [pl.ds(0, ff // 2), pl.ds(ff // 2, ff // 2)]

    def dn_part(who, i):
        return w_dn.at[half_ff[i], span(who, d_slice)]

    def fetch_dn(i):
        return net.push(w_dn_in.at[other, half_ff[i]], dn_part(z, i), at.z_dev(group))

    from_partner = [fetch_dn(0)]

    def hand_on(i):
        from_partner[i].wait_recv()
        for t in range(1, group):
            got_dn.append(net.push(dn_part(far, i), dn_part(far, i), at.z_dev(t)))

    got_dn = [net.push(w_dn_in.at[mine], d_cols(z), at.z_dev(t)) for t in range(1, group)]

    relayed = []

    def pass_rows(t):
        if t in from_chip:
            from_chip[t].wait_recv()
        else:
            arrive(relayed)
        from_mate[t] = net.push(rows.at[t, 1], rows.at[t, 0], at.mate())

    lanes = lax.broadcasted_iota(jnp.int32, (four, 128), 1)

    def up_rows(t):
        logits = mm_nt(rows[t].reshape(four, width), router_t[...])
        chosen = mask_t[t].reshape(four, 128).astype(f32) > 0
        masked = jnp.where(chosen, logits, neg_fill)
        raised = jnp.where(chosen, jnp.exp(masked - jnp.max(masked, axis=1, keepdims=True)), 0.0)
        weight = raised / jnp.sum(raised, axis=1, keepdims=True)
        weight = jnp.sum(jnp.where(lanes == expert, weight, 0.0), axis=1, keepdims=True)
        w_r[t] = jnp.broadcast_to(weight, (four, 128))

        def up(j, _):
            tile, tile_u = span(j, fine), pl.ds(pl.multiple_of(ff + j * fine, fine), fine)
            x = rows[t].reshape(four, width)
            g = mm(x, w_gu[:, tile])
            u = mm(x, w_gu[:, tile_u])
            d_pre[t, :, tile] = g.astype(bf16)
            d_pre[t, :, tile_u] = u.astype(bf16)
            hid[t, :, tile] = (g * jax.nn.sigmoid(g) * u).astype(bf16)
            return 0

        lax.fori_loop(0, ff // fine, up, 0)

    for c in masks:
        c.wait()
    pair.wait()
    from_mate[0].wait_recv()
    for c in loads:
        c.wait()
    up_rows(0)
    from_partner.append(fetch_dn(1))
    for i in near:
        pass_rows(i)
        if beyond:
            part = pl.ds((2 - i) * (two // 2), two // 2)
            relayed.append(net.push(rows.at[i, 1, part], rows.at[3, 1, part], at.chip_dev(3 - i)))
    hand_on(0)
    for t in near:
        from_mate[t].wait_recv()
        up_rows(t)
    hand_on(1)
    for t in beyond:
        pass_rows(t)
        from_mate[t].wait_recv()
        up_rows(t)
    load_dn.wait()
    arrive(got_dn)

    mates, outs = {}, []

    def finish(t):
        arrive(mates[t])

        def add_rows(i, _):
            r = span(i, step)
            own[t, r, :] = (own[t, r, :].astype(f32) + core_in[t, r, :].astype(f32)).astype(bf16)
            own_x[t, r, :] = (own_x[t, r, :].astype(f32) + core_x[t, r, :].astype(f32)).astype(bf16)
            return 0

        lax.fori_loop(0, two // step, add_rows, 0)
        if t:
            outs.append(net.push(own.at[t], db_in.at[t], at.chip_dev(t)))
            outs.append(net.push(own_x.at[t], ex_in.at[t], at.chip_dev(t)))

    used = {}
    for i, t in enumerate(order):
        d_r[...] = jnp.zeros_like(d_r)
        for c in fetched[t]:
            c.wait()

        def back_y(n, _, t=t):
            tile = span(n, wide)
            y = mm(hid[t], w_dn[:, tile]).astype(bf16).astype(f32)
            c = cot_t[:, :, tile].reshape(four, wide).astype(f32)
            w = w_r[t, :, 0:1]
            d_r[...] += jnp.broadcast_to(jnp.sum(c * y, axis=1, keepdims=True), (four, 128))
            d_y[t, :, tile] = (w * c).astype(bf16)
            cot_t[:, :, tile] = (w * y).astype(bf16).reshape(2, two, wide)
            return 0

        lax.fori_loop(0, width // wide, back_y, 0)
        kept = [
            net.copy(cot_t.at[0], out_part.at[at.slot(t, 1)]),
            net.copy(cot_t.at[1], out_part.at[at.slot(t)]),
        ]
        if i:
            finish(order[i - 1])

        def back_h(j, _, t=t):
            tile, tile_u = span(j, fine), pl.ds(pl.multiple_of(ff + j * fine, fine), fine)
            d_h = mm_nt(d_y[t], w_dn[tile, :])
            g, u = d_pre[t, :, tile].astype(f32), d_pre[t, :, tile_u].astype(f32)
            sig = jax.nn.sigmoid(g)
            d_pre[t, :, tile] = (d_h * u * sig * (1.0 + g * (1.0 - sig))).astype(bf16)
            d_pre[t, :, tile_u] = (d_h * g * sig).astype(bf16)
            return 0

        lax.fori_loop(0, ff // fine, back_h, 0)
        for c in kept:
            c.wait()
        if i + 1 < at.chips:
            fetched[order[i + 1]] = fetch(order[i + 1])
        p = i % 2
        for c in used.pop(p, []):
            net.done(c)

        def back_b(n, _, t=t, p=p):
            tile = span(n, wide)
            value = mm_nt(d_pre[t], w_gu[tile, :]).astype(bf16)
            stage[p, :, tile] = value[:two]
            own[t, :, tile] = value[two:]
            return 0

        lax.fori_loop(0, width // wide, back_b, 0)
        routed = d_r[...]
        high = routed.astype(bf16)
        low = (routed - high.astype(f32)).astype(bf16)
        none = jnp.zeros_like(high)
        extra = jnp.where(lanes == expert, high, jnp.where(lanes == expert + 64, low, none))
        stage_x[p] = extra[:two]
        own_x[t] = extra[two:]
        mates[t] = [
            net.push(stage.at[p], core_in.at[t], at.mate()),
            net.push(stage_x.at[p], core_x.at[t], at.mate()),
        ]
        used[p] = mates[t]
    finish(order[-1])
    keep = [net.copy(own.at[0], db_in.at[0]), net.copy(own_x.at[0], ex_in.at[0])]

    part = tiled(width, 256)
    per = d_slice // part

    def out_copy(slot, i):
        who = z ^ (n_slices - 1 - i // per)
        return pltpu.make_async_copy(g_tile.at[slot], ggu.at[who, span(i % per, part)], tile_sem.at[slot])

    def grad_up(i, _):
        slot = i % 2

        @pl.when(i >= 2)
        def _():
            out_copy(slot, i - 2).wait()

        who = z ^ (n_slices - 1 - i // per)
        x = rows[:, :, :, span(who * per + i % per, part)].reshape(at.chips * four, part)
        g_tile[slot] = mm_tn(x, d_pre[...].reshape(at.chips * four, ff2)).astype(bf16)
        out_copy(slot, i).start()
        return 0

    def down_copy(slot, i):
        return pltpu.make_async_copy(d_tile.at[slot], gdn.at[span(i, fine)], tile_sem.at[slot])

    def grad_down(i, _):
        slot = i % 2

        @pl.when(i >= 2)
        def _():
            down_copy(slot, i - 2).wait()

        h = hid[:, :, span(i, fine)].reshape(at.chips * four, fine)
        d_tile[slot] = mm_tn(h, d_y[...].reshape(at.chips * four, width)).astype(bf16)
        down_copy(slot, i).start()
        return 0

    n_down = ff // fine
    lax.fori_loop(0, n_down, grad_down, 0)
    for i in range(max(0, n_down - 2), n_down):
        down_copy(i % 2, i).wait()
    for t in range(1, group):
        outs.append(net.push(gdn.at[:, span(z ^ t ^ group, d_slice)], land_dn.at[t - 1], at.z_dev(t)))
    n_up, n_early = width // part, (group - 1) * per
    lax.fori_loop(0, n_early, grad_up, 0)
    for i in range(n_early - 2, n_early):
        out_copy(i % 2, i).wait()

    def grad_rest(i, _):
        slot = i % 2

        @pl.when(i >= n_early + 2)
        def _():
            out_copy(slot, i - 2).wait()

        who = z ^ (n_slices - 1 - i // per)
        x = rows[:, :, :, span(who * per + i % per, part)].reshape(at.chips * four, part)
        g_tile[slot] = mm_tn(x, d_pre[...].reshape(at.chips * four, ff2)).astype(bf16)
        out_copy(slot, i).start()
        return 0

    lax.fori_loop(n_early, n_up, grad_rest, 0)
    for i in range(n_up - 2, n_up):
        out_copy(i % 2, i).wait()
    for c in keep:
        c.wait()
    arrive(outs)
    net.sent()


def norm_kernel(
    dims, early, db, ex, ggu, gdn, out_part, x1, b, cot, mask, router_t, gains,
    gx1, do_all, gain_two, g_router, land_gu, late_gu, land_dn, out_own_sum, out_sum,
    own, own_x, half_out, half_x, swap_in, swap_x, logit, d_out, out_own, out_core, out_in, rw,
    send, recv, local,
):
    at = Place(*dims)
    net = Net(send, recv, local)
    z, e, group = at.z, at.e, at.group
    tok = x1.shape[0]
    n_parts = db.shape[0]
    loads = [net.copy(db, own), net.copy(ex, own_x)]
    load_own = {t: net.copy(out_part.at[at.slot(t)], out_own.at[t]) for t in halves(at)}
    greet(everyone(at))
    step = 16
    for c in loads:
        c.wait()

    def sums(src):
        total, total_x = own[0, src, :].astype(f32), own_x[0, src, :].astype(f32)
        for t in range(1, n_parts):
            total += own[t, src, :].astype(f32)
            total_x += own_x[t, src, :].astype(f32)
        return total, total_x

    def partner(i, _):
        total, total_x = sums(pl.ds(pl.multiple_of(tok + i * step, step), step))
        half_out[span(i, step), :] = total.astype(bf16)
        half_x[span(i, step), :] = total_x.astype(bf16)
        return 0

    lax.fori_loop(0, tok // step, partner, 0)
    swaps = [net.push(half_out, swap_in, at.z_dev(group)), net.push(half_x, swap_x, at.z_dev(group))]
    d_slice = ggu.shape[1]
    landed = []
    for t in range(1, group):
        j = z ^ t ^ group
        landed.append(net.push(ggu.at[j, pl.ds(0, d_slice // 2)], land_gu.at[t - 1], at.z_dev(t)))
        if not early:
            landed.append(net.push(gdn.at[:, span(j, d_slice)], land_dn.at[t - 1], at.z_dev(t)))
        landed.append(net.push(ggu.at[j, pl.ds(d_slice // 2, d_slice // 2)], late_gu.at[t - 1], at.z_dev(t)))
    mates = {t: net.push(out_part.at[at.slot(t, 1)], out_core.at[t], at.mate()) for t in halves(at)}
    logits = mm_nt(b[...], router_t[...])
    chosen = mask[...].astype(f32) > 0
    masked = jnp.where(chosen, logits, neg_fill)
    raised = jnp.where(chosen, jnp.exp(masked - jnp.max(masked, axis=1, keepdims=True)), 0.0)
    rw[...] = raised / jnp.sum(raised, axis=1, keepdims=True)
    outs = []
    for t in halves(at):
        load_own[t].wait()
        mates[t].wait_recv()

        def add(i, _, t=t):
            rows = span(i, step)
            out_own[t, rows, :] = (out_own[t, rows, :].astype(f32) + out_core[t, rows, :].astype(f32)).astype(bf16)
            return 0

        lax.fori_loop(0, 2 * tok // step, add, 0)
        if t:
            outs.append(net.push(out_own.at[t], out_in.at[t - 1], at.chip_dev(t)))
    arrive(swaps)
    gain_two[...] = jnp.zeros_like(gain_two)

    def owner(i, _):
        rows = span(i, step)
        grad, routed = sums(rows)
        grad += swap_in[rows, :].astype(f32)
        routed += swap_x[rows, :].astype(f32)
        routed = routed + pltpu.roll(routed, 64, 1)
        weight = rw[rows, :]
        d_logit = weight * (routed - jnp.sum(weight * routed, axis=1, keepdims=True))
        high = d_logit.astype(bf16)
        low = (d_logit - high.astype(f32)).astype(bf16)
        logit[0, rows, :] = high
        logit[1, rows, :] = low
        grad += mm(high, router_t[...]) + mm(low, router_t[...])
        value = x1[rows, :]
        r = inv_rms(value)
        c = grad * gains[1:2, :]
        back = cot[rows, :].astype(f32) + r * c - value * (r * r * r * jnp.mean(c * value, axis=-1, keepdims=True))
        gx1[rows, :] = back
        d_out[rows, :] = back.astype(bf16)
        gain_two[...] += eight(grad * value * r)
        return 0

    lax.fori_loop(0, tok // step, owner, 0)
    mine = do_all.at[span(z, tok)]
    keep = net.copy(d_out, mine)
    copies = [net.push(d_out, mine, at.z_dev(t)) for t in range(1, at.n_shard)]
    g_router[...] = mm_tn(logit[0], b[...]) + mm_tn(logit[1], b[...])
    arrive(outs)

    def out_rows(i):
        rows = span(i, step)
        total = out_own[0, rows, :].astype(f32)
        for t in range(1, at.chips):
            total += out_in[t - 1, rows, :].astype(f32)
        return total.astype(bf16)

    def own_rows(i, _):
        out_own_sum[span(i, step), :] = out_rows(i)
        return 0

    def partner_rows(i, _):
        out_sum[span(i, step), :] = out_rows(tok // step + i)
        return 0

    lax.fori_loop(0, tok // step, own_rows, 0)
    lax.fori_loop(0, tok // step, partner_rows, 0)
    keep.wait()
    arrive(copies + landed)
    net.sent()


def back_kernel(
    dims, do_h, w_out, o_h, q_h, k_h, v_h, raw_h, cos_h, sin_h, seg_h, a_h, heads_h, ggu, gdn, land_gu, late_gu, land_dn, out_sum,
    out_sum_own, small, x1, gx1, x, gains, gain_two, g_router,
    hidden, g_hidden, small_sum, g_att, g_qkv, two_gu, own_gu, two_dn, own_dn,
    do_all, w_o, o, q, k, v, raw, cos, sin, seg_col, seg_row, mix, d_qkv, dk, dv, qk_gain, a, heads,
    sum_gu, add_gu, sum_dn, add_dn, swap_in, g_out, g_core, g_in, share_own,
    parts_in, g_heads, core_in, chip_in, mine, turn_in, share_qkv, sm, sm_z, sm_core, sm_chip,
    send, recv, local,
):
    at = Place(*dims)
    net = Net(send, recv, local)
    z, e, group = at.z, at.e, at.group
    length, width = do_all.shape
    tok = x1.shape[0]
    cols = raw.shape[1]
    hd = cols - 2 * HEAD_DIM
    n_heads = hd // HEAD_DIM
    rows_e = heads.shape[2]
    d_slice = ggu.shape[1]
    scale = HEAD_DIM ** (-0.5)
    block = tok
    step = 16
    far = z ^ group

    def d_cols(ref, who):
        return ref.at[:, span(who, d_slice)]

    cut = d_slice // 2
    halves_gu = [pl.ds(0, cut), pl.ds(cut, cut)]
    load_gu = [
        [net.copy(ggu.at[far, r], sum_gu.at[i])] + [net.copy(land.at[t - 1], add_gu.at[i, t - 1]) for t in range(1, group)]
        for i, (r, land) in enumerate(zip(halves_gu, (land_gu, late_gu)))
    ]
    load_a = [net.copy(do_h, do_all), net.copy(o_h, o)]
    load_b = [
        net.copy(s, d)
        for s, d in ((w_out, w_o), (q_h, q), (k_h, k), (v_h, v), (raw_h, raw), (cos_h, cos), (sin_h, sin), (seg_h, seg_col))
    ]
    load_c = [net.copy(a_h, a), net.copy(heads_h, heads)]
    load_dn = [net.copy(d_cols(gdn, far), sum_dn)] + [net.copy(land_dn.at[t - 1], add_dn.at[t - 1]) for t in range(1, group)]
    greet(everyone(at))
    swap = net.push(out_sum, swap_in, at.z_dev(group))

    def add_up(total, adds):
        def rows_of(i, _):
            rows = span(i, step)
            value = total[rows, :].astype(f32)
            for t in range(1, group):
                value += adds[t - 1, rows, :].astype(f32)
            total[rows, :] = value.astype(bf16)
            return 0

        lax.fori_loop(0, total.shape[0] // step, rows_of, 0)

    got = []

    def send_half(i):
        for c in load_gu[i]:
            c.wait()
        add_up(sum_gu.at[i], add_gu.at[i])
        got.append(net.push(sum_gu.at[i], two_gu.at[halves_gu[i]], at.z_dev(group)))

    send_half(0)
    for t in range(1, group):
        got.append(net.push(ggu.at[z ^ t], own_gu.at[t - 1], at.z_dev(t)))

    for c in load_a:
        c.wait()
    share = share_own.shape[0]
    wide = tiled(hd, 256)
    each = wide // share

    def out_grad(i, _):
        tile = mm_tn(o[:, span(i, wide)], do_all[...]).astype(bf16)
        for j in range(each):
            g_out[each * i + j] = tile[j * share : (j + 1) * share]
        return 0

    lax.fori_loop(0, hd // wide, out_grad, 0)
    g_mates = {t: net.push(g_out.at[at.slot(t, 1)], g_core.at[t], at.mate()) for t in halves(at)}
    for c in load_b:
        c.wait()
    qk = []
    for s in range(at.n_shard):
        rows = small[s, 0:16, :].astype(f32)
        seg_row[0:1, span(s, tok)] = rows[4:5, :tok]
        qk.append(rows[2:4, :HEAD_DIM])
    qk = sum(qk[1:], qk[0])

    def mix_tile(i, _):
        tile = span(i, wide)
        mix[:, tile] = mm_nt(do_all[...], w_o[tile, :]).astype(bf16)
        return 0

    lax.fori_loop(0, hd // wide, mix_tile, 0)
    g_outs = []
    for t in halves(at):
        g_mates[t].wait_recv()

        def add(i, _, t=t):
            rows = span(i, step)
            s = at.slot(t)
            g_out[s, rows, :] = (g_out[s, rows, :].astype(f32) + g_core[t, rows, :].astype(f32)).astype(bf16)
            return 0

        lax.fori_loop(0, share // step, add, 0)
        if t:
            g_outs.append(net.push(g_out.at[at.slot(t)], g_in.at[t - 1], at.chip_dev(t)))
    send_half(1)

    dk[...] = jnp.zeros_like(dk)
    dv[...] = jnp.zeros_like(dv)
    qk_gain[...] = jnp.zeros_like(qk_gain)

    def one_head(h, _):
        lanes = span(h, HEAD_DIM)
        for i in range(length // block):
            rows, keys = pl.ds(i * block, block), pl.ds(0, (i + 1) * block)
            soft = soft_block(q, k, seg_row, seg_col, h, i, block, scale)
            d_mix = mix[rows, lanes]
            d_soft = mm_nt(d_mix, v[keys, :])
            d_scores = (soft * (d_soft - jnp.sum(soft * d_soft, axis=-1, keepdims=True))).astype(bf16)
            dv[keys, :] += mm_tn(soft.astype(bf16), d_mix)
            dk[keys, :] += mm_tn(d_scores, q[rows, lanes]) * scale
            dq = mm(d_scores, k[keys, :]) * scale
            value = raw[rows, lanes]
            back, per = rms_back(value, qk[0:1], rope_rows_back(dq, cos[rows, :], sin[rows, :]))
            d_qkv[rows, lanes] = back.astype(bf16)
            qk_gain[0:8, :] += eight(per)
        return 0

    lax.fori_loop(0, n_heads, one_head, 0)
    for i in range(length // block):
        rows = pl.ds(i * block, block)
        value = raw[rows, pl.ds(hd, HEAD_DIM)]
        back, per = rms_back(value, qk[1:2], rope_rows_back(dk[rows, :], cos[rows, :], sin[rows, :]))
        d_qkv[rows, pl.ds(hd, HEAD_DIM)] = back.astype(bf16)
        d_qkv[rows, pl.ds(hd + HEAD_DIM, HEAD_DIM)] = dv[rows, :].astype(bf16)
        qk_gain[8:16, :] += eight(per)

    arrive(g_outs)

    def own_share(i, _):
        rows = span(i, step)
        total = g_out[e, rows, :].astype(f32)
        for t in range(1, at.chips):
            total += g_in[t - 1, rows, :].astype(f32)
        share_own[rows, :] = total.astype(bf16)
        return 0

    lax.fori_loop(0, share // step, own_share, 0)
    keep_att = net.copy(share_own, g_att.at[e])
    keep_att.wait()
    atts = [lambda who: g_att.at[who]]
    att_state = spread(net, at, atts)
    for c in load_c:
        c.wait()
    wide_d = tiled(d_slice, 256)
    each_d = wide_d // rows_e

    def grad_tile(s, _):
        for j in range(d_slice // wide_d):
            some = a[:, pl.ds(pl.multiple_of(s * d_slice + j * wide_d, wide_d), wide_d)]
            tile = mm_tn(some, d_qkv[...]).astype(bf16)
            for i in range(each_d):
                g_heads[each_d * j + i, s] = tile[i * rows_e : (i + 1) * rows_e]
        return 0

    lax.fori_loop(0, at.n_shard, grad_tile, 0)
    mates = {t: net.push(g_heads.at[at.slot(t, 1)], core_in.at[t], at.mate()) for t in halves(at)}
    part = do_all

    def rows_tile(s, _):
        for j in range(d_slice // wide_d):
            some = heads[s, pl.ds(each_d * j, each_d)].reshape(wide_d, cols)
            here = pl.ds(pl.multiple_of(s * d_slice + j * wide_d, wide_d), wide_d)
            part[:, here] = mm_nt(d_qkv[...], some).astype(bf16)
        return 0

    lax.fori_loop(0, at.n_shard, rows_tile, 0)
    sums = Scatter(net, at, part, parts_in, tok, step)
    chips = []
    for t in halves(at):
        mates[t].wait_recv()
        who = at.slot(t)

        def add(s, _, t=t, who=who):
            g_heads[who, s] = (g_heads[who, s].astype(f32) + core_in[t, s].astype(f32)).astype(bf16)
            return 0

        lax.fori_loop(0, at.n_shard, add, 0)
        if t:
            chips.append(net.push(g_heads.at[who], chip_in.at[t - 1], at.chip_dev(t)))
    more = sums.advance()
    for c in load_dn:
        c.wait()
    add_up(sum_dn, add_dn)
    swap.wait_recv()

    def hidden_rows(i, _):
        rows = span(i, step)
        hidden[rows, :] = (x1[rows, :] + out_sum_own[rows, :].astype(f32) + swap_in[rows, :].astype(f32)).astype(bf16)
        return 0

    lax.fori_loop(0, tok // step, hidden_rows, 0)
    arrive(chips)

    def total(s, _):
        value = g_heads[e, s].astype(f32)
        for t in range(1, at.chips):
            value += chip_in[t - 1, s].astype(f32)
        mine[s] = value.astype(bf16)
        return 0

    lax.fori_loop(0, at.n_shard, total, 0)
    turns = [net.push(mine.at[z ^ t], turn_in.at[z], at.z_dev(t)) for t in range(1, at.n_shard)]
    turn_own = net.copy(mine.at[z], turn_in.at[z])
    got.append(net.push(sum_dn, two_dn, at.z_dev(group)))
    for t in range(1, group):
        got.append(net.push(d_cols(gdn, z ^ t), own_dn.at[t - 1], at.z_dev(t)))
    slots = sums.finish() if more else sums.last
    sm[...] = jnp.zeros_like(sm)
    gain_one = jnp.zeros((8, width), f32)

    def owner(i, gain_one):
        rows = span(i, step)
        here = pl.ds(pl.multiple_of(z * tok + i * step, step), step)
        da = part[here, :].astype(f32)
        for t in slots:
            da += parts_in[t, rows, :].astype(f32)
        back, per = rms_back(x[rows, :].astype(f32), gains[0:1, :], da)
        g_hidden[rows, :] = gx1[rows, :] + back
        return gain_one + eight(per)

    gain_one = lax.fori_loop(0, tok // step, owner, gain_one)
    row_one = jnp.sum(gain_one, axis=0, keepdims=True)
    row_two = jnp.sum(gain_two[...], axis=0, keepdims=True)
    row_q = jnp.sum(qk_gain[0:8, :], axis=0, keepdims=True)
    row_k = jnp.sum(qk_gain[8:16, :], axis=0, keepdims=True)
    for s in range(at.n_shard):
        piece = pl.ds(s * d_slice, d_slice)
        lanes = slice(s * d_slice, (s + 1) * d_slice)
        sm[s, 0:1, :] = row_one[:, lanes]
        sm[s, 1:2, :] = row_two[:, lanes]
        sm[s, 2:3, pl.ds(0, HEAD_DIM)] = row_q
        sm[s, 3:4, pl.ds(0, HEAD_DIM)] = row_k
        sm[s, 8:, :] = g_router[0 : sm.shape[1] - 8, piece]
    small_z = [net.push(sm.at[z ^ t], sm_z.at[t - 1], at.z_dev(t)) for t in range(1, at.n_shard)]
    turn_own.wait()
    arrive(turns)
    for s in range(at.n_shard):
        share_qkv[:, pl.ds(s * hd, hd)] = turn_in[s, :, pl.ds(0, hd)]
    for m in range(KV_HEADS):
        some = [s for s in range(at.n_shard) if (s * n_heads) // (HEADS // KV_HEADS) == m]
        for first, to in ((hd, HEADS + m), (hd + HEAD_DIM, HEADS + KV_HEADS + m)):
            value = turn_in[some[0], :, pl.ds(first, HEAD_DIM)].astype(f32)
            for s in some[1:]:
                value += turn_in[s, :, pl.ds(first, HEAD_DIM)].astype(f32)
            share_qkv[:, pl.ds(to * HEAD_DIM, HEAD_DIM)] = value.astype(bf16)
    keep = net.copy(share_qkv, g_qkv.at[e])
    keep.wait()
    if at.chips == 4:
        go_on = spread_near(net, at, g_qkv)
    else:
        qkvs = [lambda who: g_qkv.at[who]]
        state = spread(net, at, qkvs)
        go_on = functools.partial(pass_on, net, at, qkvs, state)
    last = pass_on(net, at, atts, att_state)
    arrive(small_z)
    value = sm[z]
    for t in range(1, at.n_shard):
        value += sm_z[t - 1]
    sm[z] = value
    c = net.push(sm.at[z], sm_core, at.mate())
    c.wait_recv()
    sm_core[...] = sm[z] + sm_core[...]
    smalls = [net.push(sm_core, sm_chip.at[t - 1], at.chip_dev(t)) for t in range(1, at.chips)]
    last += go_on()
    arrive(smalls)
    value = sm_core[...]
    for t in range(1, at.chips):
        value += sm_chip[t - 1]
    small_sum[...] = value
    arrive(last + got)
    net.sent()


def shards(
    hidden_in,
    segments,
    routes,
    norm_gains,
    qk_gains,
    w_qkv,
    w_attn_out,
    w_router,
    w_gate_up,
    w_down,
    cotangent,
):
    n_expert = lax.axis_size("expert")
    n_shard = lax.axis_size("shard")
    me_e = lax.axis_index("expert")
    me_z = lax.axis_index("shard")
    tok, width = hidden_in.shape
    exp_dev = w_gate_up.shape[1]
    experts_all = w_router.shape[2]
    d_slice, ff2 = w_gate_up.shape[2:]
    ff = ff2 // 2
    group = n_shard // exp_dev
    mine = me_z // group
    length = n_shard * tok
    h_dev = HEADS // n_shard
    hd = h_dev * HEAD_DIM
    cols = hd + 2 * HEAD_DIM
    qkv_cols = w_qkv.shape[2]
    rows_e = d_slice // n_expert
    share = hd // n_expert
    chips = n_expert // 2
    qk_part = HEAD_DIM // n_shard
    dims = (n_expert, n_shard, group)
    n_small = 16 + experts_all
    sds = jax.ShapeDtypeStruct
    vm = pltpu.VMEM
    any_spec = pl.BlockSpec(memory_space=pl.ANY)
    vmem_spec = pl.BlockSpec(memory_space=pltpu.VMEM)

    lane = jnp.arange(HEAD_DIM, dtype=jnp.int32)
    qk_placed = jnp.where((lane // qk_part == me_z)[None], jnp.tile(qk_gains[0], (1, n_shard)), jnp.zeros((), bf16))
    small = jnp.concatenate(
        [
            norm_gains[0],
            jnp.pad(qk_placed, ((0, 0), (0, d_slice - HEAD_DIM))),
            jnp.pad(segments.astype(bf16)[None], ((0, 11), (0, d_slice - tok))),
            w_router[0].T,
        ],
        axis=0,
    )
    seg_own = jnp.broadcast_to(segments.astype(f32)[:, None], (tok, 128))
    ids = jnp.arange(128, dtype=jnp.int32)
    mask = jnp.sum((routes[:, :, None] == ids[None, None, :]).astype(f32), axis=1).astype(bf16)
    cos, sin = rotary_tables(length)

    outs = [
        sds((n_shard, n_small, d_slice), bf16),
        sds((length, 128), f32),
        sds((n_shard, n_expert, rows_e, cols), bf16),
        sds((length, width), bf16),
        sds((length, cols), f32),
        sds((length, hd), bf16),
        sds((length, HEAD_DIM), bf16),
        sds((length, HEAD_DIM), bf16),
        sds((length, hd), bf16),
        sds((tok, width), f32),
        sds((tok, width), bf16),
        sds((n_shard, d_slice, ff2), bf16),
        sds((n_expert, 2 * tok, width), bf16),
        sds((n_expert, 2 * tok, 128), bf16),
        sds((2 * tok, width), bf16),
        sds((8, width), f32),
        sds((128, width), bf16),
    ]
    front = comm_call(
        functools.partial(front_kernel, dims),
        0,
        160,
        40,
        [
            vm((length, width), bf16),
            vm((n_shard, n_small, d_slice), bf16),
            vm((length, 128), f32),
            vm((n_shard, n_expert, rows_e, cols), bf16),
            vm((length, width), bf16),
            vm((length, cols), f32),
            vm((length, hd), bf16),
            vm((length, HEAD_DIM), bf16),
            vm((length, HEAD_DIM), bf16),
            vm((length, hd), bf16),
            vm((hd, width), bf16),
            vm((length, width), bf16),
            vm((n_shard - 1, tok, width), bf16),
            vm((length, HEAD_DIM), f32),
            vm((length, HEAD_DIM), f32),
            vm((8, length), f32),
            vm((tok, width), f32),
            vm((tok, width), bf16),
        ],
        outs,
        56,
        out_specs=[any_spec] * (len(outs) - 2) + [vmem_spec] * 2,
    )
    (small_all, seg_col, heads, a, raw, q, k, v, o, x1, b, gate_up, cot_all, mask_all, b_pair, gains, router_pad) = front(
        hidden_in, small, seg_own, w_qkv[0], w_attn_out[0], w_gate_up[0], cotangent, mask, cos, sin
    )
    router_t = router_pad[:experts_all]

    def route_weights(rows, chosen):
        logits = mm_nt(rows, router_t)
        masked = jnp.where(chosen, logits, neg_fill)
        raised = jnp.where(chosen, jnp.exp(masked - jnp.max(masked, axis=1, keepdims=True)), 0.0)
        return raised / jnp.sum(raised, axis=1, keepdims=True)

    per_e = (n_expert, 2 * tok)
    piece = (chips, 2 * tok)
    four = 4 * tok
    if chips <= 4:
        out_part, grad_gate_up, grad_down, db_in, ex_in, land_dn = comm_call(
            functools.partial(expert_kernel, dims),
            4,
            60,
            60,
            [
                vm((width, ff2), bf16),
                vm((ff, width), bf16),
                vm((chips, 2, 2 * tok, width), bf16),
                vm((2, 2 * tok, width), bf16),
                vm((chips, 2, 2 * tok, 128), bf16),
                vm((chips, four, ff), bf16),
                vm((chips, four, ff2), bf16),
                vm((chips, four, width), bf16),
                vm((2, 2 * tok, width), bf16),
                vm((2, 2 * tok, 128), bf16),
                vm(piece + (width,), bf16),
                vm(piece + (128,), bf16),
                vm(piece + (width,), bf16),
                vm(piece + (128,), bf16),
                vm((chips, four, 128), f32),
                vm((four, 128), f32),
                vm((2, tiled(width, 256), ff2), bf16),
                vm((2, tiled(ff, 256), width), bf16),
                pltpu.SemaphoreType.DMA((2,)),
            ],
            [
                sds(per_e + (width,), bf16),
                sds((n_shard, d_slice, ff2), bf16),
                sds((ff, width), bf16),
                sds(piece + (width,), bf16),
                sds(piece + (128,), bf16),
                sds((group - 1, ff, d_slice), bf16),
            ],
            60,
            in_specs=[any_spec] * 6 + [vmem_spec],
        )(b_pair, cot_all, mask_all, gate_up, w_gate_up[0], w_down[0], router_pad)
    else:
        rows_all = n_expert * 2 * tok
        w_mine = lax.dynamic_index_in_dim(w_gate_up[0], mine, 0, keepdims=False)
        gate_up = lax.dynamic_update_index_in_dim(gate_up, w_mine, me_z, 0)
        down = lax.all_gather(w_down[0], "shard", axis=2, tiled=True)
        down = lax.dynamic_index_in_dim(down, mine, 0, keepdims=False)
        b_rows = lax.all_gather(b_pair, "expert", axis=0, tiled=True)
        my_expert = me_e * exp_dev + mine
        rw_all = route_weights(b_rows, mask_all.reshape(rows_all, 128)[:, :experts_all] > 0)
        is_mine = ids[:experts_all] == my_expert
        rw_mine = jnp.sum(jnp.where(is_mine[None, :], rw_all, 0.0), axis=1, keepdims=True)
        w_gu = gate_up.reshape(width, ff2)
        pre = mm(b_rows, w_gu)
        g, u = pre[:, :ff], pre[:, ff:]
        sig = jax.nn.sigmoid(g)
        act = g * sig
        hidden = (act * u).astype(bf16)
        y_f = mm(hidden, down).astype(bf16).astype(f32)
        cot_f = cot_all.reshape(rows_all, width).astype(f32)
        d_route = jnp.sum(cot_f * y_f, axis=1, keepdims=True)
        out_part = (rw_mine * y_f).astype(bf16)
        d_y = (rw_mine * cot_f).astype(bf16)
        d_hidden = mm_nt(d_y, down)
        d_pre = jnp.concatenate(
            [d_hidden * u * sig * (1.0 + g * (1.0 - sig)), d_hidden * act], axis=1
        ).astype(bf16)
        d_b = mm_nt(d_pre, w_gu).astype(bf16)
        grad_down = mm_tn(hidden, d_y).astype(bf16)
        grad_gate_up = mm_tn(b_rows, d_pre).astype(bf16).reshape(n_shard, d_slice, ff2)
        high = lax.reduce_precision(d_route, 8, 7)
        low = d_route - high
        extra = jnp.where(ids[None] == my_expert, high, jnp.where(ids[None] == my_expert + 64, low, 0.0)).astype(bf16)

        def home(value):
            return lax.psum_scatter(value, "expert", scatter_dimension=0, tiled=True)[None]

        db_in, ex_in = home(d_b), home(extra)

    n_parts = db_in.shape[0]
    early = chips <= 4
    gx1, d_o, gain_two, g_router, land_gu, late_gu, norm_dn, out_own_sum, out_sum = comm_call(
        functools.partial(norm_kernel, dims, early),
        1,
        60,
        24,
        [
            vm((n_parts, 2 * tok, width), bf16),
            vm((n_parts, 2 * tok, 128), bf16),
            vm((tok, width), bf16),
            vm((tok, 128), bf16),
            vm((tok, width), bf16),
            vm((tok, 128), bf16),
            vm((2, tok, 128), bf16),
            vm((tok, width), bf16),
            vm(piece + (width,), bf16),
            vm(piece + (width,), bf16),
            vm((chips - 1, 2 * tok, width), bf16),
            vm((tok, 128), f32),
        ],
        [
            sds((tok, width), f32),
            sds((length, width), bf16),
            sds((8, width), f32),
            sds((128, width), f32),
            sds((group - 1, d_slice // 2, ff2), bf16),
            sds((group - 1, d_slice // 2, ff2), bf16),
            sds((group - 1, ff, d_slice), bf16) if not early else sds((16, 128), bf16),
            sds((tok, width), bf16),
            sds((tok, width), bf16),
        ],
        60,
        in_specs=[any_spec] * 5 + [vmem_spec] * 6,
        out_specs=[vmem_spec, any_spec, vmem_spec, vmem_spec] + [any_spec] * 3 + [vmem_spec] * 2,
    )(db_in, ex_in, grad_gate_up, grad_down, out_part.reshape(per_e + (width,)), x1, b, cotangent, mask, router_pad, gains)
    if not early:
        land_dn = norm_dn

    small_rows = (8 + -(-experts_all // 8) * 8, d_slice)
    hidden_out, grad_hidden, sums, grad_out, grad_qkv, two_gu, own_gu, two_dn, own_dn = comm_call(
        functools.partial(back_kernel, dims),
        2,
        140,
        60,
        [
            vm((length, width), bf16),
            vm((hd, width), bf16),
            vm((length, hd), bf16),
            vm((length, hd), bf16),
            vm((length, HEAD_DIM), bf16),
            vm((length, HEAD_DIM), bf16),
            vm((length, cols), f32),
            vm((length, HEAD_DIM), f32),
            vm((length, HEAD_DIM), f32),
            vm((length, 128), f32),
            vm((8, length), f32),
            vm((length, hd), bf16),
            vm((length, cols), bf16),
            vm((length, HEAD_DIM), f32),
            vm((length, HEAD_DIM), f32),
            vm((16, HEAD_DIM), f32),
            vm((length, width), bf16),
            vm((n_shard, n_expert, rows_e, cols), bf16),
            vm((2, d_slice // 2, ff2), bf16),
            vm((2, group - 1, d_slice // 2, ff2), bf16),
            vm((ff, d_slice), bf16),
            vm((group - 1, ff, d_slice), bf16),
            vm((tok, width), bf16),
            vm((n_expert, share, width), bf16),
            vm((chips, share, width), bf16),
            vm((chips - 1, share, width), bf16),
            vm((share, width), bf16),
            vm((n_shard - 1, tok, width), bf16),
            vm((n_expert, n_shard, rows_e, cols), bf16),
            vm((chips, n_shard, rows_e, cols), bf16),
            vm((chips - 1, n_shard, rows_e, cols), bf16),
            vm((n_shard, rows_e, cols), bf16),
            vm((n_shard, rows_e, cols), bf16),
            vm((rows_e, qkv_cols), bf16),
            vm((n_shard,) + small_rows, f32),
            vm((n_shard - 1,) + small_rows, f32),
            vm(small_rows, f32),
            vm((chips - 1,) + small_rows, f32),
        ],
        [
            sds((tok, width), bf16),
            sds((tok, width), f32),
            sds(small_rows, f32),
            sds((n_expert, share, width), bf16),
            sds((n_expert, rows_e, qkv_cols), bf16),
            sds((d_slice, ff2), bf16),
            sds((group - 1, d_slice, ff2), bf16),
            sds((ff, d_slice), bf16),
            sds((group - 1, ff, d_slice), bf16),
        ],
        60,
        in_specs=[any_spec] * 18 + [vmem_spec] * 8,
        out_specs=[vmem_spec] * 3 + [any_spec] * 6,
    )(
        d_o,
        w_attn_out[0],
        o,
        q,
        k,
        v,
        raw,
        cos,
        sin,
        seg_col,
        a,
        heads,
        grad_gate_up,
        grad_down,
        land_gu,
        late_gu,
        land_dn,
        out_sum,
        out_own_sum,
        small_all,
        x1,
        gx1,
        hidden_in,
        gains,
        gain_two,
        g_router,
    )

    def settle(own, others, other):
        is_own = jnp.arange(exp_dev, dtype=jnp.int32)[:, None, None] == mine
        total = jnp.where(is_own, own[None], other[None]).astype(f32)
        for t in range(group - 1):
            total += jnp.where(is_own, others[t][None], jnp.zeros((), bf16)).astype(f32)
        return total[None]

    own_gate_up = lax.dynamic_index_in_dim(grad_gate_up, me_z, 0, keepdims=False)
    own_down = lax.dynamic_slice_in_dim(grad_down, me_z * d_slice, d_slice, 1)
    qk_grad = lax.dynamic_slice_in_dim(sums[2:4, :HEAD_DIM], me_z * qk_part, qk_part, 1)
    return (
        hidden_out,
        grad_hidden,
        sums[0:2][None],
        qk_grad[None],
        grad_qkv.reshape(d_slice, qkv_cols).astype(f32)[None],
        grad_out.reshape(hd, width).astype(f32)[None],
        sums[8 : 8 + experts_all].T[None],
        settle(own_gate_up, own_gu, two_gu),
        settle(own_down, own_dn, two_dn),
    )


def solution(mesh):
    in_specs = (
        P(("expert", "shard"), None),
        P(("expert", "shard")),
        P(("expert", "shard"), None),
        P(None, None, "shard"),
        P(None, None, "shard"),
        P(None, "shard", None),
        P(None, "shard", None),
        P(None, "shard", None),
        P(None, "expert", "shard", None),
        P(None, "expert", None, "shard"),
        P(("expert", "shard"), None),
    )
    out_specs = (
        P(("expert", "shard"), None),
        P(("expert", "shard"), None),
        P(None, None, "shard"),
        P(None, None, "shard"),
        P(None, "shard", None),
        P(None, "shard", None),
        P(None, "shard", None),
        P(None, "expert", "shard", None),
        P(None, "expert", None, "shard"),
    )
    return jax.shard_map(shards, mesh=mesh, in_specs=in_specs, out_specs=out_specs, check_vma=False)
```
